32 devices in a mesh: groups: 2 (over y), pass: 16 (over z, x, core).
Axes of the slice: x: 2, y: 2, z: 4, core: 2. Of those that a mesh axis runs over, the one named last changes fastest.
Arguments:
- passage_states: bfloat16 [128, 128, 4096], P(('groups', 'pass')), parts along dimension 0, may hold values from -500 to 500
- memory_queries: bfloat16 [32, 4096], replicated, may hold values from -6 to 6
- memory_gain: bfloat16 [4096], replicated, may hold values from 0.099609375 to 1.8984375
- kv_weight: bfloat16 [4096, 512], P('pass'), may hold values from -0.09375 to 0.09375
- retrieval: int32 [128, 16], P(('groups', 'pass')), parts along dimension 0, may hold values from 0 to 63, as said below
- question_queries: bfloat16 [128, 64, 7424], P(('groups', 'pass')), parts along dimension 0, may hold values from -6 to 6
- question_kv: bfloat16 [128, 64, 512], P(('groups', 'pass')), parts along dimension 0, may hold values from -500 to 500
- question_lengths: int32 [128], P(('groups', 'pass')), parts along dimension 0, may hold values from 1 to 64, 3072 in all
Outputs:
- context: bfloat16 [128, 64, 7424], P(('groups', 'pass')), parts along dimension 0
The draws below stay inside these ranges and needn't reach their ends.
There are 2 independent parts, one for each index of `groups`. The reference program is written for one: setup_inputs(seed, part) draws one part's arguments, and reference() takes and returns one part's arrays. A program takes and returns all parts, laid end to end along the dimension named above; an argument that names none is the same for every part. Nothing has to cross between parts.
Inputs may be any that keep to these rules, and one draw needn't show every extreme that they name: `retrieval`: passage id p is the (p % 4)-th passage of device p // 4. The 16 ids of one query lie on 16 different devices; the 64 ids of one device's queries name each device's passages at most 4 times in all, and some device's exactly 4 times.
All inputs are finite; a program needn't handle non-finite values. No bound on the sum of `question_lengths` on one device may be relied on, other than what follows from the above.
Results may differ from the reference program's by a relative error of at most 0.0065.
Values may be sent and summed in bfloat16 or wider, within the bound.
No kernel may reach another device: no remote copies, remote signals or barrier semaphores. Data moves between devices by JAX's collectives and lax.ppermute only.
A program may use at most 128 MiB of HBM per device.

```python
import math
import jax
import jax.numpy as jnp
import numpy as np
from jax import lax

D = 4096
CH = 32
CHD = 128
MEM = 32
LEN = 128
P_DEV = 4
QRY_DEV = 4
QLEN = 64
TOPK = 16
H = 116
HD = 64
KVH = 4
GROUP = 29
KVW = 512
PASSAGES = 64
QUERIES = 64


def draw_passage_states(key, part):
    key = jax.random.fold_in(key, 3)
    key_base, key_chan, key_token = jax.random.split(key, 3)
    channel_scale = jnp.exp(jax.random.uniform(key_chan, (D,), jnp.float32, -1.15, 1.15))
    token_scale = jnp.exp(jax.random.uniform(key_token, (PASSAGES, LEN, 1), jnp.float32, -1.15, 1.15))
    base_values = jax.random.normal(key_base, (PASSAGES, LEN, D), jnp.float32)
    return jnp.clip(base_values * channel_scale * token_scale, -500.0, 500.0).astype(jnp.bfloat16)


def draw_question_kv(key, part):
    key = jax.random.fold_in(key, 5)
    key_base = jax.random.fold_in(key, 0)
    base_values = jax.random.normal(key_base, (QUERIES, QLEN, KVW), jnp.float32)
    return jnp.clip(base_values, -6.0, 6.0).astype(jnp.bfloat16)


def draw_retrieval(key, part):
    key = jax.random.fold_in(key, 7)
    owner_total = PASSAGES // P_DEV
    request_count = QRY_DEV * TOPK
    split_keys = jax.random.split(key, owner_total + 1)
    orders = jax.vmap(lambda single: jax.random.permutation(single, owner_total))(split_keys[:owner_total])
    slot_owner = jnp.arange(request_count) % owner_total
    owners = orders[:, slot_owner]
    local_index = jax.random.randint(split_keys[owner_total], (owner_total, request_count), 0, P_DEV)
    passage_ids = owners * P_DEV + local_index
    return passage_ids.reshape(QUERIES, TOPK).astype(jnp.int32)


def level_of(own_key, shape, pieces, smallest, top_value):
    gain, own = 1.0, jax.random.fold_in(own_key, 6)
    for axis_at, blocks in pieces:
        steps = jnp.exp(jax.random.uniform(jax.random.fold_in(own, axis_at), (blocks,), jnp.float32, smallest / len(pieces), top_value / len(pieces)))
        gain = gain * jnp.repeat(steps, shape[axis_at] // blocks).reshape([-1 if axis == axis_at else 1 for axis in range(len(shape))])
    return gain


def profile(count, total, most, slope):
    weights = [(1 << 20) // math.isqrt(grade ** slope) + 1 for grade in range(2, count + 1)]
    surplus, given = total - most - (count - 1), [1] * (count - 1)
    while surplus > 0:
        free = [i for i in range(count - 1) if given[i] < most]
        whole, budget = sum([weights[i] for i in free]), surplus
        for i in free:
            extra = min(most - given[i], max(1, budget * weights[i] // whole), surplus)
            given[i] = given[i] + extra
            surplus = surplus - extra
    return np.array([most] + given)


def uneven(rng, number_of, total, reach, lean):
    if number_of == 2:
        one = jax.random.randint(rng, (), max(1, total - reach), min(reach, total - 1) + 1)
        return jnp.stack([one, total - one])
    sizes = jnp.asarray(profile(number_of, total, reach, lean), jnp.int32)
    pairs = (number_of - 1) // 2
    source_of, receiver = sizes[1:1 + 2 * pairs:2], sizes[2:2 + 2 * pairs:2]
    room = jnp.minimum(source_of - 1, reach - receiver)
    passed = jax.random.randint(jax.random.fold_in(rng, 1), (pairs,), 0, 1 << 20) % (room + 1)
    sizes = sizes.at[1:1 + 2 * pairs:2].set(source_of - passed).at[2:2 + 2 * pairs:2].set(receiver + passed)
    return sizes[jax.random.permutation(jax.random.fold_in(rng, 2), number_of)]


def centred(rng, extent, spread, bound, pieces=(), kind=jnp.bfloat16):
    drawn = spread * jax.random.normal(rng, extent, jnp.float32)
    if pieces:
        drawn = drawn * level_of(rng, extent, pieces, -0.22, 0.18)
    return jnp.clip(drawn, -bound, bound).astype(kind)


def setup_inputs(seed: int = 0, part: int = 0) -> dict:
    key_of = jax.random.split(jax.random.key(seed), 9)
    part_splits = jax.random.split(jax.random.fold_in(key_of[8], part), 9)
    return {
        "passage_states": draw_passage_states(jax.random.fold_in(jax.random.fold_in(key_of[8], part), 71), part),
        "memory_queries": centred(key_of[1], (MEM, D), 1.0, 6.0),
        "memory_gain": jnp.clip(1.0 + 0.18 * jax.random.normal(key_of[2], (D,), jnp.float32), 0.099609375, 1.8984375).astype(jnp.bfloat16),
        "kv_weight": centred(key_of[3], (D, KVW), D ** -0.5, 0.09375, ((0, 16),)),
        "retrieval": draw_retrieval(jax.random.fold_in(jax.random.fold_in(key_of[8], part), 71), part),
        "question_queries": centred(part_splits[5], (QUERIES, QLEN, H * HD), 1.0, 6.0, ((0, 16),)),
        "question_kv": draw_question_kv(jax.random.fold_in(jax.random.fold_in(key_of[8], part), 71), part),
        "question_lengths": uneven(part_splits[7], QUERIES, QUERIES * QLEN * 3 // 4, QLEN, 2).astype(jnp.int32),
    }


def compress_passage(states, memory_queries, memory_gain):
    token_heads = states.astype(jnp.float32).reshape(LEN, CH, CHD)
    query_heads = memory_queries.astype(jnp.float32).reshape(MEM, CH, CHD)
    scores = jnp.einsum('rhc,thc->hrt', query_heads, token_heads) * (1.0 / math.sqrt(CHD))
    weights = jax.nn.softmax(scores, axis=-1).astype(jnp.bfloat16)
    pooled = jnp.einsum('hrt,thc->rhc', weights.astype(jnp.float32), token_heads).reshape(MEM, D)
    mean_square = lax.optimization_barrier(jnp.mean(pooled * pooled, axis=-1, keepdims=True))
    normed = pooled * lax.rsqrt(mean_square + 1e-06) * memory_gain.astype(jnp.float32)
    return normed.astype(jnp.bfloat16)

def key_mask(length, memory_count):
    position = jnp.arange(QLEN)
    causal = (position[None, :] <= position[:, None]) & (position[None, :] < length)
    return jnp.concatenate([jnp.ones((QLEN, memory_count), dtype=bool), causal], axis=1)

def attend_query(question, memory_kv, own_kv, length):
    half_width = KVH * HD
    key_rows = jnp.concatenate([memory_kv[:, :half_width], own_kv[:, :half_width]], axis=0)
    value_rows = jnp.concatenate([memory_kv[:, half_width:], own_kv[:, half_width:]], axis=0)
    key_rows = key_rows.astype(jnp.float32).reshape(-1, KVH, HD)
    value_rows = value_rows.astype(jnp.float32).reshape(-1, KVH, HD)
    query_heads = question.astype(jnp.float32).reshape(QLEN, KVH, GROUP, HD)
    scores = jnp.einsum('tgjd,sgd->gjts', query_heads, key_rows) * (1.0 / math.sqrt(HD))
    visible = key_mask(length, memory_kv.shape[0])
    scores = jnp.where(visible, scores, -jnp.inf)
    weights = jax.nn.softmax(scores, axis=-1).astype(jnp.bfloat16)
    context = jnp.einsum('gjts,sgd->tgjd', weights.astype(jnp.float32), value_rows).reshape(QLEN, H * HD)
    alive_rows = jnp.arange(QLEN) < length
    return jnp.where(alive_rows[:, None], context, 0.0).astype(jnp.bfloat16)

def reference(passage_states, memory_queries, memory_gain, kv_weight, retrieval, question_queries, question_kv, question_lengths):
    memory_rows = lax.map(lambda states: compress_passage(states, memory_queries, memory_gain), passage_states)
    projected = jnp.dot(memory_rows.reshape(PASSAGES * MEM, D), kv_weight, preferred_element_type=jnp.float32)
    memory_kv = projected.astype(jnp.bfloat16).reshape(PASSAGES, MEM, KVW)

    def answer(inputs):
        passage_ids, question, own_kv, length = inputs
        chosen = jnp.take(memory_kv, passage_ids, axis=0).reshape(TOPK * MEM, KVW)
        return attend_query(question, chosen, own_kv, length)
    return lax.map(answer, (retrieval, question_queries, question_kv, question_lengths))
```

```python
import functools
import math

import jax
import jax.numpy as jnp
from jax import lax
from jax.experimental import pallas as pl
from jax.experimental.pallas import tpu as pltpu
from jax.sharding import PartitionSpec as P

D = 4096
CH = 32
CHD = 128
MEM = 32
LEN = 128
QLEN = 64
TOPK = 16
H = 116
HD = 64
KVH = 4
GROUP = 29
KVW = 512

LANES = 2 * HD
PAIRS = GROUP
HALF = PAIRS * LANES
ROWS = TOPK * MEM
KEYS = 2 * (ROWS + QLEN)
NEG = -1e30
VMEM_LIMIT = 52 * 1024 * 1024


def pool_kernel(states_ref, queries_ref, gain_ref, out_ref, pooled):
    squares = jnp.zeros((MEM, CHD), jnp.float32)
    for head in range(CH):
        span = slice(head * CHD, (head + 1) * CHD)
        tokens = states_ref[0, :, span]
        scores = lax.dot_general(
            queries_ref[:, span], tokens, (((1,), (1,)), ((), ())),
            preferred_element_type=jnp.float32,
        ) * (1.0 / math.sqrt(CHD))
        scores = jnp.exp(scores - jnp.max(scores, axis=1, keepdims=True))
        weights = scores / jnp.sum(scores, axis=1, keepdims=True)
        part = jnp.dot(weights.astype(jnp.bfloat16), tokens, preferred_element_type=jnp.float32)
        pooled[:, span] = part
        squares += part * part
    mean_square = jnp.sum(squares, axis=1, keepdims=True) * (1.0 / D)
    scale = lax.rsqrt(mean_square + 1e-06)
    out_ref[0] = (pooled[...] * scale * gain_ref[...].astype(jnp.float32)).astype(jnp.bfloat16)


def pool(states, queries, gain):
    count = states.shape[0]
    return pl.pallas_call(
        pool_kernel,
        grid=(count,),
        in_specs=[
            pl.BlockSpec((1, LEN, D), lambda p: (p, 0, 0)),
            pl.BlockSpec((MEM, D), lambda p: (0, 0)),
            pl.BlockSpec((1, D), lambda p: (0, 0)),
        ],
        out_specs=pl.BlockSpec((1, MEM, D), lambda p: (p, 0, 0)),
        out_shape=jax.ShapeDtypeStruct((count, MEM, D), jnp.bfloat16),
        scratch_shapes=[pltpu.VMEM((MEM, D), jnp.float32)],
        compiler_params=pltpu.CompilerParams(vmem_limit_bytes=VMEM_LIMIT),
        cost_estimate=pl.CostEstimate(
            flops=4 * count * MEM * LEN * D, bytes_accessed=2 * count * LEN * D,
            transcendentals=count * CH * MEM * LEN,
        ),
        name="pool",
    )(states, queries, gain.reshape(1, D))


def attend_kernel(
    start_ref, length_ref, q_ref, k_ref, v_ref, own_k_ref, own_v_ref, out_ref,
    keys, values, key_side, value_side,
):
    first = (pl.program_id(0) == 0) & (pl.program_id(1) == 0)
    query = pl.program_id(1)

    @pl.when(first)
    def _():
        key_side[...] = jnp.zeros_like(key_side)
        lane = lax.broadcasted_iota(jnp.int32, (KEYS, LANES), 1)
        row = lax.broadcasted_iota(jnp.int32, (KEYS, LANES), 0)
        in_b = ((row >= ROWS) & (row < 2 * ROWS)) | (row >= 2 * ROWS + QLEN)
        ones = jnp.where((lane >= HD) == in_b, 1.0, 0.0).astype(jnp.bfloat16)
        for kind in range(3):
            value_side[kind, :, LANES:] = ones

    for slot in range(TOPK):
        start = pl.multiple_of(start_ref[query, slot], MEM)
        keys[slot * MEM:(slot + 1) * MEM, :] = k_ref[pl.ds(start, MEM), :].astype(jnp.float32)
        values[slot * MEM:(slot + 1) * MEM, :] = v_ref[pl.ds(start, MEM), :].astype(jnp.float32)
    length = length_ref[query]

    turned = jnp.transpose(keys[...]).astype(jnp.bfloat16)
    own_k = own_k_ref[0].astype(jnp.float32)
    own_turned = jnp.transpose(jnp.concatenate([own_k, own_k], axis=0))
    column = lax.broadcasted_iota(jnp.int32, (HD, LANES), 1)
    for kind in range(3):
        for member in range(2):
            g = (kind + member) // 2
            rows = slice(member * HD, (member + 1) * HD)
            key_side[kind, rows, member * ROWS:(member + 1) * ROWS] = turned[g * HD:(g + 1) * HD]
            own = own_turned[g * HD:(g + 1) * HD]
            mine = (column >= HD) if member else (column < HD)
            key_side[kind, rows, 2 * ROWS:] = jnp.where(mine, own, 0.0).astype(jnp.bfloat16)

    memory_v = values[...]
    own_v = own_v_ref[0].astype(jnp.float32)
    sides = []
    for block in (memory_v, own_v):
        swapped = pltpu.roll(block, HD, 1)
        low = lax.broadcasted_iota(jnp.int32, block.shape, 1) < HD
        sides.append((
            (jnp.where(low, block, 0.0).astype(jnp.bfloat16), jnp.where(low, swapped, 0.0).astype(jnp.bfloat16)),
            (jnp.where(low, 0.0, swapped).astype(jnp.bfloat16), jnp.where(low, 0.0, block).astype(jnp.bfloat16)),
        ))
    for kind in range(3):
        for member in range(2):
            g = (kind + member) // 2
            value_side[kind, member * ROWS:(member + 1) * ROWS, :LANES] = sides[0][member][g]
            at = 2 * ROWS + member * QLEN
            value_side[kind, at:at + QLEN, :LANES] = sides[1][member][g]

    token = lax.broadcasted_iota(jnp.int32, (QLEN, LANES), 0)
    lane = lax.broadcasted_iota(jnp.int32, (QLEN, LANES), 1)
    key = lax.rem(lane, HD)
    bias = jnp.where((key <= token) & (key < length), 0.0, NEG)
    low = lane < HD
    alive = token < length
    factor = math.log2(math.e) / math.sqrt(HD)

    def chunk(kind, tiles):
        count = len(tiles)
        lhs = jnp.concatenate([q_ref[0, :, t * LANES:(t + 1) * LANES] for t in tiles], axis=0)
        scores = jnp.dot(lhs, key_side[kind], preferred_element_type=jnp.float32)

        def spread(x):
            return jnp.concatenate([x] * count, axis=0) if count > 1 else x

        own = scores[:, 2 * ROWS:] + spread(bias)
        is_low = spread(low)
        tops = []
        for member in range(2):
            top = jnp.where(is_low == (member == 0), own, NEG)
            for at in range(member * ROWS, (member + 1) * ROWS, LANES):
                top = jnp.maximum(top, scores[:, at:at + LANES])
            tops.append(jnp.max(top, axis=1, keepdims=True))
        weights = jnp.concatenate(
            [
                jnp.exp2((scores[:, :ROWS] - tops[0]) * factor).astype(jnp.bfloat16),
                jnp.exp2((scores[:, ROWS:2 * ROWS] - tops[1]) * factor).astype(jnp.bfloat16),
                jnp.exp2((own - jnp.where(is_low, tops[0], tops[1])) * factor).astype(jnp.bfloat16),
            ],
            axis=1,
        )
        mixed = jnp.dot(weights, value_side[kind], preferred_element_type=jnp.float32)
        result = jnp.where(spread(alive), mixed[:, :LANES] / mixed[:, LANES:], 0.0)
        result = result.astype(jnp.bfloat16)
        for i, t in enumerate(tiles):
            out_ref[0, :, t * LANES:(t + 1) * LANES] = result[i * QLEN:(i + 1) * QLEN]

    half = PAIRS // 2
    step = 7
    for at in range(0, half, step):
        chunk(0, list(range(at, min(at + step, half))))
    chunk(1, [half])
    for at in range(half + 1, PAIRS, step):
        chunk(2, list(range(at, min(at + step, PAIRS))))


def attend(starts, lengths, questions, memory_kv, own_kv):
    count = questions.shape[0]
    total = memory_kv.shape[0]
    return pl.pallas_call(
        attend_kernel,
        grid_spec=pltpu.PrefetchScalarGridSpec(
            num_scalar_prefetch=2,
            grid=(2, count),
            in_specs=[
                pl.BlockSpec((1, QLEN, HALF), lambda c, q, *_: (q, 0, c)),
                pl.BlockSpec((total, LANES), lambda c, q, *_: (0, c)),
                pl.BlockSpec((total, LANES), lambda c, q, *_: (0, 2 + c)),
                pl.BlockSpec((1, QLEN, LANES), lambda c, q, *_: (q, 0, c)),
                pl.BlockSpec((1, QLEN, LANES), lambda c, q, *_: (q, 0, 2 + c)),
            ],
            out_specs=pl.BlockSpec((1, QLEN, HALF), lambda c, q, *_: (q, 0, c)),
            scratch_shapes=[
                pltpu.VMEM((ROWS, LANES), jnp.float32),
                pltpu.VMEM((ROWS, LANES), jnp.float32),
                pltpu.VMEM((3, LANES, KEYS), jnp.bfloat16),
                pltpu.VMEM((3, KEYS, 2 * LANES), jnp.bfloat16),
            ],
        ),
        out_shape=jax.ShapeDtypeStruct((count, QLEN, H * HD), jnp.bfloat16),
        compiler_params=pltpu.CompilerParams(vmem_limit_bytes=VMEM_LIMIT),
        cost_estimate=pl.CostEstimate(
            flops=4 * count * QLEN * H * HD * (ROWS + QLEN),
            bytes_accessed=4 * count * QLEN * H * HD + 2 * total * KVW,
            transcendentals=count * QLEN * H * (ROWS + QLEN),
        ),
        name="attend",
    )(starts, lengths, questions, memory_kv, memory_kv, own_kv, own_kv)


def local(
    passage_states,
    memory_queries,
    memory_gain,
    kv_weight,
    retrieval,
    question_queries,
    question_kv,
    question_lengths,
):
    own_count = passage_states.shape[0]
    whole_weight = lax.all_gather(kv_weight, "pass", axis=0, tiled=True)
    memory_rows = pool(passage_states, memory_queries, memory_gain)
    projected = jnp.dot(
        memory_rows.reshape(own_count * MEM, D), whole_weight, preferred_element_type=jnp.float32
    )
    memory_kv = projected.astype(jnp.bfloat16)
    everything = lax.all_gather(memory_kv, "pass", axis=0, tiled=True)
    return attend(retrieval * MEM, question_lengths, question_queries, everything, question_kv)


def solution(mesh):
    placed = (
        P(("groups", "pass"), None, None),
        P(),
        P(),
        P("pass", None),
        P(("groups", "pass"), None),
        P(("groups", "pass"), None, None),
        P(("groups", "pass"), None, None),
        P(("groups", "pass")),
    )
    return jax.shard_map(
        local,
        mesh=mesh,
        in_specs=placed,
        out_specs=P(("groups", "pass"), None, None),
        check_vma=False,
    )
```

```python
import functools
import math

import jax
import jax.numpy as jnp
from jax import lax
from jax.experimental import pallas as pl
from jax.experimental.pallas import tpu as pltpu
from jax.sharding import PartitionSpec as P

D = 4096
CH = 32
CHD = 128
MEM = 32
LEN = 128
QLEN = 64
TOPK = 16
H = 116
HD = 64
KVH = 4
GROUP = 29
KVW = 512

LANES = 2 * HD
PAIRS = GROUP
HALF = PAIRS * LANES
ROWS = TOPK * MEM
KEYS = 2 * (ROWS + QLEN)
NEG = -1e30
POOL_HEADS = 16
LINES = 4
CHIP = 8
MIB = 1024 * 1024


def pool_kernel(states_ref, queries_ref, gain_ref, out_ref, pooled):
    squares = jnp.zeros((MEM, CHD), jnp.float32)
    for base in range(0, CH, POOL_HEADS):
        spans = [slice(h * CHD, (h + 1) * CHD) for h in range(base, base + POOL_HEADS)]
        scores = jnp.concatenate(
            [
                lax.dot_general(
                    queries_ref[:, span], states_ref[0, :, span], (((1,), (1,)), ((), ())),
                    preferred_element_type=jnp.float32,
                )
                for span in spans
            ],
            axis=0,
        ) * (1.0 / math.sqrt(CHD))
        scores = jnp.exp(scores - jnp.max(scores, axis=1, keepdims=True))
        weights = (scores / jnp.sum(scores, axis=1, keepdims=True)).astype(jnp.bfloat16)
        for i, span in enumerate(spans):
            part = jnp.dot(
                weights[i * MEM:(i + 1) * MEM], states_ref[0, :, span], preferred_element_type=jnp.float32
            )
            pooled[:, span] = part
            squares += part * part
    mean_square = jnp.sum(squares, axis=1, keepdims=True) * (1.0 / D)
    scale = lax.rsqrt(mean_square + 1e-06)
    out_ref[...] = (pooled[...] * scale * gain_ref[...].astype(jnp.float32)).astype(jnp.bfloat16)


def pool(states, queries, gain, passage):
    return pl.pallas_call(
        pool_kernel,
        grid=(1,),
        in_specs=[
            pl.BlockSpec((1, LEN, D), lambda _: (passage, 0, 0)),
            pl.BlockSpec((MEM, D), lambda _: (0, 0)),
            pl.BlockSpec((1, D), lambda _: (0, 0)),
        ],
        out_specs=pl.BlockSpec((MEM, D), lambda _: (0, 0)),
        out_shape=jax.ShapeDtypeStruct((MEM, D), jnp.bfloat16),
        scratch_shapes=[pltpu.VMEM((MEM, D), jnp.float32)],
        compiler_params=pltpu.CompilerParams(vmem_limit_bytes=16 * MIB),
        cost_estimate=pl.CostEstimate(
            flops=4 * MEM * LEN * D, bytes_accessed=2 * LEN * D, transcendentals=CH * MEM * LEN
        ),
        name="pool",
    )(states, queries, gain.reshape(1, D))


def attend_kernel(
    lanes, half_ref, place_ref, passage_ref, length_ref, q_ref, k_ref, v_ref, own_k_ref, own_v_ref, *rest
):
    out_ref, keys, values, key_side, value_side = rest[-5:]
    query = pl.program_id(0)

    @pl.when(query == 0)
    def _():
        key_side[...] = jnp.zeros_like(key_side)
        lane = lax.broadcasted_iota(jnp.int32, (KEYS, LANES), 1)
        row = lax.broadcasted_iota(jnp.int32, (KEYS, LANES), 0)
        in_b = ((row >= ROWS) & (row < 2 * ROWS)) | (row >= 2 * ROWS + QLEN)
        ones = jnp.where((lane >= HD) == in_b, 1.0, 0.0).astype(jnp.bfloat16)
        for kind in range(3):
            value_side[kind, :, LANES:] = ones

    for slot in range(TOPK):
        passage = passage_ref[query, slot]
        if lanes:
            chip, inside = lax.div(passage, CHIP), lax.rem(passage, CHIP)
            chip_line, chip_lane = lax.div(chip, lanes), lax.rem(chip, lanes)
            back = lax.rem(place_ref[0] + lanes - chip_lane, lanes) * LINES
            passage = (back + lax.rem(place_ref[1] + LINES - chip_line, LINES)) * CHIP + inside
        start = pl.multiple_of(passage * MEM, MEM)
        keys[slot * MEM:(slot + 1) * MEM, :] = k_ref[pl.ds(start, MEM), :].astype(jnp.float32)
        values[slot * MEM:(slot + 1) * MEM, :] = v_ref[pl.ds(start, MEM), :].astype(jnp.float32)
    length = length_ref[query]

    turned = jnp.transpose(keys[...]).astype(jnp.bfloat16)
    own_k = own_k_ref[0].astype(jnp.float32)
    own_turned = jnp.transpose(jnp.concatenate([own_k, own_k], axis=0))
    column = lax.broadcasted_iota(jnp.int32, (HD, LANES), 1)
    for kind in range(3):
        for member in range(2):
            g = (kind + member) // 2
            rows = slice(member * HD, (member + 1) * HD)
            key_side[kind, rows, member * ROWS:(member + 1) * ROWS] = turned[g * HD:(g + 1) * HD]
            own = own_turned[g * HD:(g + 1) * HD]
            mine = (column >= HD) if member else (column < HD)
            key_side[kind, rows, 2 * ROWS:] = jnp.where(mine, own, 0.0).astype(jnp.bfloat16)

    memory_v = values[...]
    own_v = own_v_ref[0].astype(jnp.float32)
    sides = []
    for block in (memory_v, own_v):
        swapped = pltpu.roll(block, HD, 1)
        low = lax.broadcasted_iota(jnp.int32, block.shape, 1) < HD
        sides.append((
            (jnp.where(low, block, 0.0).astype(jnp.bfloat16), jnp.where(low, swapped, 0.0).astype(jnp.bfloat16)),
            (jnp.where(low, 0.0, swapped).astype(jnp.bfloat16), jnp.where(low, 0.0, block).astype(jnp.bfloat16)),
        ))
    for kind in range(3):
        for member in range(2):
            g = (kind + member) // 2
            value_side[kind, member * ROWS:(member + 1) * ROWS, :LANES] = sides[0][member][g]
            at = 2 * ROWS + member * QLEN
            value_side[kind, at:at + QLEN, :LANES] = sides[1][member][g]

    token = lax.broadcasted_iota(jnp.int32, (QLEN, LANES), 0)
    lane = lax.broadcasted_iota(jnp.int32, (QLEN, LANES), 1)
    key = lax.rem(lane, HD)
    bias = jnp.where((key <= token) & (key < length), 0.0, NEG)
    low = lane < HD
    alive = token < length
    factor = math.log2(math.e) / math.sqrt(HD)

    def chunk(kind, tiles):
        count = len(tiles)
        lhs = jnp.concatenate([q_ref[0, :, t * LANES:(t + 1) * LANES] for t in tiles], axis=0)
        scores = jnp.dot(lhs, key_side[kind], preferred_element_type=jnp.float32)

        def spread(x):
            return jnp.concatenate([x] * count, axis=0) if count > 1 else x

        own = scores[:, 2 * ROWS:] + spread(bias)
        is_low = spread(low)
        tops = []
        for member in range(2):
            top = jnp.where(is_low == (member == 0), own, NEG)
            for at in range(member * ROWS, (member + 1) * ROWS, LANES):
                top = jnp.maximum(top, scores[:, at:at + LANES])
            tops.append(jnp.max(top, axis=1, keepdims=True))
        weights = jnp.concatenate(
            [
                jnp.exp2((scores[:, :ROWS] - tops[0]) * factor).astype(jnp.bfloat16),
                jnp.exp2((scores[:, ROWS:2 * ROWS] - tops[1]) * factor).astype(jnp.bfloat16),
                jnp.exp2((own - jnp.where(is_low, tops[0], tops[1])) * factor).astype(jnp.bfloat16),
            ],
            axis=1,
        )
        mixed = jnp.dot(weights, value_side[kind], preferred_element_type=jnp.float32)
        result = jnp.where(spread(alive), mixed[:, :LANES] / mixed[:, LANES:], 0.0)
        result = result.astype(jnp.bfloat16)
        for i, t in enumerate(tiles):
            out_ref[0, :, t * LANES:(t + 1) * LANES] = result[i * QLEN:(i + 1) * QLEN]

    half = PAIRS // 2
    step = 7
    for at in range(0, half, step):
        chunk(0, list(range(at, min(at + step, half))))
    chunk(1, [half])
    for at in range(half + 1, PAIRS, step):
        chunk(2, list(range(at, min(at + step, PAIRS))))


def attend(lanes, half, place, retrieval, lengths, questions, memory_kv, own_kv, earlier=None):
    count = questions.shape[0]
    total = memory_kv.shape[0]
    operands = [half.reshape(1), place, retrieval, lengths, questions, memory_kv, memory_kv, own_kv, own_kv]
    in_specs = [
        pl.BlockSpec((1, QLEN, HALF), lambda q, h, *_: (q, 0, h[0])),
        pl.BlockSpec((total, LANES), lambda q, h, *_: (0, 0)),
        pl.BlockSpec((total, LANES), lambda q, h, *_: (0, 1)),
        pl.BlockSpec((1, QLEN, LANES), lambda q, h, *_: (q, 0, h[0])),
        pl.BlockSpec((1, QLEN, LANES), lambda q, h, *_: (q, 0, 2 + h[0])),
    ]
    aliases = {}
    if earlier is not None:
        aliases = {len(operands): 0}
        operands.append(earlier)
        in_specs.append(pl.BlockSpec(memory_space=pl.ANY))
    return pl.pallas_call(
        functools.partial(attend_kernel, lanes),
        grid_spec=pltpu.PrefetchScalarGridSpec(
            num_scalar_prefetch=4,
            grid=(count,),
            in_specs=in_specs,
            out_specs=pl.BlockSpec((1, QLEN, HALF), lambda q, h, *_: (q, 0, h[0])),
            scratch_shapes=[
                pltpu.VMEM((ROWS, LANES), jnp.float32),
                pltpu.VMEM((ROWS, LANES), jnp.float32),
                pltpu.VMEM((3, LANES, KEYS), jnp.bfloat16),
                pltpu.VMEM((3, KEYS, 2 * LANES), jnp.bfloat16),
            ],
        ),
        out_shape=jax.ShapeDtypeStruct((count, QLEN, H * HD), jnp.bfloat16),
        input_output_aliases=aliases,
        compiler_params=pltpu.CompilerParams(vmem_limit_bytes=36 * MIB),
        cost_estimate=pl.CostEstimate(
            flops=2 * count * QLEN * H * HD * (ROWS + QLEN),
            bytes_accessed=2 * count * QLEN * H * HD + total * KVW,
            transcendentals=count * QLEN * H * (ROWS + QLEN) // 2,
        ),
        name="attend",
    )(*operands)


def project_kernel(lanes, passages, core_ref, place_ref, *rest):
    own, other, weights, out_ref = rest[:passages], rest[passages:2 * passages], rest[2 * passages:-1], rest[-1]
    count = passages * MEM
    depth = weights[0].shape[0] // 2
    total = jnp.zeros((2 * count, weights[0].shape[1]), jnp.float32)
    core = core_ref[0]
    for i, weight in enumerate(weights):
        line = lax.rem(place_ref[1] + LINES - i % LINES, LINES)
        chip = line * lanes + lax.rem(place_ref[0] + lanes - i // LINES, lanes)
        for part in range(2):
            at = pl.multiple_of((2 * chip + (1 - core if part else core)) * depth, depth)
            rows = jnp.concatenate([x[:, pl.ds(at, depth)] for x in own + other], axis=0)
            total += jnp.dot(
                rows, weight[part * depth:(part + 1) * depth], preferred_element_type=jnp.float32
            )
    result = total.astype(jnp.bfloat16)
    out_ref[pl.ds(pl.multiple_of(core * count, count), count)] = result[:count]
    out_ref[pl.ds(pl.multiple_of((1 - core) * count, count), count)] = result[count:]


def project(lanes, core, place, own_rows, other_rows, weights):
    passages = len(own_rows)
    width = weights[0].shape[1]
    vmem = pl.BlockSpec(memory_space=pltpu.VMEM)
    smem = pl.BlockSpec(memory_space=pltpu.SMEM)
    return pl.pallas_call(
        functools.partial(project_kernel, lanes, passages),
        in_specs=[smem, smem] + [vmem] * (2 * passages + len(weights)),
        out_specs=vmem,
        out_shape=jax.ShapeDtypeStruct((2 * passages * MEM, width), jnp.bfloat16),
        compiler_params=pltpu.CompilerParams(vmem_limit_bytes=16 * MIB),
        cost_estimate=pl.CostEstimate(
            flops=4 * passages * MEM * D * width, bytes_accessed=2 * D * width, transcendentals=0
        ),
        name="project",
    )(core.reshape(1), place, *own_rows, *other_rows, *weights)


def local(
    extent,
    passage_states,
    memory_queries,
    memory_gain,
    kv_weight,
    retrieval,
    question_queries,
    question_kv,
    question_lengths,
):
    lines, lanes = LINES, extent // (2 * LINES)
    own_count = passage_states.shape[0]
    depth = kv_weight.shape[0]
    me = lax.axis_index("pass")
    core = me & 1
    place = jnp.stack([lax.rem(lax.div(me, 2), lanes), lax.div(me, 2 * lanes)])

    def number(a, b, c):
        return ((a % lines) * lanes + b % lanes) * 2 + c

    every = [(a, b, c) for a in range(lines) for b in range(lanes) for c in range(2)]

    def to_partner(x):
        return lax.ppermute(x, "pass", [(number(a, b, c), number(a, b, 1 - c)) for a, b, c in every])

    def along_line(x, k):
        return lax.ppermute(x, "pass", [(number(a, b, c), number(a + k, b, c)) for a, b, c in every])

    def along_lane(x, j):
        return lax.ppermute(x, "pass", [(number(a, b, c), number(a, b + j, c)) for a, b, c in every])

    def along_lines(block):
        return [block] + [along_line(block, k) for k in range(1, lines)]

    def all_chips(blocks):
        return blocks + [along_lane(x, j) for j in range(1, lanes) for x in blocks]

    if depth % LANES:
        memory_rows = [pool(passage_states, memory_queries, memory_gain, i) for i in range(own_count)]
        whole_weight = lax.all_gather(kv_weight, "pass", axis=0, tiled=True)
        memory_kv = jnp.dot(jnp.concatenate(memory_rows, axis=0), whole_weight, preferred_element_type=jnp.float32)
        everything = lax.all_gather(memory_kv.astype(jnp.bfloat16), "pass", axis=0, tiled=True)
        halves = everything.reshape(-1, 2, 2, LANES).transpose(2, 0, 1, 3).reshape(2, -1, 2 * LANES)
        first, second = jnp.int32(0), jnp.int32(1)
        rest = (place, retrieval, question_lengths, question_queries)
        context = attend(0, first, *rest, halves[0], question_kv)
        return attend(0, second, *rest, halves[1], question_kv, context)

    def columns(half):
        return jnp.concatenate(
            [
                lax.dynamic_slice_in_dim(kv_weight, half * LANES + at, LANES, axis=1)
                for at in (0, KVH * HD)
            ],
            axis=1,
        )

    weight = jnp.concatenate([columns(core), to_partner(columns(1 - core))], axis=0)
    weight, memory_queries = lax.optimization_barrier((weight, memory_queries))
    weights = all_chips(along_lines(weight))
    memory_rows = [pool(passage_states, memory_queries, memory_gain, i) for i in range(own_count)]
    memory_kv = project(lanes, core, place, memory_rows, [to_partner(x) for x in memory_rows], weights)
    near = jnp.concatenate(all_chips(along_lines(memory_kv)), axis=0)
    far = to_partner(near)

    rest = (place, retrieval, question_lengths, question_queries)
    context = attend(lanes, core, *rest, near, question_kv)
    return attend(lanes, 1 - core, *rest, far, question_kv, context)


def solution(mesh):
    placed = (
        P(("groups", "pass"), None, None),
        P(),
        P(),
        P("pass", None),
        P(("groups", "pass"), None),
        P(("groups", "pass"), None, None),
        P(("groups", "pass"), None, None),
        P(("groups", "pass")),
    )
    return jax.shard_map(
        functools.partial(local, mesh.shape["pass"]),
        mesh=mesh,
        in_specs=placed,
        out_specs=P(("groups", "pass"), None, None),
        check_vma=False,
    )
```

```python
import functools
import math

import jax
import jax.numpy as jnp
from jax import lax
from jax.experimental import pallas as pl
from jax.experimental.pallas import tpu as pltpu
from jax.sharding import PartitionSpec as P

D = 4096
CH = 32
CHD = 128
MEM = 32
LEN = 128
QLEN = 64
TOPK = 16
H = 116
HD = 64
KVH = 4
GROUP = 29
KVW = 512

LANES = 2 * HD
PAIRS = GROUP
HALF = PAIRS * LANES
ROWS = TOPK * MEM
KEYS = 2 * (ROWS + QLEN)
NEG = -1e30
POOL_HEADS = 16
CHIP = 8
MIB = 1024 * 1024


def place_of(chip, ring):
    line, lane = lax.div(chip, 2), lax.rem(chip, 2)
    return line + lane * (ring - 1 - 2 * line)


def chip_at(place, ring):
    lane = lax.div(place, ring // 2)
    line = place + lane * (ring - 1 - 2 * place)
    return 2 * line + lane


def pool_kernel(states_ref, queries_ref, gain_ref, out_ref, pooled):
    squares = jnp.zeros((MEM, CHD), jnp.float32)
    for base in range(0, CH, POOL_HEADS):
        spans = [slice(h * CHD, (h + 1) * CHD) for h in range(base, base + POOL_HEADS)]
        scores = jnp.concatenate(
            [
                lax.dot_general(
                    queries_ref[:, span], states_ref[0, :, span], (((1,), (1,)), ((), ())),
                    preferred_element_type=jnp.float32,
                )
                for span in spans
            ],
            axis=0,
        ) * (1.0 / math.sqrt(CHD))
        scores = jnp.exp(scores - jnp.max(scores, axis=1, keepdims=True))
        weights = (scores / jnp.sum(scores, axis=1, keepdims=True)).astype(jnp.bfloat16)
        for i, span in enumerate(spans):
            part = jnp.dot(
                weights[i * MEM:(i + 1) * MEM], states_ref[0, :, span], preferred_element_type=jnp.float32
            )
            pooled[:, span] = part
            squares += part * part
    mean_square = jnp.sum(squares, axis=1, keepdims=True) * (1.0 / D)
    scale = lax.rsqrt(mean_square + 1e-06)
    out_ref[...] = (pooled[...] * scale * gain_ref[...].astype(jnp.float32)).astype(jnp.bfloat16)


def pool(states, queries, gain):
    count = states.shape[0]
    return pl.pallas_call(
        pool_kernel,
        grid=(count,),
        in_specs=[
            pl.BlockSpec((1, LEN, D), lambda p: (p, 0, 0)),
            pl.BlockSpec((MEM, D), lambda p: (0, 0)),
            pl.BlockSpec((1, D), lambda p: (0, 0)),
        ],
        out_specs=pl.BlockSpec((MEM, D), lambda p: (p, 0)),
        out_shape=jax.ShapeDtypeStruct((count * MEM, D), jnp.bfloat16),
        scratch_shapes=[pltpu.VMEM((MEM, D), jnp.float32)],
        compiler_params=pltpu.CompilerParams(vmem_limit_bytes=16 * MIB),
        cost_estimate=pl.CostEstimate(
            flops=4 * count * MEM * LEN * D, bytes_accessed=2 * count * LEN * D,
            transcendentals=count * CH * MEM * LEN,
        ),
        name="pool",
    )(states, queries, gain.reshape(1, D))


def attend_kernel(
    ring, half_ref, place_ref, passage_ref, length_ref, q_ref, k_ref, v_ref, own_k_ref, own_v_ref, *rest
):
    out_ref, keys, values, key_side, value_side = rest[-5:]
    query = pl.program_id(0)

    @pl.when(query == 0)
    def _():
        key_side[...] = jnp.zeros_like(key_side)
        lane = lax.broadcasted_iota(jnp.int32, (KEYS, LANES), 1)
        row = lax.broadcasted_iota(jnp.int32, (KEYS, LANES), 0)
        in_b = ((row >= ROWS) & (row < 2 * ROWS)) | (row >= 2 * ROWS + QLEN)
        ones = jnp.where((lane >= HD) == in_b, 1.0, 0.0).astype(jnp.bfloat16)
        for kind in range(3):
            value_side[kind, :, LANES:] = ones

    for slot in range(TOPK):
        passage = passage_ref[query, slot]
        if ring:
            chip, inside = lax.div(passage, CHIP), lax.rem(passage, CHIP)
            passage = lax.rem(ring + place_ref[0] - place_of(chip, ring), ring) * CHIP + inside
        start = pl.multiple_of(passage * MEM, MEM)
        keys[slot * MEM:(slot + 1) * MEM, :] = k_ref[pl.ds(start, MEM), :].astype(jnp.float32)
        values[slot * MEM:(slot + 1) * MEM, :] = v_ref[pl.ds(start, MEM), :].astype(jnp.float32)
    length = length_ref[query]

    turned = jnp.transpose(keys[...]).astype(jnp.bfloat16)
    own_k = own_k_ref[0].astype(jnp.float32)
    own_turned = jnp.transpose(jnp.concatenate([own_k, own_k], axis=0))
    column = lax.broadcasted_iota(jnp.int32, (HD, LANES), 1)
    for kind in range(3):
        for member in range(2):
            g = (kind + member) // 2
            rows = slice(member * HD, (member + 1) * HD)
            key_side[kind, rows, member * ROWS:(member + 1) * ROWS] = turned[g * HD:(g + 1) * HD]
            own = own_turned[g * HD:(g + 1) * HD]
            mine = (column >= HD) if member else (column < HD)
            key_side[kind, rows, 2 * ROWS:] = jnp.where(mine, own, 0.0).astype(jnp.bfloat16)

    memory_v = values[...]
    own_v = own_v_ref[0].astype(jnp.float32)
    sides = []
    for block in (memory_v, own_v):
        swapped = pltpu.roll(block, HD, 1)
        low = lax.broadcasted_iota(jnp.int32, block.shape, 1) < HD
        sides.append((
            (jnp.where(low, block, 0.0).astype(jnp.bfloat16), jnp.where(low, swapped, 0.0).astype(jnp.bfloat16)),
            (jnp.where(low, 0.0, swapped).astype(jnp.bfloat16), jnp.where(low, 0.0, block).astype(jnp.bfloat16)),
        ))
    for kind in range(3):
        for member in range(2):
            g = (kind + member) // 2
            value_side[kind, member * ROWS:(member + 1) * ROWS, :LANES] = sides[0][member][g]
            at = 2 * ROWS + member * QLEN
            value_side[kind, at:at + QLEN, :LANES] = sides[1][member][g]

    token = lax.broadcasted_iota(jnp.int32, (QLEN, LANES), 0)
    lane = lax.broadcasted_iota(jnp.int32, (QLEN, LANES), 1)
    key = lax.rem(lane, HD)
    bias = jnp.where((key <= token) & (key < length), 0.0, NEG)
    low = lane < HD
    alive = token < length
    factor = math.log2(math.e) / math.sqrt(HD)

    def chunk(kind, tiles):
        count = len(tiles)
        lhs = jnp.concatenate([q_ref[0, :, t * LANES:(t + 1) * LANES] for t in tiles], axis=0)
        scores = jnp.dot(lhs, key_side[kind], preferred_element_type=jnp.float32)

        def spread(x):
            return jnp.concatenate([x] * count, axis=0) if count > 1 else x

        own = scores[:, 2 * ROWS:] + spread(bias)
        is_low = spread(low)
        tops = []
        for member in range(2):
            top = jnp.where(is_low == (member == 0), own, NEG)
            for at in range(member * ROWS, (member + 1) * ROWS, LANES):
                top = jnp.maximum(top, scores[:, at:at + LANES])
            tops.append(jnp.max(top, axis=1, keepdims=True))
        weights = jnp.concatenate(
            [
                jnp.exp2((scores[:, :ROWS] - tops[0]) * factor).astype(jnp.bfloat16),
                jnp.exp2((scores[:, ROWS:2 * ROWS] - tops[1]) * factor).astype(jnp.bfloat16),
                jnp.exp2((own - jnp.where(is_low, tops[0], tops[1])) * factor).astype(jnp.bfloat16),
            ],
            axis=1,
        )
        mixed = jnp.dot(weights, value_side[kind], preferred_element_type=jnp.float32)
        result = jnp.where(spread(alive), mixed[:, :LANES] / mixed[:, LANES:], 0.0)
        result = result.astype(jnp.bfloat16)
        for i, t in enumerate(tiles):
            out_ref[0, :, t * LANES:(t + 1) * LANES] = result[i * QLEN:(i + 1) * QLEN]

    half = PAIRS // 2
    step = 7
    for at in range(0, half, step):
        chunk(0, list(range(at, min(at + step, half))))
    chunk(1, [half])
    for at in range(half + 1, PAIRS, step):
        chunk(2, list(range(at, min(at + step, PAIRS))))


def attend(ring, half, place, retrieval, lengths, questions, memory_kv, own_kv, earlier=None):
    count = questions.shape[0]
    total = memory_kv.shape[0]
    operands = [half.reshape(1), place, retrieval, lengths, questions, memory_kv, memory_kv, own_kv, own_kv]
    in_specs = [
        pl.BlockSpec((1, QLEN, HALF), lambda q, h, *_: (q, 0, h[0])),
        pl.BlockSpec((total, LANES), lambda q, h, *_: (0, 0)),
        pl.BlockSpec((total, LANES), lambda q, h, *_: (0, 1)),
        pl.BlockSpec((1, QLEN, LANES), lambda q, h, *_: (q, 0, h[0])),
        pl.BlockSpec((1, QLEN, LANES), lambda q, h, *_: (q, 0, 2 + h[0])),
    ]
    aliases = {}
    if earlier is not None:
        aliases = {len(operands): 0}
        operands.append(earlier)
        in_specs.append(pl.BlockSpec(memory_space=pl.ANY))
    return pl.pallas_call(
        functools.partial(attend_kernel, ring),
        grid_spec=pltpu.PrefetchScalarGridSpec(
            num_scalar_prefetch=4,
            grid=(count,),
            in_specs=in_specs,
            out_specs=pl.BlockSpec((1, QLEN, HALF), lambda q, h, *_: (q, 0, h[0])),
            scratch_shapes=[
                pltpu.VMEM((ROWS, LANES), jnp.float32),
                pltpu.VMEM((ROWS, LANES), jnp.float32),
                pltpu.VMEM((3, LANES, KEYS), jnp.bfloat16),
                pltpu.VMEM((3, KEYS, 2 * LANES), jnp.bfloat16),
            ],
        ),
        out_shape=jax.ShapeDtypeStruct((count, QLEN, H * HD), jnp.bfloat16),
        input_output_aliases=aliases,
        compiler_params=pltpu.CompilerParams(vmem_limit_bytes=36 * MIB),
        cost_estimate=pl.CostEstimate(
            flops=2 * count * QLEN * H * HD * (ROWS + QLEN),
            bytes_accessed=2 * count * QLEN * H * HD + total * KVW,
            transcendentals=count * QLEN * H * (ROWS + QLEN) // 2,
        ),
        name="attend",
    )(*operands)


def project_kernel(ring, core_ref, place_ref, own_ref, other_ref, *rest):
    weights, out_ref = rest[:-1], rest[-1]
    count = own_ref.shape[0]
    depth = weights[0].shape[0] // 2
    total = jnp.zeros((2 * count, weights[0].shape[1]), jnp.float32)
    core = core_ref[0]
    for i, weight in enumerate(weights):
        chip = chip_at(lax.rem(ring + place_ref[0] - i, ring), ring)
        for part in range(2):
            at = pl.multiple_of((2 * chip + (1 - core if part else core)) * depth, depth)
            rows = jnp.concatenate([own_ref[:, pl.ds(at, depth)], other_ref[:, pl.ds(at, depth)]], axis=0)
            total += jnp.dot(
                rows, weight[part * depth:(part + 1) * depth], preferred_element_type=jnp.float32
            )
    result = total.astype(jnp.bfloat16)
    out_ref[pl.ds(pl.multiple_of(core * count, count), count)] = result[:count]
    out_ref[pl.ds(pl.multiple_of((1 - core) * count, count), count)] = result[count:]


def project(core, place, own_rows, other_rows, weights):
    count = own_rows.shape[0]
    width = weights[0].shape[1]
    vmem = pl.BlockSpec(memory_space=pltpu.VMEM)
    smem = pl.BlockSpec(memory_space=pltpu.SMEM)
    return pl.pallas_call(
        functools.partial(project_kernel, len(weights)),
        in_specs=[smem, smem] + [vmem] * (2 + len(weights)),
        out_specs=vmem,
        out_shape=jax.ShapeDtypeStruct((2 * count, width), jnp.bfloat16),
        compiler_params=pltpu.CompilerParams(vmem_limit_bytes=16 * MIB),
        cost_estimate=pl.CostEstimate(
            flops=4 * count * D * width, bytes_accessed=2 * D * width, transcendentals=0
        ),
        name="project",
    )(core.reshape(1), place, own_rows, other_rows, *weights)


def local(
    extent,
    passage_states,
    memory_queries,
    memory_gain,
    kv_weight,
    retrieval,
    question_queries,
    question_kv,
    question_lengths,
):
    me = lax.axis_index("pass")
    core, chip = me & 1, lax.div(me, 2)
    chips = extent // 2
    depth = kv_weight.shape[0]

    if chips != 8 or depth % LANES:
        memory_rows = pool(passage_states, memory_queries, memory_gain)
        whole_weight = lax.all_gather(kv_weight, "pass", axis=0, tiled=True)
        memory_kv = jnp.dot(memory_rows, whole_weight, preferred_element_type=jnp.float32)
        everything = lax.all_gather(memory_kv.astype(jnp.bfloat16), "pass", axis=0, tiled=True)
        halves = everything.reshape(-1, 2, 2, LANES).transpose(2, 0, 1, 3).reshape(2, -1, 2 * LANES)
        rest = (jnp.zeros((1,), jnp.int32), retrieval, question_lengths, question_queries)
        context = attend(0, jnp.int32(0), *rest, halves[0], question_kv)
        return attend(0, jnp.int32(1), *rest, halves[1], question_kv, context)

    place = place_of(chip, chips).reshape(1)
    order = [2 * line for line in range(chips // 2)] + [2 * line + 1 for line in range(chips // 2)][::-1]

    def to_partner(x):
        return lax.ppermute(x, "pass", [(i, i ^ 1) for i in range(extent)])

    def along_ring(x, step):
        pairs = [(order[p], order[(p + step) % chips]) for p in range(chips)]
        return lax.ppermute(x, "pass", [(2 * s + c, 2 * d + c) for s, d in pairs for c in range(2)])

    def all_chips(block):
        up, down = [block], [block]
        for i in range(1, chips // 2 + 1):
            up.append(along_ring(up[-1], 1))
            if i < chips // 2:
                down.append(along_ring(down[-1], -1))
        return up + down[:0:-1]

    def columns(half):
        return jnp.concatenate(
            [
                lax.dynamic_slice_in_dim(kv_weight, half * LANES + at, LANES, axis=1)
                for at in (0, KVH * HD)
            ],
            axis=1,
        )

    weight = jnp.concatenate([columns(core), to_partner(columns(1 - core))], axis=0)
    weight, memory_queries = lax.optimization_barrier((weight, memory_queries))
    weights = all_chips(weight)
    memory_rows = pool(passage_states, memory_queries, memory_gain)
    memory_kv = project(core, place, memory_rows, to_partner(memory_rows), weights)
    near = jnp.concatenate(all_chips(memory_kv), axis=0)
    far = to_partner(near)

    rest = (place, retrieval, question_lengths, question_queries)
    context = attend(chips, core, *rest, near, question_kv)
    return attend(chips, 1 - core, *rest, far, question_kv, context)


def solution(mesh):
    placed = (
        P(("groups", "pass"), None, None),
        P(),
        P(),
        P("pass", None),
        P(("groups", "pass"), None),
        P(("groups", "pass"), None, None),
        P(("groups", "pass"), None, None),
        P(("groups", "pass")),
    )
    return jax.shard_map(
        functools.partial(local, mesh.shape["pass"]),
        mesh=mesh,
        in_specs=placed,
        out_specs=P(("groups", "pass"), None, None),
        check_vma=False,
    )
```

```python
import functools
import math

import jax
import jax.numpy as jnp
from jax import lax
from jax.experimental import pallas as pl
from jax.experimental.pallas import tpu as pltpu
from jax.sharding import PartitionSpec as P

D = 4096
CH = 32
CHD = 128
MEM = 32
LEN = 128
QLEN = 64
TOPK = 16
H = 116
HD = 64
KVH = 4
GROUP = 29
KVW = 512

LANES = 2 * HD
PAIRS = GROUP
HALF = PAIRS * LANES
ROWS = TOPK * MEM
KEYS = 2 * (ROWS + QLEN)
NEG = -1e30
POOL_HEADS = 16
POOL_CALLS = 2
CHIP = 8
STEP = 8
BLOCK = 16
MIB = 1024 * 1024


def place_of(chip, ring):
    line, lane = lax.div(chip, 2), lax.rem(chip, 2)
    return line + lane * (ring - 1 - 2 * line)


def chip_at(place, ring):
    lane = lax.div(place, ring // 2)
    line = place + lane * (ring - 1 - 2 * place)
    return 2 * line + lane


def slot_of(chip, place, ring):
    mine = chip_at(place, ring)
    lines = ring // 2
    back = lax.rem(lines + lax.div(mine, 2) - lax.div(chip, 2), lines)
    return back + lines * lax.rem(lax.rem(mine, 2) + lax.rem(chip, 2), 2)


def pool_kernel(states_ref, queries_ref, gain_ref, out_ref, pooled):
    squares = jnp.zeros((MEM, CHD), jnp.float32)
    for base in range(0, CH, POOL_HEADS):
        spans = [slice(h * CHD, (h + 1) * CHD) for h in range(base, base + POOL_HEADS)]
        scores = jnp.concatenate(
            [
                lax.dot_general(
                    queries_ref[:, span], states_ref[0, :, span], (((1,), (1,)), ((), ())),
                    preferred_element_type=jnp.float32,
                )
                for span in spans
            ],
            axis=0,
        ) * (1.0 / math.sqrt(CHD))
        scores = jnp.exp(scores - jnp.max(scores, axis=1, keepdims=True))
        weights = (scores / jnp.sum(scores, axis=1, keepdims=True)).astype(jnp.bfloat16)
        for i, span in enumerate(spans):
            part = jnp.dot(
                weights[i * MEM:(i + 1) * MEM], states_ref[0, :, span], preferred_element_type=jnp.float32
            )
            pooled[:, span] = part
            squares += part * part
    mean_square = jnp.sum(squares, axis=1, keepdims=True) * (1.0 / D)
    scale = lax.rsqrt(mean_square + 1e-06)
    out_ref[...] = (pooled[...] * scale * gain_ref[...].astype(jnp.float32)).astype(jnp.bfloat16)


def pool(states, queries, gain, first, count):
    return pl.pallas_call(
        pool_kernel,
        grid=(count,),
        in_specs=[
            pl.BlockSpec((1, LEN, D), lambda p: (first + p, 0, 0)),
            pl.BlockSpec((MEM, D), lambda p: (0, 0)),
            pl.BlockSpec((1, D), lambda p: (0, 0)),
        ],
        out_specs=pl.BlockSpec((MEM, D), lambda p: (p, 0)),
        out_shape=jax.ShapeDtypeStruct((count * MEM, D), jnp.bfloat16),
        scratch_shapes=[pltpu.VMEM((MEM, D), jnp.float32)],
        compiler_params=pltpu.CompilerParams(vmem_limit_bytes=16 * MIB),
        cost_estimate=pl.CostEstimate(
            flops=4 * count * MEM * LEN * D, bytes_accessed=2 * count * LEN * D,
            transcendentals=count * CH * MEM * LEN,
        ),
        name="pool",
    )(states, queries, gain.reshape(1, D))


def attend_kernel(
    chips, half_ref, place_ref, passage_ref, length_ref, q_ref, k_ref, v_ref, own_k_ref, own_v_ref, *rest
):
    out_ref, keys, values, key_side, value_side, scores, weights, bias = rest[-8:]
    query = pl.program_id(0)

    @pl.when(query == 0)
    def _():
        key_side[...] = jnp.zeros_like(key_side)
        lane = lax.broadcasted_iota(jnp.int32, (KEYS, LANES), 1)
        row = lax.broadcasted_iota(jnp.int32, (KEYS, LANES), 0)
        in_b = ((row >= ROWS) & (row < 2 * ROWS)) | (row >= 2 * ROWS + QLEN)
        ones = jnp.where((lane >= HD) == in_b, 1.0, 0.0).astype(jnp.bfloat16)
        for g in range(2):
            value_side[g, :, LANES:] = ones

    for slot in range(TOPK):
        passage = passage_ref[query, slot]
        if chips:
            chip, inside = lax.div(passage, CHIP), lax.rem(passage, CHIP)
            passage = slot_of(chip, place_ref[0], chips) * CHIP + inside
        start = pl.multiple_of(passage * MEM, MEM)
        keys[slot * MEM:(slot + 1) * MEM, :] = k_ref[pl.ds(start, MEM), :].astype(jnp.float32)
        values[slot * MEM:(slot + 1) * MEM, :] = v_ref[pl.ds(start, MEM), :].astype(jnp.float32)
    length = length_ref[query]

    turned = jnp.transpose(keys[...]).astype(jnp.bfloat16)
    own_k = own_k_ref[0].astype(jnp.float32)
    own_turned = jnp.transpose(jnp.concatenate([own_k, own_k], axis=0))
    column = lax.broadcasted_iota(jnp.int32, (HD, LANES), 1)
    for g in range(2):
        for member in range(2):
            rows = slice(member * HD, (member + 1) * HD)
            key_side[g, rows, member * ROWS:(member + 1) * ROWS] = turned[g * HD:(g + 1) * HD]
            own = own_turned[g * HD:(g + 1) * HD]
            mine = (column >= HD) if member else (column < HD)
            key_side[g, rows, 2 * ROWS:] = jnp.where(mine, own, 0.0).astype(jnp.bfloat16)

    token = lax.broadcasted_iota(jnp.int32, (QLEN, LANES), 0)
    lane = lax.broadcasted_iota(jnp.int32, (QLEN, LANES), 1)
    key = lax.rem(lane, HD)
    bias[...] = jnp.where((key <= token) & (key < length), 0.0, NEG)
    alive = token < length
    low_tile = lane < HD
    low = lax.broadcasted_iota(jnp.int32, (BLOCK, LANES), 1) < HD
    factor = math.log2(math.e) / math.sqrt(HD)

    half = PAIRS // 2
    chunks = []
    for g in range(2):
        tiles = list(range(half + 1)) if g == 0 else list(range(half, PAIRS))
        chunks += [(g, tiles[at:at + STEP]) for at in range(0, len(tiles), STEP)]

    def key_product(i):
        g, tiles = chunks[i]
        lhs = jnp.concatenate([q_ref[0, :, t * LANES:(t + 1) * LANES] for t in tiles], axis=0)
        scores[i % 2, :len(tiles) * QLEN, :] = jnp.dot(
            lhs, key_side[g], preferred_element_type=jnp.float32
        )

    def softmax(i):
        for at in range(0, len(chunks[i][1]) * QLEN, BLOCK):
            rows = slice(at, at + BLOCK)
            own = scores[i % 2, rows, 2 * ROWS:] + bias[at % QLEN:at % QLEN + BLOCK, :]
            tops = []
            for member in range(2):
                top = jnp.where(low, own, NEG) if member == 0 else jnp.where(low, NEG, own)
                for c in range(member * ROWS, (member + 1) * ROWS, LANES):
                    top = jnp.maximum(top, scores[i % 2, rows, c:c + LANES])
                top = jnp.max(top, axis=1, keepdims=True)
                tops.append(top)
                for c in range(member * ROWS, (member + 1) * ROWS, LANES):
                    weights[i % 2, rows, c:c + LANES] = jnp.exp2(
                        (scores[i % 2, rows, c:c + LANES] - top) * factor
                    ).astype(jnp.bfloat16)
            weights[i % 2, rows, 2 * ROWS:] = jnp.exp2(
                (own - jnp.where(low, tops[0], tops[1])) * factor
            ).astype(jnp.bfloat16)

    def value_product(i):
        g, tiles = chunks[i]
        count = len(tiles)
        mixed = jnp.dot(
            weights[i % 2, :count * QLEN, :], value_side[g], preferred_element_type=jnp.float32
        )
        for n, t in enumerate(tiles):
            rows = slice(n * QLEN, (n + 1) * QLEN)
            result = jnp.where(alive, mixed[rows, :LANES] / mixed[rows, LANES:], 0.0).astype(jnp.bfloat16)
            at = slice(t * LANES, (t + 1) * LANES)
            if t == half and g == 1:
                result = jnp.where(low_tile, out_ref[0, :, at], result)
            out_ref[0, :, at] = result

    key_product(0)

    memory_v = values[...]
    own_v = own_v_ref[0].astype(jnp.float32)
    for block, spans in (
        (memory_v, ((0, ROWS), (ROWS, 2 * ROWS))),
        (own_v, ((2 * ROWS, 2 * ROWS + QLEN), (2 * ROWS + QLEN, KEYS))),
    ):
        swapped = pltpu.roll(block, HD, 1)
        lower = lax.broadcasted_iota(jnp.int32, block.shape, 1) < HD
        for g in range(2):
            first, second = (block, swapped) if g == 0 else (swapped, block)
            for (start, stop), side in zip(
                spans, (jnp.where(lower, first, 0.0), jnp.where(lower, 0.0, second))
            ):
                value_side[g, start:stop, :LANES] = side.astype(jnp.bfloat16)

    for i in range(len(chunks)):
        if i + 1 < len(chunks):
            key_product(i + 1)
        softmax(i)
        value_product(i)


def attend(chips, half, place, retrieval, lengths, questions, memory_kv, own_kv, earlier=None):
    count = questions.shape[0]
    total = memory_kv.shape[0]
    operands = [half.reshape(1), place, retrieval, lengths, questions, memory_kv, memory_kv, own_kv, own_kv]
    in_specs = [
        pl.BlockSpec((1, QLEN, HALF), lambda q, h, *_: (q, 0, h[0])),
        pl.BlockSpec((total, LANES), lambda q, h, *_: (0, 0)),
        pl.BlockSpec((total, LANES), lambda q, h, *_: (0, 1)),
        pl.BlockSpec((1, QLEN, LANES), lambda q, h, *_: (q, 0, h[0])),
        pl.BlockSpec((1, QLEN, LANES), lambda q, h, *_: (q, 0, 2 + h[0])),
    ]
    aliases = {}
    if earlier is not None:
        aliases = {len(operands): 0}
        operands.append(earlier)
        in_specs.append(pl.BlockSpec(memory_space=pl.ANY))
    return pl.pallas_call(
        functools.partial(attend_kernel, chips),
        grid_spec=pltpu.PrefetchScalarGridSpec(
            num_scalar_prefetch=4,
            grid=(count,),
            in_specs=in_specs,
            out_specs=pl.BlockSpec((1, QLEN, HALF), lambda q, h, *_: (q, 0, h[0])),
            scratch_shapes=[
                pltpu.VMEM((ROWS, LANES), jnp.float32),
                pltpu.VMEM((ROWS, LANES), jnp.float32),
                pltpu.VMEM((2, LANES, KEYS), jnp.bfloat16),
                pltpu.VMEM((2, KEYS, 2 * LANES), jnp.bfloat16),
                pltpu.VMEM((2, STEP * QLEN, KEYS), jnp.float32),
                pltpu.VMEM((2, STEP * QLEN, KEYS), jnp.bfloat16),
                pltpu.VMEM((QLEN, LANES), jnp.float32),
            ],
        ),
        out_shape=jax.ShapeDtypeStruct((count, QLEN, H * HD), jnp.bfloat16),
        input_output_aliases=aliases,
        compiler_params=pltpu.CompilerParams(vmem_limit_bytes=36 * MIB),
        cost_estimate=pl.CostEstimate(
            flops=2 * count * QLEN * H * HD * (ROWS + QLEN),
            bytes_accessed=2 * count * QLEN * H * HD + total * KVW,
            transcendentals=count * QLEN * H * (ROWS + QLEN) // 2,
        ),
        name="attend",
    )(*operands)


def project_kernel(ring, core_ref, place_ref, *rest):
    row_refs, weights, out_ref = rest[:2 * POOL_CALLS], rest[2 * POOL_CALLS:-1], rest[-1]
    count = POOL_CALLS * row_refs[0].shape[0]
    depth = weights[0].shape[0] // 2
    pieces = []
    for i in range(ring):
        if i == ring // 2:
            pieces += [(i, 0, weights[i], 0), (i, 1, weights[i + 1], 0)]
        else:
            pieces += [(i, part, weights[i + (i > ring // 2)], part * depth) for part in range(2)]
    total = jnp.zeros((2 * count, weights[0].shape[1]), jnp.float32)
    core = core_ref[0]
    for i, part, weight, top in pieces:
        chip = chip_at(lax.rem(ring + place_ref[0] - i, ring), ring)
        at = pl.multiple_of((2 * chip + (1 - core if part else core)) * depth, depth)
        rows = jnp.concatenate([x[:, pl.ds(at, depth)] for x in row_refs], axis=0)
        total += jnp.dot(rows, weight[top:top + depth], preferred_element_type=jnp.float32)
    result = total.astype(jnp.bfloat16)
    out_ref[pl.ds(pl.multiple_of(core * count, count), count)] = result[:count]
    out_ref[pl.ds(pl.multiple_of((1 - core) * count, count), count)] = result[count:]


def project(core, place, own_rows, other_rows, weights):
    count = POOL_CALLS * own_rows[0].shape[0]
    width = weights[0].shape[1]
    vmem = pl.BlockSpec(memory_space=pltpu.VMEM)
    smem = pl.BlockSpec(memory_space=pltpu.SMEM)
    return pl.pallas_call(
        functools.partial(project_kernel, len(weights) - 1),
        in_specs=[smem, smem] + [vmem] * (2 * POOL_CALLS + len(weights)),
        out_specs=vmem,
        out_shape=jax.ShapeDtypeStruct((2 * count, width), jnp.bfloat16),
        compiler_params=pltpu.CompilerParams(vmem_limit_bytes=16 * MIB),
        cost_estimate=pl.CostEstimate(
            flops=4 * count * D * width, bytes_accessed=2 * D * width, transcendentals=0
        ),
        name="project",
    )(core.reshape(1), place, *own_rows, *other_rows, *weights)


def local(
    extent,
    passage_states,
    memory_queries,
    memory_gain,
    kv_weight,
    retrieval,
    question_queries,
    question_kv,
    question_lengths,
):
    me = lax.axis_index("pass")
    core, chip = me & 1, lax.div(me, 2)
    chips = extent // 2
    depth = kv_weight.shape[0]

    if chips != 8 or depth % LANES:
        memory_rows = pool(passage_states, memory_queries, memory_gain, 0, passage_states.shape[0])
        whole_weight = lax.all_gather(kv_weight, "pass", axis=0, tiled=True)
        memory_kv = jnp.dot(memory_rows, whole_weight, preferred_element_type=jnp.float32)
        everything = lax.all_gather(memory_kv.astype(jnp.bfloat16), "pass", axis=0, tiled=True)
        halves = everything.reshape(-1, 2, 2, LANES).transpose(2, 0, 1, 3).reshape(2, -1, 2 * LANES)
        rest = (jnp.zeros((1,), jnp.int32), retrieval, question_lengths, question_queries)
        context = attend(0, jnp.int32(0), *rest, halves[0], question_kv)
        return attend(0, jnp.int32(1), *rest, halves[1], question_kv, context)

    place = place_of(chip, chips).reshape(1)
    order = [2 * line for line in range(chips // 2)] + [2 * line + 1 for line in range(chips // 2)][::-1]

    def to_partner(x):
        return lax.ppermute(x, "pass", [(i, i ^ 1) for i in range(extent)])

    def along(x, target):
        pairs = [(c, target(c // 2, c % 2)) for c in range(chips)]
        return lax.ppermute(x, "pass", [(2 * s + c, 2 * d + c) for s, d in pairs for c in range(2)])

    def along_ring(x, step):
        return along(x, lambda line, lane: order[(order.index(2 * line + lane) + step) % chips])

    def round_the_ring(block):
        up, down = [block], [block]
        for i in range(1, chips // 2):
            up.append(along_ring(up[-1], 1))
            down.append(along_ring(down[-1], -1))
        middle = block.shape[0] // 2
        halves = [along_ring(up[-1][:middle], 1), along_ring(down[-1][middle:], -1)]
        return up + halves + down[:0:-1]

    def line_by_line(block):
        lines = chips // 2
        blocks = [block]
        for k in range(1, lines):
            blocks.append(along(block, lambda line, lane: 2 * ((line + k) % lines) + lane))
        return blocks + [along(x, lambda line, lane: 2 * line + 1 - lane) for x in blocks]

    def columns(half):
        return jnp.concatenate(
            [
                lax.dynamic_slice_in_dim(kv_weight, half * LANES + at, LANES, axis=1)
                for at in (0, KVH * HD)
            ],
            axis=1,
        )

    weight = jnp.concatenate([columns(core), to_partner(columns(1 - core))], axis=0)
    weight, memory_queries = lax.optimization_barrier((weight, memory_queries))
    weights = round_the_ring(weight)
    part = passage_states.shape[0] // POOL_CALLS
    memory_rows = [
        pool(passage_states, memory_queries, memory_gain, i * part, part) for i in range(POOL_CALLS)
    ]
    memory_kv = project(core, place, memory_rows, [to_partner(x) for x in memory_rows], weights)
    near = jnp.concatenate(line_by_line(memory_kv), axis=0)
    far = to_partner(near)

    rest = (place, retrieval, question_lengths, question_queries)
    context = attend(chips, core, *rest, near, question_kv)
    return attend(chips, 1 - core, *rest, far, question_kv, context)


def solution(mesh):
    placed = (
        P(("groups", "pass"), None, None),
        P(),
        P(),
        P("pass", None),
        P(("groups", "pass"), None),
        P(("groups", "pass"), None, None),
        P(("groups", "pass"), None, None),
        P(("groups", "pass")),
    )
    return jax.shard_map(
        functools.partial(local, mesh.shape["pass"]),
        mesh=mesh,
        in_specs=placed,
        out_specs=P(("groups", "pass"), None, None),
        check_vma=False,
    )
```

```python
import functools
import math

import jax
import jax.numpy as jnp
from jax import lax
from jax.experimental import pallas as pl
from jax.experimental.pallas import tpu as pltpu
from jax.sharding import PartitionSpec as P

D = 4096
CH = 32
CHD = 128
MEM = 32
LEN = 128
QLEN = 64
TOPK = 16
H = 116
HD = 64
KVH = 4
GROUP = 29
KVW = 512

LANES = 2 * HD
PAIRS = GROUP
HALF = PAIRS * LANES
ROWS = TOPK * MEM
KEYS = 2 * (ROWS + QLEN)
NEG = -1e30
SUM_LOW, SUM_HIGH = 2.0 ** -40, 2.0 ** 60
POOL_HEADS = 16
CHIP = 8
STEP = 8
BLOCK = 16
MIB = 1024 * 1024


def place_of(chip, ring):
    line, lane = lax.div(chip, 2), lax.rem(chip, 2)
    return line + lane * (ring - 1 - 2 * line)


def chip_at(place, ring):
    lane = lax.div(place, ring // 2)
    line = place + lane * (ring - 1 - 2 * place)
    return 2 * line + lane


def slot_of(chip, place, ring):
    mine = chip_at(place, ring)
    lines = ring // 2
    back = lax.rem(lines + lax.div(mine, 2) - lax.div(chip, 2), lines)
    return back + lines * lax.rem(lax.rem(mine, 2) + lax.rem(chip, 2), 2)


def pool_kernel(states_ref, queries_ref, gain_ref, out_ref, pooled):
    squares = jnp.zeros((MEM, CHD), jnp.float32)
    for base in range(0, CH, POOL_HEADS):
        spans = [slice(h * CHD, (h + 1) * CHD) for h in range(base, base + POOL_HEADS)]
        scores = jnp.concatenate(
            [
                lax.dot_general(
                    queries_ref[:, span], states_ref[0, :, span], (((1,), (1,)), ((), ())),
                    preferred_element_type=jnp.float32,
                )
                for span in spans
            ],
            axis=0,
        ) * (1.0 / math.sqrt(CHD))
        scores = jnp.exp(scores - jnp.max(scores, axis=1, keepdims=True))
        weights = (scores / jnp.sum(scores, axis=1, keepdims=True)).astype(jnp.bfloat16)
        for i, span in enumerate(spans):
            part = jnp.dot(
                weights[i * MEM:(i + 1) * MEM], states_ref[0, :, span], preferred_element_type=jnp.float32
            )
            pooled[:, span] = part
            squares += part * part
    mean_square = jnp.sum(squares, axis=1, keepdims=True) * (1.0 / D)
    scale = lax.rsqrt(mean_square + 1e-06)
    out_ref[...] = (pooled[...] * scale * gain_ref[...].astype(jnp.float32)).astype(jnp.bfloat16)


def pool(states, queries, gain):
    count = states.shape[0]
    return pl.pallas_call(
        pool_kernel,
        grid=(count,),
        in_specs=[
            pl.BlockSpec((1, LEN, D), lambda p: (p, 0, 0)),
            pl.BlockSpec((MEM, D), lambda p: (0, 0)),
            pl.BlockSpec((1, D), lambda p: (0, 0)),
        ],
        out_specs=pl.BlockSpec((MEM, D), lambda p: (p, 0)),
        out_shape=jax.ShapeDtypeStruct((count * MEM, D), jnp.bfloat16),
        scratch_shapes=[pltpu.VMEM((MEM, D), jnp.float32)],
        compiler_params=pltpu.CompilerParams(vmem_limit_bytes=56 * MIB),
        cost_estimate=pl.CostEstimate(
            flops=4 * count * MEM * LEN * D, bytes_accessed=2 * count * LEN * D,
            transcendentals=count * CH * MEM * LEN,
        ),
        name="pool",
    )(states, queries, gain.reshape(1, D))


def attend_kernel(
    chips, half_ref, place_ref, passage_ref, length_ref, q_ref, k_ref, v_ref, own_k_ref, own_v_ref, *rest
):
    out_ref, keys, values, key_side, value_side, scores, weights, bias = rest[-8:]
    query = pl.program_id(0)

    @pl.when(query == 0)
    def _():
        key_side[...] = jnp.zeros_like(key_side)
        lane = lax.broadcasted_iota(jnp.int32, (KEYS, LANES), 1)
        row = lax.broadcasted_iota(jnp.int32, (KEYS, LANES), 0)
        in_b = ((row >= ROWS) & (row < 2 * ROWS)) | (row >= 2 * ROWS + QLEN)
        ones = jnp.where((lane >= HD) == in_b, 1.0, 0.0).astype(jnp.bfloat16)
        for g in range(2):
            value_side[g, :, LANES:] = ones

    for slot in range(TOPK):
        passage = passage_ref[query, slot]
        if chips:
            chip, inside = lax.div(passage, CHIP), lax.rem(passage, CHIP)
            passage = slot_of(chip, place_ref[0], chips) * CHIP + inside
        start = pl.multiple_of(passage * MEM, MEM)
        keys[slot * MEM:(slot + 1) * MEM, :] = k_ref[pl.ds(start, MEM), :].astype(jnp.float32)
        values[slot * MEM:(slot + 1) * MEM, :] = v_ref[pl.ds(start, MEM), :].astype(jnp.float32)
    length = length_ref[query]

    turned = jnp.transpose(keys[...]).astype(jnp.bfloat16)
    own_k = own_k_ref[0].astype(jnp.float32)
    own_turned = jnp.transpose(jnp.concatenate([own_k, own_k], axis=0))
    column = lax.broadcasted_iota(jnp.int32, (HD, LANES), 1)
    for g in range(2):
        for member in range(2):
            rows = slice(member * HD, (member + 1) * HD)
            key_side[g, rows, member * ROWS:(member + 1) * ROWS] = turned[g * HD:(g + 1) * HD]
            own = own_turned[g * HD:(g + 1) * HD]
            mine = (column >= HD) if member else (column < HD)
            key_side[g, rows, 2 * ROWS:] = jnp.where(mine, own, 0.0).astype(jnp.bfloat16)

    token = lax.broadcasted_iota(jnp.int32, (QLEN, LANES), 0)
    lane = lax.broadcasted_iota(jnp.int32, (QLEN, LANES), 1)
    key = lax.rem(lane, HD)
    bias[...] = jnp.where((key <= token) & (key < length), 0.0, NEG)
    alive = token < length
    low_tile = lane < HD
    low = lax.broadcasted_iota(jnp.int32, (BLOCK, LANES), 1) < HD
    factor = math.log2(math.e) / math.sqrt(HD)

    half = PAIRS // 2
    chunks = []
    for g in range(2):
        tiles = list(range(half + 1)) if g == 0 else list(range(half, PAIRS))
        chunks += [(g, tiles[at:at + STEP]) for at in range(0, len(tiles), STEP)]

    def key_product(i):
        g, tiles = chunks[i]
        lhs = jnp.concatenate([q_ref[0, :, t * LANES:(t + 1) * LANES] for t in tiles], axis=0)
        scores[i % 2, :len(tiles) * QLEN, :] = jnp.dot(
            lhs, key_side[g], preferred_element_type=jnp.float32
        )

    def softmax(i):
        for at in range(0, len(chunks[i][1]) * QLEN, BLOCK):
            rows = slice(at, at + BLOCK)
            own = scores[i % 2, rows, 2 * ROWS:] + bias[at % QLEN:at % QLEN + BLOCK, :]
            tops = []
            for member in range(2):
                top = jnp.where(low, own, NEG) if member == 0 else jnp.where(low, NEG, own)
                for c in range(member * ROWS, (member + 1) * ROWS, LANES):
                    top = jnp.maximum(top, scores[i % 2, rows, c:c + LANES])
                top = jnp.max(top, axis=1, keepdims=True)
                tops.append(top)
                for c in range(member * ROWS, (member + 1) * ROWS, LANES):
                    weights[i % 2, rows, c:c + LANES] = jnp.exp2(
                        (scores[i % 2, rows, c:c + LANES] - top) * factor
                    ).astype(jnp.bfloat16)
            weights[i % 2, rows, 2 * ROWS:] = jnp.exp2(
                (own - jnp.where(low, tops[0], tops[1])) * factor
            ).astype(jnp.bfloat16)

    def key_product_plain(i):
        g, tiles = chunks[i]
        lhs = jnp.concatenate([q_ref[0, :, t * LANES:(t + 1) * LANES] for t in tiles], axis=0)
        rows = slice(0, len(tiles) * QLEN)
        for c in range(0, KEYS, 2 * LANES):
            part = slice(c, min(c + 2 * LANES, KEYS))
            got = jnp.dot(lhs, key_side[g, :, part], preferred_element_type=jnp.float32) * factor
            if c == 2 * ROWS:
                got = got + jnp.concatenate([bias[...]] * len(tiles), axis=0)
            weights[i % 2, rows, part] = jnp.exp2(got).astype(jnp.bfloat16)

    def value_product(i, seen=None):
        g, tiles = chunks[i]
        count = len(tiles)
        mixed = jnp.dot(
            weights[i % 2, :count * QLEN, :], value_side[g], preferred_element_type=jnp.float32
        )
        if seen is not None:
            for at in range(0, count * QLEN, QLEN):
                sums = mixed[at:at + QLEN, LANES:]
                seen = jnp.where((sums > SUM_LOW) & (sums < SUM_HIGH), seen, 1.0)
        for n, t in enumerate(tiles):
            rows = slice(n * QLEN, (n + 1) * QLEN)
            result = jnp.where(alive, mixed[rows, :LANES] / mixed[rows, LANES:], 0.0).astype(jnp.bfloat16)
            at = slice(t * LANES, (t + 1) * LANES)
            if t == half and g == 1:
                result = jnp.where(low_tile, out_ref[0, :, at], result)
            out_ref[0, :, at] = result
        return seen

    key_product_plain(0)

    memory_v = values[...]
    own_v = own_v_ref[0].astype(jnp.float32)
    for block, spans in (
        (memory_v, ((0, ROWS), (ROWS, 2 * ROWS))),
        (own_v, ((2 * ROWS, 2 * ROWS + QLEN), (2 * ROWS + QLEN, KEYS))),
    ):
        swapped = pltpu.roll(block, HD, 1)
        lower = lax.broadcasted_iota(jnp.int32, block.shape, 1) < HD
        for g in range(2):
            first, second = (block, swapped) if g == 0 else (swapped, block)
            for (start, stop), side in zip(
                spans, (jnp.where(lower, first, 0.0), jnp.where(lower, 0.0, second))
            ):
                value_side[g, start:stop, :LANES] = side.astype(jnp.bfloat16)

    seen = jnp.zeros((QLEN, LANES), jnp.float32)
    for i in range(len(chunks)):
        if i + 1 < len(chunks):
            key_product_plain(i + 1)
        seen = value_product(i, seen)

    @pl.when(jnp.max(seen) > 0.0)
    def _():
        for i in range(len(chunks)):
            key_product(i)
            softmax(i)
            value_product(i)


def attend(chips, half, place, retrieval, lengths, questions, memory_kv, own_kv, earlier=None):
    count = questions.shape[0]
    total = memory_kv.shape[0]
    operands = [half.reshape(1), place, retrieval, lengths, questions, memory_kv, memory_kv, own_kv, own_kv]
    in_specs = [
        pl.BlockSpec((1, QLEN, HALF), lambda q, h, *_: (q, 0, h[0])),
        pl.BlockSpec((total, LANES), lambda q, h, *_: (0, 0)),
        pl.BlockSpec((total, LANES), lambda q, h, *_: (0, 1)),
        pl.BlockSpec((1, QLEN, LANES), lambda q, h, *_: (q, 0, h[0])),
        pl.BlockSpec((1, QLEN, LANES), lambda q, h, *_: (q, 0, 2 + h[0])),
    ]
    aliases = {}
    if earlier is not None:
        aliases = {len(operands): 0}
        operands.append(earlier)
        in_specs.append(pl.BlockSpec(memory_space=pl.ANY))
    return pl.pallas_call(
        functools.partial(attend_kernel, chips),
        grid_spec=pltpu.PrefetchScalarGridSpec(
            num_scalar_prefetch=4,
            grid=(count,),
            in_specs=in_specs,
            out_specs=pl.BlockSpec((1, QLEN, HALF), lambda q, h, *_: (q, 0, h[0])),
            scratch_shapes=[
                pltpu.VMEM((ROWS, LANES), jnp.float32),
                pltpu.VMEM((ROWS, LANES), jnp.float32),
                pltpu.VMEM((2, LANES, KEYS), jnp.bfloat16),
                pltpu.VMEM((2, KEYS, 2 * LANES), jnp.bfloat16),
                pltpu.VMEM((2, STEP * QLEN, KEYS), jnp.float32),
                pltpu.VMEM((2, STEP * QLEN, KEYS), jnp.bfloat16),
                pltpu.VMEM((QLEN, LANES), jnp.float32),
            ],
        ),
        out_shape=jax.ShapeDtypeStruct((count, QLEN, H * HD), jnp.bfloat16),
        input_output_aliases=aliases,
        compiler_params=pltpu.CompilerParams(vmem_limit_bytes=48 * MIB),
        cost_estimate=pl.CostEstimate(
            flops=2 * count * QLEN * H * HD * (ROWS + QLEN),
            bytes_accessed=2 * count * QLEN * H * HD + total * KVW,
            transcendentals=count * QLEN * H * (ROWS + QLEN) // 2,
        ),
        name="attend",
    )(*operands)


def project_kernel(ring, core_ref, place_ref, *rest):
    own_ref, other_ref, *weights, out_ref = rest
    count = own_ref.shape[0]
    depth = weights[0].shape[0]
    total = jnp.zeros((2 * count, weights[0].shape[1]), jnp.float32)
    core = core_ref[0]
    for n, weight in enumerate(weights):
        part, i = n // ring, n % ring
        chip = chip_at(lax.rem(ring + place_ref[0] - i, ring), ring)
        at = pl.multiple_of((2 * chip + (1 - core if part else core)) * depth, depth)
        rows = jnp.concatenate([own_ref[:, pl.ds(at, depth)], other_ref[:, pl.ds(at, depth)]], axis=0)
        total += jnp.dot(rows, weight[...], preferred_element_type=jnp.float32)
    result = total.astype(jnp.bfloat16)
    out_ref[pl.ds(pl.multiple_of(core * count, count), count)] = result[:count]
    out_ref[pl.ds(pl.multiple_of((1 - core) * count, count), count)] = result[count:]


def project(core, place, own_rows, other_rows, weights):
    count = own_rows.shape[0]
    width = weights[0].shape[1]
    vmem = pl.BlockSpec(memory_space=pltpu.VMEM)
    smem = pl.BlockSpec(memory_space=pltpu.SMEM)
    return pl.pallas_call(
        functools.partial(project_kernel, len(weights) // 2),
        in_specs=[smem, smem] + [vmem] * (2 + len(weights)),
        out_specs=vmem,
        out_shape=jax.ShapeDtypeStruct((2 * count, width), jnp.bfloat16),
        compiler_params=pltpu.CompilerParams(vmem_limit_bytes=16 * MIB),
        cost_estimate=pl.CostEstimate(
            flops=4 * count * D * width, bytes_accessed=2 * D * width, transcendentals=0
        ),
        name="project",
    )(core.reshape(1), place, own_rows, other_rows, *weights)


def local(
    extent,
    passage_states,
    memory_queries,
    memory_gain,
    kv_weight,
    retrieval,
    question_queries,
    question_kv,
    question_lengths,
):
    me = lax.axis_index("pass")
    core, chip = me & 1, lax.div(me, 2)
    chips = extent // 2
    depth = kv_weight.shape[0]

    if chips != 8 or depth % LANES:
        memory_rows = pool(passage_states, memory_queries, memory_gain)
        whole_weight = lax.all_gather(kv_weight, "pass", axis=0, tiled=True)
        memory_kv = jnp.dot(memory_rows, whole_weight, preferred_element_type=jnp.float32)
        everything = lax.all_gather(memory_kv.astype(jnp.bfloat16), "pass", axis=0, tiled=True)
        halves = everything.reshape(-1, 2, 2, LANES).transpose(2, 0, 1, 3).reshape(2, -1, 2 * LANES)
        rest = (jnp.zeros((1,), jnp.int32), retrieval, question_lengths, question_queries)
        context = attend(0, jnp.int32(0), *rest, halves[0], question_kv)
        return attend(0, jnp.int32(1), *rest, halves[1], question_kv, context)

    place = place_of(chip, chips).reshape(1)
    order = [2 * line for line in range(chips // 2)] + [2 * line + 1 for line in range(chips // 2)][::-1]

    def to_partner(x):
        return lax.ppermute(x, "pass", [(i, i ^ 1) for i in range(extent)])

    def along(x, target):
        pairs = [(c, target(c // 2, c % 2)) for c in range(chips)]
        return lax.ppermute(x, "pass", [(2 * s + c, 2 * d + c) for s, d in pairs for c in range(2)])

    def along_ring(x, step):
        return along(x, lambda line, lane: order[(order.index(2 * line + lane) + step) % chips])

    def round_the_ring(x, up, down, rounds):
        up, down = [x, up], [down]
        while len(up) <= rounds:
            up.append(along_ring(up[-1], 1))
        while len(up) + len(down) < chips:
            down.append(along_ring(down[-1], -1))
        return up + down[::-1]

    def line_by_line(block):
        lines = chips // 2
        blocks = [block]
        for k in range(1, lines):
            blocks.append(along(block, lambda line, lane: 2 * ((line + k) % lines) + lane))
        return blocks + [along(x, lambda line, lane: 2 * line + 1 - lane) for x in blocks]

    def columns(half):
        return jnp.concatenate(
            [
                lax.dynamic_slice_in_dim(kv_weight, half * LANES + at, LANES, axis=1)
                for at in (0, KVH * HD)
            ],
            axis=1,
        )

    pieces = [columns(core), to_partner(columns(1 - core))]
    hops = [along_ring(x, step) for x in pieces for step in (1, -1)]
    memory_rows = pool(passage_states, memory_queries, memory_gain)
    *hops, memory_rows = lax.optimization_barrier((*hops, memory_rows))
    weights = round_the_ring(pieces[0], hops[0], hops[1], chips // 2)
    weights += round_the_ring(pieces[1], hops[2], hops[3], chips // 2 - 1)
    memory_kv = project(core, place, memory_rows, to_partner(memory_rows), weights)
    near = jnp.concatenate(line_by_line(memory_kv), axis=0)
    far = to_partner(near)

    rest = (place, retrieval, question_lengths, question_queries)
    context = attend(chips, core, *rest, near, question_kv)
    return attend(chips, 1 - core, *rest, far, question_kv, context)


def solution(mesh):
    placed = (
        P(("groups", "pass"), None, None),
        P(),
        P(),
        P("pass", None),
        P(("groups", "pass"), None),
        P(("groups", "pass"), None, None),
        P(("groups", "pass"), None, None),
        P(("groups", "pass")),
    )
    return jax.shard_map(
        functools.partial(local, mesh.shape["pass"]),
        mesh=mesh,
        in_specs=placed,
        out_specs=P(("groups", "pass"), None, None),
        check_vma=False,
    )
```

```python
import functools
import math

import jax
import jax.numpy as jnp
from jax import lax
from jax.experimental import pallas as pl
from jax.experimental.pallas import tpu as pltpu
from jax.sharding import PartitionSpec as P

D = 4096
CH = 32
CHD = 128
MEM = 32
LEN = 128
QLEN = 64
TOPK = 16
H = 116
HD = 64
KVH = 4
GROUP = 29
KVW = 512

LANES = 2 * HD
PAIRS = GROUP
HALF = PAIRS * LANES
ROWS = TOPK * MEM
KEYS = 2 * (ROWS + QLEN)
NEG = -1e30
SUM_LOW, SUM_HIGH = 2.0 ** -40, 2.0 ** 60
POOL_HEADS = 16
CHIP = 8
STEP = 8
POOL_TURNS = ((0, 1), (2,), (3,))
SOURCE_OF = (0,) * 2 + (1,) * 8 + (2,) * 6
STAGES = (
    (tuple(range(2)), True, SOURCE_OF),
    (tuple(range(2, 10)), False, SOURCE_OF),
    (tuple(range(10, TOPK)), False, SOURCE_OF),
)
MIB = 1024 * 1024


def place_of(chip, ring):
    line, lane = lax.div(chip, 2), lax.rem(chip, 2)
    return line + lane * (ring - 1 - 2 * line)


def chip_at(place, ring):
    lane = lax.div(place, ring // 2)
    line = place + lane * (ring - 1 - 2 * place)
    return 2 * line + lane


def pool_kernel(states_ref, queries_ref, gain_ref, out_ref, pooled):
    squares = jnp.zeros((MEM, CHD), jnp.float32)
    for base in range(0, CH, POOL_HEADS):
        spans = [slice(h * CHD, (h + 1) * CHD) for h in range(base, base + POOL_HEADS)]
        scores = jnp.concatenate(
            [
                lax.dot_general(
                    queries_ref[:, span], states_ref[0, :, span], (((1,), (1,)), ((), ())),
                    preferred_element_type=jnp.float32,
                )
                for span in spans
            ],
            axis=0,
        ) * (1.0 / math.sqrt(CHD))
        scores = jnp.exp(scores - jnp.max(scores, axis=1, keepdims=True))
        weights = (scores / jnp.sum(scores, axis=1, keepdims=True)).astype(jnp.bfloat16)
        for i, span in enumerate(spans):
            part = jnp.dot(
                weights[i * MEM:(i + 1) * MEM], states_ref[0, :, span], preferred_element_type=jnp.float32
            )
            pooled[:, span] = part
            squares += part * part
    mean_square = jnp.sum(squares, axis=1, keepdims=True) * (1.0 / D)
    scale = lax.rsqrt(mean_square + 1e-06)
    out_ref[...] = (pooled[...] * scale * gain_ref[...].astype(jnp.float32).reshape(1, D)).astype(jnp.bfloat16)


def pool(states, queries, gain, passage):
    return pl.pallas_call(
        pool_kernel,
        grid=(1,),
        in_specs=[
            pl.BlockSpec((1, LEN, D), lambda _: (passage, 0, 0)),
            pl.BlockSpec((MEM, D), lambda _: (0, 0)),
            pl.BlockSpec((D,), lambda _: (0,)),
        ],
        out_specs=pl.BlockSpec((MEM, D), lambda _: (0, 0)),
        out_shape=jax.ShapeDtypeStruct((MEM, D), jnp.bfloat16),
        scratch_shapes=[pltpu.VMEM((MEM, D), jnp.float32)],
        compiler_params=pltpu.CompilerParams(vmem_limit_bytes=52 * MIB),
        cost_estimate=pl.CostEstimate(
            flops=4 * MEM * LEN * D, bytes_accessed=2 * LEN * D, transcendentals=CH * MEM * LEN
        ),
        name="pool",
    )(states, queries, gain)


def attend_kernel(plan, half_ref, start_ref, length_ref, *rest):
    positions, with_own, first, last, source_of = plan
    rest = list(rest)
    q_ref = rest.pop(0)
    sources = {source: rest.pop(0) for source in sorted({source_of[p] for p in needed_positions(plan)})}
    own_k_ref, own_v_ref = (rest.pop(0), rest.pop(0)) if with_own or last else (None, None)
    sums_ref = None if first else rest.pop(0)
    scratch_count = 11 if last else 7
    out_ref = rest[-scratch_count - 1]
    keys, values, key_side, value_side, weights, bias, marker = rest[-scratch_count:][:7]
    query = pl.program_id(0)
    count = MEM * len(positions) + (QLEN if with_own else 0)
    whole = count // LANES * LANES
    width = 2 * count

    @pl.when(query == 0)
    def _():
        key_side[...] = jnp.zeros_like(key_side)
        lane = lax.broadcasted_iota(jnp.int32, (width, LANES), 1)
        row = lax.broadcasted_iota(jnp.int32, (width, LANES), 0)
        in_b = ((row >= whole) & (row < 2 * whole)) | (row >= 2 * whole + HD)
        ones = jnp.where((lane >= HD) == in_b, 1.0, 0.0).astype(jnp.bfloat16)
        for g in range(2):
            value_side[g, :, LANES:] = ones

    def fetch(position):
        start = pl.multiple_of(start_ref[query, position], MEM)
        source = sources[source_of[position]]
        return (
            source[pl.ds(start, MEM), :LANES].astype(jnp.float32),
            source[pl.ds(start, MEM), LANES:].astype(jnp.float32),
        )

    for n, position in enumerate(positions):
        rows = slice(n * MEM, (n + 1) * MEM)
        keys[rows, :], values[rows, :] = fetch(position)
    if with_own:
        keys[count - QLEN:count, :] = own_k_ref[0].astype(jnp.float32)
        values[count - QLEN:count, :] = own_v_ref[0].astype(jnp.float32)
    length = length_ref[query]
    factor = math.log2(math.e) / math.sqrt(HD)

    def fill_keys(block, tail, side, at):
        turned = jnp.transpose(block).astype(jnp.bfloat16)
        size = block.shape[0]
        if tail is not None:
            both = jnp.transpose(jnp.concatenate([tail, tail], axis=0))
            column = lax.broadcasted_iota(jnp.int32, (HD, LANES), 1)
        for g in range(2):
            for member in range(2):
                rows = slice(member * HD, (member + 1) * HD)
                side[g, rows, member * size:(member + 1) * size] = turned[g * HD:(g + 1) * HD]
                if tail is not None:
                    mine = (column >= HD) if member else (column < HD)
                    side[g, rows, at:at + LANES] = jnp.where(
                        mine, both[g * HD:(g + 1) * HD], 0.0
                    ).astype(jnp.bfloat16)

    def fill_values(block, tail, side, at):
        size = block.shape[0]
        parts = [(block, 0, size)]
        if tail is not None:
            parts.append((tail, at, HD))
        for part, start, step in parts:
            swapped = pltpu.roll(part, HD, 1)
            lower = lax.broadcasted_iota(jnp.int32, part.shape, 1) < HD
            for g in range(2):
                one, two = (part, swapped) if g == 0 else (swapped, part)
                side[g, start:start + step, :LANES] = jnp.where(lower, one, 0.0).astype(jnp.bfloat16)
                side[g, start + step:start + 2 * step, :LANES] = jnp.where(lower, 0.0, two).astype(
                    jnp.bfloat16
                )

    tail = slice(whole, count)
    fill_keys(keys[:whole], keys[tail] if count > whole else None, key_side, 2 * whole)
    if with_own:
        token = lax.broadcasted_iota(jnp.int32, (QLEN, LANES), 0)
        key = lax.broadcasted_iota(jnp.int32, (QLEN, LANES), 1) - (LANES - QLEN)
        bias[...] = jnp.where((key < 0) | ((key <= token) & (key < length)), 0.0, NEG)

    half = PAIRS // 2
    chunks = []
    for g in range(2):
        tiles = list(range(half + 1)) if g == 0 else list(range(half, PAIRS))
        chunks += [
            (g, tiles[at:at + STEP], (g * len(tiles) + at) * QLEN) for at in range(0, len(tiles), STEP)
        ]

    def questions(tiles):
        return jnp.concatenate([q_ref[0, :, t * LANES:(t + 1) * LANES] for t in tiles], axis=0)

    def key_product(i):
        g, tiles, _ = chunks[i]
        lhs = questions(tiles)
        rows = slice(0, len(tiles) * QLEN)
        for c in range(0, width, 2 * LANES):
            part = slice(c, min(c + 2 * LANES, width))
            got = jnp.dot(lhs, key_side[g, :, part], preferred_element_type=jnp.float32) * factor
            if with_own:
                got = got + jnp.concatenate(
                    [jnp.concatenate([bias[...]] * len(tiles), axis=0)] * 2, axis=1
                )
            weights[i % 2, rows, part] = jnp.exp2(got).astype(jnp.bfloat16)

    def finish(i, mixed):
        g, tiles, _ = chunks[i]
        token = lax.broadcasted_iota(jnp.int32, (QLEN, LANES), 0)
        low = lax.broadcasted_iota(jnp.int32, (QLEN, LANES), 1) < HD
        for n, t in enumerate(tiles):
            rows = slice(n * QLEN, (n + 1) * QLEN)
            result = jnp.where(token < length, mixed[rows, :LANES] / mixed[rows, LANES:], 0.0)
            result = result.astype(jnp.bfloat16)
            at = slice(t * LANES, (t + 1) * LANES)
            if t == half and g == 1:
                result = jnp.where(low, out_ref[0, :, at], result)
            out_ref[0, :, at] = result

    def value_product(i, seen):
        g, tiles, base = chunks[i]
        size = len(tiles) * QLEN
        mixed = jnp.dot(weights[i % 2, :size, :], value_side[g], preferred_element_type=jnp.float32)
        if not first:
            mixed = mixed + sums_ref[0, base:base + size, :]
        if not last:
            out_ref[0, base:base + size, :] = mixed
            return seen
        for at in range(0, size, QLEN):
            total = mixed[at:at + QLEN, LANES:]
            seen = jnp.where((total > SUM_LOW) & (total < SUM_HIGH), seen, 1.0)
        finish(i, mixed)
        return seen

    key_product(0)
    fill_values(values[:whole], values[tail] if count > whole else None, value_side, 2 * whole)
    seen = jnp.zeros((QLEN, LANES), jnp.float32)
    for i in range(len(chunks)):
        if i + 1 < len(chunks):
            key_product(i + 1)
        seen = value_product(i, seen)
    if not last:
        return

    marker[0] = jnp.max(seen)
    all_keys, all_values, scores, all_weights = rest[-4:]

    @pl.when(marker[0] > 0.0)
    def _():
        own = (own_k_ref[0].astype(jnp.float32), own_v_ref[0].astype(jnp.float32))
        fetched = [fetch(position) for position in range(TOPK)]
        memory = [jnp.concatenate([x[n] for x in fetched], axis=0) for n in range(2)]
        all_keys[...] = jnp.zeros_like(all_keys)
        fill_keys(memory[0], own[0], all_keys, 2 * ROWS)
        fill_values(memory[1], own[1], all_values, 2 * ROWS)
        lane = lax.broadcasted_iota(jnp.int32, (KEYS, LANES), 1)
        row = lax.broadcasted_iota(jnp.int32, (KEYS, LANES), 0)
        in_b = ((row >= ROWS) & (row < 2 * ROWS)) | (row >= 2 * ROWS + QLEN)
        for g in range(2):
            all_values[g, :, LANES:] = jnp.where((lane >= HD) == in_b, 1.0, 0.0).astype(jnp.bfloat16)
        token = lax.broadcasted_iota(jnp.int32, (QLEN, LANES), 0)
        key = lax.rem(lax.broadcasted_iota(jnp.int32, (QLEN, LANES), 1), HD)
        causal = jnp.where((key <= token) & (key < length), 0.0, NEG)
        low = lax.broadcasted_iota(jnp.int32, (QLEN, LANES), 1) < HD
        for i, (g, tiles, _) in enumerate(chunks):
            size = len(tiles) * QLEN
            scores[:size, :] = jnp.dot(questions(tiles), all_keys[g], preferred_element_type=jnp.float32)

            def soften(n, carry):
                rows = pl.ds(pl.multiple_of(n * QLEN, QLEN), QLEN)
                own_scores = scores[rows, 2 * ROWS:] + causal
                tops = []
                for member in range(2):
                    span = slice(member * ROWS, (member + 1) * ROWS)
                    top = jnp.max(jnp.where(low == (member == 0), own_scores, NEG), axis=1, keepdims=True)
                    top = jnp.maximum(top, jnp.max(scores[rows, span], axis=1, keepdims=True))
                    all_weights[rows, span] = jnp.exp2((scores[rows, span] - top) * factor).astype(
                        jnp.bfloat16
                    )
                    tops.append(top)
                all_weights[rows, 2 * ROWS:] = jnp.exp2(
                    (own_scores - jnp.where(low, tops[0], tops[1])) * factor
                ).astype(jnp.bfloat16)
                return carry

            lax.fori_loop(0, len(tiles), soften, 0)
            finish(i, jnp.dot(all_weights[:size, :], all_values[g], preferred_element_type=jnp.float32))


def needed_positions(plan):
    positions, _, _, last, _ = plan
    return list(range(TOPK)) if last else positions


def attend(stage, half, starts, lengths, questions, own_kv, sources, sums=None, earlier=None):
    positions, with_own, source_of = stage
    first, last = sums is None, max(positions) == TOPK - 1
    plan = (positions, with_own, first, last, source_of)
    count = questions.shape[0]
    keys = MEM * len(positions) + (QLEN if with_own else 0)
    grouped = (1, 2 * (PAIRS // 2 + 1) * QLEN, 2 * LANES)
    operands = [half.reshape(1), starts, lengths, questions]
    in_specs = [pl.BlockSpec((1, QLEN, HALF), lambda q, h, *_: (q, 0, h[0]))]
    for source in sorted({source_of[p] for p in needed_positions(plan)}):
        operands.append(sources[source])
        in_specs.append(pl.BlockSpec(sources[source].shape, lambda q, *_: (0, 0)))
    if with_own or last:
        operands += [own_kv, own_kv]
        in_specs.append(pl.BlockSpec((1, QLEN, LANES), lambda q, h, *_: (q, 0, h[0])))
        in_specs.append(pl.BlockSpec((1, QLEN, LANES), lambda q, h, *_: (q, 0, 2 + h[0])))
    if not first:
        operands.append(sums)
        in_specs.append(pl.BlockSpec(grouped, lambda q, *_: (q, 0, 0)))
    aliases = {}
    if earlier is not None:
        aliases = {len(operands): 0}
        operands.append(earlier)
        in_specs.append(pl.BlockSpec(memory_space=pl.ANY))
    if last:
        out_shape = jax.ShapeDtypeStruct((count, QLEN, H * HD), jnp.bfloat16)
        out_spec = pl.BlockSpec((1, QLEN, HALF), lambda q, h, *_: (q, 0, h[0]))
    else:
        out_shape = jax.ShapeDtypeStruct((count,) + grouped[1:], jnp.float32)
        out_spec = pl.BlockSpec(grouped, lambda q, *_: (q, 0, 0))
    scratch = [
        pltpu.VMEM((keys, LANES), jnp.float32),
        pltpu.VMEM((keys, LANES), jnp.float32),
        pltpu.VMEM((2, LANES, 2 * keys), jnp.bfloat16),
        pltpu.VMEM((2, 2 * keys, 2 * LANES), jnp.bfloat16),
        pltpu.VMEM((2, STEP * QLEN, 2 * keys), jnp.bfloat16),
        pltpu.VMEM((QLEN, LANES), jnp.float32),
        pltpu.SMEM((1,), jnp.float32),
    ]
    if last:
        scratch += [
            pltpu.VMEM((2, LANES, KEYS), jnp.bfloat16),
            pltpu.VMEM((2, KEYS, 2 * LANES), jnp.bfloat16),
            pltpu.VMEM((STEP * QLEN, KEYS), jnp.float32),
            pltpu.VMEM((STEP * QLEN, KEYS), jnp.bfloat16),
        ]
    return pl.pallas_call(
        functools.partial(attend_kernel, plan),
        grid_spec=pltpu.PrefetchScalarGridSpec(
            num_scalar_prefetch=3, grid=(count,), in_specs=in_specs, out_specs=out_spec,
            scratch_shapes=scratch,
        ),
        out_shape=out_shape,
        input_output_aliases=aliases,
        compiler_params=pltpu.CompilerParams(vmem_limit_bytes=48 * MIB),
        cost_estimate=pl.CostEstimate(
            flops=2 * count * QLEN * H * HD * keys,
            bytes_accessed=2 * count * QLEN * H * HD,
            transcendentals=count * QLEN * H * keys // 2,
        ),
        name="attend",
    )(*operands)


def project_kernel(ring, passages, core_ref, place_ref, *rest):
    row_refs, weights, out_ref = rest[:2 * passages], rest[2 * passages:-1], rest[-1]
    count = passages * MEM
    depth = weights[0].shape[0]
    total = jnp.zeros((2 * count, weights[0].shape[1]), jnp.float32)
    core = core_ref[0]
    for n, weight in enumerate(weights):
        part, i = n // ring, n % ring
        chip = chip_at(lax.rem(ring + place_ref[0] - i, ring), ring)
        at = pl.multiple_of((2 * chip + (1 - core if part else core)) * depth, depth)
        rows = jnp.concatenate([x[:, pl.ds(at, depth)] for x in row_refs], axis=0)
        total += jnp.dot(rows, weight[...], preferred_element_type=jnp.float32)
    result = total.astype(jnp.bfloat16)
    out_ref[pl.ds(pl.multiple_of(core * count, count), count)] = result[:count]
    out_ref[pl.ds(pl.multiple_of((1 - core) * count, count), count)] = result[count:]


def project(core, place, own_rows, other_rows, weights):
    count = len(own_rows) * MEM
    width = weights[0].shape[1]
    vmem = pl.BlockSpec(memory_space=pltpu.VMEM)
    smem = pl.BlockSpec(memory_space=pltpu.SMEM)
    return pl.pallas_call(
        functools.partial(project_kernel, len(weights) // 2, len(own_rows)),
        in_specs=[smem, smem] + [vmem] * (2 * len(own_rows) + len(weights)),
        out_specs=vmem,
        out_shape=jax.ShapeDtypeStruct((2 * count, width), jnp.bfloat16),
        compiler_params=pltpu.CompilerParams(vmem_limit_bytes=16 * MIB),
        cost_estimate=pl.CostEstimate(
            flops=4 * count * D * width, bytes_accessed=2 * D * width, transcendentals=0
        ),
        name="project",
    )(core.reshape(1), place, *own_rows, *other_rows, *weights)


def local(
    extent,
    passage_states,
    memory_queries,
    memory_gain,
    kv_weight,
    retrieval,
    question_queries,
    question_kv,
    question_lengths,
):
    me = lax.axis_index("pass")
    core, chip = me & 1, lax.div(me, 2)
    chips = extent // 2
    depth = kv_weight.shape[0]
    own_count = passage_states.shape[0]

    if chips != 8 or depth % LANES:
        memory_rows = [pool(passage_states, memory_queries, memory_gain, i) for i in range(own_count)]
        whole_weight = lax.all_gather(kv_weight, "pass", axis=0, tiled=True)
        memory_kv = jnp.dot(
            jnp.concatenate(memory_rows, axis=0), whole_weight, preferred_element_type=jnp.float32
        )
        everything = lax.all_gather(memory_kv.astype(jnp.bfloat16), "pass", axis=0, tiled=True)
        halves = everything.reshape(-1, 2, 2, LANES).transpose(2, 0, 1, 3).reshape(2, -1, 2 * LANES)
        context = None
        for half in range(2):
            sums = None
            for positions, with_own, _ in STAGES:
                stage = (positions, with_own, (0,) * TOPK)
                last = max(positions) == TOPK - 1
                got = attend(
                    stage, jnp.int32(half), retrieval * MEM, question_lengths, question_queries, question_kv,
                    [halves[half]], sums, context if last else None,
                )
                sums, context = (sums, got) if last else (got, context)
        return context

    place = place_of(chip, chips).reshape(1)
    order = [2 * line for line in range(chips // 2)] + [2 * line + 1 for line in range(chips // 2)][::-1]

    def to_partner(x):
        return lax.ppermute(x, "pass", [(i, i ^ 1) for i in range(extent)])

    def along(x, target):
        pairs = [(c, target(c // 2, c % 2)) for c in range(chips)]
        return lax.ppermute(x, "pass", [(2 * s + c, 2 * d + c) for s, d in pairs for c in range(2)])

    def along_ring(x, step):
        return along(x, lambda line, lane: order[(order.index(2 * line + lane) + step) % chips])

    def columns(half):
        return jnp.concatenate(
            [
                lax.dynamic_slice_in_dim(kv_weight, half * LANES + at, LANES, axis=1)
                for at in (0, KVH * HD)
            ],
            axis=1,
        )

    up = [[columns(core)], [to_partner(columns(1 - core))]]
    down = [[x[0]] for x in up]
    memory_rows = []
    for turn in range(1, chips // 2):
        for piece in range(2):
            up[piece].append(along_ring(up[piece][-1], 1))
            down[piece].append(along_ring(down[piece][-1], -1))
        passages = POOL_TURNS[turn - 1]
        rows = [pool(passage_states, memory_queries, memory_gain, i) for i in passages]
        down[1][-1], rows = lax.optimization_barrier((down[1][-1], rows))
        memory_rows += rows
    up[0].append(along_ring(up[0][-1], 1))
    down[1].append(along_ring(down[1][-1], -1))
    weights = [x for piece in range(2) for x in up[piece] + down[piece][:0:-1]]
    memory_kv = project(core, place, memory_rows, [to_partner(x) for x in memory_rows], weights)

    lines = chips // 2
    line_blocks = [
        along(memory_kv, lambda line, lane: 2 * ((line + k) % lines) + lane) for k in range(1, lines)
    ]
    of_chip = lax.div(retrieval, CHIP)
    back = lax.rem(lines + lax.div(chip, 2) - lax.div(of_chip, 2), lines)
    slot = back + lines * lax.rem(lax.rem(chip, 2) + lax.rem(of_chip, 2), 2)
    at = 2 * slot + lax.rem(lax.div(retrieval, CHIP // 2), 2)
    row = MEM * lax.rem(retrieval, CHIP)
    row += CHIP * MEM * (slot - jnp.where(slot > lines, lines + 1, jnp.where(slot > 0, 1, 0)))
    wanted = lax.broadcasted_iota(jnp.int32, (1, TOPK, 1), 1)
    starts = jnp.sum(jnp.where(at[:, None, :] == wanted, row[:, None, :], 0), axis=2)

    rest = (starts, question_lengths, question_queries, question_kv)
    near, far = [memory_kv], [to_partner(memory_kv)]
    lane_blocks = [along(memory_kv, lambda line, lane: 2 * line + 1 - lane)]
    near_sums = attend(STAGES[0], core, *rest, near)
    far_sums = attend(STAGES[0], 1 - core, *rest, far)
    *line_blocks, near_sums, far_sums = lax.optimization_barrier((*line_blocks, near_sums, far_sums))
    lane_blocks += [along(x, lambda line, lane: 2 * line + 1 - lane) for x in line_blocks]
    near.append(jnp.concatenate(line_blocks + lane_blocks[:1], axis=0))
    far.append(to_partner(near[-1]))
    near_sums = attend(STAGES[1], core, *rest, near, near_sums)
    far_sums = attend(STAGES[1], 1 - core, *rest, far, far_sums)
    *lane_blocks, near_sums = lax.optimization_barrier((*lane_blocks[1:], near_sums))
    near.append(jnp.concatenate(lane_blocks, axis=0))
    far.append(to_partner(near[-1]))
    context = attend(STAGES[2], core, *rest, near, near_sums)
    return attend(STAGES[2], 1 - core, *rest, far, far_sums, context)


def solution(mesh):
    placed = (
        P(("groups", "pass"), None, None),
        P(),
        P(),
        P("pass", None),
        P(("groups", "pass"), None),
        P(("groups", "pass"), None, None),
        P(("groups", "pass"), None, None),
        P(("groups", "pass")),
    )
    return jax.shard_map(
        functools.partial(local, mesh.shape["pass"]),
        mesh=mesh,
        in_specs=placed,
        out_specs=P(("groups", "pass"), None, None),
        check_vma=False,
    )
```

```python
import functools
import math

import jax
import jax.numpy as jnp
from jax import lax
from jax.experimental import pallas as pl
from jax.experimental.pallas import tpu as pltpu
from jax.sharding import PartitionSpec as P

D = 4096
CH = 32
CHD = 128
MEM = 32
LEN = 128
QLEN = 64
TOPK = 16
H = 116
HD = 64
KVH = 4
GROUP = 29
KVW = 512

LANES = 2 * HD
PAIRS = GROUP
HALF = PAIRS * LANES
ROWS = TOPK * MEM
KEYS = 2 * (ROWS + QLEN)
NEG = -1e30
SUM_LOW, SUM_HIGH = 2.0 ** -40, 2.0 ** 60
CHIP = 8
STEP = 8
GROUP_QUERIES = 2
MIB = 1024 * 1024


def place_of(chip, ring):
    line, lane = lax.div(chip, 2), lax.rem(chip, 2)
    return line + lane * (ring - 1 - 2 * line)


def chip_at(place, ring):
    lane = lax.div(place, ring // 2)
    line = place + lane * (ring - 1 - 2 * place)
    return 2 * line + lane


def pool_kernel(states_ref, queries_ref, gain_ref, out_ref, pooled, squares):
    step = pl.program_id(0)
    passages = states_ref.shape[0]
    heads = CHD // MEM
    stacked = jnp.concatenate(
        [queries_ref[:, i * CHD:(i + 1) * CHD] for i in range(heads)], axis=0
    ).astype(jnp.float32)
    turned = jnp.transpose(stacked)
    head_of = lax.broadcasted_iota(jnp.int32, (CHD, CHD), 1) // MEM
    side = jnp.concatenate(
        [jnp.where(head_of == i, turned, 0.0).astype(jnp.bfloat16) for i in range(heads)], axis=0
    )
    tokens = states_ref[...].reshape(passages * LEN, heads * CHD)
    scores = jnp.dot(tokens, side, preferred_element_type=jnp.float32) * (1.0 / math.sqrt(CHD))
    for p in range(passages):
        part = scores[p * LEN:(p + 1) * LEN]
        part = jnp.exp(part - jnp.max(part, axis=0, keepdims=True))
        weights = (part / jnp.sum(part, axis=0, keepdims=True)).astype(jnp.bfloat16)
        mixed = lax.dot_general(
            weights, states_ref[p], (((0,), (0,)), ((), ())), preferred_element_type=jnp.float32
        )
        rows = slice(p * MEM, (p + 1) * MEM)
        total = jnp.zeros((MEM, CHD), jnp.float32)
        for i in range(heads):
            block = mixed[i * MEM:(i + 1) * MEM, i * CHD:(i + 1) * CHD]
            at = pl.multiple_of(step * (heads * CHD) + i * CHD, CHD)
            pooled[rows, pl.ds(at, CHD)] = block
            total += block * block
        squares[rows, :] = total + jnp.where(step == 0, 0.0, squares[rows, :])

    @pl.when(step == pl.num_programs(0) - 1)
    def _():
        mean_square = jnp.sum(squares[...], axis=1, keepdims=True) * (1.0 / D)
        scale = lax.rsqrt(mean_square + 1e-06)
        gain = gain_ref[...].astype(jnp.float32).reshape(1, D)
        out_ref[...] = (pooled[...] * scale * gain).astype(jnp.bfloat16)


def pool(states, queries, gain):
    count = states.shape[0]
    width = CHD // MEM * CHD
    return pl.pallas_call(
        pool_kernel,
        grid=(D // width,),
        in_specs=[
            pl.BlockSpec((count, LEN, width), lambda j: (0, 0, j)),
            pl.BlockSpec((MEM, width), lambda j: (0, j)),
            pl.BlockSpec((D,), lambda j: (0,)),
        ],
        out_specs=pl.BlockSpec((count * MEM, D), lambda j: (0, 0)),
        out_shape=jax.ShapeDtypeStruct((count * MEM, D), jnp.bfloat16),
        scratch_shapes=[
            pltpu.VMEM((count * MEM, D), jnp.float32),
            pltpu.VMEM((count * MEM, CHD), jnp.float32),
        ],
        compiler_params=pltpu.CompilerParams(vmem_limit_bytes=52 * MIB),
        cost_estimate=pl.CostEstimate(
            flops=4 * count * MEM * LEN * D, bytes_accessed=2 * count * LEN * D,
            transcendentals=count * CH * MEM * LEN,
        ),
        name="pool",
    )(states, queries, gain)


def attend_kernel(g, half_ref, start_ref, length_ref, q_ref, kv_ref, own_k_ref, own_v_ref, *rest):
    tile_ref = rest[0] if g else None
    out_ref, memory, key_side, value_side, weights, marker, scores, all_weights = rest[-8:]
    step = pl.program_id(0)
    group = q_ref.shape[0]
    factor = math.log2(math.e) / math.sqrt(HD)
    token = lax.broadcasted_iota(jnp.int32, (QLEN, LANES), 0)
    low = lax.broadcasted_iota(jnp.int32, (QLEN, LANES), 1) < HD
    own_key = lax.rem(lax.broadcasted_iota(jnp.int32, (QLEN, LANES), 1), HD)
    lengths = [length_ref[step * group + u] for u in range(group)]
    causal = [jnp.where((own_key <= token) & (own_key < n), 0.0, NEG) for n in lengths]

    @pl.when(step == 0)
    def _():
        lane = lax.broadcasted_iota(jnp.int32, (KEYS, LANES), 1)
        row = lax.broadcasted_iota(jnp.int32, (KEYS, LANES), 0)
        in_b = ((row >= ROWS) & (row < 2 * ROWS)) | (row >= 2 * ROWS + QLEN)
        ones = jnp.where((lane >= HD) == in_b, 1.0, 0.0).astype(jnp.bfloat16)
        for u in range(group):
            key_side[u] = jnp.zeros((LANES, KEYS), jnp.bfloat16)
            value_side[u, :, LANES:] = ones

    def fill_keys(u):
        for slot in range(TOPK):
            start = pl.multiple_of(start_ref[step * group + u, slot], MEM)
            memory[u, slot * MEM:(slot + 1) * MEM, :] = kv_ref[pl.ds(start, MEM), :].astype(jnp.float32)
        turned = jnp.transpose(memory[u])[:HD].astype(jnp.bfloat16)
        own = own_k_ref[u].astype(jnp.float32)
        own = jnp.transpose(jnp.concatenate([own, own], axis=0))[g * HD:(g + 1) * HD]
        column = lax.broadcasted_iota(jnp.int32, (HD, LANES), 1)
        for member in range(2):
            rows = slice(member * HD, (member + 1) * HD)
            key_side[u, rows, member * ROWS:(member + 1) * ROWS] = turned
            mine = (column >= HD) if member else (column < HD)
            key_side[u, rows, 2 * ROWS:] = jnp.where(mine, own, 0.0).astype(jnp.bfloat16)

    def fill_values(u):
        own = own_v_ref[u].astype(jnp.float32)
        parts = (
            (pltpu.roll(memory[u], HD, 1), memory[u], 0, ROWS),
            (pltpu.roll(own, HD, 1) if g else own, own if g else pltpu.roll(own, HD, 1), 2 * ROWS, QLEN),
        )
        for in_low, in_high, at, size in parts:
            lower = lax.broadcasted_iota(jnp.int32, in_low.shape, 1) < HD
            value_side[u, at:at + size, :LANES] = jnp.where(lower, in_low, 0.0).astype(jnp.bfloat16)
            value_side[u, at + size:at + 2 * size, :LANES] = jnp.where(lower, 0.0, in_high).astype(
                jnp.bfloat16
            )

    tiles = list(range(PAIRS // 2 + 1))
    chunks = [(u, tiles[at:at + STEP]) for u in range(group) for at in range(0, len(tiles), STEP)]

    def questions(u, span):
        return jnp.concatenate([q_ref[u, :, t * LANES:(t + 1) * LANES] for t in span], axis=0)

    def key_product(i):
        u, span = chunks[i]
        lhs = questions(u, span)
        for c in range(0, KEYS, 2 * LANES):
            part = slice(c, min(c + 2 * LANES, KEYS))
            got = jnp.dot(lhs, key_side[u, :, part], preferred_element_type=jnp.float32) * factor
            if c == 2 * ROWS:
                got = got + jnp.concatenate([causal[u]] * len(span), axis=0)
            weights[i % 2, :len(span) * QLEN, part] = jnp.exp2(got).astype(jnp.bfloat16)

    def finish(i, mixed):
        u, span = chunks[i]
        for n, t in enumerate(span):
            rows = slice(n * QLEN, (n + 1) * QLEN)
            result = jnp.where(token < lengths[u], mixed[rows, :LANES] / mixed[rows, LANES:], 0.0)
            result = result.astype(jnp.bfloat16)
            if g and t == 0:
                result = jnp.where(low, tile_ref[u], result)
            out_ref[u, :, t * LANES:(t + 1) * LANES] = result

    def value_product(i, seen):
        u, span = chunks[i]
        size = len(span) * QLEN
        mixed = jnp.dot(weights[i % 2, :size, :], value_side[u], preferred_element_type=jnp.float32)
        for at in range(0, size, QLEN):
            total = mixed[at:at + QLEN, LANES:]
            seen[u] = jnp.where((total > SUM_LOW) & (total < SUM_HIGH), seen[u], 1.0)
        finish(i, mixed)

    seen = [jnp.zeros((QLEN, LANES), jnp.float32) for _ in range(group)]
    fill_keys(0)
    key_product(0)
    fill_values(0)
    for i, (u, _) in enumerate(chunks):
        if i + 1 < len(chunks):
            if chunks[i + 1][0] != u:
                fill_keys(u + 1)
            key_product(i + 1)
        value_product(i, seen)
        if i + 1 < len(chunks) and chunks[i + 1][0] != u:
            fill_values(u + 1)
    for u in range(group):
        marker[u] = jnp.max(seen[u])

    for u in range(group):

        @pl.when(marker[u] > 0.0)
        def _(u=u):
            for i, (owner, span) in enumerate(chunks):
                if owner != u:
                    continue
                size = len(span) * QLEN
                scores[:size, :] = jnp.dot(
                    questions(u, span), key_side[u], preferred_element_type=jnp.float32
                )

                def soften(n, carry):
                    rows = pl.ds(pl.multiple_of(n * QLEN, QLEN), QLEN)
                    own_scores = scores[rows, 2 * ROWS:] + causal[u]
                    tops = []
                    for member in range(2):
                        columns = slice(member * ROWS, (member + 1) * ROWS)
                        top = jnp.where(low, own_scores, NEG) if member == 0 else jnp.where(low, NEG, own_scores)
                        top = jnp.maximum(
                            jnp.max(top, axis=1, keepdims=True),
                            jnp.max(scores[rows, columns], axis=1, keepdims=True),
                        )
                        all_weights[rows, columns] = jnp.exp2(
                            (scores[rows, columns] - top) * factor
                        ).astype(jnp.bfloat16)
                        tops.append(top)
                    all_weights[rows, 2 * ROWS:] = jnp.exp2(
                        (own_scores - jnp.where(low, tops[0], tops[1])) * factor
                    ).astype(jnp.bfloat16)
                    return carry

                lax.fori_loop(0, len(span), soften, 0)
                finish(
                    i, jnp.dot(all_weights[:size, :], value_side[u], preferred_element_type=jnp.float32)
                )


def attend(g, half, starts, lengths, questions, own_kv, memory_kv, earlier=None):
    count = questions.shape[0]
    width = (PAIRS // 2 + 1) * LANES
    shift = HALF - width if g else 0

    def columns(q, h, *_):
        return q * GROUP_QUERIES, 0, pl.multiple_of(h[0] * HALF + shift, LANES)

    block = (pl.Element(GROUP_QUERIES), pl.Element(QLEN), pl.Element(width))
    own_block = (GROUP_QUERIES, QLEN, LANES)
    operands = [half.reshape(1), starts, lengths, questions, memory_kv, own_kv, own_kv]
    in_specs = [
        pl.BlockSpec(block, columns),
        pl.BlockSpec(memory_kv.shape, lambda q, *_: (0, 0)),
        pl.BlockSpec(own_block, lambda q, h, *_: (q, 0, h[0])),
        pl.BlockSpec(own_block, lambda q, h, *_: (q, 0, 2 + h[0])),
    ]
    aliases = {}
    if earlier is not None:
        aliases = {len(operands): 0}
        operands.append(earlier)
        if g:
            in_specs.append(pl.BlockSpec(own_block, lambda q, h, *_: (q, 0, h[0] * PAIRS + PAIRS // 2)))
        else:
            in_specs.append(pl.BlockSpec(memory_space=pl.ANY))
    return pl.pallas_call(
        functools.partial(attend_kernel, g),
        grid_spec=pltpu.PrefetchScalarGridSpec(
            num_scalar_prefetch=3,
            grid=(count // GROUP_QUERIES,),
            in_specs=in_specs,
            out_specs=pl.BlockSpec(block, columns),
            scratch_shapes=[
                pltpu.VMEM((GROUP_QUERIES, ROWS, LANES), jnp.float32),
                pltpu.VMEM((GROUP_QUERIES, LANES, KEYS), jnp.bfloat16),
                pltpu.VMEM((GROUP_QUERIES, KEYS, 2 * LANES), jnp.bfloat16),
                pltpu.VMEM((2, STEP * QLEN, KEYS), jnp.bfloat16),
                pltpu.SMEM((GROUP_QUERIES,), jnp.float32),
                pltpu.VMEM((STEP * QLEN, KEYS), jnp.float32),
                pltpu.VMEM((STEP * QLEN, KEYS), jnp.bfloat16),
            ],
        ),
        out_shape=jax.ShapeDtypeStruct((count, QLEN, H * HD), jnp.bfloat16),
        input_output_aliases=aliases,
        compiler_params=pltpu.CompilerParams(vmem_limit_bytes=48 * MIB),
        cost_estimate=pl.CostEstimate(
            flops=8 * count * QLEN * H * HD * (ROWS + QLEN) // 2,
            bytes_accessed=count * QLEN * H * HD,
            transcendentals=count * QLEN * H * (ROWS + QLEN) // 4,
        ),
        name="attend",
    )(*operands)


def project_kernel(ring, core_ref, place_ref, *rest):
    own_ref, other_ref, *weights, first_ref, second_ref = rest
    count = own_ref.shape[0]
    depth = weights[0].shape[0]
    total = jnp.zeros((2 * count, weights[0].shape[1]), jnp.float32)
    core = core_ref[0]
    for n, weight in enumerate(weights):
        part, i = n // ring, n % ring
        chip = chip_at(lax.rem(ring + place_ref[0] - i, ring), ring)
        at = pl.multiple_of((2 * chip + (1 - core if part else core)) * depth, depth)
        rows = jnp.concatenate([own_ref[:, pl.ds(at, depth)], other_ref[:, pl.ds(at, depth)]], axis=0)
        total += jnp.dot(rows, weight[...], preferred_element_type=jnp.float32)
    keys, values = total[:, :LANES], total[:, LANES:]
    low = lax.broadcasted_iota(jnp.int32, keys.shape, 1) < HD
    for out_ref, result in (
        (first_ref, jnp.where(low, keys, pltpu.roll(values, HD, 1))),
        (second_ref, jnp.where(low, pltpu.roll(keys, HD, 1), values)),
    ):
        result = result.astype(jnp.bfloat16)
        out_ref[pl.ds(pl.multiple_of(core * count, count), count)] = result[:count]
        out_ref[pl.ds(pl.multiple_of((1 - core) * count, count), count)] = result[count:]


def project(core, place, own_rows, other_rows, weights):
    count = own_rows.shape[0]
    width = weights[0].shape[1]
    vmem = pl.BlockSpec(memory_space=pltpu.VMEM)
    smem = pl.BlockSpec(memory_space=pltpu.SMEM)
    return pl.pallas_call(
        functools.partial(project_kernel, len(weights) // 2),
        in_specs=[smem, smem] + [vmem] * (2 + len(weights)),
        out_specs=[vmem, vmem],
        out_shape=[jax.ShapeDtypeStruct((2 * count, LANES), jnp.bfloat16)] * 2,
        compiler_params=pltpu.CompilerParams(vmem_limit_bytes=16 * MIB),
        cost_estimate=pl.CostEstimate(
            flops=4 * count * D * width, bytes_accessed=2 * D * width, transcendentals=0
        ),
        name="project",
    )(core.reshape(1), place, own_rows, other_rows, *weights)


def local(
    extent,
    passage_states,
    memory_queries,
    memory_gain,
    kv_weight,
    retrieval,
    question_queries,
    question_kv,
    question_lengths,
):
    me = lax.axis_index("pass")
    core, chip = me & 1, lax.div(me, 2)
    chips = extent // 2
    depth = kv_weight.shape[0]

    if chips != 8 or depth % LANES:
        memory_rows = pool(passage_states, memory_queries, memory_gain)
        whole_weight = lax.all_gather(kv_weight, "pass", axis=0, tiled=True)
        memory_kv = jnp.dot(memory_rows, whole_weight, preferred_element_type=jnp.float32)
        everything = lax.all_gather(memory_kv.astype(jnp.bfloat16), "pass", axis=0, tiled=True)
        by_head = everything.reshape(-1, 2, KVH, HD).transpose(2, 0, 1, 3).reshape(KVH, -1, LANES)
        rest = (retrieval * MEM, question_lengths, question_queries, question_kv)
        context = None
        for g in range(2):
            for half in range(2):
                context = attend(g, jnp.int32(half), *rest, by_head[2 * half + g], context)
        return context

    place = place_of(chip, chips).reshape(1)
    order = [2 * line for line in range(chips // 2)] + [2 * line + 1 for line in range(chips // 2)][::-1]

    def to_partner(x):
        return lax.ppermute(x, "pass", [(i, i ^ 1) for i in range(extent)])

    def along(x, target):
        pairs = [(c, target(c // 2, c % 2)) for c in range(chips)]
        return lax.ppermute(x, "pass", [(2 * s + c, 2 * d + c) for s, d in pairs for c in range(2)])

    def along_ring(x, step):
        return along(x, lambda line, lane: order[(order.index(2 * line + lane) + step) % chips])

    def round_the_ring(x, up, down, rounds):
        up, down = [x, up], [down]
        while len(up) <= rounds:
            up.append(along_ring(up[-1], 1))
        while len(up) + len(down) < chips:
            down.append(along_ring(down[-1], -1))
        return up + down[::-1]

    def columns(half):
        return jnp.concatenate(
            [
                lax.dynamic_slice_in_dim(kv_weight, half * LANES + at, LANES, axis=1)
                for at in (0, KVH * HD)
            ],
            axis=1,
        )

    pieces = [columns(core), to_partner(columns(1 - core))]
    hops = [along_ring(x, step) for x in pieces for step in (1, -1)]
    memory_rows = pool(passage_states, memory_queries, memory_gain)
    *hops, memory_rows = lax.optimization_barrier((*hops, memory_rows))
    weights = round_the_ring(pieces[0], hops[0], hops[1], chips // 2)
    weights += round_the_ring(pieces[1], hops[2], hops[3], chips // 2 - 1)
    by_head = project(core, place, memory_rows, to_partner(memory_rows), weights)

    lines = chips // 2
    of_chip = lax.div(retrieval, CHIP)
    back = lax.rem(lines + lax.div(chip, 2) - lax.div(of_chip, 2), lines)
    slot = back + lines * lax.rem(lax.rem(chip, 2) + lax.rem(of_chip, 2), 2)
    starts = (slot * CHIP + lax.rem(retrieval, CHIP)) * MEM

    def along_lines(block):
        return [along(block, lambda line, lane: 2 * ((line + k) % lines) + lane) for k in range(1, lines)]

    def to_lane(blocks):
        return [along(x, lambda line, lane: 2 * line + 1 - lane) for x in blocks]

    rest = (starts, question_lengths, question_queries, question_kv)
    first, second = by_head
    line_blocks = along_lines(first)
    second, *line_blocks = lax.optimization_barrier((second, *line_blocks))
    second_blocks = along_lines(second)
    first_blocks = [first] + line_blocks
    near = jnp.concatenate(first_blocks + to_lane(first_blocks), axis=0)
    far = to_partner(near)
    context = attend(0, core, *rest, near)
    context, *second_blocks = lax.optimization_barrier((context, second, *second_blocks))
    lane_blocks = to_lane(second_blocks)
    context = attend(0, 1 - core, *rest, far, context)
    context, *lane_blocks = lax.optimization_barrier((context, *lane_blocks))
    near = jnp.concatenate(second_blocks + lane_blocks, axis=0)
    far = to_partner(near)
    context = attend(1, core, *rest, near, context)
    return attend(1, 1 - core, *rest, far, context)


def solution(mesh):
    placed = (
        P(("groups", "pass"), None, None),
        P(),
        P(),
        P("pass", None),
        P(("groups", "pass"), None),
        P(("groups", "pass"), None, None),
        P(("groups", "pass"), None, None),
        P(("groups", "pass")),
    )
    return jax.shard_map(
        functools.partial(local, mesh.shape["pass"]),
        mesh=mesh,
        in_specs=placed,
        out_specs=P(("groups", "pass"), None, None),
        check_vma=False,
    )
```

```python
import functools
import math

import jax
import jax.numpy as jnp
from jax import lax
from jax.experimental import pallas as pl
from jax.experimental.pallas import tpu as pltpu
from jax.sharding import PartitionSpec as P

D = 4096
CH = 32
CHD = 128
MEM = 32
LEN = 128
QLEN = 64
TOPK = 16
H = 116
HD = 64
KVH = 4
GROUP = 29
KVW = 512

LANES = 2 * HD
PAIRS = GROUP
HALF = PAIRS * LANES
ROWS = TOPK * MEM
KEYS = 2 * (ROWS + QLEN)
NEG = -1e30
SUM_LOW, SUM_HIGH = 2.0 ** -40, 2.0 ** 60
POOL_WIDTH = 1024
CHIP = 8
STEP = 15
BLOCK = 16
MIB = 1024 * 1024


def place_of(chip, ring):
    line, lane = lax.div(chip, 2), lax.rem(chip, 2)
    return line + lane * (ring - 1 - 2 * line)


def chip_at(place, ring):
    lane = lax.div(place, ring // 2)
    line = place + lane * (ring - 1 - 2 * place)
    return 2 * line + lane


def slot_of(chip, place, ring):
    mine = chip_at(place, ring)
    lines = ring // 2
    back = lax.rem(lines + lax.div(mine, 2) - lax.div(chip, 2), lines)
    return back + lines * lax.rem(lax.rem(mine, 2) + lax.rem(chip, 2), 2)


def pool_kernel(states_ref, queries_ref, gain_ref, out_ref, pooled, squares):
    step = pl.program_id(0)
    passages, width = states_ref.shape[0], states_ref.shape[2]
    two = 2 * CHD
    blocks = []
    for at in range(0, width, two):
        zero = jnp.zeros((MEM, CHD), jnp.bfloat16)
        lhs = jnp.concatenate(
            [
                jnp.concatenate([queries_ref[:, at:at + CHD], zero], axis=1),
                jnp.concatenate([zero, queries_ref[:, at + CHD:at + two]], axis=1),
            ],
            axis=0,
        )
        for p in range(0, passages, 2):
            tokens = states_ref[p:p + 2, :, at:at + two].reshape(2 * LEN, two)
            scores = lax.dot_general(
                lhs, tokens, (((1,), (1,)), ((), ())), preferred_element_type=jnp.float32
            ) * (1.0 / math.sqrt(CHD))
            blocks.append((at, p, tokens, scores))
    zero = jnp.zeros((2 * MEM, LEN), jnp.bfloat16)
    totals = [jnp.zeros((MEM, CHD), jnp.float32)] * passages
    for at, p, tokens, scores in blocks:
        rows = []
        for n in range(2):
            part = scores[:, n * LEN:(n + 1) * LEN]
            part = jnp.exp(part - jnp.max(part, axis=1, keepdims=True))
            part = (part / jnp.sum(part, axis=1, keepdims=True)).astype(jnp.bfloat16)
            rows.append(jnp.concatenate([zero, part] if n else [part, zero], axis=1))
        mixed = jnp.dot(jnp.concatenate(rows, axis=0), tokens, preferred_element_type=jnp.float32)
        for n in range(2):
            for head in range(2):
                top = (2 * n + head) * MEM
                block = mixed[top:top + MEM, head * CHD:(head + 1) * CHD]
                column = pl.multiple_of(step * width + at + head * CHD, CHD)
                pooled[(p + n) * MEM:(p + n + 1) * MEM, pl.ds(column, CHD)] = block
                totals[p + n] = totals[p + n] + block * block
    for p in range(passages):
        rows = slice(p * MEM, (p + 1) * MEM)
        squares[rows, :] = totals[p] + jnp.where(step == 0, 0.0, squares[rows, :])

    @pl.when(step == pl.num_programs(0) - 1)
    def _():
        mean_square = jnp.sum(squares[...], axis=1, keepdims=True) * (1.0 / D)
        scale = lax.rsqrt(mean_square + 1e-06)
        gain = gain_ref[...].astype(jnp.float32).reshape(1, D)
        out_ref[...] = (pooled[...] * scale * gain).astype(jnp.bfloat16)


def pool(states, queries, gain):
    count = states.shape[0]
    return pl.pallas_call(
        pool_kernel,
        grid=(D // POOL_WIDTH,),
        in_specs=[
            pl.BlockSpec((count, LEN, POOL_WIDTH), lambda j: (0, 0, j)),
            pl.BlockSpec((MEM, POOL_WIDTH), lambda j: (0, j)),
            pl.BlockSpec((D,), lambda j: (0,)),
        ],
        out_specs=pl.BlockSpec((count * MEM, D), lambda j: (0, 0)),
        out_shape=jax.ShapeDtypeStruct((count * MEM, D), jnp.bfloat16),
        scratch_shapes=[
            pltpu.VMEM((count * MEM, D), jnp.float32),
            pltpu.VMEM((count * MEM, CHD), jnp.float32),
        ],
        compiler_params=pltpu.CompilerParams(vmem_limit_bytes=52 * MIB),
        cost_estimate=pl.CostEstimate(
            flops=4 * count * MEM * LEN * D, bytes_accessed=2 * count * LEN * D,
            transcendentals=count * CH * MEM * LEN,
        ),
        name="pool",
    )(states, queries, gain)


def attend_kernel(
    chips, half_ref, place_ref, passage_ref, length_ref, q_ref, k_ref, v_ref, own_k_ref, own_v_ref, *rest
):
    out_ref, keys, values, key_side, value_side, scores, weights, bias = rest[-8:]
    query = pl.program_id(0)

    @pl.when(query == 0)
    def _():
        key_side[...] = jnp.zeros_like(key_side)
        lane = lax.broadcasted_iota(jnp.int32, (KEYS, LANES), 1)
        row = lax.broadcasted_iota(jnp.int32, (KEYS, LANES), 0)
        in_b = ((row >= ROWS) & (row < 2 * ROWS)) | (row >= 2 * ROWS + QLEN)
        ones = jnp.where((lane >= HD) == in_b, 1.0, 0.0).astype(jnp.bfloat16)
        for g in range(2):
            value_side[g, :, LANES:] = ones

    for slot in range(TOPK):
        passage = passage_ref[query, slot]
        if chips:
            chip, inside = lax.div(passage, CHIP), lax.rem(passage, CHIP)
            passage = slot_of(chip, place_ref[0], chips) * CHIP + inside
        start = pl.multiple_of(passage * MEM, MEM)
        keys[slot * MEM:(slot + 1) * MEM, :] = k_ref[pl.ds(start, MEM), :].astype(jnp.float32)
        values[slot * MEM:(slot + 1) * MEM, :] = v_ref[pl.ds(start, MEM), :].astype(jnp.float32)
    length = length_ref[query]

    turned = jnp.transpose(keys[...]).astype(jnp.bfloat16)
    own_k = own_k_ref[0].astype(jnp.float32)
    own_turned = jnp.transpose(jnp.concatenate([own_k, own_k], axis=0))
    column = lax.broadcasted_iota(jnp.int32, (HD, LANES), 1)
    for g in range(2):
        for member in range(2):
            rows = slice(member * HD, (member + 1) * HD)
            key_side[g, rows, member * ROWS:(member + 1) * ROWS] = turned[g * HD:(g + 1) * HD]
            own = own_turned[g * HD:(g + 1) * HD]
            mine = (column >= HD) if member else (column < HD)
            key_side[g, rows, 2 * ROWS:] = jnp.where(mine, own, 0.0).astype(jnp.bfloat16)

    token = lax.broadcasted_iota(jnp.int32, (QLEN, LANES), 0)
    lane = lax.broadcasted_iota(jnp.int32, (QLEN, LANES), 1)
    key = lax.rem(lane, HD)
    bias[...] = jnp.where((key <= token) & (key < length), 0.0, NEG)
    alive = token < length
    low_tile = lane < HD
    low = lax.broadcasted_iota(jnp.int32, (BLOCK, LANES), 1) < HD
    factor = math.log2(math.e) / math.sqrt(HD)

    half = PAIRS // 2
    chunks = []
    for g in range(2):
        tiles = list(range(half + 1)) if g == 0 else list(range(half, PAIRS))
        chunks += [(g, tiles[at:at + STEP]) for at in range(0, len(tiles), STEP)]

    def key_product(i):
        g, tiles = chunks[i]
        lhs = jnp.concatenate([q_ref[0, :, t * LANES:(t + 1) * LANES] for t in tiles], axis=0)
        scores[i % 2, :len(tiles) * QLEN, :] = jnp.dot(
            lhs, key_side[g], preferred_element_type=jnp.float32
        )

    def softmax(i):
        for at in range(0, len(chunks[i][1]) * QLEN, BLOCK):
            rows = slice(at, at + BLOCK)
            own = scores[i % 2, rows, 2 * ROWS:] + bias[at % QLEN:at % QLEN + BLOCK, :]
            tops = []
            for member in range(2):
                top = jnp.where(low, own, NEG) if member == 0 else jnp.where(low, NEG, own)
                for c in range(member * ROWS, (member + 1) * ROWS, LANES):
                    top = jnp.maximum(top, scores[i % 2, rows, c:c + LANES])
                top = jnp.max(top, axis=1, keepdims=True)
                tops.append(top)
                for c in range(member * ROWS, (member + 1) * ROWS, LANES):
                    weights[i % 2, rows, c:c + LANES] = jnp.exp2(
                        (scores[i % 2, rows, c:c + LANES] - top) * factor
                    ).astype(jnp.bfloat16)
            weights[i % 2, rows, 2 * ROWS:] = jnp.exp2(
                (own - jnp.where(low, tops[0], tops[1])) * factor
            ).astype(jnp.bfloat16)

    def key_product_plain(i):
        g, tiles = chunks[i]
        lhs = jnp.concatenate([q_ref[0, :, t * LANES:(t + 1) * LANES] for t in tiles], axis=0)
        rows = slice(0, len(tiles) * QLEN)
        for c in range(0, KEYS, 2 * LANES):
            part = slice(c, min(c + 2 * LANES, KEYS))
            got = jnp.dot(lhs, key_side[g, :, part], preferred_element_type=jnp.float32) * factor
            if c == 2 * ROWS:
                got = got + jnp.concatenate([bias[...]] * len(tiles), axis=0)
            weights[i % 2, rows, part] = jnp.exp2(got).astype(jnp.bfloat16)

    def value_product(i, seen=None):
        g, tiles = chunks[i]
        count = len(tiles)
        mixed = jnp.dot(
            weights[i % 2, :count * QLEN, :], value_side[g], preferred_element_type=jnp.float32
        )
        if seen is not None:
            for at in range(0, count * QLEN, QLEN):
                sums = mixed[at:at + QLEN, LANES:]
                seen = jnp.where((sums > SUM_LOW) & (sums < SUM_HIGH), seen, 1.0)
        for n, t in enumerate(tiles):
            rows = slice(n * QLEN, (n + 1) * QLEN)
            result = jnp.where(alive, mixed[rows, :LANES] / mixed[rows, LANES:], 0.0).astype(jnp.bfloat16)
            at = slice(t * LANES, (t + 1) * LANES)
            if t == half and g == 1:
                result = jnp.where(low_tile, out_ref[0, :, at], result)
            out_ref[0, :, at] = result
        return seen

    key_product_plain(0)

    memory_v = values[...]
    own_v = own_v_ref[0].astype(jnp.float32)
    for block, spans in (
        (memory_v, ((0, ROWS), (ROWS, 2 * ROWS))),
        (own_v, ((2 * ROWS, 2 * ROWS + QLEN), (2 * ROWS + QLEN, KEYS))),
    ):
        swapped = pltpu.roll(block, HD, 1)
        lower = lax.broadcasted_iota(jnp.int32, block.shape, 1) < HD
        for g in range(2):
            first, second = (block, swapped) if g == 0 else (swapped, block)
            for (start, stop), side in zip(
                spans, (jnp.where(lower, first, 0.0), jnp.where(lower, 0.0, second))
            ):
                value_side[g, start:stop, :LANES] = side.astype(jnp.bfloat16)

    seen = jnp.zeros((QLEN, LANES), jnp.float32)
    for i in range(len(chunks)):
        if i + 1 < len(chunks):
            key_product_plain(i + 1)
        seen = value_product(i, seen)

    @pl.when(jnp.max(seen) > 0.0)
    def _():
        for i in range(len(chunks)):
            key_product(i)
            softmax(i)
            value_product(i)


def attend(chips, half, place, retrieval, lengths, questions, memory_kv, own_kv, earlier=None):
    count = questions.shape[0]
    total = memory_kv.shape[0]
    operands = [half.reshape(1), place, retrieval, lengths, questions, memory_kv, memory_kv, own_kv, own_kv]
    in_specs = [
        pl.BlockSpec((1, QLEN, HALF), lambda q, h, *_: (q, 0, h[0])),
        pl.BlockSpec((total, LANES), lambda q, h, *_: (0, 0)),
        pl.BlockSpec((total, LANES), lambda q, h, *_: (0, 1)),
        pl.BlockSpec((1, QLEN, LANES), lambda q, h, *_: (q, 0, h[0])),
        pl.BlockSpec((1, QLEN, LANES), lambda q, h, *_: (q, 0, 2 + h[0])),
    ]
    aliases = {}
    if earlier is not None:
        aliases = {len(operands): 0}
        operands.append(earlier)
        in_specs.append(pl.BlockSpec(memory_space=pl.ANY))
    return pl.pallas_call(
        functools.partial(attend_kernel, chips),
        grid_spec=pltpu.PrefetchScalarGridSpec(
            num_scalar_prefetch=4,
            grid=(count,),
            in_specs=in_specs,
            out_specs=pl.BlockSpec((1, QLEN, HALF), lambda q, h, *_: (q, 0, h[0])),
            scratch_shapes=[
                pltpu.VMEM((ROWS, LANES), jnp.float32),
                pltpu.VMEM((ROWS, LANES), jnp.float32),
                pltpu.VMEM((2, LANES, KEYS), jnp.bfloat16),
                pltpu.VMEM((2, KEYS, 2 * LANES), jnp.bfloat16),
                pltpu.VMEM((2, STEP * QLEN, KEYS), jnp.float32),
                pltpu.VMEM((2, STEP * QLEN, KEYS), jnp.bfloat16),
                pltpu.VMEM((QLEN, LANES), jnp.float32),
            ],
        ),
        out_shape=jax.ShapeDtypeStruct((count, QLEN, H * HD), jnp.bfloat16),
        input_output_aliases=aliases,
        compiler_params=pltpu.CompilerParams(vmem_limit_bytes=48 * MIB),
        cost_estimate=pl.CostEstimate(
            flops=2 * count * QLEN * H * HD * (ROWS + QLEN),
            bytes_accessed=2 * count * QLEN * H * HD + total * KVW,
            transcendentals=count * QLEN * H * (ROWS + QLEN) // 2,
        ),
        name="attend",
    )(*operands)


def project_kernel(ring, core_ref, place_ref, *rest):
    own_ref, other_ref, *weights, out_ref = rest
    count = own_ref.shape[0]
    depth = weights[0].shape[0]
    total = jnp.zeros((2 * count, weights[0].shape[1]), jnp.float32)
    core = core_ref[0]
    for n, weight in enumerate(weights):
        part, i = n // ring, n % ring
        chip = chip_at(lax.rem(ring + place_ref[0] - i, ring), ring)
        at = pl.multiple_of((2 * chip + (1 - core if part else core)) * depth, depth)
        rows = jnp.concatenate([own_ref[:, pl.ds(at, depth)], other_ref[:, pl.ds(at, depth)]], axis=0)
        total += jnp.dot(rows, weight[...], preferred_element_type=jnp.float32)
    result = total.astype(jnp.bfloat16)
    out_ref[pl.ds(pl.multiple_of(core * count, count), count)] = result[:count]
    out_ref[pl.ds(pl.multiple_of((1 - core) * count, count), count)] = result[count:]


def project(core, place, own_rows, other_rows, weights):
    count = own_rows.shape[0]
    width = weights[0].shape[1]
    vmem = pl.BlockSpec(memory_space=pltpu.VMEM)
    smem = pl.BlockSpec(memory_space=pltpu.SMEM)
    return pl.pallas_call(
        functools.partial(project_kernel, len(weights) // 2),
        in_specs=[smem, smem] + [vmem] * (2 + len(weights)),
        out_specs=vmem,
        out_shape=jax.ShapeDtypeStruct((2 * count, width), jnp.bfloat16),
        compiler_params=pltpu.CompilerParams(vmem_limit_bytes=16 * MIB),
        cost_estimate=pl.CostEstimate(
            flops=4 * count * D * width, bytes_accessed=2 * D * width, transcendentals=0
        ),
        name="project",
    )(core.reshape(1), place, own_rows, other_rows, *weights)


def local(
    extent,
    passage_states,
    memory_queries,
    memory_gain,
    kv_weight,
    retrieval,
    question_queries,
    question_kv,
    question_lengths,
):
    me = lax.axis_index("pass")
    core, chip = me & 1, lax.div(me, 2)
    chips = extent // 2
    depth = kv_weight.shape[0]

    if chips != 8 or depth % LANES:
        memory_rows = pool(passage_states, memory_queries, memory_gain)
        whole_weight = lax.all_gather(kv_weight, "pass", axis=0, tiled=True)
        memory_kv = jnp.dot(memory_rows, whole_weight, preferred_element_type=jnp.float32)
        everything = lax.all_gather(memory_kv.astype(jnp.bfloat16), "pass", axis=0, tiled=True)
        halves = everything.reshape(-1, 2, 2, LANES).transpose(2, 0, 1, 3).reshape(2, -1, 2 * LANES)
        rest = (jnp.zeros((1,), jnp.int32), retrieval, question_lengths, question_queries)
        context = attend(0, jnp.int32(0), *rest, halves[0], question_kv)
        return attend(0, jnp.int32(1), *rest, halves[1], question_kv, context)

    place = place_of(chip, chips).reshape(1)
    order = [2 * line for line in range(chips // 2)] + [2 * line + 1 for line in range(chips // 2)][::-1]

    def to_partner(x):
        return lax.ppermute(x, "pass", [(i, i ^ 1) for i in range(extent)])

    def along(x, target):
        pairs = [(c, target(c // 2, c % 2)) for c in range(chips)]
        return lax.ppermute(x, "pass", [(2 * s + c, 2 * d + c) for s, d in pairs for c in range(2)])

    def along_ring(x, step):
        return along(x, lambda line, lane: order[(order.index(2 * line + lane) + step) % chips])

    def round_the_ring(x, up, down, rounds):
        up, down = [x, up], [down]
        while len(up) <= rounds:
            up.append(along_ring(up[-1], 1))
        while len(up) + len(down) < chips:
            down.append(along_ring(down[-1], -1))
        return up + down[::-1]

    def line_by_line(block):
        lines = chips // 2
        blocks = [block]
        for k in range(1, lines):
            blocks.append(along(block, lambda line, lane: 2 * ((line + k) % lines) + lane))
        return blocks + [along(x, lambda line, lane: 2 * line + 1 - lane) for x in blocks]

    def columns(half):
        return jnp.concatenate(
            [
                lax.dynamic_slice_in_dim(kv_weight, half * LANES + at, LANES, axis=1)
                for at in (0, KVH * HD)
            ],
            axis=1,
        )

    pieces = [columns(core), to_partner(columns(1 - core))]
    hops = [along_ring(x, step) for x in pieces for step in (1, -1)]
    memory_rows = pool(passage_states, memory_queries, memory_gain)
    *hops, memory_rows = lax.optimization_barrier((*hops, memory_rows))
    weights = round_the_ring(pieces[0], hops[0], hops[1], chips // 2)
    weights += round_the_ring(pieces[1], hops[2], hops[3], chips // 2 - 1)
    memory_kv = project(core, place, memory_rows, to_partner(memory_rows), weights)
    near = jnp.concatenate(line_by_line(memory_kv), axis=0)
    far = to_partner(near)

    rest = (place, retrieval, question_lengths, question_queries)
    context = attend(chips, core, *rest, near, question_kv)
    return attend(chips, 1 - core, *rest, far, question_kv, context)


def solution(mesh):
    placed = (
        P(("groups", "pass"), None, None),
        P(),
        P(),
        P("pass", None),
        P(("groups", "pass"), None),
        P(("groups", "pass"), None, None),
        P(("groups", "pass"), None, None),
        P(("groups", "pass")),
    )
    return jax.shard_map(
        functools.partial(local, mesh.shape["pass"]),
        mesh=mesh,
        in_specs=placed,
        out_specs=P(("groups", "pass"), None, None),
        check_vma=False,
    )
```

```python
import functools
import math

import jax
import jax.numpy as jnp
from jax import lax
from jax.experimental import pallas as pl
from jax.experimental.pallas import tpu as pltpu
from jax.sharding import PartitionSpec as P

D = 4096
CH = 32
CHD = 128
MEM = 32
LEN = 128
QLEN = 64
TOPK = 16
H = 116
HD = 64
KVH = 4
GROUP = 29
KVW = 512

LANES = 2 * HD
PAIRS = GROUP
HALF = PAIRS * LANES
ROWS = TOPK * MEM
KEYS = 2 * (ROWS + QLEN)
NEG = -1e30
SUM_LOW, SUM_HIGH = 2.0 ** -40, 2.0 ** 60
POOL_WIDTH = 1024
CHIP = 8
STEP = 8
BLOCK = 16
MIB = 1024 * 1024


def place_of(chip, ring):
    line, lane = lax.div(chip, 2), lax.rem(chip, 2)
    return line + lane * (ring - 1 - 2 * line)


def chip_at(place, ring):
    lane = lax.div(place, ring // 2)
    line = place + lane * (ring - 1 - 2 * place)
    return 2 * line + lane


def pool_kernel(states_hbm, queries_hbm, gain_hbm, out_ref, states, queries, gain, pooled, arrived):
    passages = states_hbm.shape[0]
    two = 2 * CHD
    groups = D // POOL_WIDTH
    small = [
        pltpu.make_async_copy(queries_hbm, queries, arrived.at[groups]),
        pltpu.make_async_copy(gain_hbm, gain, arrived.at[groups + 1]),
    ]
    large = [
        pltpu.make_async_copy(
            states_hbm.at[:, :, pl.ds(j * POOL_WIDTH, POOL_WIDTH)], states.at[j], arrived.at[j]
        )
        for j in range(groups)
    ]
    for copy in small[:1] + large + small[1:]:
        copy.start()
    small[0].wait()
    zero = jnp.zeros((MEM, CHD), jnp.bfloat16)
    blank = jnp.zeros((2 * MEM, LEN), jnp.bfloat16)
    totals = [jnp.zeros((MEM, CHD), jnp.float32)] * passages
    for j in range(groups):
        large[j].wait()
        blocks = []
        for at in range(0, POOL_WIDTH, two):
            column = j * POOL_WIDTH + at
            lhs = jnp.concatenate(
                [
                    jnp.concatenate([queries[:, column:column + CHD], zero], axis=1),
                    jnp.concatenate([zero, queries[:, column + CHD:column + two]], axis=1),
                ],
                axis=0,
            )
            for p in range(0, passages, 2):
                tokens = states[j, p:p + 2, :, at:at + two].reshape(2 * LEN, two)
                scores = lax.dot_general(
                    lhs, tokens, (((1,), (1,)), ((), ())), preferred_element_type=jnp.float32
                ) * (1.0 / math.sqrt(CHD))
                blocks.append((column, p, tokens, scores))
        for column, p, tokens, scores in blocks:
            rows = []
            for n in range(2):
                part = scores[:, n * LEN:(n + 1) * LEN]
                part = jnp.exp(part - jnp.max(part, axis=1, keepdims=True))
                part = (part / jnp.sum(part, axis=1, keepdims=True)).astype(jnp.bfloat16)
                rows.append(jnp.concatenate([blank, part] if n else [part, blank], axis=1))
            mixed = jnp.dot(jnp.concatenate(rows, axis=0), tokens, preferred_element_type=jnp.float32)
            for n in range(2):
                for head in range(2):
                    top = (2 * n + head) * MEM
                    block = mixed[top:top + MEM, head * CHD:(head + 1) * CHD]
                    place = slice(column + head * CHD, column + (head + 1) * CHD)
                    pooled[(p + n) * MEM:(p + n + 1) * MEM, place] = block
                    totals[p + n] = totals[p + n] + block * block
    small[1].wait()
    mean_square = jnp.sum(jnp.concatenate(totals, axis=0), axis=1, keepdims=True) * (1.0 / D)
    scale = lax.rsqrt(mean_square + 1e-06)
    factor = gain[...].astype(jnp.float32).reshape(1, D)
    out_ref[...] = (pooled[...] * scale * factor).astype(jnp.bfloat16)


def pool(states, queries, gain):
    count = states.shape[0]
    groups = D // POOL_WIDTH
    hbm = pl.BlockSpec(memory_space=pltpu.HBM)
    return pl.pallas_call(
        pool_kernel,
        in_specs=[hbm] * 3,
        out_specs=pl.BlockSpec(memory_space=pltpu.VMEM),
        out_shape=jax.ShapeDtypeStruct((count * MEM, D), jnp.bfloat16),
        scratch_shapes=[
            pltpu.VMEM((groups, count, LEN, POOL_WIDTH), jnp.bfloat16),
            pltpu.VMEM((MEM, D), jnp.bfloat16),
            pltpu.VMEM((D,), jnp.bfloat16),
            pltpu.VMEM((count * MEM, D), jnp.float32),
            pltpu.SemaphoreType.DMA((groups + 2,)),
        ],
        compiler_params=pltpu.CompilerParams(vmem_limit_bytes=56 * MIB),
        cost_estimate=pl.CostEstimate(
            flops=4 * count * MEM * LEN * D, bytes_accessed=2 * count * LEN * D,
            transcendentals=count * CH * MEM * LEN,
        ),
        name="pool",
    )(states, queries, gain)


def attend_kernel(half_ref, start_ref, length_ref, q_hbm, kv_ref, own_kv_ref, *rest):
    out_hbm = rest[-13]
    (
        questions, answers, memory, key_side, value_side, weights, bias, marker, scores, all_weights,
        arrived, sent,
    ) = rest[-12:]
    count = q_hbm.shape[0]
    half_at = pl.multiple_of(half_ref[0] * HALF, LANES)
    own_at = pl.multiple_of(half_ref[0] * LANES, LANES)
    factor = math.log2(math.e) / math.sqrt(HD)

    def fetch(query):
        return pltpu.make_async_copy(
            q_hbm.at[query, :, pl.ds(half_at, HALF)], questions.at[query], arrived.at[query]
        )

    def send(query):
        return pltpu.make_async_copy(
            answers.at[query], out_hbm.at[query, :, pl.ds(half_at, HALF)], sent.at[query]
        )

    for query in range(count):
        fetch(query).start()

    lane = lax.broadcasted_iota(jnp.int32, (KEYS, LANES), 1)
    row = lax.broadcasted_iota(jnp.int32, (KEYS, LANES), 0)
    in_b = ((row >= ROWS) & (row < 2 * ROWS)) | (row >= 2 * ROWS + QLEN)
    ones = jnp.where((lane >= HD) == in_b, 1.0, 0.0).astype(jnp.bfloat16)
    key_side[...] = jnp.zeros_like(key_side)
    for g in range(2):
        value_side[g, :, LANES:] = ones

    half = PAIRS // 2
    chunks = []
    for g in range(2):
        tiles = list(range(half + 1)) if g == 0 else list(range(half, PAIRS))
        chunks += [(g, tiles[at:at + STEP]) for at in range(0, len(tiles), STEP)]

    def answer(query, carry):
        for slot in range(TOPK):
            start = pl.multiple_of(start_ref[query, slot], MEM)
            memory[slot * MEM:(slot + 1) * MEM, :] = kv_ref[pl.ds(start, MEM), :].astype(jnp.float32)
        length = length_ref[query]

        turned = jnp.transpose(memory[:, :LANES]).astype(jnp.bfloat16)
        own_k = own_kv_ref[query, :, pl.ds(own_at, LANES)].astype(jnp.float32)
        own_turned = jnp.transpose(jnp.concatenate([own_k, own_k], axis=0))
        column = lax.broadcasted_iota(jnp.int32, (HD, LANES), 1)
        for g in range(2):
            for member in range(2):
                rows = slice(member * HD, (member + 1) * HD)
                key_side[g, rows, member * ROWS:(member + 1) * ROWS] = turned[g * HD:(g + 1) * HD]
                own = own_turned[g * HD:(g + 1) * HD]
                mine = (column >= HD) if member else (column < HD)
                key_side[g, rows, 2 * ROWS:] = jnp.where(mine, own, 0.0).astype(jnp.bfloat16)

        token = lax.broadcasted_iota(jnp.int32, (QLEN, LANES), 0)
        low = lax.broadcasted_iota(jnp.int32, (QLEN, LANES), 1) < HD
        key = lax.rem(lax.broadcasted_iota(jnp.int32, (QLEN, LANES), 1), HD)
        bias[...] = jnp.where((key <= token) & (key < length), 0.0, NEG)
        alive = token < length
        fetch(query).wait()

        def stacked(tiles):
            return jnp.concatenate([questions[query, :, t * LANES:(t + 1) * LANES] for t in tiles], axis=0)

        def key_product(i):
            g, tiles = chunks[i]
            lhs = stacked(tiles)
            for c in range(0, KEYS, 2 * LANES):
                part = slice(c, min(c + 2 * LANES, KEYS))
                got = jnp.dot(lhs, key_side[g, :, part], preferred_element_type=jnp.float32) * factor
                if c == 2 * ROWS:
                    got = got + jnp.concatenate([bias[...]] * len(tiles), axis=0)
                weights[i % 2, :len(tiles) * QLEN, part] = jnp.exp2(got).astype(jnp.bfloat16)

        def finish(i, mixed):
            g, tiles = chunks[i]
            for n, t in enumerate(tiles):
                rows = slice(n * QLEN, (n + 1) * QLEN)
                result = jnp.where(alive, mixed[rows, :LANES] / mixed[rows, LANES:], 0.0)
                result = result.astype(jnp.bfloat16)
                at = slice(t * LANES, (t + 1) * LANES)
                if t == half and g == 1:
                    result = jnp.where(low, answers[query, :, at], result)
                answers[query, :, at] = result

        def value_product(i, seen):
            g, tiles = chunks[i]
            size = len(tiles) * QLEN
            mixed = jnp.dot(weights[i % 2, :size, :], value_side[g], preferred_element_type=jnp.float32)
            for at in range(0, size, QLEN):
                sums = mixed[at:at + QLEN, LANES:]
                seen = jnp.where((sums > SUM_LOW) & (sums < SUM_HIGH), seen, 1.0)
            finish(i, mixed)
            return seen

        key_product(0)

        own_v_at = pl.multiple_of(own_at + KVH * HD, LANES)
        own_v = own_kv_ref[query, :, pl.ds(own_v_at, LANES)].astype(jnp.float32)
        for block, at in ((memory[:, LANES:], 0), (own_v, 2 * ROWS)):
            size = block.shape[0]
            swapped = pltpu.roll(block, HD, 1)
            lower = lax.broadcasted_iota(jnp.int32, block.shape, 1) < HD
            for g in range(2):
                one, two = (block, swapped) if g == 0 else (swapped, block)
                value_side[g, at:at + size, :LANES] = jnp.where(lower, one, 0.0).astype(jnp.bfloat16)
                value_side[g, at + size:at + 2 * size, :LANES] = jnp.where(lower, 0.0, two).astype(
                    jnp.bfloat16
                )

        seen = jnp.zeros((QLEN, LANES), jnp.float32)
        for i in range(len(chunks)):
            if i + 1 < len(chunks):
                key_product(i + 1)
            seen = value_product(i, seen)
        marker[0] = jnp.max(seen)

        @pl.when(marker[0] > 0.0)
        def _():
            for i, (g, tiles) in enumerate(chunks):
                size = len(tiles) * QLEN
                scores[:size, :] = jnp.dot(stacked(tiles), key_side[g], preferred_element_type=jnp.float32)

                def soften(n, carry):
                    rows = pl.ds(pl.multiple_of(n * QLEN, QLEN), QLEN)
                    own_scores = scores[rows, 2 * ROWS:] + bias[...]
                    tops = []
                    for member in range(2):
                        columns = slice(member * ROWS, (member + 1) * ROWS)
                        top = jnp.where(low, own_scores, NEG) if member == 0 else jnp.where(low, NEG, own_scores)
                        top = jnp.maximum(
                            jnp.max(top, axis=1, keepdims=True),
                            jnp.max(scores[rows, columns], axis=1, keepdims=True),
                        )
                        all_weights[rows, columns] = jnp.exp2(
                            (scores[rows, columns] - top) * factor
                        ).astype(jnp.bfloat16)
                        tops.append(top)
                    all_weights[rows, 2 * ROWS:] = jnp.exp2(
                        (own_scores - jnp.where(low, tops[0], tops[1])) * factor
                    ).astype(jnp.bfloat16)
                    return carry

                lax.fori_loop(0, len(tiles), soften, 0)
                finish(
                    i, jnp.dot(all_weights[:size, :], value_side[g], preferred_element_type=jnp.float32)
                )

        send(query).start()
        return carry

    lax.fori_loop(0, count, answer, 0)
    for query in range(count):
        send(query).wait()


def attend(half, starts, lengths, questions, memory_kv, own_kv, earlier=None):
    count = questions.shape[0]
    hbm, vmem, smem = (pl.BlockSpec(memory_space=x) for x in (pltpu.HBM, pltpu.VMEM, pltpu.SMEM))
    operands = [half.reshape(1), starts, lengths, questions, memory_kv, own_kv]
    in_specs = [smem, smem, smem, hbm, vmem, vmem]
    aliases = {}
    if earlier is not None:
        aliases = {len(operands): 0}
        operands.append(earlier)
        in_specs.append(hbm)
    return pl.pallas_call(
        attend_kernel,
        in_specs=in_specs,
        out_specs=hbm,
        out_shape=jax.ShapeDtypeStruct((count, QLEN, H * HD), jnp.bfloat16),
        scratch_shapes=[
            pltpu.VMEM((count, QLEN, HALF), jnp.bfloat16),
            pltpu.VMEM((count, QLEN, HALF), jnp.bfloat16),
            pltpu.VMEM((ROWS, 2 * LANES), jnp.float32),
            pltpu.VMEM((2, LANES, KEYS), jnp.bfloat16),
            pltpu.VMEM((2, KEYS, 2 * LANES), jnp.bfloat16),
            pltpu.VMEM((2, STEP * QLEN, KEYS), jnp.bfloat16),
            pltpu.VMEM((QLEN, LANES), jnp.float32),
            pltpu.SMEM((1,), jnp.float32),
            pltpu.VMEM((STEP * QLEN, KEYS), jnp.float32),
            pltpu.VMEM((STEP * QLEN, KEYS), jnp.bfloat16),
            pltpu.SemaphoreType.DMA((count,)),
            pltpu.SemaphoreType.DMA((count,)),
        ],
        input_output_aliases=aliases,
        compiler_params=pltpu.CompilerParams(vmem_limit_bytes=40 * MIB),
        cost_estimate=pl.CostEstimate(
            flops=2 * count * QLEN * H * HD * (ROWS + QLEN),
            bytes_accessed=2 * count * QLEN * H * HD,
            transcendentals=count * QLEN * H * (ROWS + QLEN) // 2,
        ),
        name="attend",
    )(*operands)


def project_kernel(ring, core_ref, place_ref, own_hbm, other_ref, *rest):
    weights, (out_ref, own, arrived) = rest[:-3], rest[-3:]
    count = own.shape[0]
    depth = weights[0].shape[0]
    core = core_ref[0]
    pieces = []
    for n, weight in enumerate(weights):
        part, i = n // ring, n % ring
        chip = chip_at(lax.rem(ring + place_ref[0] - i, ring), ring)
        columns = pl.ds(pl.multiple_of((2 * chip + (1 - core if part else core)) * depth, depth), depth)
        copy = pltpu.make_async_copy(own_hbm.at[:, columns], own.at[:, columns], arrived.at[n])
        copy.start()
        pieces.append((weight, columns, copy))
    total = jnp.zeros((2 * count, weights[0].shape[1]), jnp.float32)
    for weight, columns, copy in pieces:
        copy.wait()
        rows = jnp.concatenate([own[:, columns], other_ref[:, columns]], axis=0)
        total += jnp.dot(rows, weight[...], preferred_element_type=jnp.float32)
    result = total.astype(jnp.bfloat16)
    out_ref[pl.ds(pl.multiple_of(core * count, count), count)] = result[:count]
    out_ref[pl.ds(pl.multiple_of((1 - core) * count, count), count)] = result[count:]


def project(core, place, own_rows, other_rows, weights):
    count = own_rows.shape[0]
    width = weights[0].shape[1]
    vmem = pl.BlockSpec(memory_space=pltpu.VMEM)
    smem = pl.BlockSpec(memory_space=pltpu.SMEM)
    return pl.pallas_call(
        functools.partial(project_kernel, len(weights) // 2),
        in_specs=[smem, smem, pl.BlockSpec(memory_space=pltpu.HBM)] + [vmem] * (1 + len(weights)),
        out_specs=vmem,
        scratch_shapes=[pltpu.VMEM(own_rows.shape, jnp.bfloat16), pltpu.SemaphoreType.DMA((len(weights),))],
        out_shape=jax.ShapeDtypeStruct((2 * count, width), jnp.bfloat16),
        compiler_params=pltpu.CompilerParams(vmem_limit_bytes=16 * MIB),
        cost_estimate=pl.CostEstimate(
            flops=4 * count * D * width, bytes_accessed=2 * D * width, transcendentals=0
        ),
        name="project",
    )(core.reshape(1), place, own_rows, other_rows, *weights)


def local(
    extent,
    passage_states,
    memory_queries,
    memory_gain,
    kv_weight,
    retrieval,
    question_queries,
    question_kv,
    question_lengths,
):
    me = lax.axis_index("pass")
    core, chip = me & 1, lax.div(me, 2)
    chips = extent // 2
    depth = kv_weight.shape[0]

    if chips != 8 or depth % LANES:
        memory_rows = pool(passage_states, memory_queries, memory_gain)
        whole_weight = lax.all_gather(kv_weight, "pass", axis=0, tiled=True)
        memory_kv = jnp.dot(memory_rows, whole_weight, preferred_element_type=jnp.float32)
        everything = lax.all_gather(memory_kv.astype(jnp.bfloat16), "pass", axis=0, tiled=True)
        halves = everything.reshape(-1, 2, 2, LANES).transpose(2, 0, 1, 3).reshape(2, -1, 2 * LANES)
        rest = (retrieval * MEM, question_lengths, question_queries)
        context = attend(jnp.int32(0), *rest, halves[0], question_kv)
        return attend(jnp.int32(1), *rest, halves[1], question_kv, context)

    place = place_of(chip, chips).reshape(1)
    order = [2 * line for line in range(chips // 2)] + [2 * line + 1 for line in range(chips // 2)][::-1]

    def to_partner(x):
        return lax.ppermute(x, "pass", [(i, i ^ 1) for i in range(extent)])

    def along(x, target):
        pairs = [(c, target(c // 2, c % 2)) for c in range(chips)]
        return lax.ppermute(x, "pass", [(2 * s + c, 2 * d + c) for s, d in pairs for c in range(2)])

    def along_ring(x, step):
        return along(x, lambda line, lane: order[(order.index(2 * line + lane) + step) % chips])

    def round_the_ring(x, up, down, rounds):
        up, down = [x, up], [down]
        while len(up) <= rounds:
            up.append(along_ring(up[-1], 1))
        while len(up) + len(down) < chips:
            down.append(along_ring(down[-1], -1))
        return up + down[::-1]

    def line_by_line(block):
        lines = chips // 2
        blocks = [block]
        for k in range(1, lines):
            blocks.append(along(block, lambda line, lane: 2 * ((line + k) % lines) + lane))
        return blocks + [along(x, lambda line, lane: 2 * line + 1 - lane) for x in blocks]

    def columns(half):
        return jnp.concatenate(
            [
                lax.dynamic_slice_in_dim(kv_weight, half * LANES + at, LANES, axis=1)
                for at in (0, KVH * HD)
            ],
            axis=1,
        )

    pieces = [columns(core), to_partner(columns(1 - core))]
    hops = [along_ring(x, step) for x in pieces for step in (1, -1)]
    memory_rows = pool(passage_states, memory_queries, memory_gain)
    *hops, memory_rows = lax.optimization_barrier((*hops, memory_rows))
    weights = round_the_ring(pieces[0], hops[0], hops[1], chips // 2)
    weights += round_the_ring(pieces[1], hops[2], hops[3], chips // 2 - 1)
    memory_kv = project(core, place, memory_rows, to_partner(memory_rows), weights)
    near = jnp.concatenate(line_by_line(memory_kv), axis=0)
    far = to_partner(near)

    lines = chips // 2
    of_chip = lax.div(retrieval, CHIP)
    back = lax.rem(lines + lax.div(chip, 2) - lax.div(of_chip, 2), lines)
    slot = back + lines * lax.rem(lax.rem(chip, 2) + lax.rem(of_chip, 2), 2)
    starts = (slot * CHIP + lax.rem(retrieval, CHIP)) * MEM
    rest = (starts, question_lengths, question_queries)
    context = attend(core, *rest, near, question_kv)
    return attend(1 - core, *rest, far, question_kv, context)


def solution(mesh):
    placed = (
        P(("groups", "pass"), None, None),
        P(),
        P(),
        P("pass", None),
        P(("groups", "pass"), None),
        P(("groups", "pass"), None, None),
        P(("groups", "pass"), None, None),
        P(("groups", "pass")),
    )
    return jax.shard_map(
        functools.partial(local, mesh.shape["pass"]),
        mesh=mesh,
        in_specs=placed,
        out_specs=P(("groups", "pass"), None, None),
        check_vma=False,
    )
```

```python
import functools
import math

import jax
import jax.numpy as jnp
from jax import lax
from jax.experimental import pallas as pl
from jax.experimental.pallas import tpu as pltpu
from jax.sharding import PartitionSpec as P

D = 4096
CH = 32
CHD = 128
MEM = 32
LEN = 128
QLEN = 64
TOPK = 16
H = 116
HD = 64
KVH = 4
GROUP = 29
KVW = 512

LANES = 2 * HD
PAIRS = GROUP
HALF = PAIRS * LANES
ROWS = TOPK * MEM
KEYS = 2 * (ROWS + QLEN)
NEG = -1e30
SUM_LOW, SUM_HIGH = 2.0 ** -40, 2.0 ** 60
POOL_WIDTH = 1024
POOL_CALLS = 2
CHIP = 8
STEP = 8
BLOCK = 16
MIB = 1024 * 1024


def place_of(chip, ring):
    line, lane = lax.div(chip, 2), lax.rem(chip, 2)
    return line + lane * (ring - 1 - 2 * line)


def chip_at(place, ring):
    lane = lax.div(place, ring // 2)
    line = place + lane * (ring - 1 - 2 * place)
    return 2 * line + lane


def pool_kernel(first, states_hbm, queries_hbm, gain_hbm, out_ref, states, queries, gain, pooled, arrived):
    passages = states.shape[1]
    two = 2 * CHD
    groups = D // POOL_WIDTH
    small = [
        pltpu.make_async_copy(queries_hbm, queries, arrived.at[groups]),
        pltpu.make_async_copy(gain_hbm, gain, arrived.at[groups + 1]),
    ]
    large = [
        pltpu.make_async_copy(
            states_hbm.at[pl.ds(first, passages), :, pl.ds(j * POOL_WIDTH, POOL_WIDTH)],
            states.at[j],
            arrived.at[j],
        )
        for j in range(groups)
    ]
    for copy in small[:1] + large + small[1:]:
        copy.start()
    small[0].wait()
    zero = jnp.zeros((MEM, CHD), jnp.bfloat16)
    blank = jnp.zeros((2 * MEM, LEN), jnp.bfloat16)
    totals = [jnp.zeros((MEM, CHD), jnp.float32)] * passages
    for j in range(groups):
        large[j].wait()
        blocks = []
        for at in range(0, POOL_WIDTH, two):
            column = j * POOL_WIDTH + at
            lhs = jnp.concatenate(
                [
                    jnp.concatenate([queries[:, column:column + CHD], zero], axis=1),
                    jnp.concatenate([zero, queries[:, column + CHD:column + two]], axis=1),
                ],
                axis=0,
            )
            for p in range(0, passages, 2):
                tokens = states[j, p:p + 2, :, at:at + two].reshape(2 * LEN, two)
                scores = lax.dot_general(
                    lhs, tokens, (((1,), (1,)), ((), ())), preferred_element_type=jnp.float32
                ) * (1.0 / math.sqrt(CHD))
                blocks.append((column, p, tokens, scores))
        for column, p, tokens, scores in blocks:
            rows = []
            for n in range(2):
                part = scores[:, n * LEN:(n + 1) * LEN]
                part = jnp.exp(part - jnp.max(part, axis=1, keepdims=True))
                part = (part / jnp.sum(part, axis=1, keepdims=True)).astype(jnp.bfloat16)
                rows.append(jnp.concatenate([blank, part] if n else [part, blank], axis=1))
            mixed = jnp.dot(jnp.concatenate(rows, axis=0), tokens, preferred_element_type=jnp.float32)
            for n in range(2):
                for head in range(2):
                    top = (2 * n + head) * MEM
                    block = mixed[top:top + MEM, head * CHD:(head + 1) * CHD]
                    place = slice(column + head * CHD, column + (head + 1) * CHD)
                    pooled[(p + n) * MEM:(p + n + 1) * MEM, place] = block
                    totals[p + n] = totals[p + n] + block * block
    small[1].wait()
    mean_square = jnp.sum(jnp.concatenate(totals, axis=0), axis=1, keepdims=True) * (1.0 / D)
    scale = lax.rsqrt(mean_square + 1e-06)
    factor = gain[...].astype(jnp.float32).reshape(1, D)
    out_ref[...] = (pooled[...] * scale * factor).astype(jnp.bfloat16)


def pool(states, queries, gain, first, count):
    groups = D // POOL_WIDTH
    hbm = pl.BlockSpec(memory_space=pltpu.HBM)
    return pl.pallas_call(
        functools.partial(pool_kernel, first),
        in_specs=[hbm] * 3,
        out_specs=pl.BlockSpec(memory_space=pltpu.VMEM),
        out_shape=jax.ShapeDtypeStruct((count * MEM, D), jnp.bfloat16),
        scratch_shapes=[
            pltpu.VMEM((groups, count, LEN, POOL_WIDTH), jnp.bfloat16),
            pltpu.VMEM((MEM, D), jnp.bfloat16),
            pltpu.VMEM((D,), jnp.bfloat16),
            pltpu.VMEM((count * MEM, D), jnp.float32),
            pltpu.SemaphoreType.DMA((groups + 2,)),
        ],
        compiler_params=pltpu.CompilerParams(vmem_limit_bytes=56 * MIB),
        cost_estimate=pl.CostEstimate(
            flops=4 * count * MEM * LEN * D, bytes_accessed=2 * count * LEN * D,
            transcendentals=count * CH * MEM * LEN,
        ),
        name="pool",
    )(states, queries, gain)


def attend_kernel(half_ref, start_ref, length_ref, q_hbm, kv_ref, own_kv_ref, *rest):
    out_hbm = rest[-13]
    (
        questions, answers, memory, key_side, value_side, weights, bias, marker, scores, all_weights,
        arrived, sent,
    ) = rest[-12:]
    count = q_hbm.shape[0]
    half_at = pl.multiple_of(half_ref[0] * HALF, LANES)
    own_at = pl.multiple_of(half_ref[0] * LANES, LANES)
    factor = math.log2(math.e) / math.sqrt(HD)

    def fetch(query):
        return pltpu.make_async_copy(
            q_hbm.at[query, :, pl.ds(half_at, HALF)], questions.at[query], arrived.at[query]
        )

    def send(query):
        return pltpu.make_async_copy(
            answers.at[query], out_hbm.at[query, :, pl.ds(half_at, HALF)], sent.at[query]
        )

    for query in range(count):
        fetch(query).start()

    lane = lax.broadcasted_iota(jnp.int32, (KEYS, LANES), 1)
    row = lax.broadcasted_iota(jnp.int32, (KEYS, LANES), 0)
    in_b = ((row >= ROWS) & (row < 2 * ROWS)) | (row >= 2 * ROWS + QLEN)
    ones = jnp.where((lane >= HD) == in_b, 1.0, 0.0).astype(jnp.bfloat16)
    key_side[...] = jnp.zeros_like(key_side)
    for g in range(2):
        value_side[g, :, LANES:] = ones

    half = PAIRS // 2
    chunks = []
    for g in range(2):
        tiles = list(range(half + 1)) if g == 0 else list(range(half, PAIRS))
        chunks += [(g, tiles[at:at + STEP]) for at in range(0, len(tiles), STEP)]

    def answer(query, carry):
        for slot in range(TOPK):
            start = pl.multiple_of(start_ref[query, slot], MEM)
            memory[slot * MEM:(slot + 1) * MEM, :] = kv_ref[pl.ds(start, MEM), :]
        length = length_ref[query]

        turned = jnp.transpose(memory[:, :LANES])
        own_k = own_kv_ref[query, :, pl.ds(own_at, LANES)]
        own_turned = jnp.transpose(jnp.concatenate([own_k, own_k], axis=0))
        column = lax.broadcasted_iota(jnp.int32, (HD, LANES), 1)
        for g in range(2):
            for member in range(2):
                rows = slice(member * HD, (member + 1) * HD)
                key_side[g, rows, member * ROWS:(member + 1) * ROWS] = turned[g * HD:(g + 1) * HD]
                own = own_turned[g * HD:(g + 1) * HD]
                mine = (column >= HD) if member else (column < HD)
                key_side[g, rows, 2 * ROWS:] = jnp.where(mine, own, jnp.zeros_like(own))

        token = lax.broadcasted_iota(jnp.int32, (QLEN, LANES), 0)
        low = lax.broadcasted_iota(jnp.int32, (QLEN, LANES), 1) < HD
        key = lax.rem(lax.broadcasted_iota(jnp.int32, (QLEN, LANES), 1), HD)
        bias[...] = jnp.where((key <= token) & (key < length), 0.0, NEG)
        alive = token < length
        sample = lax.div(key, HD // STEP)
        fetch(query).wait()

        def stacked(tiles):
            return jnp.concatenate([questions[query, :, t * LANES:(t + 1) * LANES] for t in tiles], axis=0)

        def key_product(i):
            g, tiles = chunks[i]
            lhs = stacked(tiles)
            for c in range(0, KEYS, 2 * LANES):
                part = slice(c, min(c + 2 * LANES, KEYS))
                got = jnp.dot(lhs, key_side[g, :, part], preferred_element_type=jnp.float32) * factor
                if c == 2 * ROWS:
                    got = got + jnp.concatenate([bias[...]] * len(tiles), axis=0)
                weights[i % 2, :len(tiles) * QLEN, part] = jnp.exp2(got).astype(jnp.bfloat16)

        def finish(i, mixed):
            g, tiles = chunks[i]
            for n, t in enumerate(tiles):
                rows = slice(n * QLEN, (n + 1) * QLEN)
                sums = mixed[rows, LANES:]
                inverse = pl.reciprocal(sums, approx=True)
                inverse = inverse * (2.0 - sums * inverse)
                result = jnp.where(alive, mixed[rows, :LANES] * inverse, 0.0).astype(jnp.bfloat16)
                at = slice(t * LANES, (t + 1) * LANES)
                if t == half and g == 1:
                    result = jnp.where(low, answers[query, :, at], result)
                answers[query, :, at] = result

        def value_product(i, seen):
            g, tiles = chunks[i]
            size = len(tiles) * QLEN
            mixed = jnp.dot(weights[i % 2, :size, :], value_side[g], preferred_element_type=jnp.float32)
            sums = mixed[:QLEN, LANES:]
            for n in range(1, len(tiles)):
                sums = jnp.where(sample == n, mixed[n * QLEN:(n + 1) * QLEN, LANES:], sums)
            seen = jnp.where((sums > SUM_LOW) & (sums < SUM_HIGH), seen, 1.0)
            finish(i, mixed)
            return seen

        key_product(0)

        own_v_at = pl.multiple_of(own_at + KVH * HD, LANES)
        own_v = own_kv_ref[query, :, pl.ds(own_v_at, LANES)]
        for block, at in ((memory[:, LANES:], 0), (own_v, 2 * ROWS)):
            size = block.shape[0]
            swapped = jnp.concatenate([block[:, HD:], block[:, :HD]], axis=1)
            lower = lax.broadcasted_iota(jnp.int32, block.shape, 1) < HD
            zero = jnp.zeros_like(block)
            for g in range(2):
                one, two = (block, swapped) if g == 0 else (swapped, block)
                value_side[g, at:at + size, :LANES] = jnp.where(lower, one, zero)
                value_side[g, at + size:at + 2 * size, :LANES] = jnp.where(lower, zero, two)

        seen = jnp.zeros((QLEN, LANES), jnp.float32)
        for i in range(len(chunks)):
            if i + 1 < len(chunks):
                key_product(i + 1)
            seen = value_product(i, seen)
        marker[0] = jnp.max(seen)

        @pl.when(marker[0] > 0.0)
        def _():
            for i, (g, tiles) in enumerate(chunks):
                size = len(tiles) * QLEN
                scores[:size, :] = jnp.dot(stacked(tiles), key_side[g], preferred_element_type=jnp.float32)

                def soften(n, carry):
                    rows = pl.ds(pl.multiple_of(n * QLEN, QLEN), QLEN)
                    own_scores = scores[rows, 2 * ROWS:] + bias[...]
                    tops = []
                    for member in range(2):
                        columns = slice(member * ROWS, (member + 1) * ROWS)
                        top = jnp.where(low, own_scores, NEG) if member == 0 else jnp.where(low, NEG, own_scores)
                        top = jnp.maximum(
                            jnp.max(top, axis=1, keepdims=True),
                            jnp.max(scores[rows, columns], axis=1, keepdims=True),
                        )
                        all_weights[rows, columns] = jnp.exp2(
                            (scores[rows, columns] - top) * factor
                        ).astype(jnp.bfloat16)
                        tops.append(top)
                    all_weights[rows, 2 * ROWS:] = jnp.exp2(
                        (own_scores - jnp.where(low, tops[0], tops[1])) * factor
                    ).astype(jnp.bfloat16)
                    return carry

                lax.fori_loop(0, len(tiles), soften, 0)
                finish(
                    i, jnp.dot(all_weights[:size, :], value_side[g], preferred_element_type=jnp.float32)
                )

        send(query).start()
        return carry

    lax.fori_loop(0, count, answer, 0)
    for query in range(count):
        send(query).wait()


def attend(half, starts, lengths, questions, memory_kv, own_kv, earlier=None):
    count = questions.shape[0]
    hbm, vmem, smem = (pl.BlockSpec(memory_space=x) for x in (pltpu.HBM, pltpu.VMEM, pltpu.SMEM))
    operands = [half.reshape(1), starts, lengths, questions, memory_kv, own_kv]
    in_specs = [smem, smem, smem, hbm, vmem, vmem]
    aliases = {}
    if earlier is not None:
        aliases = {len(operands): 0}
        operands.append(earlier)
        in_specs.append(hbm)
    return pl.pallas_call(
        attend_kernel,
        in_specs=in_specs,
        out_specs=hbm,
        out_shape=jax.ShapeDtypeStruct((count, QLEN, H * HD), jnp.bfloat16),
        scratch_shapes=[
            pltpu.VMEM((count, QLEN, HALF), jnp.bfloat16),
            pltpu.VMEM((count, QLEN, HALF), jnp.bfloat16),
            pltpu.VMEM((ROWS, 2 * LANES), jnp.bfloat16),
            pltpu.VMEM((2, LANES, KEYS), jnp.bfloat16),
            pltpu.VMEM((2, KEYS, 2 * LANES), jnp.bfloat16),
            pltpu.VMEM((2, STEP * QLEN, KEYS), jnp.bfloat16),
            pltpu.VMEM((QLEN, LANES), jnp.float32),
            pltpu.SMEM((1,), jnp.float32),
            pltpu.VMEM((STEP * QLEN, KEYS), jnp.float32),
            pltpu.VMEM((STEP * QLEN, KEYS), jnp.bfloat16),
            pltpu.SemaphoreType.DMA((count,)),
            pltpu.SemaphoreType.DMA((count,)),
        ],
        input_output_aliases=aliases,
        compiler_params=pltpu.CompilerParams(vmem_limit_bytes=50 * MIB),
        cost_estimate=pl.CostEstimate(
            flops=2 * count * QLEN * H * HD * (ROWS + QLEN),
            bytes_accessed=2 * count * QLEN * H * HD,
            transcendentals=count * QLEN * H * (ROWS + QLEN) // 2,
        ),
        name="attend",
    )(*operands)


def project_kernel(ring, parts, core_ref, place_ref, *rest):
    row_refs, weights, out_ref = rest[:2 * parts], rest[2 * parts:-1], rest[-1]
    count = parts * row_refs[0].shape[0]
    depth = weights[0].shape[0]
    total = jnp.zeros((2 * count, weights[0].shape[1]), jnp.float32)
    core = core_ref[0]
    for n, weight in enumerate(weights):
        part, i = n // ring, n % ring
        chip = chip_at(lax.rem(ring + place_ref[0] - i, ring), ring)
        at = pl.multiple_of((2 * chip + (1 - core if part else core)) * depth, depth)
        rows = jnp.concatenate([x[:, pl.ds(at, depth)] for x in row_refs], axis=0)
        total += jnp.dot(rows, weight[...], preferred_element_type=jnp.float32)
    result = total.astype(jnp.bfloat16)
    out_ref[pl.ds(pl.multiple_of(core * count, count), count)] = result[:count]
    out_ref[pl.ds(pl.multiple_of((1 - core) * count, count), count)] = result[count:]


def project(core, place, own_rows, other_rows, weights):
    count = len(own_rows) * own_rows[0].shape[0]
    width = weights[0].shape[1]
    vmem = pl.BlockSpec(memory_space=pltpu.VMEM)
    smem = pl.BlockSpec(memory_space=pltpu.SMEM)
    return pl.pallas_call(
        functools.partial(project_kernel, len(weights) // 2, len(own_rows)),
        in_specs=[smem, smem] + [vmem] * (2 * len(own_rows) + len(weights)),
        out_specs=vmem,
        out_shape=jax.ShapeDtypeStruct((2 * count, width), jnp.bfloat16),
        compiler_params=pltpu.CompilerParams(vmem_limit_bytes=16 * MIB),
        cost_estimate=pl.CostEstimate(
            flops=4 * count * D * width, bytes_accessed=2 * D * width, transcendentals=0
        ),
        name="project",
    )(core.reshape(1), place, *own_rows, *other_rows, *weights)


def local(
    extent,
    passage_states,
    memory_queries,
    memory_gain,
    kv_weight,
    retrieval,
    question_queries,
    question_kv,
    question_lengths,
):
    me = lax.axis_index("pass")
    core, chip = me & 1, lax.div(me, 2)
    chips = extent // 2
    depth = kv_weight.shape[0]
    own_count = passage_states.shape[0]

    if chips != 8 or depth % LANES:
        memory_rows = pool(passage_states, memory_queries, memory_gain, 0, own_count)
        whole_weight = lax.all_gather(kv_weight, "pass", axis=0, tiled=True)
        memory_kv = jnp.dot(memory_rows, whole_weight, preferred_element_type=jnp.float32)
        everything = lax.all_gather(memory_kv.astype(jnp.bfloat16), "pass", axis=0, tiled=True)
        halves = everything.reshape(-1, 2, 2, LANES).transpose(2, 0, 1, 3).reshape(2, -1, 2 * LANES)
        rest = (retrieval * MEM, question_lengths, question_queries)
        context = attend(jnp.int32(0), *rest, halves[0], question_kv)
        return attend(jnp.int32(1), *rest, halves[1], question_kv, context)

    place = place_of(chip, chips).reshape(1)
    order = [2 * line for line in range(chips // 2)] + [2 * line + 1 for line in range(chips // 2)][::-1]

    def to_partner(x):
        return lax.ppermute(x, "pass", [(i, i ^ 1) for i in range(extent)])

    def along(x, target):
        pairs = [(c, target(c // 2, c % 2)) for c in range(chips)]
        return lax.ppermute(x, "pass", [(2 * s + c, 2 * d + c) for s, d in pairs for c in range(2)])

    def along_ring(x, step):
        return along(x, lambda line, lane: order[(order.index(2 * line + lane) + step) % chips])

    def line_by_line(block):
        lines = chips // 2
        blocks = [block]
        for k in range(1, lines):
            blocks.append(along(block, lambda line, lane: 2 * ((line + k) % lines) + lane))
        return blocks + [along(x, lambda line, lane: 2 * line + 1 - lane) for x in blocks]

    def columns(half):
        return jnp.concatenate(
            [
                lax.dynamic_slice_in_dim(kv_weight, half * LANES + at, LANES, axis=1)
                for at in (0, KVH * HD)
            ],
            axis=1,
        )

    up = [[columns(core)], [to_partner(columns(1 - core))]]
    down = [[x[0]] for x in up]
    memory_rows = []
    for turn in range(1, chips // 2):
        for piece in range(2):
            up[piece].append(along_ring(up[piece][-1], 1))
            down[piece].append(along_ring(down[piece][-1], -1))
        if turn <= POOL_CALLS:
            part = own_count // POOL_CALLS
            rows = pool(passage_states, memory_queries, memory_gain, (turn - 1) * part, part)
            *hops, rows = lax.optimization_barrier((*(x[-1] for x in up + down), rows))
            for chain, hop in zip(up + down, hops):
                chain[-1] = hop
            memory_rows.append(rows)
    up[0].append(along_ring(up[0][-1], 1))
    down[1].append(along_ring(down[1][-1], -1))
    weights = [x for piece in range(2) for x in up[piece] + down[piece][:0:-1]]
    memory_kv = project(core, place, memory_rows, [to_partner(x) for x in memory_rows], weights)
    near = jnp.concatenate(line_by_line(memory_kv), axis=0)
    far = to_partner(near)

    lines = chips // 2
    of_chip = lax.div(retrieval, CHIP)
    back = lax.rem(lines + lax.div(chip, 2) - lax.div(of_chip, 2), lines)
    slot = back + lines * lax.rem(lax.rem(chip, 2) + lax.rem(of_chip, 2), 2)
    starts = (slot * CHIP + lax.rem(retrieval, CHIP)) * MEM
    rest = (starts, question_lengths, question_queries)
    context = attend(core, *rest, near, question_kv)
    return attend(1 - core, *rest, far, question_kv, context)


def solution(mesh):
    placed = (
        P(("groups", "pass"), None, None),
        P(),
        P(),
        P("pass", None),
        P(("groups", "pass"), None),
        P(("groups", "pass"), None, None),
        P(("groups", "pass"), None, None),
        P(("groups", "pass")),
    )
    return jax.shard_map(
        functools.partial(local, mesh.shape["pass"]),
        mesh=mesh,
        in_specs=placed,
        out_specs=P(("groups", "pass"), None, None),
        check_vma=False,
    )
```

```python
import functools
import math

import jax
import jax.numpy as jnp
from jax import lax
from jax.experimental import pallas as pl
from jax.experimental.pallas import tpu as pltpu
from jax.sharding import PartitionSpec as P

D = 4096
CH = 32
CHD = 128
MEM = 32
LEN = 128
QLEN = 64
TOPK = 16
H = 116
HD = 64
KVH = 4
GROUP = 29
KVW = 512

LANES = 2 * HD
PAIRS = GROUP
HALF = PAIRS * LANES
ROWS = TOPK * MEM
KEYS = 2 * (ROWS + QLEN)
NEG = -1e30
SUM_LOW, SUM_HIGH = 2.0 ** -40, 2.0 ** 60
POOL_WIDTH = 1024
FIRST_COST = 8 * 10**9
PROJECT_COST = 8
CHIP = 8
STEP = 5
BLOCK = 16
MIB = 1024 * 1024


def place_of(chip, ring):
    line, lane = lax.div(chip, 2), lax.rem(chip, 2)
    return line + lane * (ring - 1 - 2 * line)


def chip_at(place, ring):
    lane = lax.div(place, ring // 2)
    line = place + lane * (ring - 1 - 2 * place)
    return 2 * line + lane


def split_kernel(core_ref, weight_ref, mine_ref, theirs_ref):
    for out_ref, half in ((mine_ref, core_ref[0]), (theirs_ref, 1 - core_ref[0])):
        for n in range(2):
            at = pl.multiple_of(half * LANES + n * KVH * HD, LANES)
            out_ref[:, n * LANES:(n + 1) * LANES] = weight_ref[:, pl.ds(at, LANES)]


def split(core, weight):
    vmem = pl.BlockSpec(memory_space=pltpu.VMEM)
    return pl.pallas_call(
        split_kernel,
        in_specs=[pl.BlockSpec(memory_space=pltpu.SMEM), vmem],
        out_specs=[vmem, vmem],
        out_shape=[jax.ShapeDtypeStruct((weight.shape[0], 2 * LANES), weight.dtype)] * 2,
        compiler_params=pltpu.CompilerParams(vmem_limit_bytes=8 * MIB),
        cost_estimate=pl.CostEstimate(flops=FIRST_COST, bytes_accessed=4 * weight.size, transcendentals=0),
        name="split",
    )(core.reshape(1), weight)


def pool_kernel(states, queries, gain, out_ref, pooled):
    passages = states.shape[0]
    two = 2 * CHD
    zero = jnp.zeros((MEM, CHD), jnp.bfloat16)
    blank = jnp.zeros((2 * MEM, LEN), jnp.bfloat16)
    totals = [jnp.zeros((MEM, CHD), jnp.float32)] * passages
    for base in range(0, D, POOL_WIDTH):
        blocks = []
        for column in range(base, base + POOL_WIDTH, two):
            lhs = jnp.concatenate(
                [
                    jnp.concatenate([queries[:, column:column + CHD], zero], axis=1),
                    jnp.concatenate([zero, queries[:, column + CHD:column + two]], axis=1),
                ],
                axis=0,
            )
            for p in range(0, passages, 2):
                tokens = states[p:p + 2, :, column:column + two].reshape(2 * LEN, two)
                scores = lax.dot_general(
                    lhs, tokens, (((1,), (1,)), ((), ())), preferred_element_type=jnp.float32
                ) * (1.0 / math.sqrt(CHD))
                blocks.append((column, p, tokens, scores))
        for column, p, tokens, scores in blocks:
            rows = []
            for n in range(2):
                part = scores[:, n * LEN:(n + 1) * LEN]
                part = jnp.exp(part - jnp.max(part, axis=1, keepdims=True))
                part = (part / jnp.sum(part, axis=1, keepdims=True)).astype(jnp.bfloat16)
                rows.append(jnp.concatenate([blank, part] if n else [part, blank], axis=1))
            mixed = jnp.dot(jnp.concatenate(rows, axis=0), tokens, preferred_element_type=jnp.float32)
            for n in range(2):
                for head in range(2):
                    top = (2 * n + head) * MEM
                    block = mixed[top:top + MEM, head * CHD:(head + 1) * CHD]
                    place = slice(column + head * CHD, column + (head + 1) * CHD)
                    pooled[(p + n) * MEM:(p + n + 1) * MEM, place] = block
                    totals[p + n] = totals[p + n] + block * block
    mean_square = jnp.sum(jnp.concatenate(totals, axis=0), axis=1, keepdims=True) * (1.0 / D)
    scale = lax.rsqrt(mean_square + 1e-06)
    factor = gain[...].astype(jnp.float32).reshape(1, D)
    out_ref[...] = (pooled[...] * scale * factor).astype(jnp.bfloat16)


def pool(states, queries, gain):
    count = states.shape[0]
    vmem = pl.BlockSpec(memory_space=pltpu.VMEM)
    return pl.pallas_call(
        pool_kernel,
        in_specs=[vmem] * 3,
        out_specs=vmem,
        out_shape=jax.ShapeDtypeStruct((count * MEM, D), jnp.bfloat16),
        scratch_shapes=[pltpu.VMEM((count * MEM, D), jnp.float32)],
        compiler_params=pltpu.CompilerParams(vmem_limit_bytes=20 * MIB),
        cost_estimate=pl.CostEstimate(
            flops=4 * count * MEM * LEN * D, bytes_accessed=2 * count * LEN * D,
            transcendentals=count * CH * MEM * LEN,
        ),
        name="pool",
    )(states, queries, gain)


def attend_kernel(half_ref, start_ref, length_ref, q_ref, kv_ref, own_kv_ref, *rest):
    out_hbm = rest[-11]
    (
        answers, memory, key_side, value_side, weights, bias, marker, scores, all_weights, sent,
    ) = rest[-10:]
    count = q_ref.shape[0]
    half_at = pl.multiple_of(half_ref[0] * HALF, LANES)
    own_at = pl.multiple_of(half_ref[0] * LANES, LANES)
    factor = math.log2(math.e) / math.sqrt(HD)

    def send(query):
        return pltpu.make_async_copy(
            answers.at[query], out_hbm.at[query, :, pl.ds(half_at, HALF)], sent.at[query]
        )

    lane = lax.broadcasted_iota(jnp.int32, (KEYS, LANES), 1)
    row = lax.broadcasted_iota(jnp.int32, (KEYS, LANES), 0)
    in_b = ((row >= ROWS) & (row < 2 * ROWS)) | (row >= 2 * ROWS + QLEN)
    ones = jnp.where((lane >= HD) == in_b, 1.0, 0.0).astype(jnp.bfloat16)
    key_side[...] = jnp.zeros_like(key_side)
    for g in range(2):
        value_side[g, :, LANES:] = ones

    half = PAIRS // 2
    chunks = []
    for g in range(2):
        tiles = list(range(half + 1)) if g == 0 else list(range(half, PAIRS))
        chunks += [(g, tiles[at:at + STEP]) for at in range(0, len(tiles), STEP)]

    def answer(query, carry):
        for slot in range(TOPK):
            start = pl.multiple_of(start_ref[query, slot], MEM)
            memory[slot * MEM:(slot + 1) * MEM, :] = kv_ref[pl.ds(start, MEM), :]
        length = length_ref[query]

        turned = jnp.transpose(memory[:, :LANES])
        own_k = own_kv_ref[query, :, pl.ds(own_at, LANES)]
        own_turned = jnp.transpose(jnp.concatenate([own_k, own_k], axis=0))
        column = lax.broadcasted_iota(jnp.int32, (HD, LANES), 1)
        for g in range(2):
            for member in range(2):
                rows = slice(member * HD, (member + 1) * HD)
                key_side[g, rows, member * ROWS:(member + 1) * ROWS] = turned[g * HD:(g + 1) * HD]
                own = own_turned[g * HD:(g + 1) * HD]
                mine = (column >= HD) if member else (column < HD)
                key_side[g, rows, 2 * ROWS:] = jnp.where(mine, own, jnp.zeros_like(own))

        token = lax.broadcasted_iota(jnp.int32, (QLEN, LANES), 0)
        low = lax.broadcasted_iota(jnp.int32, (QLEN, LANES), 1) < HD
        key = lax.rem(lax.broadcasted_iota(jnp.int32, (QLEN, LANES), 1), HD)
        bias[...] = jnp.where((key <= token) & (key < length), 0.0, NEG)
        alive = token < length
        sample = lax.div(key, HD // STEP)

        def stacked(tiles):
            return jnp.concatenate(
                [q_ref[query, :, pl.ds(pl.multiple_of(half_at + t * LANES, LANES), LANES)] for t in tiles], axis=0
            )

        def key_product(i):
            g, tiles = chunks[i]
            lhs = stacked(tiles)
            for c in range(0, KEYS, 2 * LANES):
                part = slice(c, min(c + 2 * LANES, KEYS))
                got = jnp.dot(lhs, key_side[g, :, part], preferred_element_type=jnp.float32) * factor
                if c == 2 * ROWS:
                    got = got + jnp.concatenate([bias[...]] * len(tiles), axis=0)
                weights[i % 2, :len(tiles) * QLEN, part] = jnp.exp2(got).astype(jnp.bfloat16)

        def finish(i, mixed):
            g, tiles = chunks[i]
            for n, t in enumerate(tiles):
                rows = slice(n * QLEN, (n + 1) * QLEN)
                sums = mixed[rows, LANES:]
                inverse = pl.reciprocal(sums, approx=True)
                inverse = inverse * (2.0 - sums * inverse)
                result = jnp.where(alive, mixed[rows, :LANES] * inverse, 0.0).astype(jnp.bfloat16)
                at = slice(t * LANES, (t + 1) * LANES)
                if t == half and g == 1:
                    result = jnp.where(low, answers[query, :, at], result)
                answers[query, :, at] = result

        def value_product(i, seen):
            g, tiles = chunks[i]
            size = len(tiles) * QLEN
            mixed = jnp.dot(weights[i % 2, :size, :], value_side[g], preferred_element_type=jnp.float32)
            sums = mixed[:QLEN, LANES:]
            for n in range(1, len(tiles)):
                sums = jnp.where(sample == n, mixed[n * QLEN:(n + 1) * QLEN, LANES:], sums)
            seen = jnp.where((sums > SUM_LOW) & (sums < SUM_HIGH), seen, 1.0)
            finish(i, mixed)
            return seen

        key_product(0)

        own_v_at = pl.multiple_of(own_at + KVH * HD, LANES)
        own_v = own_kv_ref[query, :, pl.ds(own_v_at, LANES)]
        for block, at in ((memory[:, LANES:], 0), (own_v, 2 * ROWS)):
            size = block.shape[0]
            swapped = jnp.concatenate([block[:, HD:], block[:, :HD]], axis=1)
            lower = lax.broadcasted_iota(jnp.int32, block.shape, 1) < HD
            zero = jnp.zeros_like(block)
            for g in range(2):
                one, two = (block, swapped) if g == 0 else (swapped, block)
                value_side[g, at:at + size, :LANES] = jnp.where(lower, one, zero)
                value_side[g, at + size:at + 2 * size, :LANES] = jnp.where(lower, zero, two)

        seen = jnp.zeros((QLEN, LANES), jnp.float32)
        for i in range(len(chunks)):
            if i + 1 < len(chunks):
                key_product(i + 1)
            seen = value_product(i, seen)
        marker[0] = jnp.max(seen)

        @pl.when(marker[0] > 0.0)
        def _():
            for i, (g, tiles) in enumerate(chunks):
                size = len(tiles) * QLEN
                scores[:size, :] = jnp.dot(stacked(tiles), key_side[g], preferred_element_type=jnp.float32)

                def soften(n, carry):
                    rows = pl.ds(pl.multiple_of(n * QLEN, QLEN), QLEN)
                    own_scores = scores[rows, 2 * ROWS:] + bias[...]
                    tops = []
                    for member in range(2):
                        columns = slice(member * ROWS, (member + 1) * ROWS)
                        top = jnp.where(low, own_scores, NEG) if member == 0 else jnp.where(low, NEG, own_scores)
                        top = jnp.maximum(
                            jnp.max(top, axis=1, keepdims=True),
                            jnp.max(scores[rows, columns], axis=1, keepdims=True),
                        )
                        all_weights[rows, columns] = jnp.exp2(
                            (scores[rows, columns] - top) * factor
                        ).astype(jnp.bfloat16)
                        tops.append(top)
                    all_weights[rows, 2 * ROWS:] = jnp.exp2(
                        (own_scores - jnp.where(low, tops[0], tops[1])) * factor
                    ).astype(jnp.bfloat16)
                    return carry

                lax.fori_loop(0, len(tiles), soften, 0)
                finish(
                    i, jnp.dot(all_weights[:size, :], value_side[g], preferred_element_type=jnp.float32)
                )

        send(query).start()
        return carry

    lax.fori_loop(0, count, answer, 0)
    for query in range(count):
        send(query).wait()


def attend(half, starts, lengths, questions, memory_kv, own_kv, earlier=None):
    count = questions.shape[0]
    hbm, vmem, smem = (pl.BlockSpec(memory_space=x) for x in (pltpu.HBM, pltpu.VMEM, pltpu.SMEM))
    operands = [half.reshape(1), starts, lengths, questions, memory_kv, own_kv]
    in_specs = [smem, smem, smem, vmem, vmem, vmem]
    aliases = {}
    if earlier is not None:
        aliases = {len(operands): 0}
        operands.append(earlier)
        in_specs.append(hbm)
    return pl.pallas_call(
        attend_kernel,
        in_specs=in_specs,
        out_specs=hbm,
        out_shape=jax.ShapeDtypeStruct((count, QLEN, H * HD), jnp.bfloat16),
        scratch_shapes=[
            pltpu.VMEM((count, QLEN, HALF), jnp.bfloat16),
            pltpu.VMEM((ROWS, 2 * LANES), jnp.bfloat16),
            pltpu.VMEM((2, LANES, KEYS), jnp.bfloat16),
            pltpu.VMEM((2, KEYS, 2 * LANES), jnp.bfloat16),
            pltpu.VMEM((2, STEP * QLEN, KEYS), jnp.bfloat16),
            pltpu.VMEM((QLEN, LANES), jnp.float32),
            pltpu.SMEM((1,), jnp.float32),
            pltpu.VMEM((STEP * QLEN, KEYS), jnp.float32),
            pltpu.VMEM((STEP * QLEN, KEYS), jnp.bfloat16),
            pltpu.SemaphoreType.DMA((count,)),
        ],
        input_output_aliases=aliases,
        compiler_params=pltpu.CompilerParams(vmem_limit_bytes=32 * MIB),
        cost_estimate=pl.CostEstimate(
            flops=2 * count * QLEN * H * HD * (ROWS + QLEN),
            bytes_accessed=2 * count * QLEN * H * HD,
            transcendentals=count * QLEN * H * (ROWS + QLEN) // 2,
        ),
        name="attend",
    )(*operands)


def project_kernel(ring, core_ref, place_ref, *rest):
    own_ref, other_ref, *weights, out_ref = rest
    count = own_ref.shape[0]
    depth = weights[0].shape[0]
    total = jnp.zeros((2 * count, weights[0].shape[1]), jnp.float32)
    core = core_ref[0]
    for n, weight in enumerate(weights):
        part, i = n // ring, n % ring
        chip = chip_at(lax.rem(ring + place_ref[0] - i, ring), ring)
        at = pl.multiple_of((2 * chip + (1 - core if part else core)) * depth, depth)
        rows = jnp.concatenate([own_ref[:, pl.ds(at, depth)], other_ref[:, pl.ds(at, depth)]], axis=0)
        total += jnp.dot(rows, weight[...], preferred_element_type=jnp.float32)
    result = total.astype(jnp.bfloat16)
    out_ref[pl.ds(pl.multiple_of(core * count, count), count)] = result[:count]
    out_ref[pl.ds(pl.multiple_of((1 - core) * count, count), count)] = result[count:]


def project(core, place, own_rows, other_rows, weights):
    count = own_rows.shape[0]
    width = weights[0].shape[1]
    vmem = pl.BlockSpec(memory_space=pltpu.VMEM)
    smem = pl.BlockSpec(memory_space=pltpu.SMEM)
    return pl.pallas_call(
        functools.partial(project_kernel, len(weights) // 2),
        in_specs=[smem, smem] + [vmem] * (2 + len(weights)),
        out_specs=vmem,
        out_shape=jax.ShapeDtypeStruct((2 * count, width), jnp.bfloat16),
        compiler_params=pltpu.CompilerParams(vmem_limit_bytes=16 * MIB),
        cost_estimate=pl.CostEstimate(
            flops=PROJECT_COST * 4 * count * D * width, bytes_accessed=2 * D * width, transcendentals=0
        ),
        name="project",
    )(core.reshape(1), place, own_rows, other_rows, *weights)


def local(
    extent,
    passage_states,
    memory_queries,
    memory_gain,
    kv_weight,
    retrieval,
    question_queries,
    question_kv,
    question_lengths,
):
    me = lax.axis_index("pass")
    core, chip = me & 1, lax.div(me, 2)
    chips = extent // 2
    depth = kv_weight.shape[0]

    if chips != 8 or depth % LANES:
        memory_rows = pool(passage_states, memory_queries, memory_gain)
        whole_weight = lax.all_gather(kv_weight, "pass", axis=0, tiled=True)
        memory_kv = jnp.dot(memory_rows, whole_weight, preferred_element_type=jnp.float32)
        everything = lax.all_gather(memory_kv.astype(jnp.bfloat16), "pass", axis=0, tiled=True)
        halves = everything.reshape(-1, 2, 2, LANES).transpose(2, 0, 1, 3).reshape(2, -1, 2 * LANES)
        rest = (retrieval * MEM, question_lengths, question_queries)
        context = attend(jnp.int32(0), *rest, halves[0], question_kv)
        return attend(jnp.int32(1), *rest, halves[1], question_kv, context)

    place = place_of(chip, chips).reshape(1)
    order = [2 * line for line in range(chips // 2)] + [2 * line + 1 for line in range(chips // 2)][::-1]

    def to_partner(x):
        return lax.ppermute(x, "pass", [(i, i ^ 1) for i in range(extent)])

    def along(x, target):
        pairs = [(c, target(c // 2, c % 2)) for c in range(chips)]
        return lax.ppermute(x, "pass", [(2 * s + c, 2 * d + c) for s, d in pairs for c in range(2)])

    def along_ring(x, step):
        return along(x, lambda line, lane: order[(order.index(2 * line + lane) + step) % chips])

    def line_by_line(block):
        lines = chips // 2
        blocks = [block]
        for k in range(1, lines):
            blocks.append(along(block, lambda line, lane: 2 * ((line + k) % lines) + lane))
        return blocks + [along(x, lambda line, lane: 2 * line + 1 - lane) for x in blocks]

    mine, theirs = split(core, kv_weight)
    up = [[mine], [to_partner(theirs)]]
    down = [[x[0]] for x in up]
    for turn in range(1, chips // 2):
        for piece in range(2):
            up[piece].append(along_ring(up[piece][-1], 1))
            down[piece].append(along_ring(down[piece][-1], -1))
        if turn == 1:
            memory_rows = pool(passage_states, memory_queries, memory_gain)
            *hops, memory_rows = lax.optimization_barrier((*(x[-1] for x in up + down), memory_rows))
            for chain, hop in zip(up + down, hops):
                chain[-1] = hop
    up[0].append(along_ring(up[0][-1], 1))
    down[1].append(along_ring(down[1][-1], -1))
    weights = [x for piece in range(2) for x in up[piece] + down[piece][:0:-1]]
    memory_kv = project(core, place, memory_rows, to_partner(memory_rows), weights)
    near = jnp.concatenate(line_by_line(memory_kv), axis=0)
    far = to_partner(near)

    lines = chips // 2
    of_chip = lax.div(retrieval, CHIP)
    back = lax.rem(lines + lax.div(chip, 2) - lax.div(of_chip, 2), lines)
    slot = back + lines * lax.rem(lax.rem(chip, 2) + lax.rem(of_chip, 2), 2)
    starts = (slot * CHIP + lax.rem(retrieval, CHIP)) * MEM
    rest = (starts, question_lengths, question_queries)
    context = attend(core, *rest, near, question_kv)
    return attend(1 - core, *rest, far, question_kv, context)


def solution(mesh):
    placed = (
        P(("groups", "pass"), None, None),
        P(),
        P(),
        P("pass", None),
        P(("groups", "pass"), None),
        P(("groups", "pass"), None, None),
        P(("groups", "pass"), None, None),
        P(("groups", "pass")),
    )
    return jax.shard_map(
        functools.partial(local, mesh.shape["pass"]),
        mesh=mesh,
        in_specs=placed,
        out_specs=P(("groups", "pass"), None, None),
        check_vma=False,
    )
```

```python
import functools
import math

import jax
import jax.numpy as jnp
from jax import lax
from jax.experimental import pallas as pl
from jax.experimental.pallas import tpu as pltpu
from jax.sharding import PartitionSpec as P

D = 4096
CH = 32
CHD = 128
MEM = 32
LEN = 128
QLEN = 64
TOPK = 16
H = 116
HD = 64
KVH = 4
GROUP = 29
KVW = 512

LANES = 2 * HD
PAIRS = GROUP
HALF = PAIRS * LANES
ROWS = TOPK * MEM
KEYS = 2 * (ROWS + QLEN)
NEG = -1e30
SUM_LOW, SUM_HIGH = 2.0 ** -40, 2.0 ** 60
POOL_WIDTH = 1024
FIRST_COST = 8 * 10**9
PROJECT_COST = 8
CHIP = 8
STEP = 4
BLOCK = 16
MIB = 1024 * 1024


def place_of(chip, ring):
    line, lane = lax.div(chip, 2), lax.rem(chip, 2)
    return line + lane * (ring - 1 - 2 * line)


def chip_at(place, ring):
    lane = lax.div(place, ring // 2)
    line = place + lane * (ring - 1 - 2 * place)
    return 2 * line + lane


def split_kernel(core_ref, weight_ref, mine_ref, theirs_ref):
    for out_ref, half in ((mine_ref, core_ref[0]), (theirs_ref, 1 - core_ref[0])):
        for n in range(2):
            at = pl.multiple_of(half * LANES + n * KVH * HD, LANES)
            out_ref[:, n * LANES:(n + 1) * LANES] = weight_ref[:, pl.ds(at, LANES)]


def split(core, weight):
    vmem = pl.BlockSpec(memory_space=pltpu.VMEM)
    return pl.pallas_call(
        split_kernel,
        in_specs=[pl.BlockSpec(memory_space=pltpu.SMEM), vmem],
        out_specs=[vmem, vmem],
        out_shape=[jax.ShapeDtypeStruct((weight.shape[0], 2 * LANES), weight.dtype)] * 2,
        compiler_params=pltpu.CompilerParams(vmem_limit_bytes=8 * MIB),
        cost_estimate=pl.CostEstimate(flops=FIRST_COST, bytes_accessed=4 * weight.size, transcendentals=0),
        name="split",
    )(core.reshape(1), weight)


def pool_kernel(states, queries, gain, out_ref, pooled):
    passages = states.shape[0]
    two = 2 * CHD
    zero = jnp.zeros((MEM, CHD), jnp.bfloat16)
    blank = jnp.zeros((2 * MEM, LEN), jnp.bfloat16)
    totals = [jnp.zeros((MEM, CHD), jnp.float32)] * passages
    for base in range(0, D, POOL_WIDTH):
        blocks = []
        for column in range(base, base + POOL_WIDTH, two):
            lhs = jnp.concatenate(
                [
                    jnp.concatenate([queries[:, column:column + CHD], zero], axis=1),
                    jnp.concatenate([zero, queries[:, column + CHD:column + two]], axis=1),
                ],
                axis=0,
            )
            for p in range(0, passages, 2):
                tokens = states[p:p + 2, :, column:column + two].reshape(2 * LEN, two)
                scores = lax.dot_general(
                    lhs, tokens, (((1,), (1,)), ((), ())), preferred_element_type=jnp.float32
                ) * (1.0 / math.sqrt(CHD))
                blocks.append((column, p, tokens, scores))
        for column, p, tokens, scores in blocks:
            rows = []
            for n in range(2):
                part = scores[:, n * LEN:(n + 1) * LEN]
                part = jnp.exp(part - jnp.max(part, axis=1, keepdims=True))
                part = (part / jnp.sum(part, axis=1, keepdims=True)).astype(jnp.bfloat16)
                rows.append(jnp.concatenate([blank, part] if n else [part, blank], axis=1))
            mixed = jnp.dot(jnp.concatenate(rows, axis=0), tokens, preferred_element_type=jnp.float32)
            for n in range(2):
                for head in range(2):
                    top = (2 * n + head) * MEM
                    block = mixed[top:top + MEM, head * CHD:(head + 1) * CHD]
                    place = slice(column + head * CHD, column + (head + 1) * CHD)
                    pooled[(p + n) * MEM:(p + n + 1) * MEM, place] = block
                    totals[p + n] = totals[p + n] + block * block
    mean_square = jnp.sum(jnp.concatenate(totals, axis=0), axis=1, keepdims=True) * (1.0 / D)
    scale = lax.rsqrt(mean_square + 1e-06)
    factor = gain[...].astype(jnp.float32).reshape(1, D)
    out_ref[...] = (pooled[...] * scale * factor).astype(jnp.bfloat16)


def pool(states, queries, gain):
    count = states.shape[0]
    vmem = pl.BlockSpec(memory_space=pltpu.VMEM)
    return pl.pallas_call(
        pool_kernel,
        in_specs=[vmem] * 3,
        out_specs=vmem,
        out_shape=jax.ShapeDtypeStruct((count * MEM, D), jnp.bfloat16),
        scratch_shapes=[pltpu.VMEM((count * MEM, D), jnp.float32)],
        compiler_params=pltpu.CompilerParams(vmem_limit_bytes=20 * MIB),
        cost_estimate=pl.CostEstimate(
            flops=4 * count * MEM * LEN * D, bytes_accessed=2 * count * LEN * D,
            transcendentals=count * CH * MEM * LEN,
        ),
        name="pool",
    )(states, queries, gain)


def attend_kernel(half_ref, start_ref, length_ref, q_hbm, kv_ref, own_kv_ref, *rest):
    out_hbm = rest[-13]
    (
        questions, answers, memory, key_side, value_side, weights, bias, marker, scores, all_weights,
        arrived, sent,
    ) = rest[-12:]
    count = q_hbm.shape[0]
    half_at = pl.multiple_of(half_ref[0] * HALF, LANES)
    own_at = pl.multiple_of(half_ref[0] * LANES, LANES)
    factor = math.log2(math.e) / math.sqrt(HD)

    def fetch(query):
        return pltpu.make_async_copy(
            q_hbm.at[query, :, pl.ds(half_at, HALF)], questions.at[query], arrived.at[query]
        )

    def send(query):
        return pltpu.make_async_copy(
            answers.at[query], out_hbm.at[query, :, pl.ds(half_at, HALF)], sent.at[query]
        )

    fetch(0).start()
    lane = lax.broadcasted_iota(jnp.int32, (KEYS, LANES), 1)
    row = lax.broadcasted_iota(jnp.int32, (KEYS, LANES), 0)
    in_b = ((row >= ROWS) & (row < 2 * ROWS)) | (row >= 2 * ROWS + QLEN)
    ones = jnp.where((lane >= HD) == in_b, 1.0, 0.0).astype(jnp.bfloat16)
    key_side[...] = jnp.zeros_like(key_side)
    for g in range(2):
        value_side[g, :, LANES:] = ones

    half = PAIRS // 2
    chunks = []
    for g in range(2):
        tiles = list(range(half + 1)) if g == 0 else list(range(half, PAIRS))
        chunks += [(g, tiles[at:at + STEP]) for at in range(0, len(tiles), STEP)]

    def answer(query, carry):
        for slot in range(TOPK):
            start = pl.multiple_of(start_ref[query, slot], MEM)
            memory[slot * MEM:(slot + 1) * MEM, :] = kv_ref[pl.ds(start, MEM), :]
        length = length_ref[query]

        turned = jnp.transpose(memory[:, :LANES])
        own_k = own_kv_ref[query, :, pl.ds(own_at, LANES)]
        own_turned = jnp.transpose(jnp.concatenate([own_k, own_k], axis=0))
        column = lax.broadcasted_iota(jnp.int32, (HD, LANES), 1)
        for g in range(2):
            for member in range(2):
                rows = slice(member * HD, (member + 1) * HD)
                key_side[g, rows, member * ROWS:(member + 1) * ROWS] = turned[g * HD:(g + 1) * HD]
                own = own_turned[g * HD:(g + 1) * HD]
                mine = (column >= HD) if member else (column < HD)
                key_side[g, rows, 2 * ROWS:] = jnp.where(mine, own, jnp.zeros_like(own))

        token = lax.broadcasted_iota(jnp.int32, (QLEN, LANES), 0)
        low = lax.broadcasted_iota(jnp.int32, (QLEN, LANES), 1) < HD
        key = lax.rem(lax.broadcasted_iota(jnp.int32, (QLEN, LANES), 1), HD)
        bias[...] = jnp.where((key <= token) & (key < length), 0.0, NEG)
        alive = token < length
        sample = lax.div(key, HD // STEP)

        fetch(query).wait()

        @pl.when(query + 1 < count)
        def _():
            fetch(query + 1).start()

        def stacked(tiles):
            return jnp.concatenate([questions[query, :, t * LANES:(t + 1) * LANES] for t in tiles], axis=0)

        def key_product(i):
            g, tiles = chunks[i]
            lhs = stacked(tiles)
            for c in range(0, KEYS, 2 * LANES):
                part = slice(c, min(c + 2 * LANES, KEYS))
                got = jnp.dot(lhs, key_side[g, :, part], preferred_element_type=jnp.float32) * factor
                if c == 2 * ROWS:
                    got = got + jnp.concatenate([bias[...]] * len(tiles), axis=0)
                weights[i % 2, :len(tiles) * QLEN, part] = jnp.exp2(got).astype(jnp.bfloat16)

        def finish(i, mixed):
            g, tiles = chunks[i]
            for n, t in enumerate(tiles):
                rows = slice(n * QLEN, (n + 1) * QLEN)
                sums = mixed[rows, LANES:]
                inverse = pl.reciprocal(sums, approx=True)
                inverse = inverse * (2.0 - sums * inverse)
                result = jnp.where(alive, mixed[rows, :LANES] * inverse, 0.0).astype(jnp.bfloat16)
                at = slice(t * LANES, (t + 1) * LANES)
                if t == half and g == 1:
                    result = jnp.where(low, answers[query, :, at], result)
                answers[query, :, at] = result

        def value_product(i, seen):
            g, tiles = chunks[i]
            size = len(tiles) * QLEN
            mixed = jnp.dot(weights[i % 2, :size, :], value_side[g], preferred_element_type=jnp.float32)
            sums = mixed[:QLEN, LANES:]
            for n in range(1, len(tiles)):
                sums = jnp.where(sample == n, mixed[n * QLEN:(n + 1) * QLEN, LANES:], sums)
            seen = jnp.where((sums > SUM_LOW) & (sums < SUM_HIGH), seen, 1.0)
            finish(i, mixed)
            return seen

        key_product(0)

        own_v_at = pl.multiple_of(own_at + KVH * HD, LANES)
        own_v = own_kv_ref[query, :, pl.ds(own_v_at, LANES)]
        for block, at in ((memory[:, LANES:], 0), (own_v, 2 * ROWS)):
            size = block.shape[0]
            swapped = jnp.concatenate([block[:, HD:], block[:, :HD]], axis=1)
            lower = lax.broadcasted_iota(jnp.int32, block.shape, 1) < HD
            zero = jnp.zeros_like(block)
            for g in range(2):
                one, two = (block, swapped) if g == 0 else (swapped, block)
                value_side[g, at:at + size, :LANES] = jnp.where(lower, one, zero)
                value_side[g, at + size:at + 2 * size, :LANES] = jnp.where(lower, zero, two)

        seen = jnp.zeros((QLEN, LANES), jnp.float32)
        for i in range(len(chunks)):
            if i + 1 < len(chunks):
                key_product(i + 1)
            seen = value_product(i, seen)
        marker[0] = jnp.max(seen)

        @pl.when(marker[0] > 0.0)
        def _():
            for i, (g, tiles) in enumerate(chunks):
                size = len(tiles) * QLEN
                scores[:size, :] = jnp.dot(stacked(tiles), key_side[g], preferred_element_type=jnp.float32)

                def soften(n, carry):
                    rows = pl.ds(pl.multiple_of(n * QLEN, QLEN), QLEN)
                    own_scores = scores[rows, 2 * ROWS:] + bias[...]
                    tops = []
                    for member in range(2):
                        columns = slice(member * ROWS, (member + 1) * ROWS)
                        top = jnp.where(low, own_scores, NEG) if member == 0 else jnp.where(low, NEG, own_scores)
                        top = jnp.maximum(
                            jnp.max(top, axis=1, keepdims=True),
                            jnp.max(scores[rows, columns], axis=1, keepdims=True),
                        )
                        all_weights[rows, columns] = jnp.exp2(
                            (scores[rows, columns] - top) * factor
                        ).astype(jnp.bfloat16)
                        tops.append(top)
                    all_weights[rows, 2 * ROWS:] = jnp.exp2(
                        (own_scores - jnp.where(low, tops[0], tops[1])) * factor
                    ).astype(jnp.bfloat16)
                    return carry

                lax.fori_loop(0, len(tiles), soften, 0)
                finish(
                    i, jnp.dot(all_weights[:size, :], value_side[g], preferred_element_type=jnp.float32)
                )

        send(query).start()
        return carry

    lax.fori_loop(0, count, answer, 0)
    for query in range(count):
        send(query).wait()


def attend(half, starts, lengths, questions, memory_kv, own_kv, earlier=None):
    count = questions.shape[0]
    hbm, vmem, smem = (pl.BlockSpec(memory_space=x) for x in (pltpu.HBM, pltpu.VMEM, pltpu.SMEM))
    operands = [half.reshape(1), starts, lengths, questions, memory_kv, own_kv]
    in_specs = [smem, smem, smem, hbm, vmem, vmem]
    aliases = {}
    if earlier is not None:
        aliases = {len(operands): 0}
        operands.append(earlier)
        in_specs.append(hbm)
    return pl.pallas_call(
        attend_kernel,
        in_specs=in_specs,
        out_specs=hbm,
        out_shape=jax.ShapeDtypeStruct((count, QLEN, H * HD), jnp.bfloat16),
        scratch_shapes=[
            pltpu.VMEM((count, QLEN, HALF), jnp.bfloat16),
            pltpu.VMEM((count, QLEN, HALF), jnp.bfloat16),
            pltpu.VMEM((ROWS, 2 * LANES), jnp.bfloat16),
            pltpu.VMEM((2, LANES, KEYS), jnp.bfloat16),
            pltpu.VMEM((2, KEYS, 2 * LANES), jnp.bfloat16),
            pltpu.VMEM((2, STEP * QLEN, KEYS), jnp.bfloat16),
            pltpu.VMEM((QLEN, LANES), jnp.float32),
            pltpu.SMEM((1,), jnp.float32),
            pltpu.VMEM((STEP * QLEN, KEYS), jnp.float32),
            pltpu.VMEM((STEP * QLEN, KEYS), jnp.bfloat16),
            pltpu.SemaphoreType.DMA((count,)),
            pltpu.SemaphoreType.DMA((count,)),
        ],
        input_output_aliases=aliases,
        compiler_params=pltpu.CompilerParams(vmem_limit_bytes=50 * MIB),
        cost_estimate=pl.CostEstimate(
            flops=2 * count * QLEN * H * HD * (ROWS + QLEN),
            bytes_accessed=2 * count * QLEN * H * HD,
            transcendentals=count * QLEN * H * (ROWS + QLEN) // 2,
        ),
        name="attend",
    )(*operands)


def project_kernel(ring, pieces, more, core_ref, place_ref, own_ref, other_ref, *rest):
    weights, rest = rest[:len(pieces)], rest[len(pieces):]
    out_ref = rest[-1]
    count = own_ref.shape[0]
    depth = weights[0].shape[0]
    core = core_ref[0]
    total = jnp.zeros((2 * count, weights[0].shape[1]), jnp.float32) if more else rest[0][...]
    for (part, i), weight in zip(pieces, weights):
        chip = chip_at(lax.rem(ring + place_ref[0] - i, ring), ring)
        at = pl.multiple_of((2 * chip + (1 - core if part else core)) * depth, depth)
        rows = jnp.concatenate([own_ref[:, pl.ds(at, depth)], other_ref[:, pl.ds(at, depth)]], axis=0)
        total += jnp.dot(rows, weight[...], preferred_element_type=jnp.float32)
    if more:
        out_ref[...] = total
        return
    result = total.astype(jnp.bfloat16)
    out_ref[pl.ds(pl.multiple_of(core * count, count), count)] = result[:count]
    out_ref[pl.ds(pl.multiple_of((1 - core) * count, count), count)] = result[count:]


def project(ring, core, place, own_rows, other_rows, weights, sums=None):
    count = own_rows.shape[0]
    pieces, blocks = tuple(weights), list(weights.values())
    width = blocks[0].shape[1]
    vmem = pl.BlockSpec(memory_space=pltpu.VMEM)
    smem = pl.BlockSpec(memory_space=pltpu.SMEM)
    more = sums is None
    operands = [own_rows, other_rows, *blocks] + ([] if more else [sums])
    return pl.pallas_call(
        functools.partial(project_kernel, ring, pieces, more),
        in_specs=[smem, smem] + [vmem] * len(operands),
        out_specs=vmem,
        out_shape=jax.ShapeDtypeStruct((2 * count, width), jnp.float32 if more else jnp.bfloat16),
        compiler_params=pltpu.CompilerParams(vmem_limit_bytes=16 * MIB),
        cost_estimate=pl.CostEstimate(
            flops=PROJECT_COST * 4 * count * D * width, bytes_accessed=2 * D * width, transcendentals=0
        ),
        name="project",
    )(core.reshape(1), place, *operands)


def local(
    extent,
    passage_states,
    memory_queries,
    memory_gain,
    kv_weight,
    retrieval,
    question_queries,
    question_kv,
    question_lengths,
):
    me = lax.axis_index("pass")
    core, chip = me & 1, lax.div(me, 2)
    chips = extent // 2
    depth = kv_weight.shape[0]

    if chips != 8 or depth % LANES:
        memory_rows = pool(passage_states, memory_queries, memory_gain)
        whole_weight = lax.all_gather(kv_weight, "pass", axis=0, tiled=True)
        memory_kv = jnp.dot(memory_rows, whole_weight, preferred_element_type=jnp.float32)
        everything = lax.all_gather(memory_kv.astype(jnp.bfloat16), "pass", axis=0, tiled=True)
        halves = everything.reshape(-1, 2, 2, LANES).transpose(2, 0, 1, 3).reshape(2, -1, 2 * LANES)
        rest = (retrieval * MEM, question_lengths, question_queries)
        context = attend(jnp.int32(0), *rest, halves[0], question_kv)
        return attend(jnp.int32(1), *rest, halves[1], question_kv, context)

    place = place_of(chip, chips).reshape(1)
    order = [2 * line for line in range(chips // 2)] + [2 * line + 1 for line in range(chips // 2)][::-1]

    def to_partner(x):
        return lax.ppermute(x, "pass", [(i, i ^ 1) for i in range(extent)])

    def along(x, target):
        pairs = [(c, target(c // 2, c % 2)) for c in range(chips)]
        return lax.ppermute(x, "pass", [(2 * s + c, 2 * d + c) for s, d in pairs for c in range(2)])

    def along_ring(x, step):
        return along(x, lambda line, lane: order[(order.index(2 * line + lane) + step) % chips])

    def line_by_line(block):
        lines = chips // 2
        blocks = [block]
        for k in range(1, lines):
            blocks.append(along(block, lambda line, lane: 2 * ((line + k) % lines) + lane))
        return blocks + [along(x, lambda line, lane: 2 * line + 1 - lane) for x in blocks]

    mine, theirs = split(core, kv_weight)
    up = [[mine], [to_partner(theirs)]]
    down = [[x[0]] for x in up]

    def blocks(turns):
        found = {}
        for part in range(2):
            for turn in turns:
                if turn < len(up[part]):
                    found[part, turn] = up[part][turn]
                if 0 < turn < len(down[part]):
                    found[part, chips - turn] = down[part][turn]
        return found

    for turn in range(1, chips // 2):
        for part in range(2):
            up[part].append(along_ring(up[part][-1], 1))
            down[part].append(along_ring(down[part][-1], -1))
        if turn == 1:
            beside = rows = pool(passage_states, memory_queries, memory_gain)
        elif turn == 3:
            beside = project(chips, core, place, rows, other_rows, blocks((0, 1, 2)))
        else:
            continue
        *hops, beside = lax.optimization_barrier((*(x[-1] for x in up + down), beside))
        for chain, hop in zip(up + down, hops):
            chain[-1] = hop
        if turn == 1:
            rows = beside
            other_rows = to_partner(rows)
    up[0].append(along_ring(up[0][-1], 1))
    down[1].append(along_ring(down[1][-1], -1))
    memory_kv = project(chips, core, place, rows, other_rows, blocks((3, 4)), beside)
    near = jnp.concatenate(line_by_line(memory_kv), axis=0)
    far = to_partner(near)

    lines = chips // 2
    of_chip = lax.div(retrieval, CHIP)
    back = lax.rem(lines + lax.div(chip, 2) - lax.div(of_chip, 2), lines)
    slot = back + lines * lax.rem(lax.rem(chip, 2) + lax.rem(of_chip, 2), 2)
    starts = (slot * CHIP + lax.rem(retrieval, CHIP)) * MEM
    rest = (starts, question_lengths, question_queries)
    context = attend(core, *rest, near, question_kv)
    return attend(1 - core, *rest, far, question_kv, context)


def solution(mesh):
    placed = (
        P(("groups", "pass"), None, None),
        P(),
        P(),
        P("pass", None),
        P(("groups", "pass"), None),
        P(("groups", "pass"), None, None),
        P(("groups", "pass"), None, None),
        P(("groups", "pass")),
    )
    return jax.shard_map(
        functools.partial(local, mesh.shape["pass"]),
        mesh=mesh,
        in_specs=placed,
        out_specs=P(("groups", "pass"), None, None),
        check_vma=False,
    )
```

```python
import functools
import math

import jax
import jax.numpy as jnp
from jax import lax
from jax.experimental import pallas as pl
from jax.experimental.pallas import tpu as pltpu
from jax.sharding import PartitionSpec as P

D = 4096
CH = 32
CHD = 128
MEM = 32
LEN = 128
QLEN = 64
TOPK = 16
H = 116
HD = 64
KVH = 4
GROUP = 29
KVW = 512

LANES = 2 * HD
PAIRS = GROUP
HALF = PAIRS * LANES
ROWS = TOPK * MEM
KEYS = 2 * (ROWS + QLEN)
NEG = -1e30
SUM_LOW, SUM_HIGH = 2.0 ** -40, 2.0 ** 60
POOL_WIDTH = 1024
FIRST_COST = 8 * 10**9
PROJECT_COST = 8
CHIP = 8
STEP = 5
BLOCK = 16
MIB = 1024 * 1024


def place_of(chip, ring):
    line, lane = lax.div(chip, 2), lax.rem(chip, 2)
    return line + lane * (ring - 1 - 2 * line)


def chip_at(place, ring):
    lane = lax.div(place, ring // 2)
    line = place + lane * (ring - 1 - 2 * place)
    return 2 * line + lane


def split_kernel(core_ref, weight_ref, mine_ref, theirs_ref):
    for out_ref, half in ((mine_ref, core_ref[0]), (theirs_ref, 1 - core_ref[0])):
        for n in range(2):
            at = pl.multiple_of(half * LANES + n * KVH * HD, LANES)
            out_ref[:, n * LANES:(n + 1) * LANES] = weight_ref[:, pl.ds(at, LANES)]


def split(core, weight):
    vmem = pl.BlockSpec(memory_space=pltpu.VMEM)
    return pl.pallas_call(
        split_kernel,
        in_specs=[pl.BlockSpec(memory_space=pltpu.SMEM), vmem],
        out_specs=[vmem, vmem],
        out_shape=[jax.ShapeDtypeStruct((weight.shape[0], 2 * LANES), weight.dtype)] * 2,
        compiler_params=pltpu.CompilerParams(vmem_limit_bytes=8 * MIB),
        cost_estimate=pl.CostEstimate(flops=FIRST_COST, bytes_accessed=4 * weight.size, transcendentals=0),
        name="split",
    )(core.reshape(1), weight)


def pool_kernel(states, queries, gain, out_ref, pooled):
    passages = states.shape[0]
    two = 2 * CHD
    zero = jnp.zeros((MEM, CHD), jnp.bfloat16)
    blank = jnp.zeros((2 * MEM, LEN), jnp.bfloat16)
    totals = [jnp.zeros((MEM, CHD), jnp.float32)] * passages
    for base in range(0, D, POOL_WIDTH):
        blocks = []
        for column in range(base, base + POOL_WIDTH, two):
            lhs = jnp.concatenate(
                [
                    jnp.concatenate([queries[:, column:column + CHD], zero], axis=1),
                    jnp.concatenate([zero, queries[:, column + CHD:column + two]], axis=1),
                ],
                axis=0,
            )
            for p in range(0, passages, 2):
                tokens = states[p:p + 2, :, column:column + two].reshape(2 * LEN, two)
                scores = lax.dot_general(
                    lhs, tokens, (((1,), (1,)), ((), ())), preferred_element_type=jnp.float32
                ) * (1.0 / math.sqrt(CHD))
                blocks.append((column, p, tokens, scores))
        for column, p, tokens, scores in blocks:
            rows = []
            for n in range(2):
                part = scores[:, n * LEN:(n + 1) * LEN]
                part = jnp.exp(part - jnp.max(part, axis=1, keepdims=True))
                part = (part / jnp.sum(part, axis=1, keepdims=True)).astype(jnp.bfloat16)
                rows.append(jnp.concatenate([blank, part] if n else [part, blank], axis=1))
            mixed = jnp.dot(jnp.concatenate(rows, axis=0), tokens, preferred_element_type=jnp.float32)
            for n in range(2):
                for head in range(2):
                    top = (2 * n + head) * MEM
                    block = mixed[top:top + MEM, head * CHD:(head + 1) * CHD]
                    place = slice(column + head * CHD, column + (head + 1) * CHD)
                    pooled[(p + n) * MEM:(p + n + 1) * MEM, place] = block
                    totals[p + n] = totals[p + n] + block * block
    mean_square = jnp.sum(jnp.concatenate(totals, axis=0), axis=1, keepdims=True) * (1.0 / D)
    scale = lax.rsqrt(mean_square + 1e-06)
    factor = gain[...].astype(jnp.float32).reshape(1, D)
    out_ref[...] = (pooled[...] * scale * factor).astype(jnp.bfloat16)


def pool(states, queries, gain):
    count = states.shape[0]
    vmem = pl.BlockSpec(memory_space=pltpu.VMEM)
    return pl.pallas_call(
        pool_kernel,
        in_specs=[vmem] * 3,
        out_specs=vmem,
        out_shape=jax.ShapeDtypeStruct((count * MEM, D), jnp.bfloat16),
        scratch_shapes=[pltpu.VMEM((count * MEM, D), jnp.float32)],
        compiler_params=pltpu.CompilerParams(vmem_limit_bytes=20 * MIB),
        cost_estimate=pl.CostEstimate(
            flops=4 * count * MEM * LEN * D, bytes_accessed=2 * count * LEN * D,
            transcendentals=count * CH * MEM * LEN,
        ),
        name="pool",
    )(states, queries, gain)


def attend_kernel(half_ref, start_ref, length_ref, q_ref, kv_ref, own_kv_ref, *rest):
    out_hbm = rest[-11]
    (
        answers, memory, key_side, value_side, weights, bias, marker, scores, all_weights, sent,
    ) = rest[-10:]
    count = q_ref.shape[0]
    half_at = pl.multiple_of(half_ref[0] * HALF, LANES)
    own_at = pl.multiple_of(half_ref[0] * LANES, LANES)
    factor = math.log2(math.e) / math.sqrt(HD)

    def send(query):
        return pltpu.make_async_copy(
            answers.at[query], out_hbm.at[query, :, pl.ds(half_at, HALF)], sent.at[query]
        )

    lane = lax.broadcasted_iota(jnp.int32, (KEYS, LANES), 1)
    row = lax.broadcasted_iota(jnp.int32, (KEYS, LANES), 0)
    in_b = ((row >= ROWS) & (row < 2 * ROWS)) | (row >= 2 * ROWS + QLEN)
    ones = jnp.where((lane >= HD) == in_b, 1.0, 0.0).astype(jnp.bfloat16)
    key_side[...] = jnp.zeros_like(key_side)
    for g in range(2):
        value_side[g, :, LANES:] = ones

    half = PAIRS // 2
    chunks = []
    for g in range(2):
        tiles = list(range(half + 1)) if g == 0 else list(range(half, PAIRS))
        chunks += [(g, tiles[at:at + STEP]) for at in range(0, len(tiles), STEP)]

    def answer(query, carry):
        for slot in range(TOPK):
            start = pl.multiple_of(start_ref[query, slot], MEM)
            memory[slot * MEM:(slot + 1) * MEM, :] = kv_ref[pl.ds(start, MEM), :]
        length = length_ref[query]

        turned = jnp.transpose(memory[:, :LANES])
        own_k = own_kv_ref[query, :, pl.ds(own_at, LANES)]
        own_turned = jnp.transpose(jnp.concatenate([own_k, own_k], axis=0))
        column = lax.broadcasted_iota(jnp.int32, (HD, LANES), 1)
        for g in range(2):
            for member in range(2):
                rows = slice(member * HD, (member + 1) * HD)
                key_side[g, rows, member * ROWS:(member + 1) * ROWS] = turned[g * HD:(g + 1) * HD]
                own = own_turned[g * HD:(g + 1) * HD]
                mine = (column >= HD) if member else (column < HD)
                key_side[g, rows, 2 * ROWS:] = jnp.where(mine, own, jnp.zeros_like(own))

        token = lax.broadcasted_iota(jnp.int32, (QLEN, LANES), 0)
        low = lax.broadcasted_iota(jnp.int32, (QLEN, LANES), 1) < HD
        key = lax.rem(lax.broadcasted_iota(jnp.int32, (QLEN, LANES), 1), HD)
        bias[...] = jnp.where((key <= token) & (key < length), 0.0, NEG)
        alive = token < length
        sample = lax.div(key, HD // STEP)

        def stacked(tiles):
            return jnp.concatenate(
                [q_ref[query, :, pl.ds(pl.multiple_of(half_at + t * LANES, LANES), LANES)] for t in tiles], axis=0
            )

        def key_product(i):
            g, tiles = chunks[i]
            lhs = stacked(tiles)
            for c in range(0, KEYS, 2 * LANES):
                part = slice(c, min(c + 2 * LANES, KEYS))
                got = jnp.dot(lhs, key_side[g, :, part], preferred_element_type=jnp.float32) * factor
                if c == 2 * ROWS:
                    got = got + jnp.concatenate([bias[...]] * len(tiles), axis=0)
                weights[i % 2, :len(tiles) * QLEN, part] = jnp.exp2(got).astype(jnp.bfloat16)

        def finish(i, mixed):
            g, tiles = chunks[i]
            for n, t in enumerate(tiles):
                rows = slice(n * QLEN, (n + 1) * QLEN)
                sums = mixed[rows, LANES:]
                inverse = pl.reciprocal(sums, approx=True)
                inverse = inverse * (2.0 - sums * inverse)
                result = jnp.where(alive, mixed[rows, :LANES] * inverse, 0.0).astype(jnp.bfloat16)
                at = slice(t * LANES, (t + 1) * LANES)
                if t == half and g == 1:
                    result = jnp.where(low, answers[query, :, at], result)
                answers[query, :, at] = result

        def value_product(i, seen):
            g, tiles = chunks[i]
            size = len(tiles) * QLEN
            mixed = jnp.dot(weights[i % 2, :size, :], value_side[g], preferred_element_type=jnp.float32)
            sums = mixed[:QLEN, LANES:]
            for n in range(1, len(tiles)):
                sums = jnp.where(sample == n, mixed[n * QLEN:(n + 1) * QLEN, LANES:], sums)
            seen = jnp.where((sums > SUM_LOW) & (sums < SUM_HIGH), seen, 1.0)
            finish(i, mixed)
            return seen

        key_product(0)

        own_v_at = pl.multiple_of(own_at + KVH * HD, LANES)
        own_v = own_kv_ref[query, :, pl.ds(own_v_at, LANES)]
        for block, at in ((memory[:, LANES:], 0), (own_v, 2 * ROWS)):
            size = block.shape[0]
            swapped = jnp.concatenate([block[:, HD:], block[:, :HD]], axis=1)
            lower = lax.broadcasted_iota(jnp.int32, block.shape, 1) < HD
            zero = jnp.zeros_like(block)
            for g in range(2):
                one, two = (block, swapped) if g == 0 else (swapped, block)
                value_side[g, at:at + size, :LANES] = jnp.where(lower, one, zero)
                value_side[g, at + size:at + 2 * size, :LANES] = jnp.where(lower, zero, two)

        seen = jnp.zeros((QLEN, LANES), jnp.float32)
        for i in range(len(chunks)):
            if i + 1 < len(chunks):
                key_product(i + 1)
            seen = value_product(i, seen)
        marker[0] = jnp.max(seen)

        @pl.when(marker[0] > 0.0)
        def _():
            for i, (g, tiles) in enumerate(chunks):
                size = len(tiles) * QLEN
                scores[:size, :] = jnp.dot(stacked(tiles), key_side[g], preferred_element_type=jnp.float32)

                def soften(n, carry):
                    rows = pl.ds(pl.multiple_of(n * QLEN, QLEN), QLEN)
                    own_scores = scores[rows, 2 * ROWS:] + bias[...]
                    tops = []
                    for member in range(2):
                        columns = slice(member * ROWS, (member + 1) * ROWS)
                        top = jnp.where(low, own_scores, NEG) if member == 0 else jnp.where(low, NEG, own_scores)
                        top = jnp.maximum(
                            jnp.max(top, axis=1, keepdims=True),
                            jnp.max(scores[rows, columns], axis=1, keepdims=True),
                        )
                        all_weights[rows, columns] = jnp.exp2(
                            (scores[rows, columns] - top) * factor
                        ).astype(jnp.bfloat16)
                        tops.append(top)
                    all_weights[rows, 2 * ROWS:] = jnp.exp2(
                        (own_scores - jnp.where(low, tops[0], tops[1])) * factor
                    ).astype(jnp.bfloat16)
                    return carry

                lax.fori_loop(0, len(tiles), soften, 0)
                finish(
                    i, jnp.dot(all_weights[:size, :], value_side[g], preferred_element_type=jnp.float32)
                )

        send(query).start()
        return carry

    lax.fori_loop(0, count, answer, 0)
    for query in range(count):
        send(query).wait()


def attend(half, starts, lengths, questions, memory_kv, own_kv, earlier=None):
    count = questions.shape[0]
    hbm, vmem, smem = (pl.BlockSpec(memory_space=x) for x in (pltpu.HBM, pltpu.VMEM, pltpu.SMEM))
    operands = [half.reshape(1), starts, lengths, questions, memory_kv, own_kv]
    in_specs = [smem, smem, smem, vmem, vmem, vmem]
    aliases = {}
    if earlier is not None:
        aliases = {len(operands): 0}
        operands.append(earlier)
        in_specs.append(hbm)
    return pl.pallas_call(
        attend_kernel,
        in_specs=in_specs,
        out_specs=hbm,
        out_shape=jax.ShapeDtypeStruct((count, QLEN, H * HD), jnp.bfloat16),
        scratch_shapes=[
            pltpu.VMEM((count, QLEN, HALF), jnp.bfloat16),
            pltpu.VMEM((ROWS, 2 * LANES), jnp.bfloat16),
            pltpu.VMEM((2, LANES, KEYS), jnp.bfloat16),
            pltpu.VMEM((2, KEYS, 2 * LANES), jnp.bfloat16),
            pltpu.VMEM((2, STEP * QLEN, KEYS), jnp.bfloat16),
            pltpu.VMEM((QLEN, LANES), jnp.float32),
            pltpu.SMEM((1,), jnp.float32),
            pltpu.VMEM((STEP * QLEN, KEYS), jnp.float32),
            pltpu.VMEM((STEP * QLEN, KEYS), jnp.bfloat16),
            pltpu.SemaphoreType.DMA((count,)),
        ],
        input_output_aliases=aliases,
        compiler_params=pltpu.CompilerParams(vmem_limit_bytes=48 * MIB),
        cost_estimate=pl.CostEstimate(
            flops=2 * count * QLEN * H * HD * (ROWS + QLEN),
            bytes_accessed=2 * count * QLEN * H * HD,
            transcendentals=count * QLEN * H * (ROWS + QLEN) // 2,
        ),
        name="attend",
    )(*operands)


def project_kernel(ring, pieces, more, core_ref, place_ref, own_ref, other_ref, *rest):
    weights, rest = rest[:len(pieces)], rest[len(pieces):]
    out_ref = rest[-1]
    count = own_ref.shape[0]
    depth = weights[0].shape[0]
    core = core_ref[0]
    total = jnp.zeros((2 * count, weights[0].shape[1]), jnp.float32) if more else rest[0][...]
    for (part, i), weight in zip(pieces, weights):
        chip = chip_at(lax.rem(ring + place_ref[0] - i, ring), ring)
        at = pl.multiple_of((2 * chip + (1 - core if part else core)) * depth, depth)
        rows = jnp.concatenate([own_ref[:, pl.ds(at, depth)], other_ref[:, pl.ds(at, depth)]], axis=0)
        total += jnp.dot(rows, weight[...], preferred_element_type=jnp.float32)
    if more:
        out_ref[...] = total
        return
    result = total.astype(jnp.bfloat16)
    out_ref[pl.ds(pl.multiple_of(core * count, count), count)] = result[:count]
    out_ref[pl.ds(pl.multiple_of((1 - core) * count, count), count)] = result[count:]


def project(ring, core, place, own_rows, other_rows, weights, sums=None):
    count = own_rows.shape[0]
    pieces, blocks = tuple(weights), list(weights.values())
    width = blocks[0].shape[1]
    vmem = pl.BlockSpec(memory_space=pltpu.VMEM)
    smem = pl.BlockSpec(memory_space=pltpu.SMEM)
    more = sums is None
    operands = [own_rows, other_rows, *blocks] + ([] if more else [sums])
    return pl.pallas_call(
        functools.partial(project_kernel, ring, pieces, more),
        in_specs=[smem, smem] + [vmem] * len(operands),
        out_specs=vmem,
        out_shape=jax.ShapeDtypeStruct((2 * count, width), jnp.float32 if more else jnp.bfloat16),
        compiler_params=pltpu.CompilerParams(vmem_limit_bytes=16 * MIB),
        cost_estimate=pl.CostEstimate(
            flops=PROJECT_COST * 4 * count * D * width, bytes_accessed=2 * D * width, transcendentals=0
        ),
        name="project",
    )(core.reshape(1), place, *operands)


def local(
    extent,
    passage_states,
    memory_queries,
    memory_gain,
    kv_weight,
    retrieval,
    question_queries,
    question_kv,
    question_lengths,
):
    me = lax.axis_index("pass")
    core, chip = me & 1, lax.div(me, 2)
    chips = extent // 2
    depth = kv_weight.shape[0]

    if chips != 8 or depth % LANES:
        memory_rows = pool(passage_states, memory_queries, memory_gain)
        whole_weight = lax.all_gather(kv_weight, "pass", axis=0, tiled=True)
        memory_kv = jnp.dot(memory_rows, whole_weight, preferred_element_type=jnp.float32)
        everything = lax.all_gather(memory_kv.astype(jnp.bfloat16), "pass", axis=0, tiled=True)
        halves = everything.reshape(-1, 2, 2, LANES).transpose(2, 0, 1, 3).reshape(2, -1, 2 * LANES)
        rest = (retrieval * MEM, question_lengths, question_queries)
        context = attend(jnp.int32(0), *rest, halves[0], question_kv)
        return attend(jnp.int32(1), *rest, halves[1], question_kv, context)

    place = place_of(chip, chips).reshape(1)
    order = [2 * line for line in range(chips // 2)] + [2 * line + 1 for line in range(chips // 2)][::-1]

    def to_partner(x):
        return lax.ppermute(x, "pass", [(i, i ^ 1) for i in range(extent)])

    def along(x, target):
        pairs = [(c, target(c // 2, c % 2)) for c in range(chips)]
        return lax.ppermute(x, "pass", [(2 * s + c, 2 * d + c) for s, d in pairs for c in range(2)])

    def along_ring(x, step):
        return along(x, lambda line, lane: order[(order.index(2 * line + lane) + step) % chips])

    def line_by_line(block):
        lines = chips // 2

        def lane_of(x):
            return along(x, lambda line, lane: 2 * line + 1 - lane)

        near = {k: along(block, lambda line, lane: 2 * ((line + k) % lines) + lane) for k in (2, 1, 3)}
        far = {0: lane_of(block)}
        far[3] = along(block, lambda line, lane: 2 * ((line + 3) % lines) + 1 - lane)
        far[1], far[2] = lane_of(near[1]), lane_of(near[2])
        return [block, near[1], near[2], near[3], far[0], far[1], far[2], far[3]]

    mine, theirs = split(core, kv_weight)
    up = [[mine], [to_partner(theirs)]]
    down = [[x[0]] for x in up]

    def blocks(turns):
        found = {}
        for part in range(2):
            for turn in turns:
                if turn < len(up[part]):
                    found[part, turn] = up[part][turn]
                if 0 < turn < len(down[part]):
                    found[part, chips - turn] = down[part][turn]
        return found

    for turn in range(1, chips // 2):
        for part in range(2):
            up[part].append(along_ring(up[part][-1], 1))
            down[part].append(along_ring(down[part][-1], -1))
        if turn == 1:
            rows = pool(passage_states, memory_queries, memory_gain)
            *hops, rows = lax.optimization_barrier((*(x[-1] for x in up + down), rows))
            for chain, hop in zip(up + down, hops):
                chain[-1] = hop
            other_rows = to_partner(rows)
    up[0].append(along_ring(up[0][-1], 1))
    down[1].append(along_ring(down[1][-1], -1))
    early = project(chips, core, place, rows, other_rows, blocks((0, 1, 2)))
    memory_kv = project(chips, core, place, rows, other_rows, blocks((3, 4)), early)
    near = jnp.concatenate(line_by_line(memory_kv), axis=0)
    far = to_partner(near)

    lines = chips // 2
    of_chip = lax.div(retrieval, CHIP)
    back = lax.rem(lines + lax.div(chip, 2) - lax.div(of_chip, 2), lines)
    slot = back + lines * lax.rem(lax.rem(chip, 2) + lax.rem(of_chip, 2), 2)
    starts = (slot * CHIP + lax.rem(retrieval, CHIP)) * MEM
    rest = (starts, question_lengths, question_queries)
    context = attend(core, *rest, near, question_kv)
    return attend(1 - core, *rest, far, question_kv, context)


def solution(mesh):
    placed = (
        P(("groups", "pass"), None, None),
        P(),
        P(),
        P("pass", None),
        P(("groups", "pass"), None),
        P(("groups", "pass"), None, None),
        P(("groups", "pass"), None, None),
        P(("groups", "pass")),
    )
    return jax.shard_map(
        functools.partial(local, mesh.shape["pass"]),
        mesh=mesh,
        in_specs=placed,
        out_specs=P(("groups", "pass"), None, None),
        check_vma=False,
    )
```

```python
import functools
import math

import jax
import jax.numpy as jnp
from jax import lax
from jax.experimental import pallas as pl
from jax.experimental.pallas import tpu as pltpu
from jax.sharding import PartitionSpec as P

D = 4096
CH = 32
CHD = 128
MEM = 32
LEN = 128
QLEN = 64
TOPK = 16
H = 116
HD = 64
KVH = 4
GROUP = 29
KVW = 512

LANES = 2 * HD
PAIRS = GROUP
HALF = PAIRS * LANES
ROWS = TOPK * MEM
KEYS = 2 * (ROWS + QLEN)
NEG = -1e30
SUM_LOW, SUM_HIGH = 2.0 ** -40, 2.0 ** 60
POOL_WIDTH = 1024
FIRST_COST = 8 * 10**9
CHIP = 8
STEP = 3
BLOCK = 16
MIB = 1024 * 1024


def place_of(chip, ring):
    line, lane = lax.div(chip, 2), lax.rem(chip, 2)
    return line + lane * (ring - 1 - 2 * line)


def chip_at(place, ring):
    lane = lax.div(place, ring // 2)
    line = place + lane * (ring - 1 - 2 * place)
    return 2 * line + lane


def split_kernel(core_ref, weight_ref, mine_ref, theirs_ref):
    for out_ref, half in ((mine_ref, core_ref[0]), (theirs_ref, 1 - core_ref[0])):
        for n in range(2):
            at = pl.multiple_of(half * LANES + n * KVH * HD, LANES)
            out_ref[:, n * LANES:(n + 1) * LANES] = weight_ref[:, pl.ds(at, LANES)]


def split(core, weight):
    vmem = pl.BlockSpec(memory_space=pltpu.VMEM)
    return pl.pallas_call(
        split_kernel,
        in_specs=[pl.BlockSpec(memory_space=pltpu.SMEM), vmem],
        out_specs=[vmem, vmem],
        out_shape=[jax.ShapeDtypeStruct((weight.shape[0], 2 * LANES), weight.dtype)] * 2,
        compiler_params=pltpu.CompilerParams(vmem_limit_bytes=8 * MIB),
        cost_estimate=pl.CostEstimate(flops=FIRST_COST, bytes_accessed=4 * weight.size, transcendentals=0),
        name="split",
    )(core.reshape(1), weight)


def pool_kernel(states, queries, gain, out_ref, pooled):
    passages = states.shape[0]
    two = 2 * CHD
    zero = jnp.zeros((MEM, CHD), jnp.bfloat16)
    blank = jnp.zeros((2 * MEM, LEN), jnp.bfloat16)
    totals = [jnp.zeros((MEM, CHD), jnp.float32)] * passages
    for base in range(0, D, POOL_WIDTH):
        blocks = []
        for column in range(base, base + POOL_WIDTH, two):
            lhs = jnp.concatenate(
                [
                    jnp.concatenate([queries[:, column:column + CHD], zero], axis=1),
                    jnp.concatenate([zero, queries[:, column + CHD:column + two]], axis=1),
                ],
                axis=0,
            )
            for p in range(0, passages, 2):
                tokens = states[p:p + 2, :, column:column + two].reshape(2 * LEN, two)
                scores = lax.dot_general(
                    lhs, tokens, (((1,), (1,)), ((), ())), preferred_element_type=jnp.float32
                ) * (1.0 / math.sqrt(CHD))
                blocks.append((column, p, tokens, scores))
        for column, p, tokens, scores in blocks:
            rows = []
            for n in range(2):
                part = scores[:, n * LEN:(n + 1) * LEN]
                part = jnp.exp(part - jnp.max(part, axis=1, keepdims=True))
                part = (part / jnp.sum(part, axis=1, keepdims=True)).astype(jnp.bfloat16)
                rows.append(jnp.concatenate([blank, part] if n else [part, blank], axis=1))
            mixed = jnp.dot(jnp.concatenate(rows, axis=0), tokens, preferred_element_type=jnp.float32)
            for n in range(2):
                for head in range(2):
                    top = (2 * n + head) * MEM
                    block = mixed[top:top + MEM, head * CHD:(head + 1) * CHD]
                    place = slice(column + head * CHD, column + (head + 1) * CHD)
                    pooled[(p + n) * MEM:(p + n + 1) * MEM, place] = block
                    totals[p + n] = totals[p + n] + block * block
    mean_square = jnp.sum(jnp.concatenate(totals, axis=0), axis=1, keepdims=True) * (1.0 / D)
    scale = lax.rsqrt(mean_square + 1e-06)
    factor = gain[...].astype(jnp.float32).reshape(1, D)
    out_ref[...] = (pooled[...] * scale * factor).astype(jnp.bfloat16)


def pool(states, queries, gain):
    count = states.shape[0]
    vmem = pl.BlockSpec(memory_space=pltpu.VMEM)
    return pl.pallas_call(
        pool_kernel,
        in_specs=[vmem] * 3,
        out_specs=vmem,
        out_shape=jax.ShapeDtypeStruct((count * MEM, D), jnp.bfloat16),
        scratch_shapes=[pltpu.VMEM((count * MEM, D), jnp.float32)],
        compiler_params=pltpu.CompilerParams(vmem_limit_bytes=20 * MIB),
        cost_estimate=pl.CostEstimate(
            flops=4 * count * MEM * LEN * D, bytes_accessed=2 * count * LEN * D,
            transcendentals=count * CH * MEM * LEN,
        ),
        name="pool",
    )(states, queries, gain)


def ask(half, questions_hbm, asked, semaphore):
    at = pl.multiple_of(half * HALF, LANES)
    return pltpu.make_async_copy(questions_hbm.at[:, :, pl.ds(at, HALF)], asked, semaphore)


def attend_kernel(ahead, half_ref, start_ref, length_ref, q_ref, kv_ref, own_kv_ref, *rest):
    if ahead:
        coming = ask(1 - half_ref[0], rest[-14], rest[-12], rest[-1])
        coming.start()
        out_hbm, rest = rest[-13], rest[:-1]
    else:
        out_hbm = rest[-11]
    (
        answers, memory, key_side, value_side, weights, bias, marker, scores, all_weights, sent,
    ) = rest[-10:]
    count = q_ref.shape[0]
    half_at = pl.multiple_of(half_ref[0] * HALF, LANES)
    own_at = pl.multiple_of(half_ref[0] * LANES, LANES)
    factor = math.log2(math.e) / math.sqrt(HD)

    def send(query):
        return pltpu.make_async_copy(
            answers.at[query], out_hbm.at[query, :, pl.ds(half_at, HALF)], sent.at[query]
        )

    lane = lax.broadcasted_iota(jnp.int32, (KEYS, LANES), 1)
    row = lax.broadcasted_iota(jnp.int32, (KEYS, LANES), 0)
    in_b = ((row >= ROWS) & (row < 2 * ROWS)) | (row >= 2 * ROWS + QLEN)
    ones = jnp.where((lane >= HD) == in_b, 1.0, 0.0).astype(jnp.bfloat16)
    key_side[...] = jnp.zeros_like(key_side)
    for g in range(2):
        value_side[g, :, LANES:] = ones

    half = PAIRS // 2
    chunks = []
    for g in range(2):
        tiles = list(range(half + 1)) if g == 0 else list(range(half, PAIRS))
        chunks += [(g, tiles[at:at + STEP]) for at in range(0, len(tiles), STEP)]

    def answer(query, carry):
        for slot in range(TOPK):
            start = pl.multiple_of(start_ref[query, slot], MEM)
            memory[slot * MEM:(slot + 1) * MEM, :] = kv_ref[pl.ds(start, MEM), :]
        length = length_ref[query]

        turned = jnp.transpose(memory[:, :LANES])
        own_k = own_kv_ref[query, :, pl.ds(own_at, LANES)]
        own_turned = jnp.transpose(jnp.concatenate([own_k, own_k], axis=0))
        column = lax.broadcasted_iota(jnp.int32, (HD, LANES), 1)
        for g in range(2):
            for member in range(2):
                rows = slice(member * HD, (member + 1) * HD)
                key_side[g, rows, member * ROWS:(member + 1) * ROWS] = turned[g * HD:(g + 1) * HD]
                own = own_turned[g * HD:(g + 1) * HD]
                mine = (column >= HD) if member else (column < HD)
                key_side[g, rows, 2 * ROWS:] = jnp.where(mine, own, jnp.zeros_like(own))

        token = lax.broadcasted_iota(jnp.int32, (QLEN, LANES), 0)
        low = lax.broadcasted_iota(jnp.int32, (QLEN, LANES), 1) < HD
        key = lax.rem(lax.broadcasted_iota(jnp.int32, (QLEN, LANES), 1), HD)
        bias[...] = jnp.where((key <= token) & (key < length), 0.0, NEG)
        alive = token < length
        sample = lax.div(key, HD // STEP)

        def stacked(tiles):
            return jnp.concatenate(
                [q_ref[query, :, t * LANES:(t + 1) * LANES] for t in tiles], axis=0
            )

        def key_product(i):
            g, tiles = chunks[i]
            lhs = stacked(tiles)
            for c in range(0, KEYS, 2 * LANES):
                part = slice(c, min(c + 2 * LANES, KEYS))
                got = jnp.dot(lhs, key_side[g, :, part], preferred_element_type=jnp.float32) * factor
                if c == 2 * ROWS:
                    got = got + jnp.concatenate([bias[...]] * len(tiles), axis=0)
                weights[i % 2, :len(tiles) * QLEN, part] = jnp.exp2(got).astype(jnp.bfloat16)

        def finish(i, mixed):
            g, tiles = chunks[i]
            for n, t in enumerate(tiles):
                rows = slice(n * QLEN, (n + 1) * QLEN)
                sums = mixed[rows, LANES:]
                inverse = pl.reciprocal(sums, approx=True)
                inverse = inverse * (2.0 - sums * inverse)
                result = jnp.where(alive, mixed[rows, :LANES] * inverse, 0.0).astype(jnp.bfloat16)
                at = slice(t * LANES, (t + 1) * LANES)
                if t == half and g == 1:
                    result = jnp.where(low, answers[query, :, at], result)
                answers[query, :, at] = result

        def value_product(i, seen):
            g, tiles = chunks[i]
            size = len(tiles) * QLEN
            mixed = jnp.dot(weights[i % 2, :size, :], value_side[g], preferred_element_type=jnp.float32)
            sums = mixed[:QLEN, LANES:]
            for n in range(1, len(tiles)):
                sums = jnp.where(sample == n, mixed[n * QLEN:(n + 1) * QLEN, LANES:], sums)
            seen = jnp.where((sums > SUM_LOW) & (sums < SUM_HIGH), seen, 1.0)
            finish(i, mixed)
            return seen

        key_product(0)

        own_v_at = pl.multiple_of(own_at + KVH * HD, LANES)
        own_v = own_kv_ref[query, :, pl.ds(own_v_at, LANES)]
        for block, at in ((memory[:, LANES:], 0), (own_v, 2 * ROWS)):
            size = block.shape[0]
            swapped = jnp.concatenate([block[:, HD:], block[:, :HD]], axis=1)
            lower = lax.broadcasted_iota(jnp.int32, block.shape, 1) < HD
            zero = jnp.zeros_like(block)
            for g in range(2):
                one, two = (block, swapped) if g == 0 else (swapped, block)
                value_side[g, at:at + size, :LANES] = jnp.where(lower, one, zero)
                value_side[g, at + size:at + 2 * size, :LANES] = jnp.where(lower, zero, two)

        seen = jnp.zeros((QLEN, LANES), jnp.float32)
        for i in range(len(chunks)):
            if i + 1 < len(chunks):
                key_product(i + 1)
            seen = value_product(i, seen)
        marker[0] = jnp.max(seen)

        @pl.when(marker[0] > 0.0)
        def _():
            for i, (g, tiles) in enumerate(chunks):
                size = len(tiles) * QLEN
                scores[:size, :] = jnp.dot(stacked(tiles), key_side[g], preferred_element_type=jnp.float32)

                def soften(n, carry):
                    rows = pl.ds(pl.multiple_of(n * QLEN, QLEN), QLEN)
                    own_scores = scores[rows, 2 * ROWS:] + bias[...]
                    tops = []
                    for member in range(2):
                        columns = slice(member * ROWS, (member + 1) * ROWS)
                        top = jnp.where(low, own_scores, NEG) if member == 0 else jnp.where(low, NEG, own_scores)
                        top = jnp.maximum(
                            jnp.max(top, axis=1, keepdims=True),
                            jnp.max(scores[rows, columns], axis=1, keepdims=True),
                        )
                        all_weights[rows, columns] = jnp.exp2(
                            (scores[rows, columns] - top) * factor
                        ).astype(jnp.bfloat16)
                        tops.append(top)
                    all_weights[rows, 2 * ROWS:] = jnp.exp2(
                        (own_scores - jnp.where(low, tops[0], tops[1])) * factor
                    ).astype(jnp.bfloat16)
                    return carry

                lax.fori_loop(0, len(tiles), soften, 0)
                finish(
                    i, jnp.dot(all_weights[:size, :], value_side[g], preferred_element_type=jnp.float32)
                )

        send(query).start()
        return carry

    lax.fori_loop(0, count, answer, 0)
    for query in range(count):
        send(query).wait()
    if ahead:
        coming.wait()


def attend(half, starts, lengths, asked, memory_kv, own_kv, earlier=None, questions=None):
    count = asked.shape[0]
    ahead = questions is not None
    hbm, vmem, smem = (pl.BlockSpec(memory_space=x) for x in (pltpu.HBM, pltpu.VMEM, pltpu.SMEM))
    operands = [half.reshape(1), starts, lengths, asked, memory_kv, own_kv]
    in_specs = [smem, smem, smem, vmem, vmem, vmem]
    aliases = {}
    if earlier is not None:
        aliases = {len(operands): 0}
        operands.append(earlier)
        in_specs.append(hbm)
    out_specs = [hbm]
    out_shape = [jax.ShapeDtypeStruct((count, QLEN, H * HD), jnp.bfloat16)]
    extra = []
    if ahead:
        operands.append(questions)
        in_specs.append(hbm)
        out_specs.append(vmem)
        out_shape.append(jax.ShapeDtypeStruct(asked.shape, asked.dtype))
        extra = [pltpu.SemaphoreType.DMA]
    got = pl.pallas_call(
        functools.partial(attend_kernel, ahead),
        in_specs=in_specs,
        out_specs=out_specs,
        out_shape=out_shape,
        scratch_shapes=[
            pltpu.VMEM((count, QLEN, HALF), jnp.bfloat16),
            pltpu.VMEM((ROWS, 2 * LANES), jnp.bfloat16),
            pltpu.VMEM((2, LANES, KEYS), jnp.bfloat16),
            pltpu.VMEM((2, KEYS, 2 * LANES), jnp.bfloat16),
            pltpu.VMEM((2, STEP * QLEN, KEYS), jnp.bfloat16),
            pltpu.VMEM((QLEN, LANES), jnp.float32),
            pltpu.SMEM((1,), jnp.float32),
            pltpu.VMEM((STEP * QLEN, KEYS), jnp.float32),
            pltpu.VMEM((STEP * QLEN, KEYS), jnp.bfloat16),
            pltpu.SemaphoreType.DMA((count,)),
            *extra,
        ],
        input_output_aliases=aliases,
        compiler_params=pltpu.CompilerParams(vmem_limit_bytes=24 * MIB),
        cost_estimate=pl.CostEstimate(
            flops=2 * count * QLEN * H * HD * (ROWS + QLEN),
            bytes_accessed=2 * count * QLEN * H * HD,
            transcendentals=count * QLEN * H * (ROWS + QLEN) // 2,
        ),
        name="attend",
    )(*operands)
    return got if ahead else got[0]


def project_kernel(ring, pieces, more, core_ref, place_ref, own_ref, other_ref, *rest):
    weights, rest = rest[:len(pieces)], rest[len(pieces):]
    if more:
        questions_hbm, out_ref, asked, arrived = rest
        coming = ask(core_ref[0], questions_hbm, asked, arrived)
        coming.start()
    else:
        out_ref = rest[-1]
    count = own_ref.shape[0]
    depth = weights[0].shape[0]
    core = core_ref[0]
    total = jnp.zeros((2 * count, weights[0].shape[1]), jnp.float32) if more else rest[0][...]
    for (part, i), weight in zip(pieces, weights):
        chip = chip_at(lax.rem(ring + place_ref[0] - i, ring), ring)
        at = pl.multiple_of((2 * chip + (1 - core if part else core)) * depth, depth)
        rows = jnp.concatenate([own_ref[:, pl.ds(at, depth)], other_ref[:, pl.ds(at, depth)]], axis=0)
        total += jnp.dot(rows, weight[...], preferred_element_type=jnp.float32)
    if more:
        out_ref[...] = total
        coming.wait()
        return
    result = total.astype(jnp.bfloat16)
    out_ref[pl.ds(pl.multiple_of(core * count, count), count)] = result[:count]
    out_ref[pl.ds(pl.multiple_of((1 - core) * count, count), count)] = result[count:]


def project(ring, core, place, own_rows, other_rows, weights, questions=None, sums=None):
    count = own_rows.shape[0]
    pieces, blocks = tuple(weights), list(weights.values())
    width = blocks[0].shape[1]
    hbm, vmem, smem = (pl.BlockSpec(memory_space=x) for x in (pltpu.HBM, pltpu.VMEM, pltpu.SMEM))
    more = sums is None
    operands = [own_rows, other_rows, *blocks, questions if more else sums]
    in_specs = [smem, smem] + [vmem] * (2 + len(blocks)) + [hbm if more else vmem]
    if more:
        asked = questions.shape[:2] + (HALF,)
        out_shape = [
            jax.ShapeDtypeStruct((2 * count, width), jnp.float32),
            jax.ShapeDtypeStruct(asked, questions.dtype),
        ]
    else:
        out_shape = jax.ShapeDtypeStruct((2 * count, width), jnp.bfloat16)
    return pl.pallas_call(
        functools.partial(project_kernel, ring, pieces, more),
        in_specs=in_specs,
        out_specs=[vmem, vmem] if more else vmem,
        out_shape=out_shape,
        scratch_shapes=[pltpu.SemaphoreType.DMA] if more else [],
        compiler_params=pltpu.CompilerParams(vmem_limit_bytes=16 * MIB),
        cost_estimate=pl.CostEstimate(
            flops=4 * count * D * width, bytes_accessed=2 * D * width, transcendentals=0
        ),
        name="project",
    )(core.reshape(1), place, *operands)


def local(
    extent,
    passage_states,
    memory_queries,
    memory_gain,
    kv_weight,
    retrieval,
    question_queries,
    question_kv,
    question_lengths,
):
    me = lax.axis_index("pass")
    core, chip = me & 1, lax.div(me, 2)
    chips = extent // 2
    depth = kv_weight.shape[0]

    if chips != 8 or depth % LANES:
        memory_rows = pool(passage_states, memory_queries, memory_gain)
        whole_weight = lax.all_gather(kv_weight, "pass", axis=0, tiled=True)
        memory_kv = jnp.dot(memory_rows, whole_weight, preferred_element_type=jnp.float32)
        everything = lax.all_gather(memory_kv.astype(jnp.bfloat16), "pass", axis=0, tiled=True)
        halves = everything.reshape(-1, 2, 2, LANES).transpose(2, 0, 1, 3).reshape(2, -1, 2 * LANES)
        context = None
        for half in range(2):
            asked = question_queries[:, :, half * HALF:(half + 1) * HALF]
            context = attend(
                jnp.int32(half), retrieval * MEM, question_lengths, asked, halves[half], question_kv, context
            )
        return context

    place = place_of(chip, chips).reshape(1)
    order = [2 * line for line in range(chips // 2)] + [2 * line + 1 for line in range(chips // 2)][::-1]

    def to_partner(x):
        return lax.ppermute(x, "pass", [(i, i ^ 1) for i in range(extent)])

    def along(x, target):
        pairs = [(c, target(c // 2, c % 2)) for c in range(chips)]
        return lax.ppermute(x, "pass", [(2 * s + c, 2 * d + c) for s, d in pairs for c in range(2)])

    def along_ring(x, step):
        return along(x, lambda line, lane: order[(order.index(2 * line + lane) + step) % chips])

    def line_by_line(block):
        lines = chips // 2

        def lane_of(x):
            return along(x, lambda line, lane: 2 * line + 1 - lane)

        near = {k: along(block, lambda line, lane: 2 * ((line + k) % lines) + lane) for k in (2, 1, 3)}
        own_line = [block, near[1], near[2], near[3]]
        return own_line + [lane_of(x) for x in own_line]

    mine, theirs = split(core, kv_weight)
    up = [[mine], [to_partner(theirs)]]
    down = [[x[0]] for x in up]

    def blocks(turns):
        found = {}
        for part in range(2):
            for turn in turns:
                if turn < len(up[part]):
                    found[part, turn] = up[part][turn]
                if 0 < turn < len(down[part]):
                    found[part, chips - turn] = down[part][turn]
        return found

    for turn in range(1, chips // 2):
        for part in range(2):
            up[part].append(along_ring(up[part][-1], 1))
            down[part].append(along_ring(down[part][-1], -1))
        if turn == 1:
            rows = pool(passage_states, memory_queries, memory_gain)
            *hops, rows = lax.optimization_barrier((*(x[-1] for x in up + down), rows))
            for chain, hop in zip(up + down, hops):
                chain[-1] = hop
            other_rows = to_partner(rows)
    up[0].append(along_ring(up[0][-1], 1))
    down[1].append(along_ring(down[1][-1], -1))
    early, asked = project(chips, core, place, rows, other_rows, blocks((0, 1, 2)), questions=question_queries)
    memory_kv = project(chips, core, place, rows, other_rows, blocks((3, 4)), sums=early)
    near = jnp.concatenate(line_by_line(memory_kv), axis=0)
    far = to_partner(near)

    lines = chips // 2
    of_chip = lax.div(retrieval, CHIP)
    back = lax.rem(lines + lax.div(chip, 2) - lax.div(of_chip, 2), lines)
    slot = back + lines * lax.rem(lax.rem(chip, 2) + lax.rem(of_chip, 2), 2)
    starts = (slot * CHIP + lax.rem(retrieval, CHIP)) * MEM
    context, other = attend(
        core, starts, question_lengths, asked, near, question_kv, questions=question_queries
    )
    return attend(1 - core, starts, question_lengths, other, far, question_kv, context)


def solution(mesh):
    placed = (
        P(("groups", "pass"), None, None),
        P(),
        P(),
        P("pass", None),
        P(("groups", "pass"), None),
        P(("groups", "pass"), None, None),
        P(("groups", "pass"), None, None),
        P(("groups", "pass")),
    )
    return jax.shard_map(
        functools.partial(local, mesh.shape["pass"]),
        mesh=mesh,
        in_specs=placed,
        out_specs=P(("groups", "pass"), None, None),
        check_vma=False,
    )
```

```python
import functools
import math

import jax
import jax.numpy as jnp
from jax import lax
from jax.experimental import pallas as pl
from jax.experimental.pallas import tpu as pltpu
from jax.sharding import PartitionSpec as P

D = 4096
CH = 32
CHD = 128
MEM = 32
LEN = 128
QLEN = 64
TOPK = 16
H = 116
HD = 64
KVH = 4
GROUP = 29
KVW = 512

LANES = 2 * HD
PAIRS = GROUP
HALF = PAIRS * LANES
ROWS = TOPK * MEM
KEYS = 2 * (ROWS + QLEN)
NEG = -1e30
SUM_LOW, SUM_HIGH = 2.0 ** -40, 2.0 ** 60
POOL_WIDTH = 1024
FIRST_COST = 8 * 10**9
CHIP = 8
STEP = 5
BLOCK = 16
MIB = 1024 * 1024


def place_of(chip, ring):
    line, lane = lax.div(chip, 2), lax.rem(chip, 2)
    return line + lane * (ring - 1 - 2 * line)


def chip_at(place, ring):
    lane = lax.div(place, ring // 2)
    line = place + lane * (ring - 1 - 2 * place)
    return 2 * line + lane


def split_kernel(core_ref, weight_ref, mine_ref, theirs_ref):
    for out_ref, half in ((mine_ref, core_ref[0]), (theirs_ref, 1 - core_ref[0])):
        for n in range(2):
            at = pl.multiple_of(half * LANES + n * KVH * HD, LANES)
            out_ref[:, n * LANES:(n + 1) * LANES] = weight_ref[:, pl.ds(at, LANES)]


def split(core, weight):
    vmem = pl.BlockSpec(memory_space=pltpu.VMEM)
    return pl.pallas_call(
        split_kernel,
        in_specs=[pl.BlockSpec(memory_space=pltpu.SMEM), vmem],
        out_specs=[vmem, vmem],
        out_shape=[jax.ShapeDtypeStruct((weight.shape[0], 2 * LANES), weight.dtype)] * 2,
        compiler_params=pltpu.CompilerParams(vmem_limit_bytes=8 * MIB),
        cost_estimate=pl.CostEstimate(flops=FIRST_COST, bytes_accessed=4 * weight.size, transcendentals=0),
        name="split",
    )(core.reshape(1), weight)


def pool_kernel(states, queries, gain, out_ref, pooled):
    passages = states.shape[0]
    two = 2 * CHD
    zero = jnp.zeros((MEM, CHD), jnp.bfloat16)
    blank = jnp.zeros((2 * MEM, LEN), jnp.bfloat16)
    totals = [jnp.zeros((MEM, CHD), jnp.float32)] * passages
    for base in range(0, D, POOL_WIDTH):
        blocks = []
        for column in range(base, base + POOL_WIDTH, two):
            lhs = jnp.concatenate(
                [
                    jnp.concatenate([queries[:, column:column + CHD], zero], axis=1),
                    jnp.concatenate([zero, queries[:, column + CHD:column + two]], axis=1),
                ],
                axis=0,
            )
            for p in range(0, passages, 2):
                tokens = states[p:p + 2, :, column:column + two].reshape(2 * LEN, two)
                scores = lax.dot_general(
                    lhs, tokens, (((1,), (1,)), ((), ())), preferred_element_type=jnp.float32
                ) * (1.0 / math.sqrt(CHD))
                blocks.append((column, p, tokens, scores))
        for column, p, tokens, scores in blocks:
            rows = []
            for n in range(2):
                part = scores[:, n * LEN:(n + 1) * LEN]
                part = jnp.exp(part - jnp.max(part, axis=1, keepdims=True))
                part = (part / jnp.sum(part, axis=1, keepdims=True)).astype(jnp.bfloat16)
                rows.append(jnp.concatenate([blank, part] if n else [part, blank], axis=1))
            mixed = jnp.dot(jnp.concatenate(rows, axis=0), tokens, preferred_element_type=jnp.float32)
            for n in range(2):
                for head in range(2):
                    top = (2 * n + head) * MEM
                    block = mixed[top:top + MEM, head * CHD:(head + 1) * CHD]
                    place = slice(column + head * CHD, column + (head + 1) * CHD)
                    pooled[(p + n) * MEM:(p + n + 1) * MEM, place] = block
                    totals[p + n] = totals[p + n] + block * block
    mean_square = jnp.sum(jnp.concatenate(totals, axis=0), axis=1, keepdims=True) * (1.0 / D)
    scale = lax.rsqrt(mean_square + 1e-06)
    factor = gain[...].astype(jnp.float32).reshape(1, D)
    out_ref[...] = (pooled[...] * scale * factor).astype(jnp.bfloat16)


def pool(states, queries, gain):
    count = states.shape[0]
    vmem = pl.BlockSpec(memory_space=pltpu.VMEM)
    return pl.pallas_call(
        pool_kernel,
        in_specs=[vmem] * 3,
        out_specs=vmem,
        out_shape=jax.ShapeDtypeStruct((count * MEM, D), jnp.bfloat16),
        scratch_shapes=[pltpu.VMEM((count * MEM, D), jnp.float32)],
        compiler_params=pltpu.CompilerParams(vmem_limit_bytes=20 * MIB),
        cost_estimate=pl.CostEstimate(
            flops=4 * count * MEM * LEN * D, bytes_accessed=2 * count * LEN * D,
            transcendentals=count * CH * MEM * LEN,
        ),
        name="pool",
    )(states, queries, gain)


def attend_kernel(half_ref, start_ref, length_ref, q_hbm, kv_ref, own_kv_ref, *rest):
    out_hbm = rest[-13]
    (
        questions, answers, memory, key_side, value_side, weights, bias, marker, scores, all_weights,
        arrived, sent,
    ) = rest[-12:]
    count = q_hbm.shape[0]
    half_at = pl.multiple_of(half_ref[0] * HALF, LANES)
    own_at = pl.multiple_of(half_ref[0] * LANES, LANES)
    factor = math.log2(math.e) / math.sqrt(HD)

    def fetch(query):
        return pltpu.make_async_copy(
            q_hbm.at[query, :, pl.ds(half_at, HALF)], questions.at[query], arrived.at[query]
        )

    def send(query):
        return pltpu.make_async_copy(
            answers.at[query], out_hbm.at[query, :, pl.ds(half_at, HALF)], sent.at[query]
        )

    fetch(0).start()
    lane = lax.broadcasted_iota(jnp.int32, (KEYS, LANES), 1)
    row = lax.broadcasted_iota(jnp.int32, (KEYS, LANES), 0)
    in_b = ((row >= ROWS) & (row < 2 * ROWS)) | (row >= 2 * ROWS + QLEN)
    ones = jnp.where((lane >= HD) == in_b, 1.0, 0.0).astype(jnp.bfloat16)
    key_side[...] = jnp.zeros_like(key_side)
    for g in range(2):
        value_side[g, :, LANES:] = ones

    half = PAIRS // 2
    chunks = []
    for g in range(2):
        tiles = list(range(half + 1)) if g == 0 else list(range(half, PAIRS))
        chunks += [(g, tiles[at:at + STEP]) for at in range(0, len(tiles), STEP)]

    def answer(query, carry):
        for slot in range(TOPK):
            start = pl.multiple_of(start_ref[query, slot], MEM)
            memory[slot * MEM:(slot + 1) * MEM, :] = kv_ref[pl.ds(start, MEM), :]
        length = length_ref[query]

        turned = jnp.transpose(memory[:, :LANES])
        own_k = own_kv_ref[query, :, pl.ds(own_at, LANES)]
        own_turned = jnp.transpose(jnp.concatenate([own_k, own_k], axis=0))
        column = lax.broadcasted_iota(jnp.int32, (HD, LANES), 1)
        for g in range(2):
            for member in range(2):
                rows = slice(member * HD, (member + 1) * HD)
                key_side[g, rows, member * ROWS:(member + 1) * ROWS] = turned[g * HD:(g + 1) * HD]
                own = own_turned[g * HD:(g + 1) * HD]
                mine = (column >= HD) if member else (column < HD)
                key_side[g, rows, 2 * ROWS:] = jnp.where(mine, own, jnp.zeros_like(own))

        token = lax.broadcasted_iota(jnp.int32, (QLEN, LANES), 0)
        low = lax.broadcasted_iota(jnp.int32, (QLEN, LANES), 1) < HD
        key = lax.rem(lax.broadcasted_iota(jnp.int32, (QLEN, LANES), 1), HD)
        bias[...] = jnp.where((key <= token) & (key < length), 0.0, NEG)
        alive = token < length
        sample = lax.div(key, HD // STEP)

        fetch(query).wait()

        @pl.when(query + 1 < count)
        def _():
            fetch(query + 1).start()

        def stacked(tiles):
            return jnp.concatenate([questions[query, :, t * LANES:(t + 1) * LANES] for t in tiles], axis=0)

        def key_product(i):
            g, tiles = chunks[i]
            lhs = stacked(tiles)
            for c in range(0, KEYS, 2 * LANES):
                part = slice(c, min(c + 2 * LANES, KEYS))
                got = jnp.dot(lhs, key_side[g, :, part], preferred_element_type=jnp.float32) * factor
                if c == 2 * ROWS:
                    got = got + jnp.concatenate([bias[...]] * len(tiles), axis=0)
                weights[i % 2, :len(tiles) * QLEN, part] = jnp.exp2(got).astype(jnp.bfloat16)

        def finish(i, mixed):
            g, tiles = chunks[i]
            for n, t in enumerate(tiles):
                rows = slice(n * QLEN, (n + 1) * QLEN)
                sums = mixed[rows, LANES:]
                inverse = pl.reciprocal(sums, approx=True)
                inverse = inverse * (2.0 - sums * inverse)
                result = jnp.where(alive, mixed[rows, :LANES] * inverse, 0.0).astype(jnp.bfloat16)
                at = slice(t * LANES, (t + 1) * LANES)
                if t == half and g == 1:
                    result = jnp.where(low, answers[query, :, at], result)
                answers[query, :, at] = result

        def value_product(i, seen):
            g, tiles = chunks[i]
            size = len(tiles) * QLEN
            mixed = jnp.dot(weights[i % 2, :size, :], value_side[g], preferred_element_type=jnp.float32)
            sums = mixed[:QLEN, LANES:]
            for n in range(1, len(tiles)):
                sums = jnp.where(sample == n, mixed[n * QLEN:(n + 1) * QLEN, LANES:], sums)
            seen = jnp.where((sums > SUM_LOW) & (sums < SUM_HIGH), seen, 1.0)
            finish(i, mixed)
            return seen

        key_product(0)

        own_v_at = pl.multiple_of(own_at + KVH * HD, LANES)
        own_v = own_kv_ref[query, :, pl.ds(own_v_at, LANES)]
        for block, at in ((memory[:, LANES:], 0), (own_v, 2 * ROWS)):
            size = block.shape[0]
            swapped = jnp.concatenate([block[:, HD:], block[:, :HD]], axis=1)
            lower = lax.broadcasted_iota(jnp.int32, block.shape, 1) < HD
            zero = jnp.zeros_like(block)
            for g in range(2):
                one, two = (block, swapped) if g == 0 else (swapped, block)
                value_side[g, at:at + size, :LANES] = jnp.where(lower, one, zero)
                value_side[g, at + size:at + 2 * size, :LANES] = jnp.where(lower, zero, two)

        seen = jnp.zeros((QLEN, LANES), jnp.float32)
        for i in range(len(chunks)):
            if i + 1 < len(chunks):
                key_product(i + 1)
            seen = value_product(i, seen)
        marker[0] = jnp.max(seen)

        @pl.when(marker[0] > 0.0)
        def _():
            for i, (g, tiles) in enumerate(chunks):
                size = len(tiles) * QLEN
                scores[:size, :] = jnp.dot(stacked(tiles), key_side[g], preferred_element_type=jnp.float32)

                def soften(n, carry):
                    rows = pl.ds(pl.multiple_of(n * QLEN, QLEN), QLEN)
                    own_scores = scores[rows, 2 * ROWS:] + bias[...]
                    tops = []
                    for member in range(2):
                        columns = slice(member * ROWS, (member + 1) * ROWS)
                        top = jnp.where(low, own_scores, NEG) if member == 0 else jnp.where(low, NEG, own_scores)
                        top = jnp.maximum(
                            jnp.max(top, axis=1, keepdims=True),
                            jnp.max(scores[rows, columns], axis=1, keepdims=True),
                        )
                        all_weights[rows, columns] = jnp.exp2(
                            (scores[rows, columns] - top) * factor
                        ).astype(jnp.bfloat16)
                        tops.append(top)
                    all_weights[rows, 2 * ROWS:] = jnp.exp2(
                        (own_scores - jnp.where(low, tops[0], tops[1])) * factor
                    ).astype(jnp.bfloat16)
                    return carry

                lax.fori_loop(0, len(tiles), soften, 0)
                finish(
                    i, jnp.dot(all_weights[:size, :], value_side[g], preferred_element_type=jnp.float32)
                )

        send(query).start()
        return carry

    lax.fori_loop(0, count, answer, 0)
    for query in range(count):
        send(query).wait()


def attend(half, starts, lengths, questions, memory_kv, own_kv, earlier=None):
    count = questions.shape[0]
    hbm, vmem, smem = (pl.BlockSpec(memory_space=x) for x in (pltpu.HBM, pltpu.VMEM, pltpu.SMEM))
    operands = [half.reshape(1), starts, lengths, questions, memory_kv, own_kv]
    in_specs = [smem, smem, smem, hbm, vmem, vmem]
    aliases = {}
    if earlier is not None:
        aliases = {len(operands): 0}
        operands.append(earlier)
        in_specs.append(hbm)
    return pl.pallas_call(
        attend_kernel,
        in_specs=in_specs,
        out_specs=hbm,
        out_shape=jax.ShapeDtypeStruct((count, QLEN, H * HD), jnp.bfloat16),
        scratch_shapes=[
            pltpu.VMEM((count, QLEN, HALF), jnp.bfloat16),
            pltpu.VMEM((count, QLEN, HALF), jnp.bfloat16),
            pltpu.VMEM((ROWS, 2 * LANES), jnp.bfloat16),
            pltpu.VMEM((2, LANES, KEYS), jnp.bfloat16),
            pltpu.VMEM((2, KEYS, 2 * LANES), jnp.bfloat16),
            pltpu.VMEM((2, STEP * QLEN, KEYS), jnp.bfloat16),
            pltpu.VMEM((QLEN, LANES), jnp.float32),
            pltpu.SMEM((1,), jnp.float32),
            pltpu.VMEM((STEP * QLEN, KEYS), jnp.float32),
            pltpu.VMEM((STEP * QLEN, KEYS), jnp.bfloat16),
            pltpu.SemaphoreType.DMA((count,)),
            pltpu.SemaphoreType.DMA((count,)),
        ],
        input_output_aliases=aliases,
        compiler_params=pltpu.CompilerParams(vmem_limit_bytes=50 * MIB),
        cost_estimate=pl.CostEstimate(
            flops=2 * count * QLEN * H * HD * (ROWS + QLEN),
            bytes_accessed=2 * count * QLEN * H * HD,
            transcendentals=count * QLEN * H * (ROWS + QLEN) // 2,
        ),
        name="attend",
    )(*operands)


def project_kernel(ring, pieces, more, core_ref, place_ref, own_ref, other_ref, *rest):
    weights, rest = rest[:len(pieces)], rest[len(pieces):]
    out_ref = rest[-1]
    count = own_ref.shape[0]
    depth = weights[0].shape[0]
    core = core_ref[0]
    total = jnp.zeros((2 * count, weights[0].shape[1]), jnp.float32) if more else rest[0][...]
    for (part, i), weight in zip(pieces, weights):
        chip = chip_at(lax.rem(ring + place_ref[0] - i, ring), ring)
        at = pl.multiple_of((2 * chip + (1 - core if part else core)) * depth, depth)
        rows = jnp.concatenate([own_ref[:, pl.ds(at, depth)], other_ref[:, pl.ds(at, depth)]], axis=0)
        total += jnp.dot(rows, weight[...], preferred_element_type=jnp.float32)
    if more:
        out_ref[...] = total
        return
    result = total.astype(jnp.bfloat16)
    out_ref[pl.ds(pl.multiple_of(core * count, count), count)] = result[:count]
    out_ref[pl.ds(pl.multiple_of((1 - core) * count, count), count)] = result[count:]


def project(ring, core, place, own_rows, other_rows, weights, sums=None):
    count = own_rows.shape[0]
    pieces, blocks = tuple(weights), list(weights.values())
    width = blocks[0].shape[1]
    vmem = pl.BlockSpec(memory_space=pltpu.VMEM)
    smem = pl.BlockSpec(memory_space=pltpu.SMEM)
    more = sums is None
    operands = [own_rows, other_rows, *blocks] + ([] if more else [sums])
    return pl.pallas_call(
        functools.partial(project_kernel, ring, pieces, more),
        in_specs=[smem, smem] + [vmem] * len(operands),
        out_specs=vmem,
        out_shape=jax.ShapeDtypeStruct((2 * count, width), jnp.float32 if more else jnp.bfloat16),
        compiler_params=pltpu.CompilerParams(vmem_limit_bytes=16 * MIB),
        cost_estimate=pl.CostEstimate(
            flops=4 * count * D * width, bytes_accessed=2 * D * width, transcendentals=0
        ),
        name="project",
    )(core.reshape(1), place, *operands)


def local(
    extent,
    passage_states,
    memory_queries,
    memory_gain,
    kv_weight,
    retrieval,
    question_queries,
    question_kv,
    question_lengths,
):
    me = lax.axis_index("pass")
    core, chip = me & 1, lax.div(me, 2)
    chips = extent // 2
    depth = kv_weight.shape[0]

    if chips != 8 or depth % LANES:
        memory_rows = pool(passage_states, memory_queries, memory_gain)
        whole_weight = lax.all_gather(kv_weight, "pass", axis=0, tiled=True)
        memory_kv = jnp.dot(memory_rows, whole_weight, preferred_element_type=jnp.float32)
        everything = lax.all_gather(memory_kv.astype(jnp.bfloat16), "pass", axis=0, tiled=True)
        halves = everything.reshape(-1, 2, 2, LANES).transpose(2, 0, 1, 3).reshape(2, -1, 2 * LANES)
        rest = (retrieval * MEM, question_lengths, question_queries)
        context = attend(jnp.int32(0), *rest, halves[0], question_kv)
        return attend(jnp.int32(1), *rest, halves[1], question_kv, context)

    place = place_of(chip, chips).reshape(1)
    order = [2 * line for line in range(chips // 2)] + [2 * line + 1 for line in range(chips // 2)][::-1]

    def to_partner(x):
        return lax.ppermute(x, "pass", [(i, i ^ 1) for i in range(extent)])

    def along(x, target):
        pairs = [(c, target(c // 2, c % 2)) for c in range(chips)]
        return lax.ppermute(x, "pass", [(2 * s + c, 2 * d + c) for s, d in pairs for c in range(2)])

    def along_ring(x, step):
        return along(x, lambda line, lane: order[(order.index(2 * line + lane) + step) % chips])

    def line_by_line(block):
        lines = chips // 2

        def lane_of(x):
            return along(x, lambda line, lane: 2 * line + 1 - lane)

        near = {k: along(block, lambda line, lane: 2 * ((line + k) % lines) + lane) for k in (2, 1, 3)}
        far = {0: lane_of(block)}
        far[3] = along(block, lambda line, lane: 2 * ((line + 3) % lines) + 1 - lane)
        far[1], far[2] = lane_of(near[1]), lane_of(near[2])
        return [block, near[1], near[2], near[3], far[0], far[1], far[2], far[3]]

    mine, theirs = split(core, kv_weight)
    up = [[mine], [to_partner(theirs)]]
    down = [[x[0]] for x in up]

    def blocks(turns):
        found = {}
        for part in range(2):
            for turn in turns:
                if turn < len(up[part]):
                    found[part, turn] = up[part][turn]
                if 0 < turn < len(down[part]):
                    found[part, chips - turn] = down[part][turn]
        return found

    for turn in range(1, chips // 2):
        for part in range(2):
            up[part].append(along_ring(up[part][-1], 1))
            down[part].append(along_ring(down[part][-1], -1))
        if turn == 1:
            rows = pool(passage_states, memory_queries, memory_gain)
            *hops, rows = lax.optimization_barrier((*(x[-1] for x in up + down), rows))
            for chain, hop in zip(up + down, hops):
                chain[-1] = hop
            other_rows = to_partner(rows)
    up[0].append(along_ring(up[0][-1], 1))
    down[1].append(along_ring(down[1][-1], -1))
    early = project(chips, core, place, rows, other_rows, blocks((0, 1, 2)))
    memory_kv = project(chips, core, place, rows, other_rows, blocks((3, 4)), early)
    near = jnp.concatenate(line_by_line(memory_kv), axis=0)
    far = to_partner(near)

    lines = chips // 2
    of_chip = lax.div(retrieval, CHIP)
    back = lax.rem(lines + lax.div(chip, 2) - lax.div(of_chip, 2), lines)
    slot = back + lines * lax.rem(lax.rem(chip, 2) + lax.rem(of_chip, 2), 2)
    starts = (slot * CHIP + lax.rem(retrieval, CHIP)) * MEM
    rest = (starts, question_lengths, question_queries)
    context = attend(core, *rest, near, question_kv)
    return attend(1 - core, *rest, far, question_kv, context)


def solution(mesh):
    placed = (
        P(("groups", "pass"), None, None),
        P(),
        P(),
        P("pass", None),
        P(("groups", "pass"), None),
        P(("groups", "pass"), None, None),
        P(("groups", "pass"), None, None),
        P(("groups", "pass")),
    )
    return jax.shard_map(
        functools.partial(local, mesh.shape["pass"]),
        mesh=mesh,
        in_specs=placed,
        out_specs=P(("groups", "pass"), None, None),
        check_vma=False,
    )
```

```python
import functools
import math

import jax
import jax.numpy as jnp
from jax import lax
from jax.experimental import pallas as pl
from jax.experimental.pallas import tpu as pltpu
from jax.sharding import PartitionSpec as P

D = 4096
CH = 32
CHD = 128
MEM = 32
LEN = 128
QLEN = 64
TOPK = 16
H = 116
HD = 64
KVH = 4
GROUP = 29
KVW = 512

LANES = 2 * HD
PAIRS = GROUP
HALF = PAIRS * LANES
ROWS = TOPK * MEM
KEYS = 2 * (ROWS + QLEN)
NEG = -1e30
SUM_LOW, SUM_HIGH = 2.0 ** -40, 2.0 ** 60
POOL_WIDTH = 1024
FIRST_COST = 8 * 10**9
CHIP = 8
STEP = 5
BLOCK = 16
MIB = 1024 * 1024


def place_of(chip, ring):
    line, lane = lax.div(chip, 2), lax.rem(chip, 2)
    return line + lane * (ring - 1 - 2 * line)


def chip_at(place, ring):
    lane = lax.div(place, ring // 2)
    line = place + lane * (ring - 1 - 2 * place)
    return 2 * line + lane


def split_kernel(core_ref, weight_ref, mine_ref, theirs_ref):
    for out_ref, half in ((mine_ref, core_ref[0]), (theirs_ref, 1 - core_ref[0])):
        for n in range(2):
            at = pl.multiple_of(half * LANES + n * KVH * HD, LANES)
            out_ref[:, n * LANES:(n + 1) * LANES] = weight_ref[:, pl.ds(at, LANES)]


def split(core, weight):
    vmem = pl.BlockSpec(memory_space=pltpu.VMEM)
    return pl.pallas_call(
        split_kernel,
        in_specs=[pl.BlockSpec(memory_space=pltpu.SMEM), vmem],
        out_specs=[vmem, vmem],
        out_shape=[jax.ShapeDtypeStruct((weight.shape[0], 2 * LANES), weight.dtype)] * 2,
        compiler_params=pltpu.CompilerParams(vmem_limit_bytes=8 * MIB),
        cost_estimate=pl.CostEstimate(flops=FIRST_COST, bytes_accessed=4 * weight.size, transcendentals=0),
        name="split",
    )(core.reshape(1), weight)


def pool_kernel(states, queries, gain, out_ref, pooled):
    passages = states.shape[0]
    two = 2 * CHD
    zero = jnp.zeros((MEM, CHD), jnp.bfloat16)
    blank = jnp.zeros((2 * MEM, LEN), jnp.bfloat16)
    totals = [jnp.zeros((MEM, CHD), jnp.float32)] * passages
    for base in range(0, D, POOL_WIDTH):
        blocks = []
        for column in range(base, base + POOL_WIDTH, two):
            lhs = jnp.concatenate(
                [
                    jnp.concatenate([queries[:, column:column + CHD], zero], axis=1),
                    jnp.concatenate([zero, queries[:, column + CHD:column + two]], axis=1),
                ],
                axis=0,
            )
            for p in range(0, passages, 2):
                tokens = states[p:p + 2, :, column:column + two].reshape(2 * LEN, two)
                scores = lax.dot_general(
                    lhs, tokens, (((1,), (1,)), ((), ())), preferred_element_type=jnp.float32
                ) * (1.0 / math.sqrt(CHD))
                blocks.append((column, p, tokens, scores))
        for column, p, tokens, scores in blocks:
            rows = []
            for n in range(2):
                part = scores[:, n * LEN:(n + 1) * LEN]
                part = jnp.exp(part - jnp.max(part, axis=1, keepdims=True))
                part = (part / jnp.sum(part, axis=1, keepdims=True)).astype(jnp.bfloat16)
                rows.append(jnp.concatenate([blank, part] if n else [part, blank], axis=1))
            mixed = jnp.dot(jnp.concatenate(rows, axis=0), tokens, preferred_element_type=jnp.float32)
            for n in range(2):
                for head in range(2):
                    top = (2 * n + head) * MEM
                    block = mixed[top:top + MEM, head * CHD:(head + 1) * CHD]
                    place = slice(column + head * CHD, column + (head + 1) * CHD)
                    pooled[(p + n) * MEM:(p + n + 1) * MEM, place] = block
                    totals[p + n] = totals[p + n] + block * block
    mean_square = jnp.sum(jnp.concatenate(totals, axis=0), axis=1, keepdims=True) * (1.0 / D)
    scale = lax.rsqrt(mean_square + 1e-06)
    factor = gain[...].astype(jnp.float32).reshape(1, D)
    out_ref[...] = (pooled[...] * scale * factor).astype(jnp.bfloat16)


def pool(states, queries, gain):
    count = states.shape[0]
    vmem = pl.BlockSpec(memory_space=pltpu.VMEM)
    return pl.pallas_call(
        pool_kernel,
        in_specs=[vmem] * 3,
        out_specs=vmem,
        out_shape=jax.ShapeDtypeStruct((count * MEM, D), jnp.bfloat16),
        scratch_shapes=[pltpu.VMEM((count * MEM, D), jnp.float32)],
        compiler_params=pltpu.CompilerParams(vmem_limit_bytes=20 * MIB),
        cost_estimate=pl.CostEstimate(
            flops=4 * count * MEM * LEN * D, bytes_accessed=2 * count * LEN * D,
            transcendentals=count * CH * MEM * LEN,
        ),
        name="pool",
    )(states, queries, gain)


def attend_kernel(begun, ahead, half_ref, start_ref, length_ref, q_hbm, kv_ref, own_kv_ref, *rest):
    if ahead:
        other_at = pl.multiple_of((1 - half_ref[0]) * HALF, LANES)
        coming = pltpu.make_async_copy(q_hbm.at[0, :, pl.ds(other_at, HALF)], rest[-14], rest[-1])
        coming.start()
        out_hbm, rest = rest[-15], rest[:-1]
    else:
        out_hbm = rest[-13]
    (
        questions, answers, memory, key_side, value_side, weights, bias, marker, scores, all_weights,
        arrived, sent,
    ) = rest[-12:]
    count = q_hbm.shape[0]
    half_at = pl.multiple_of(half_ref[0] * HALF, LANES)
    own_at = pl.multiple_of(half_ref[0] * LANES, LANES)
    factor = math.log2(math.e) / math.sqrt(HD)

    def fetch(query):
        return pltpu.make_async_copy(
            q_hbm.at[query, :, pl.ds(half_at, HALF)], questions.at[query], arrived.at[query]
        )

    def send(query):
        return pltpu.make_async_copy(
            answers.at[query], out_hbm.at[query, :, pl.ds(half_at, HALF)], sent.at[query]
        )

    if begun:
        questions[0] = rest[0][...]
    else:
        fetch(0).start()
    lane = lax.broadcasted_iota(jnp.int32, (KEYS, LANES), 1)
    row = lax.broadcasted_iota(jnp.int32, (KEYS, LANES), 0)
    in_b = ((row >= ROWS) & (row < 2 * ROWS)) | (row >= 2 * ROWS + QLEN)
    ones = jnp.where((lane >= HD) == in_b, 1.0, 0.0).astype(jnp.bfloat16)
    key_side[...] = jnp.zeros_like(key_side)
    for g in range(2):
        value_side[g, :, LANES:] = ones

    half = PAIRS // 2
    chunks = []
    for g in range(2):
        tiles = list(range(half + 1)) if g == 0 else list(range(half, PAIRS))
        chunks += [(g, tiles[at:at + STEP]) for at in range(0, len(tiles), STEP)]

    def answer(query, carry):
        for slot in range(TOPK):
            start = pl.multiple_of(start_ref[query, slot], MEM)
            memory[slot * MEM:(slot + 1) * MEM, :] = kv_ref[pl.ds(start, MEM), :]
        length = length_ref[query]

        turned = jnp.transpose(memory[:, :LANES])
        own_k = own_kv_ref[query, :, pl.ds(own_at, LANES)]
        own_turned = jnp.transpose(jnp.concatenate([own_k, own_k], axis=0))
        column = lax.broadcasted_iota(jnp.int32, (HD, LANES), 1)
        for g in range(2):
            for member in range(2):
                rows = slice(member * HD, (member + 1) * HD)
                key_side[g, rows, member * ROWS:(member + 1) * ROWS] = turned[g * HD:(g + 1) * HD]
                own = own_turned[g * HD:(g + 1) * HD]
                mine = (column >= HD) if member else (column < HD)
                key_side[g, rows, 2 * ROWS:] = jnp.where(mine, own, jnp.zeros_like(own))

        token = lax.broadcasted_iota(jnp.int32, (QLEN, LANES), 0)
        low = lax.broadcasted_iota(jnp.int32, (QLEN, LANES), 1) < HD
        key = lax.rem(lax.broadcasted_iota(jnp.int32, (QLEN, LANES), 1), HD)
        bias[...] = jnp.where((key <= token) & (key < length), 0.0, NEG)
        alive = token < length
        sample = lax.div(key, HD // STEP)

        if begun:

            @pl.when(query > 0)
            def _():
                fetch(query).wait()
        else:
            fetch(query).wait()

        @pl.when(query + 1 < count)
        def _():
            fetch(query + 1).start()

        def stacked(tiles):
            return jnp.concatenate([questions[query, :, t * LANES:(t + 1) * LANES] for t in tiles], axis=0)

        def key_product(i):
            g, tiles = chunks[i]
            lhs = stacked(tiles)
            for c in range(0, KEYS, 2 * LANES):
                part = slice(c, min(c + 2 * LANES, KEYS))
                got = jnp.dot(lhs, key_side[g, :, part], preferred_element_type=jnp.float32) * factor
                if c == 2 * ROWS:
                    got = got + jnp.concatenate([bias[...]] * len(tiles), axis=0)
                weights[i % 2, :len(tiles) * QLEN, part] = jnp.exp2(got).astype(jnp.bfloat16)

        def finish(i, mixed):
            g, tiles = chunks[i]
            for n, t in enumerate(tiles):
                rows = slice(n * QLEN, (n + 1) * QLEN)
                sums = mixed[rows, LANES:]
                inverse = pl.reciprocal(sums, approx=True)
                inverse = inverse * (2.0 - sums * inverse)
                result = jnp.where(alive, mixed[rows, :LANES] * inverse, 0.0).astype(jnp.bfloat16)
                at = slice(t * LANES, (t + 1) * LANES)
                if t == half and g == 1:
                    result = jnp.where(low, answers[query, :, at], result)
                answers[query, :, at] = result

        def value_product(i, seen):
            g, tiles = chunks[i]
            size = len(tiles) * QLEN
            mixed = jnp.dot(weights[i % 2, :size, :], value_side[g], preferred_element_type=jnp.float32)
            sums = mixed[:QLEN, LANES:]
            for n in range(1, len(tiles)):
                sums = jnp.where(sample == n, mixed[n * QLEN:(n + 1) * QLEN, LANES:], sums)
            seen = jnp.where((sums > SUM_LOW) & (sums < SUM_HIGH), seen, 1.0)
            finish(i, mixed)
            return seen

        key_product(0)

        own_v_at = pl.multiple_of(own_at + KVH * HD, LANES)
        own_v = own_kv_ref[query, :, pl.ds(own_v_at, LANES)]
        for block, at in ((memory[:, LANES:], 0), (own_v, 2 * ROWS)):
            size = block.shape[0]
            swapped = jnp.concatenate([block[:, HD:], block[:, :HD]], axis=1)
            lower = lax.broadcasted_iota(jnp.int32, block.shape, 1) < HD
            zero = jnp.zeros_like(block)
            for g in range(2):
                one, two = (block, swapped) if g == 0 else (swapped, block)
                value_side[g, at:at + size, :LANES] = jnp.where(lower, one, zero)
                value_side[g, at + size:at + 2 * size, :LANES] = jnp.where(lower, zero, two)

        seen = jnp.zeros((QLEN, LANES), jnp.float32)
        for i in range(len(chunks)):
            if i + 1 < len(chunks):
                key_product(i + 1)
            seen = value_product(i, seen)
        marker[0] = jnp.max(seen)

        @pl.when(marker[0] > 0.0)
        def _():
            for i, (g, tiles) in enumerate(chunks):
                size = len(tiles) * QLEN
                scores[:size, :] = jnp.dot(stacked(tiles), key_side[g], preferred_element_type=jnp.float32)

                def soften(n, carry):
                    rows = pl.ds(pl.multiple_of(n * QLEN, QLEN), QLEN)
                    own_scores = scores[rows, 2 * ROWS:] + bias[...]
                    tops = []
                    for member in range(2):
                        columns = slice(member * ROWS, (member + 1) * ROWS)
                        top = jnp.where(low, own_scores, NEG) if member == 0 else jnp.where(low, NEG, own_scores)
                        top = jnp.maximum(
                            jnp.max(top, axis=1, keepdims=True),
                            jnp.max(scores[rows, columns], axis=1, keepdims=True),
                        )
                        all_weights[rows, columns] = jnp.exp2(
                            (scores[rows, columns] - top) * factor
                        ).astype(jnp.bfloat16)
                        tops.append(top)
                    all_weights[rows, 2 * ROWS:] = jnp.exp2(
                        (own_scores - jnp.where(low, tops[0], tops[1])) * factor
                    ).astype(jnp.bfloat16)
                    return carry

                lax.fori_loop(0, len(tiles), soften, 0)
                finish(
                    i, jnp.dot(all_weights[:size, :], value_side[g], preferred_element_type=jnp.float32)
                )

        send(query).start()
        return carry

    lax.fori_loop(0, count, answer, 0)
    for query in range(count):
        send(query).wait()
    if ahead:
        coming.wait()


def attend(half, starts, lengths, questions, memory_kv, own_kv, earlier=None, begun=None, ahead=False):
    count = questions.shape[0]
    hbm, vmem, smem = (pl.BlockSpec(memory_space=x) for x in (pltpu.HBM, pltpu.VMEM, pltpu.SMEM))
    operands = [half.reshape(1), starts, lengths, questions, memory_kv, own_kv]
    in_specs = [smem, smem, smem, hbm, vmem, vmem]
    aliases = {}
    if begun is not None:
        operands.append(begun)
        in_specs.append(vmem)
    if earlier is not None:
        aliases = {len(operands): 0}
        operands.append(earlier)
        in_specs.append(hbm)
    out_specs, extra = [hbm], []
    out_shape = [jax.ShapeDtypeStruct((count, QLEN, H * HD), jnp.bfloat16)]
    if ahead:
        out_specs.append(vmem)
        out_shape.append(jax.ShapeDtypeStruct((QLEN, HALF), jnp.bfloat16))
        extra = [pltpu.SemaphoreType.DMA]
    got = pl.pallas_call(
        functools.partial(attend_kernel, begun is not None, ahead),
        in_specs=in_specs,
        out_specs=out_specs,
        out_shape=out_shape,
        scratch_shapes=[
            pltpu.VMEM((count, QLEN, HALF), jnp.bfloat16),
            pltpu.VMEM((count, QLEN, HALF), jnp.bfloat16),
            pltpu.VMEM((ROWS, 2 * LANES), jnp.bfloat16),
            pltpu.VMEM((2, LANES, KEYS), jnp.bfloat16),
            pltpu.VMEM((2, KEYS, 2 * LANES), jnp.bfloat16),
            pltpu.VMEM((2, STEP * QLEN, KEYS), jnp.bfloat16),
            pltpu.VMEM((QLEN, LANES), jnp.float32),
            pltpu.SMEM((1,), jnp.float32),
            pltpu.VMEM((STEP * QLEN, KEYS), jnp.float32),
            pltpu.VMEM((STEP * QLEN, KEYS), jnp.bfloat16),
            pltpu.SemaphoreType.DMA((count,)),
            pltpu.SemaphoreType.DMA((count,)),
            *extra,
        ],
        input_output_aliases=aliases,
        compiler_params=pltpu.CompilerParams(vmem_limit_bytes=50 * MIB),
        cost_estimate=pl.CostEstimate(
            flops=2 * count * QLEN * H * HD * (ROWS + QLEN),
            bytes_accessed=2 * count * QLEN * H * HD,
            transcendentals=count * QLEN * H * (ROWS + QLEN) // 2,
        ),
        name="attend",
    )(*operands)
    return got if ahead else got[0]


def project_kernel(ring, pieces, more, core_ref, place_ref, own_ref, other_ref, *rest):
    weights, rest = rest[:len(pieces)], rest[len(pieces):]
    out_ref = rest[-1]
    count = own_ref.shape[0]
    depth = weights[0].shape[0]
    core = core_ref[0]
    total = jnp.zeros((2 * count, weights[0].shape[1]), jnp.float32) if more else rest[0][...]
    for (part, i), weight in zip(pieces, weights):
        chip = chip_at(lax.rem(ring + place_ref[0] - i, ring), ring)
        at = pl.multiple_of((2 * chip + (1 - core if part else core)) * depth, depth)
        rows = jnp.concatenate([own_ref[:, pl.ds(at, depth)], other_ref[:, pl.ds(at, depth)]], axis=0)
        total += jnp.dot(rows, weight[...], preferred_element_type=jnp.float32)
    if more:
        out_ref[...] = total
        return
    result = total.astype(jnp.bfloat16)
    out_ref[pl.ds(pl.multiple_of(core * count, count), count)] = result[:count]
    out_ref[pl.ds(pl.multiple_of((1 - core) * count, count), count)] = result[count:]


def project(ring, core, place, own_rows, other_rows, weights, sums=None):
    count = own_rows.shape[0]
    pieces, blocks = tuple(weights), list(weights.values())
    width = blocks[0].shape[1]
    vmem = pl.BlockSpec(memory_space=pltpu.VMEM)
    smem = pl.BlockSpec(memory_space=pltpu.SMEM)
    more = sums is None
    operands = [own_rows, other_rows, *blocks] + ([] if more else [sums])
    return pl.pallas_call(
        functools.partial(project_kernel, ring, pieces, more),
        in_specs=[smem, smem] + [vmem] * len(operands),
        out_specs=vmem,
        out_shape=jax.ShapeDtypeStruct((2 * count, width), jnp.float32 if more else jnp.bfloat16),
        compiler_params=pltpu.CompilerParams(vmem_limit_bytes=16 * MIB),
        cost_estimate=pl.CostEstimate(
            flops=count * D * width, bytes_accessed=32 * D * width, transcendentals=0
        ),
        name="project",
    )(core.reshape(1), place, *operands)


def local(
    extent,
    passage_states,
    memory_queries,
    memory_gain,
    kv_weight,
    retrieval,
    question_queries,
    question_kv,
    question_lengths,
):
    me = lax.axis_index("pass")
    core, chip = me & 1, lax.div(me, 2)
    chips = extent // 2
    depth = kv_weight.shape[0]

    if chips != 8 or depth % LANES:
        memory_rows = pool(passage_states, memory_queries, memory_gain)
        whole_weight = lax.all_gather(kv_weight, "pass", axis=0, tiled=True)
        memory_kv = jnp.dot(memory_rows, whole_weight, preferred_element_type=jnp.float32)
        everything = lax.all_gather(memory_kv.astype(jnp.bfloat16), "pass", axis=0, tiled=True)
        halves = everything.reshape(-1, 2, 2, LANES).transpose(2, 0, 1, 3).reshape(2, -1, 2 * LANES)
        rest = (retrieval * MEM, question_lengths, question_queries)
        context = attend(jnp.int32(0), *rest, halves[0], question_kv)
        return attend(jnp.int32(1), *rest, halves[1], question_kv, context)

    place = place_of(chip, chips).reshape(1)
    order = [2 * line for line in range(chips // 2)] + [2 * line + 1 for line in range(chips // 2)][::-1]

    def to_partner(x):
        return lax.ppermute(x, "pass", [(i, i ^ 1) for i in range(extent)])

    def along(x, target):
        pairs = [(c, target(c // 2, c % 2)) for c in range(chips)]
        return lax.ppermute(x, "pass", [(2 * s + c, 2 * d + c) for s, d in pairs for c in range(2)])

    def along_ring(x, step):
        return along(x, lambda line, lane: order[(order.index(2 * line + lane) + step) % chips])

    def line_by_line(block):
        lines = chips // 2

        def lane_of(x):
            return along(x, lambda line, lane: 2 * line + 1 - lane)

        near = {k: along(block, lambda line, lane: 2 * ((line + k) % lines) + lane) for k in (2, 1, 3)}
        far = {0: lane_of(block)}
        far[3] = along(block, lambda line, lane: 2 * ((line + 3) % lines) + 1 - lane)
        far[1], far[2] = lane_of(near[1]), lane_of(near[2])
        return [block, near[1], near[2], near[3], far[0], far[1], far[2], far[3]]

    mine, theirs = split(core, kv_weight)
    up = [[mine], [to_partner(theirs)]]
    down = [[x[0]] for x in up]

    def blocks(turns):
        found = {}
        for part in range(2):
            for turn in turns:
                if turn < len(up[part]):
                    found[part, turn] = up[part][turn]
                if 0 < turn < len(down[part]):
                    found[part, chips - turn] = down[part][turn]
        return found

    for turn in range(1, chips // 2):
        for part in range(2):
            up[part].append(along_ring(up[part][-1], 1))
            down[part].append(along_ring(down[part][-1], -1))
        if turn == 1:
            rows = pool(passage_states, memory_queries, memory_gain)
            *hops, rows = lax.optimization_barrier((*(x[-1] for x in up + down), rows))
            for chain, hop in zip(up + down, hops):
                chain[-1] = hop
            other_rows = to_partner(rows)
    up[0].append(along_ring(up[0][-1], 1))
    down[1].append(along_ring(down[1][-1], -1))
    early = project(chips, core, place, rows, other_rows, blocks((0, 1, 2)))
    memory_kv = project(chips, core, place, rows, other_rows, blocks((3, 4)), early)
    near = jnp.concatenate(line_by_line(memory_kv), axis=0)
    far = to_partner(near)

    lines = chips // 2
    of_chip = lax.div(retrieval, CHIP)
    back = lax.rem(lines + lax.div(chip, 2) - lax.div(of_chip, 2), lines)
    slot = back + lines * lax.rem(lax.rem(chip, 2) + lax.rem(of_chip, 2), 2)
    starts = (slot * CHIP + lax.rem(retrieval, CHIP)) * MEM
    rest = (starts, question_lengths, question_queries)
    context, begun = attend(core, *rest, near, question_kv, ahead=True)
    return attend(1 - core, *rest, far, question_kv, context, begun)


def solution(mesh):
    placed = (
        P(("groups", "pass"), None, None),
        P(),
        P(),
        P("pass", None),
        P(("groups", "pass"), None),
        P(("groups", "pass"), None, None),
        P(("groups", "pass"), None, None),
        P(("groups", "pass")),
    )
    return jax.shard_map(
        functools.partial(local, mesh.shape["pass"]),
        mesh=mesh,
        in_specs=placed,
        out_specs=P(("groups", "pass"), None, None),
        check_vma=False,
    )
```

```python
import functools
import math

import jax
import jax.numpy as jnp
from jax import lax
from jax.experimental import pallas as pl
from jax.experimental.pallas import tpu as pltpu
from jax.sharding import PartitionSpec as P

D = 4096
CH = 32
CHD = 128
MEM = 32
LEN = 128
QLEN = 64
TOPK = 16
H = 116
HD = 64
KVH = 4
GROUP = 29
KVW = 512

LANES = 2 * HD
PAIRS = GROUP
HALF = PAIRS * LANES
ROWS = TOPK * MEM
KEYS = 2 * (ROWS + QLEN)
NEG = -1e30
SUM_LOW, SUM_HIGH = 2.0 ** -40, 2.0 ** 60
POOL_WIDTH = 1024
FIRST_COST = 8 * 10**9
CHIP = 8
STEP = 5
BLOCK = 16
MIB = 1024 * 1024


def place_of(chip, ring):
    line, lane = lax.div(chip, 2), lax.rem(chip, 2)
    return line + lane * (ring - 1 - 2 * line)


def chip_at(place, ring):
    lane = lax.div(place, ring // 2)
    line = place + lane * (ring - 1 - 2 * place)
    return 2 * line + lane


def split_kernel(core_ref, weight_ref, mine_ref, theirs_ref):
    for out_ref, half in ((mine_ref, core_ref[0]), (theirs_ref, 1 - core_ref[0])):
        for n in range(2):
            at = pl.multiple_of(half * LANES + n * KVH * HD, LANES)
            out_ref[:, n * LANES:(n + 1) * LANES] = weight_ref[:, pl.ds(at, LANES)]


def split(core, weight):
    vmem = pl.BlockSpec(memory_space=pltpu.VMEM)
    return pl.pallas_call(
        split_kernel,
        in_specs=[pl.BlockSpec(memory_space=pltpu.SMEM), vmem],
        out_specs=[vmem, vmem],
        out_shape=[jax.ShapeDtypeStruct((weight.shape[0], 2 * LANES), weight.dtype)] * 2,
        compiler_params=pltpu.CompilerParams(vmem_limit_bytes=8 * MIB),
        cost_estimate=pl.CostEstimate(flops=FIRST_COST, bytes_accessed=4 * weight.size, transcendentals=0),
        name="split",
    )(core.reshape(1), weight)


def pool_kernel(states, queries, gain, out_ref, pooled):
    passages = states.shape[0]
    two = 2 * CHD
    zero = jnp.zeros((MEM, CHD), jnp.bfloat16)
    blank = jnp.zeros((2 * MEM, LEN), jnp.bfloat16)
    totals = [jnp.zeros((MEM, CHD), jnp.float32)] * passages
    for base in range(0, D, POOL_WIDTH):
        blocks = []
        for column in range(base, base + POOL_WIDTH, two):
            lhs = jnp.concatenate(
                [
                    jnp.concatenate([queries[:, column:column + CHD], zero], axis=1),
                    jnp.concatenate([zero, queries[:, column + CHD:column + two]], axis=1),
                ],
                axis=0,
            )
            for p in range(0, passages, 2):
                tokens = states[p:p + 2, :, column:column + two].reshape(2 * LEN, two)
                scores = lax.dot_general(
                    lhs, tokens, (((1,), (1,)), ((), ())), preferred_element_type=jnp.float32
                ) * (1.0 / math.sqrt(CHD))
                blocks.append((column, p, tokens, scores))
        for column, p, tokens, scores in blocks:
            rows = []
            for n in range(2):
                part = scores[:, n * LEN:(n + 1) * LEN]
                part = jnp.exp(part - jnp.max(part, axis=1, keepdims=True))
                part = (part / jnp.sum(part, axis=1, keepdims=True)).astype(jnp.bfloat16)
                rows.append(jnp.concatenate([blank, part] if n else [part, blank], axis=1))
            mixed = jnp.dot(jnp.concatenate(rows, axis=0), tokens, preferred_element_type=jnp.float32)
            for n in range(2):
                for head in range(2):
                    top = (2 * n + head) * MEM
                    block = mixed[top:top + MEM, head * CHD:(head + 1) * CHD]
                    place = slice(column + head * CHD, column + (head + 1) * CHD)
                    pooled[(p + n) * MEM:(p + n + 1) * MEM, place] = block
                    totals[p + n] = totals[p + n] + block * block
    mean_square = jnp.sum(jnp.concatenate(totals, axis=0), axis=1, keepdims=True) * (1.0 / D)
    scale = lax.rsqrt(mean_square + 1e-06)
    factor = gain[...].astype(jnp.float32).reshape(1, D)
    out_ref[...] = (pooled[...] * scale * factor).astype(jnp.bfloat16)


def pool(states, queries, gain):
    count = states.shape[0]
    vmem = pl.BlockSpec(memory_space=pltpu.VMEM)
    return pl.pallas_call(
        pool_kernel,
        in_specs=[vmem] * 3,
        out_specs=vmem,
        out_shape=jax.ShapeDtypeStruct((count * MEM, D), jnp.bfloat16),
        scratch_shapes=[pltpu.VMEM((count * MEM, D), jnp.float32)],
        compiler_params=pltpu.CompilerParams(vmem_limit_bytes=20 * MIB),
        cost_estimate=pl.CostEstimate(
            flops=4 * count * MEM * LEN * D, bytes_accessed=2 * count * LEN * D,
            transcendentals=count * CH * MEM * LEN,
        ),
        name="pool",
    )(states, queries, gain)


def attend_kernel(begun, ahead, half_ref, start_ref, length_ref, q_hbm, kv_ref, own_kv_ref, *rest):
    if ahead:
        other_at = pl.multiple_of((1 - half_ref[0]) * HALF, LANES)
        coming = pltpu.make_async_copy(q_hbm.at[0, :, pl.ds(other_at, HALF)], rest[-14], rest[-1])
        coming.start()
        out_hbm, rest = rest[-15], rest[:-1]
    else:
        out_hbm = rest[-13]
    (
        questions, answers, memory, key_side, value_side, weights, bias, marker, scores, all_weights,
        arrived, sent,
    ) = rest[-12:]
    count = q_hbm.shape[0]
    half_at = pl.multiple_of(half_ref[0] * HALF, LANES)
    own_at = pl.multiple_of(half_ref[0] * LANES, LANES)
    factor = math.log2(math.e) / math.sqrt(HD)

    def fetch(query):
        return pltpu.make_async_copy(
            q_hbm.at[query, :, pl.ds(half_at, HALF)], questions.at[query], arrived.at[query]
        )

    def send(query):
        return pltpu.make_async_copy(
            answers.at[query], out_hbm.at[query, :, pl.ds(half_at, HALF)], sent.at[query]
        )

    if begun:
        questions[0] = rest[0][...]
    else:
        fetch(0).start()
    lane = lax.broadcasted_iota(jnp.int32, (KEYS, LANES), 1)
    row = lax.broadcasted_iota(jnp.int32, (KEYS, LANES), 0)
    in_b = ((row >= ROWS) & (row < 2 * ROWS)) | (row >= 2 * ROWS + QLEN)
    ones = jnp.where((lane >= HD) == in_b, 1.0, 0.0).astype(jnp.bfloat16)
    key_side[...] = jnp.zeros_like(key_side)
    for g in range(2):
        value_side[g, :, LANES:] = ones

    half = PAIRS // 2
    chunks = []
    for g in range(2):
        tiles = list(range(half + 1)) if g == 0 else list(range(half, PAIRS))
        chunks += [(g, tiles[at:at + STEP]) for at in range(0, len(tiles), STEP)]

    def answer(query, carry):
        for slot in range(TOPK):
            start = pl.multiple_of(start_ref[query, slot], MEM)
            memory[slot * MEM:(slot + 1) * MEM, :] = kv_ref[pl.ds(start, MEM), :]
        length = length_ref[query]

        turned = jnp.transpose(memory[:, :LANES])
        own_k = own_kv_ref[query, :, pl.ds(own_at, LANES)]
        own_turned = jnp.transpose(jnp.concatenate([own_k, own_k], axis=0))
        column = lax.broadcasted_iota(jnp.int32, (HD, LANES), 1)
        for g in range(2):
            for member in range(2):
                rows = slice(member * HD, (member + 1) * HD)
                key_side[g, rows, member * ROWS:(member + 1) * ROWS] = turned[g * HD:(g + 1) * HD]
                own = own_turned[g * HD:(g + 1) * HD]
                mine = (column >= HD) if member else (column < HD)
                key_side[g, rows, 2 * ROWS:] = jnp.where(mine, own, jnp.zeros_like(own))

        token = lax.broadcasted_iota(jnp.int32, (QLEN, LANES), 0)
        low = lax.broadcasted_iota(jnp.int32, (QLEN, LANES), 1) < HD
        key = lax.rem(lax.broadcasted_iota(jnp.int32, (QLEN, LANES), 1), HD)
        bias[...] = jnp.where((key <= token) & (key < length), 0.0, NEG)
        alive = token < length
        sample = lax.div(key, HD // STEP)

        own_v_at = pl.multiple_of(own_at + KVH * HD, LANES)
        own_v = own_kv_ref[query, :, pl.ds(own_v_at, LANES)]
        for block, at in ((memory[:, LANES:], 0), (own_v, 2 * ROWS)):
            size = block.shape[0]
            swapped = jnp.concatenate([block[:, HD:], block[:, :HD]], axis=1)
            lower = lax.broadcasted_iota(jnp.int32, block.shape, 1) < HD
            zero = jnp.zeros_like(block)
            for g in range(2):
                one, two = (block, swapped) if g == 0 else (swapped, block)
                value_side[g, at:at + size, :LANES] = jnp.where(lower, one, zero)
                value_side[g, at + size:at + 2 * size, :LANES] = jnp.where(lower, zero, two)

        if begun:

            @pl.when(query > 0)
            def _():
                fetch(query).wait()
        else:
            fetch(query).wait()

        @pl.when(query + 1 < count)
        def _():
            fetch(query + 1).start()

        def stacked(tiles):
            return jnp.concatenate([questions[query, :, t * LANES:(t + 1) * LANES] for t in tiles], axis=0)

        def key_product(i):
            g, tiles = chunks[i]
            lhs = stacked(tiles)
            for c in range(0, KEYS, ROWS):
                part = slice(c, min(c + ROWS, KEYS))
                got = jnp.dot(lhs, key_side[g, :, part], preferred_element_type=jnp.float32) * factor
                if c == 2 * ROWS:
                    got = got + jnp.concatenate([bias[...]] * len(tiles), axis=0)
                weights[i % 2, :len(tiles) * QLEN, part] = jnp.exp2(got).astype(jnp.bfloat16)

        def finish(i, mixed):
            g, tiles = chunks[i]
            for n, t in enumerate(tiles):
                rows = slice(n * QLEN, (n + 1) * QLEN)
                sums = mixed[rows, LANES:]
                inverse = pl.reciprocal(sums, approx=True)
                inverse = inverse * (2.0 - sums * inverse)
                result = jnp.where(alive, mixed[rows, :LANES] * inverse, 0.0).astype(jnp.bfloat16)
                at = slice(t * LANES, (t + 1) * LANES)
                if t == half and g == 1:
                    result = jnp.where(low, answers[query, :, at], result)
                answers[query, :, at] = result

        def value_product(i, seen):
            g, tiles = chunks[i]
            size = len(tiles) * QLEN
            mixed = jnp.dot(weights[i % 2, :size, :], value_side[g], preferred_element_type=jnp.float32)
            sums = mixed[:QLEN, LANES:]
            for n in range(1, len(tiles)):
                sums = jnp.where(sample == n, mixed[n * QLEN:(n + 1) * QLEN, LANES:], sums)
            seen = jnp.where((sums > SUM_LOW) & (sums < SUM_HIGH), seen, 1.0)
            finish(i, mixed)
            return seen

        key_product(0)
        seen = jnp.zeros((QLEN, LANES), jnp.float32)
        for i in range(len(chunks)):
            if i + 1 < len(chunks):
                key_product(i + 1)
            seen = value_product(i, seen)
        marker[0] = jnp.max(seen)

        @pl.when(marker[0] > 0.0)
        def _():
            for i, (g, tiles) in enumerate(chunks):
                size = len(tiles) * QLEN
                scores[:size, :] = jnp.dot(stacked(tiles), key_side[g], preferred_element_type=jnp.float32)

                def soften(n, carry):
                    rows = pl.ds(pl.multiple_of(n * QLEN, QLEN), QLEN)
                    own_scores = scores[rows, 2 * ROWS:] + bias[...]
                    tops = []
                    for member in range(2):
                        columns = slice(member * ROWS, (member + 1) * ROWS)
                        top = jnp.where(low, own_scores, NEG) if member == 0 else jnp.where(low, NEG, own_scores)
                        top = jnp.maximum(
                            jnp.max(top, axis=1, keepdims=True),
                            jnp.max(scores[rows, columns], axis=1, keepdims=True),
                        )
                        all_weights[rows, columns] = jnp.exp2(
                            (scores[rows, columns] - top) * factor
                        ).astype(jnp.bfloat16)
                        tops.append(top)
                    all_weights[rows, 2 * ROWS:] = jnp.exp2(
                        (own_scores - jnp.where(low, tops[0], tops[1])) * factor
                    ).astype(jnp.bfloat16)
                    return carry

                lax.fori_loop(0, len(tiles), soften, 0)
                finish(
                    i, jnp.dot(all_weights[:size, :], value_side[g], preferred_element_type=jnp.float32)
                )

        send(query).start()
        return carry

    lax.fori_loop(0, count, answer, 0)
    for query in range(count):
        send(query).wait()
    if ahead:
        coming.wait()


def attend(half, starts, lengths, questions, memory_kv, own_kv, earlier=None, begun=None, ahead=False):
    count = questions.shape[0]
    hbm, vmem, smem = (pl.BlockSpec(memory_space=x) for x in (pltpu.HBM, pltpu.VMEM, pltpu.SMEM))
    operands = [half.reshape(1), starts, lengths, questions, memory_kv, own_kv]
    in_specs = [smem, smem, smem, hbm, vmem, vmem]
    aliases = {}
    if begun is not None:
        operands.append(begun)
        in_specs.append(vmem)
    if earlier is not None:
        aliases = {len(operands): 0}
        operands.append(earlier)
        in_specs.append(hbm)
    out_specs, extra = [hbm], []
    out_shape = [jax.ShapeDtypeStruct((count, QLEN, H * HD), jnp.bfloat16)]
    if ahead:
        out_specs.append(vmem)
        out_shape.append(jax.ShapeDtypeStruct((QLEN, HALF), jnp.bfloat16))
        extra = [pltpu.SemaphoreType.DMA]
    got = pl.pallas_call(
        functools.partial(attend_kernel, begun is not None, ahead),
        in_specs=in_specs,
        out_specs=out_specs,
        out_shape=out_shape,
        scratch_shapes=[
            pltpu.VMEM((count, QLEN, HALF), jnp.bfloat16),
            pltpu.VMEM((count, QLEN, HALF), jnp.bfloat16),
            pltpu.VMEM((ROWS, 2 * LANES), jnp.bfloat16),
            pltpu.VMEM((2, LANES, KEYS), jnp.bfloat16),
            pltpu.VMEM((2, KEYS, 2 * LANES), jnp.bfloat16),
            pltpu.VMEM((2, STEP * QLEN, KEYS), jnp.bfloat16),
            pltpu.VMEM((QLEN, LANES), jnp.float32),
            pltpu.SMEM((1,), jnp.float32),
            pltpu.VMEM((STEP * QLEN, KEYS), jnp.float32),
            pltpu.VMEM((STEP * QLEN, KEYS), jnp.bfloat16),
            pltpu.SemaphoreType.DMA((count,)),
            pltpu.SemaphoreType.DMA((count,)),
            *extra,
        ],
        input_output_aliases=aliases,
        compiler_params=pltpu.CompilerParams(vmem_limit_bytes=50 * MIB),
        cost_estimate=pl.CostEstimate(
            flops=2 * count * QLEN * H * HD * (ROWS + QLEN),
            bytes_accessed=2 * count * QLEN * H * HD,
            transcendentals=count * QLEN * H * (ROWS + QLEN) // 2,
        ),
        name="attend",
    )(*operands)
    return got if ahead else got[0]


def project_kernel(ring, pieces, more, core_ref, place_ref, own_ref, other_ref, *rest):
    weights, rest = rest[:len(pieces)], rest[len(pieces):]
    out_ref = rest[-1]
    count = own_ref.shape[0]
    depth = weights[0].shape[0]
    core = core_ref[0]
    total = jnp.zeros((2 * count, weights[0].shape[1]), jnp.float32) if more else rest[0][...]
    for (part, i), weight in zip(pieces, weights):
        chip = chip_at(lax.rem(ring + place_ref[0] - i, ring), ring)
        at = pl.multiple_of((2 * chip + (1 - core if part else core)) * depth, depth)
        rows = jnp.concatenate([own_ref[:, pl.ds(at, depth)], other_ref[:, pl.ds(at, depth)]], axis=0)
        total += jnp.dot(rows, weight[...], preferred_element_type=jnp.float32)
    if more:
        out_ref[...] = total
        return
    result = total.astype(jnp.bfloat16)
    out_ref[pl.ds(pl.multiple_of(core * count, count), count)] = result[:count]
    out_ref[pl.ds(pl.multiple_of((1 - core) * count, count), count)] = result[count:]


def project(ring, core, place, own_rows, other_rows, weights, sums=None):
    count = own_rows.shape[0]
    pieces, blocks = tuple(weights), list(weights.values())
    width = blocks[0].shape[1]
    vmem = pl.BlockSpec(memory_space=pltpu.VMEM)
    smem = pl.BlockSpec(memory_space=pltpu.SMEM)
    more = sums is None
    operands = [own_rows, other_rows, *blocks] + ([] if more else [sums])
    return pl.pallas_call(
        functools.partial(project_kernel, ring, pieces, more),
        in_specs=[smem, smem] + [vmem] * len(operands),
        out_specs=vmem,
        out_shape=jax.ShapeDtypeStruct((2 * count, width), jnp.float32 if more else jnp.bfloat16),
        compiler_params=pltpu.CompilerParams(vmem_limit_bytes=16 * MIB),
        cost_estimate=pl.CostEstimate(
            flops=count * D * width, bytes_accessed=32 * D * width, transcendentals=0
        ),
        name="project",
    )(core.reshape(1), place, *operands)


def local(
    extent,
    passage_states,
    memory_queries,
    memory_gain,
    kv_weight,
    retrieval,
    question_queries,
    question_kv,
    question_lengths,
):
    me = lax.axis_index("pass")
    core, chip = me & 1, lax.div(me, 2)
    chips = extent // 2
    depth = kv_weight.shape[0]

    if chips != 8 or depth % LANES:
        memory_rows = pool(passage_states, memory_queries, memory_gain)
        whole_weight = lax.all_gather(kv_weight, "pass", axis=0, tiled=True)
        memory_kv = jnp.dot(memory_rows, whole_weight, preferred_element_type=jnp.float32)
        everything = lax.all_gather(memory_kv.astype(jnp.bfloat16), "pass", axis=0, tiled=True)
        halves = everything.reshape(-1, 2, 2, LANES).transpose(2, 0, 1, 3).reshape(2, -1, 2 * LANES)
        rest = (retrieval * MEM, question_lengths, question_queries)
        context = attend(jnp.int32(0), *rest, halves[0], question_kv)
        return attend(jnp.int32(1), *rest, halves[1], question_kv, context)

    place = place_of(chip, chips).reshape(1)
    order = [2 * line for line in range(chips // 2)] + [2 * line + 1 for line in range(chips // 2)][::-1]

    def to_partner(x):
        return lax.ppermute(x, "pass", [(i, i ^ 1) for i in range(extent)])

    def along(x, target):
        pairs = [(c, target(c // 2, c % 2)) for c in range(chips)]
        return lax.ppermute(x, "pass", [(2 * s + c, 2 * d + c) for s, d in pairs for c in range(2)])

    def along_ring(x, step):
        return along(x, lambda line, lane: order[(order.index(2 * line + lane) + step) % chips])

    def line_by_line(block):
        lines = chips // 2

        def lane_of(x):
            return along(x, lambda line, lane: 2 * line + 1 - lane)

        near = {k: along(block, lambda line, lane: 2 * ((line + k) % lines) + lane) for k in (2, 1, 3)}
        far = {0: lane_of(block)}
        far[3] = along(block, lambda line, lane: 2 * ((line + 3) % lines) + 1 - lane)
        far[1], far[2] = lane_of(near[1]), lane_of(near[2])
        return [block, near[1], near[2], near[3], far[0], far[1], far[2], far[3]]

    mine, theirs = split(core, kv_weight)
    up = [[mine], [to_partner(theirs)]]
    down = [[x[0]] for x in up]

    def blocks(turns):
        found = {}
        for part in range(2):
            for turn in turns:
                if turn < len(up[part]):
                    found[part, turn] = up[part][turn]
                if 0 < turn < len(down[part]):
                    found[part, chips - turn] = down[part][turn]
        return found

    for turn in range(1, chips // 2):
        for part in range(2):
            up[part].append(along_ring(up[part][-1], 1))
            down[part].append(along_ring(down[part][-1], -1))
        if turn == 1:
            rows = pool(passage_states, memory_queries, memory_gain)
            *hops, rows = lax.optimization_barrier((*(x[-1] for x in up + down), rows))
            for chain, hop in zip(up + down, hops):
                chain[-1] = hop
            other_rows = to_partner(rows)
    up[0].append(along_ring(up[0][-1], 1))
    down[1].append(along_ring(down[1][-1], -1))
    early = project(chips, core, place, rows, other_rows, blocks((0, 1, 2)))
    memory_kv = project(chips, core, place, rows, other_rows, blocks((3, 4)), early)
    near = jnp.concatenate(line_by_line(memory_kv), axis=0)
    far = to_partner(near)

    lines = chips // 2
    of_chip = lax.div(retrieval, CHIP)
    back = lax.rem(lines + lax.div(chip, 2) - lax.div(of_chip, 2), lines)
    slot = back + lines * lax.rem(lax.rem(chip, 2) + lax.rem(of_chip, 2), 2)
    starts = (slot * CHIP + lax.rem(retrieval, CHIP)) * MEM
    rest = (starts, question_lengths, question_queries)
    context, begun = attend(core, *rest, near, question_kv, ahead=True)
    return attend(1 - core, *rest, far, question_kv, context, begun)


def solution(mesh):
    placed = (
        P(("groups", "pass"), None, None),
        P(),
        P(),
        P("pass", None),
        P(("groups", "pass"), None),
        P(("groups", "pass"), None, None),
        P(("groups", "pass"), None, None),
        P(("groups", "pass")),
    )
    return jax.shard_map(
        functools.partial(local, mesh.shape["pass"]),
        mesh=mesh,
        in_specs=placed,
        out_specs=P(("groups", "pass"), None, None),
        check_vma=False,
    )
```

```python
import functools
import math

import jax
import jax.numpy as jnp
from jax import lax
from jax.experimental import pallas as pl
from jax.experimental.pallas import tpu as pltpu
from jax.sharding import PartitionSpec as P

D = 4096
CH = 32
CHD = 128
MEM = 32
LEN = 128
QLEN = 64
TOPK = 16
H = 116
HD = 64
KVH = 4
GROUP = 29
KVW = 512

LANES = 2 * HD
PAIRS = GROUP
HALF = PAIRS * LANES
ROWS = TOPK * MEM
KEYS = 2 * (ROWS + QLEN)
NEG = -1e30
SUM_LOW, SUM_HIGH = 2.0 ** -40, 2.0 ** 60
POOL_WIDTH = 1024
FIRST_COST = 8 * 10**9
CHIP = 8
STEP = 5
BLOCK = 16
MIB = 1024 * 1024


def place_of(chip, ring):
    line, lane = lax.div(chip, 2), lax.rem(chip, 2)
    return line + lane * (ring - 1 - 2 * line)


def chip_at(place, ring):
    lane = lax.div(place, ring // 2)
    line = place + lane * (ring - 1 - 2 * place)
    return 2 * line + lane


def split_kernel(core_ref, weight_ref, mine_ref, theirs_ref):
    for out_ref, half in ((mine_ref, core_ref[0]), (theirs_ref, 1 - core_ref[0])):
        for n in range(2):
            at = pl.multiple_of(half * LANES + n * KVH * HD, LANES)
            out_ref[:, n * LANES:(n + 1) * LANES] = weight_ref[:, pl.ds(at, LANES)]


def split(core, weight):
    vmem = pl.BlockSpec(memory_space=pltpu.VMEM)
    return pl.pallas_call(
        split_kernel,
        in_specs=[pl.BlockSpec(memory_space=pltpu.SMEM), vmem],
        out_specs=[vmem, vmem],
        out_shape=[jax.ShapeDtypeStruct((weight.shape[0], 2 * LANES), weight.dtype)] * 2,
        compiler_params=pltpu.CompilerParams(vmem_limit_bytes=8 * MIB),
        cost_estimate=pl.CostEstimate(flops=FIRST_COST, bytes_accessed=4 * weight.size, transcendentals=0),
        name="split",
    )(core.reshape(1), weight)


def pool_kernel(states, queries, gain, out_ref, pooled):
    passages = states.shape[0]
    two = 2 * CHD
    zero = jnp.zeros((MEM, CHD), jnp.bfloat16)
    blank = jnp.zeros((2 * MEM, LEN), jnp.bfloat16)
    totals = [jnp.zeros((MEM, CHD), jnp.float32)] * passages
    for base in range(0, D, POOL_WIDTH):
        blocks = []
        for column in range(base, base + POOL_WIDTH, two):
            lhs = jnp.concatenate(
                [
                    jnp.concatenate([queries[:, column:column + CHD], zero], axis=1),
                    jnp.concatenate([zero, queries[:, column + CHD:column + two]], axis=1),
                ],
                axis=0,
            )
            for p in range(0, passages, 2):
                tokens = states[p:p + 2, :, column:column + two].reshape(2 * LEN, two)
                scores = lax.dot_general(
                    lhs, tokens, (((1,), (1,)), ((), ())), preferred_element_type=jnp.float32
                ) * (1.0 / math.sqrt(CHD))
                blocks.append((column, p, tokens, scores))
        for column, p, tokens, scores in blocks:
            rows = []
            for n in range(2):
                part = scores[:, n * LEN:(n + 1) * LEN]
                part = jnp.exp(part - jnp.max(part, axis=1, keepdims=True))
                part = (part / jnp.sum(part, axis=1, keepdims=True)).astype(jnp.bfloat16)
                rows.append(jnp.concatenate([blank, part] if n else [part, blank], axis=1))
            mixed = jnp.dot(jnp.concatenate(rows, axis=0), tokens, preferred_element_type=jnp.float32)
            for n in range(2):
                for head in range(2):
                    top = (2 * n + head) * MEM
                    block = mixed[top:top + MEM, head * CHD:(head + 1) * CHD]
                    place = slice(column + head * CHD, column + (head + 1) * CHD)
                    pooled[(p + n) * MEM:(p + n + 1) * MEM, place] = block
                    totals[p + n] = totals[p + n] + block * block
    mean_square = jnp.sum(jnp.concatenate(totals, axis=0), axis=1, keepdims=True) * (1.0 / D)
    scale = lax.rsqrt(mean_square + 1e-06)
    factor = gain[...].astype(jnp.float32).reshape(1, D)
    out_ref[...] = (pooled[...] * scale * factor).astype(jnp.bfloat16)


def pool(states, queries, gain):
    count = states.shape[0]
    vmem = pl.BlockSpec(memory_space=pltpu.VMEM)
    return pl.pallas_call(
        pool_kernel,
        in_specs=[vmem] * 3,
        out_specs=vmem,
        out_shape=jax.ShapeDtypeStruct((count * MEM, D), jnp.bfloat16),
        scratch_shapes=[pltpu.VMEM((count * MEM, D), jnp.float32)],
        compiler_params=pltpu.CompilerParams(vmem_limit_bytes=12 * MIB),
        cost_estimate=pl.CostEstimate(
            flops=4 * count * MEM * LEN * D, bytes_accessed=2 * count * LEN * D,
            transcendentals=count * CH * MEM * LEN,
        ),
        name="pool",
    )(states, queries, gain)


def attend_kernel(begun, ahead, half_ref, start_ref, length_ref, q_hbm, kv_ref, own_kv_ref, *rest):
    if ahead:
        other_at = pl.multiple_of((1 - half_ref[0]) * HALF, LANES)
        coming = pltpu.make_async_copy(q_hbm.at[0, :, pl.ds(other_at, HALF)], rest[-14], rest[-1])
        coming.start()
        out_hbm, rest = rest[-15], rest[:-1]
    else:
        out_hbm = rest[-13]
    (
        questions, answers, memory, key_side, value_side, weights, bias, marker, scores, all_weights,
        arrived, sent,
    ) = rest[-12:]
    count = q_hbm.shape[0]
    half_at = pl.multiple_of(half_ref[0] * HALF, LANES)
    own_at = pl.multiple_of(half_ref[0] * LANES, LANES)
    factor = math.log2(math.e) / math.sqrt(HD)

    def fetch(query):
        return pltpu.make_async_copy(
            q_hbm.at[query, :, pl.ds(half_at, HALF)], questions.at[query], arrived.at[query]
        )

    def send(query):
        return pltpu.make_async_copy(
            answers.at[query], out_hbm.at[query, :, pl.ds(half_at, HALF)], sent.at[query]
        )

    if begun:
        questions[0] = rest[0][...]
    else:
        fetch(0).start()
    lane = lax.broadcasted_iota(jnp.int32, (KEYS, LANES), 1)
    row = lax.broadcasted_iota(jnp.int32, (KEYS, LANES), 0)
    in_b = ((row >= ROWS) & (row < 2 * ROWS)) | (row >= 2 * ROWS + QLEN)
    ones = jnp.where((lane >= HD) == in_b, 1.0, 0.0).astype(jnp.bfloat16)
    key_side[...] = jnp.zeros_like(key_side)
    for g in range(2):
        value_side[g, :, LANES:] = ones

    half = PAIRS // 2
    chunks = []
    for g in range(2):
        tiles = list(range(half + 1)) if g == 0 else list(range(half, PAIRS))
        chunks += [(g, tiles[at:at + STEP]) for at in range(0, len(tiles), STEP)]

    def answer(query, carry):
        for slot in range(TOPK):
            start = pl.multiple_of(start_ref[query, slot], MEM)
            memory[slot * MEM:(slot + 1) * MEM, :] = kv_ref[pl.ds(start, MEM), :]
        length = length_ref[query]

        turned = jnp.transpose(memory[:, :LANES])
        own_k = own_kv_ref[query, :, pl.ds(own_at, LANES)]
        own_turned = jnp.transpose(jnp.concatenate([own_k, own_k], axis=0))
        column = lax.broadcasted_iota(jnp.int32, (HD, LANES), 1)
        for g in range(2):
            for member in range(2):
                rows = slice(member * HD, (member + 1) * HD)
                key_side[g, rows, member * ROWS:(member + 1) * ROWS] = turned[g * HD:(g + 1) * HD]
                own = own_turned[g * HD:(g + 1) * HD]
                mine = (column >= HD) if member else (column < HD)
                key_side[g, rows, 2 * ROWS:] = jnp.where(mine, own, jnp.zeros_like(own))

        token = lax.broadcasted_iota(jnp.int32, (QLEN, LANES), 0)
        low = lax.broadcasted_iota(jnp.int32, (QLEN, LANES), 1) < HD
        key = lax.rem(lax.broadcasted_iota(jnp.int32, (QLEN, LANES), 1), HD)
        bias[...] = jnp.where((key <= token) & (key < length), 0.0, NEG)
        alive = token < length
        sample = lax.div(key, HD // STEP)

        own_v_at = pl.multiple_of(own_at + KVH * HD, LANES)
        own_v = own_kv_ref[query, :, pl.ds(own_v_at, LANES)]
        for block, at in ((memory[:, LANES:], 0), (own_v, 2 * ROWS)):
            size = block.shape[0]
            swapped = jnp.concatenate([block[:, HD:], block[:, :HD]], axis=1)
            lower = lax.broadcasted_iota(jnp.int32, block.shape, 1) < HD
            zero = jnp.zeros_like(block)
            for g in range(2):
                one, two = (block, swapped) if g == 0 else (swapped, block)
                value_side[g, at:at + size, :LANES] = jnp.where(lower, one, zero)
                value_side[g, at + size:at + 2 * size, :LANES] = jnp.where(lower, zero, two)

        if begun:

            @pl.when(query > 0)
            def _():
                fetch(query).wait()
        else:
            fetch(query).wait()

        @pl.when(query + 1 < count)
        def _():
            fetch(query + 1).start()

        def stacked(tiles):
            return jnp.concatenate([questions[query, :, t * LANES:(t + 1) * LANES] for t in tiles], axis=0)

        def key_product(i):
            g, tiles = chunks[i]
            lhs = stacked(tiles)
            for c in range(0, KEYS, ROWS):
                part = slice(c, min(c + ROWS, KEYS))
                got = jnp.dot(lhs, key_side[g, :, part], preferred_element_type=jnp.float32) * factor
                if c == 2 * ROWS:
                    got = got + jnp.concatenate([bias[...]] * len(tiles), axis=0)
                weights[i % 2, :len(tiles) * QLEN, part] = jnp.exp2(got).astype(jnp.bfloat16)

        def finish(i, mixed):
            g, tiles = chunks[i]
            for n, t in enumerate(tiles):
                rows = slice(n * QLEN, (n + 1) * QLEN)
                sums = mixed[rows, LANES:]
                inverse = pl.reciprocal(sums, approx=True)
                inverse = inverse * (2.0 - sums * inverse)
                result = jnp.where(alive, mixed[rows, :LANES] * inverse, 0.0).astype(jnp.bfloat16)
                at = slice(t * LANES, (t + 1) * LANES)
                if t == half and g == 1:
                    result = jnp.where(low, answers[query, :, at], result)
                answers[query, :, at] = result

        def value_product(i, seen):
            g, tiles = chunks[i]
            size = len(tiles) * QLEN
            mixed = jnp.dot(weights[i % 2, :size, :], value_side[g], preferred_element_type=jnp.float32)
            sums = mixed[:QLEN, LANES:]
            for n in range(1, len(tiles)):
                sums = jnp.where(sample == n, mixed[n * QLEN:(n + 1) * QLEN, LANES:], sums)
            seen = jnp.where((sums > SUM_LOW) & (sums < SUM_HIGH), seen, 1.0)
            finish(i, mixed)
            return seen

        key_product(0)
        seen = jnp.zeros((QLEN, LANES), jnp.float32)
        for i in range(len(chunks)):
            if i + 1 < len(chunks):
                key_product(i + 1)
            seen = value_product(i, seen)
        marker[0] = jnp.max(seen)

        @pl.when(marker[0] > 0.0)
        def _():
            for i, (g, tiles) in enumerate(chunks):
                size = len(tiles) * QLEN
                scores[:size, :] = jnp.dot(stacked(tiles), key_side[g], preferred_element_type=jnp.float32)

                def soften(n, carry):
                    rows = pl.ds(pl.multiple_of(n * QLEN, QLEN), QLEN)
                    own_scores = scores[rows, 2 * ROWS:] + bias[...]
                    tops = []
                    for member in range(2):
                        columns = slice(member * ROWS, (member + 1) * ROWS)
                        top = jnp.where(low, own_scores, NEG) if member == 0 else jnp.where(low, NEG, own_scores)
                        top = jnp.maximum(
                            jnp.max(top, axis=1, keepdims=True),
                            jnp.max(scores[rows, columns], axis=1, keepdims=True),
                        )
                        all_weights[rows, columns] = jnp.exp2(
                            (scores[rows, columns] - top) * factor
                        ).astype(jnp.bfloat16)
                        tops.append(top)
                    all_weights[rows, 2 * ROWS:] = jnp.exp2(
                        (own_scores - jnp.where(low, tops[0], tops[1])) * factor
                    ).astype(jnp.bfloat16)
                    return carry

                lax.fori_loop(0, len(tiles), soften, 0)
                finish(
                    i, jnp.dot(all_weights[:size, :], value_side[g], preferred_element_type=jnp.float32)
                )

        send(query).start()
        return carry

    lax.fori_loop(0, count, answer, 0)
    for query in range(count):
        send(query).wait()
    if ahead:
        coming.wait()


def attend(half, starts, lengths, questions, memory_kv, own_kv, earlier=None, begun=None, ahead=False):
    count = questions.shape[0]
    hbm, vmem, smem = (pl.BlockSpec(memory_space=x) for x in (pltpu.HBM, pltpu.VMEM, pltpu.SMEM))
    operands = [half.reshape(1), starts, lengths, questions, memory_kv, own_kv]
    in_specs = [smem, smem, smem, hbm, vmem, vmem]
    aliases = {}
    if begun is not None:
        operands.append(begun)
        in_specs.append(vmem)
    if earlier is not None:
        aliases = {len(operands): 0}
        operands.append(earlier)
        in_specs.append(hbm)
    out_specs, extra = [hbm], []
    out_shape = [jax.ShapeDtypeStruct((count, QLEN, H * HD), jnp.bfloat16)]
    if ahead:
        out_specs.append(vmem)
        out_shape.append(jax.ShapeDtypeStruct((QLEN, HALF), jnp.bfloat16))
        extra = [pltpu.SemaphoreType.DMA]
    got = pl.pallas_call(
        functools.partial(attend_kernel, begun is not None, ahead),
        in_specs=in_specs,
        out_specs=out_specs,
        out_shape=out_shape,
        scratch_shapes=[
            pltpu.VMEM((count, QLEN, HALF), jnp.bfloat16),
            pltpu.VMEM((count, QLEN, HALF), jnp.bfloat16),
            pltpu.VMEM((ROWS, 2 * LANES), jnp.bfloat16),
            pltpu.VMEM((2, LANES, KEYS), jnp.bfloat16),
            pltpu.VMEM((2, KEYS, 2 * LANES), jnp.bfloat16),
            pltpu.VMEM((2, STEP * QLEN, KEYS), jnp.bfloat16),
            pltpu.VMEM((QLEN, LANES), jnp.float32),
            pltpu.SMEM((1,), jnp.float32),
            pltpu.VMEM((STEP * QLEN, KEYS), jnp.float32),
            pltpu.VMEM((STEP * QLEN, KEYS), jnp.bfloat16),
            pltpu.SemaphoreType.DMA((count,)),
            pltpu.SemaphoreType.DMA((count,)),
            *extra,
        ],
        input_output_aliases=aliases,
        compiler_params=pltpu.CompilerParams(vmem_limit_bytes=50 * MIB),
        cost_estimate=pl.CostEstimate(
            flops=2 * count * QLEN * H * HD * (ROWS + QLEN),
            bytes_accessed=2 * count * QLEN * H * HD,
            transcendentals=count * QLEN * H * (ROWS + QLEN) // 2,
        ),
        name="attend",
    )(*operands)
    return got if ahead else got[0]


def project_kernel(ring, pieces, more, core_ref, place_ref, own_ref, other_ref, *rest):
    weights, rest = rest[:len(pieces)], rest[len(pieces):]
    out_ref = rest[-1]
    count = own_ref.shape[0]
    depth = weights[0].shape[0]
    core = core_ref[0]
    total = jnp.zeros((2 * count, weights[0].shape[1]), jnp.float32) if more else rest[0][...]
    for (part, i), weight in zip(pieces, weights):
        chip = chip_at(lax.rem(ring + place_ref[0] - i, ring), ring)
        at = pl.multiple_of((2 * chip + (1 - core if part else core)) * depth, depth)
        rows = jnp.concatenate([own_ref[:, pl.ds(at, depth)], other_ref[:, pl.ds(at, depth)]], axis=0)
        total += jnp.dot(rows, weight[...], preferred_element_type=jnp.float32)
    if more:
        out_ref[...] = total
        return
    result = total.astype(jnp.bfloat16)
    out_ref[pl.ds(pl.multiple_of(core * count, count), count)] = result[:count]
    out_ref[pl.ds(pl.multiple_of((1 - core) * count, count), count)] = result[count:]


def project(ring, core, place, own_rows, other_rows, weights, sums=None):
    count = own_rows.shape[0]
    pieces, blocks = tuple(weights), list(weights.values())
    width = blocks[0].shape[1]
    vmem = pl.BlockSpec(memory_space=pltpu.VMEM)
    smem = pl.BlockSpec(memory_space=pltpu.SMEM)
    more = sums is None
    operands = [own_rows, other_rows, *blocks] + ([] if more else [sums])
    return pl.pallas_call(
        functools.partial(project_kernel, ring, pieces, more),
        in_specs=[smem, smem] + [vmem] * len(operands),
        out_specs=vmem,
        out_shape=jax.ShapeDtypeStruct((2 * count, width), jnp.float32 if more else jnp.bfloat16),
        compiler_params=pltpu.CompilerParams(vmem_limit_bytes=6 * MIB),
        cost_estimate=pl.CostEstimate(
            flops=count * D * width, bytes_accessed=32 * D * width, transcendentals=0
        ),
        name="project",
    )(core.reshape(1), place, *operands)


def local(
    extent,
    passage_states,
    memory_queries,
    memory_gain,
    kv_weight,
    retrieval,
    question_queries,
    question_kv,
    question_lengths,
):
    me = lax.axis_index("pass")
    core, chip = me & 1, lax.div(me, 2)
    chips = extent // 2
    depth = kv_weight.shape[0]

    if chips != 8 or depth % LANES:
        memory_rows = pool(passage_states, memory_queries, memory_gain)
        whole_weight = lax.all_gather(kv_weight, "pass", axis=0, tiled=True)
        memory_kv = jnp.dot(memory_rows, whole_weight, preferred_element_type=jnp.float32)
        everything = lax.all_gather(memory_kv.astype(jnp.bfloat16), "pass", axis=0, tiled=True)
        halves = everything.reshape(-1, 2, 2, LANES).transpose(2, 0, 1, 3).reshape(2, -1, 2 * LANES)
        rest = (retrieval * MEM, question_lengths, question_queries)
        context = attend(jnp.int32(0), *rest, halves[0], question_kv)
        return attend(jnp.int32(1), *rest, halves[1], question_kv, context)

    place = place_of(chip, chips).reshape(1)
    order = [2 * line for line in range(chips // 2)] + [2 * line + 1 for line in range(chips // 2)][::-1]

    def to_partner(x):
        return lax.ppermute(x, "pass", [(i, i ^ 1) for i in range(extent)])

    def along(x, target):
        pairs = [(c, target(c // 2, c % 2)) for c in range(chips)]
        return lax.ppermute(x, "pass", [(2 * s + c, 2 * d + c) for s, d in pairs for c in range(2)])

    def along_ring(x, step):
        return along(x, lambda line, lane: order[(order.index(2 * line + lane) + step) % chips])

    def line_by_line(block):
        lines = chips // 2

        def lane_of(x):
            return along(x, lambda line, lane: 2 * line + 1 - lane)

        near = {k: along(block, lambda line, lane: 2 * ((line + k) % lines) + lane) for k in (2, 1, 3)}
        far = {0: lane_of(block)}
        far[3] = along(block, lambda line, lane: 2 * ((line + 3) % lines) + 1 - lane)
        far[1], far[2] = lane_of(near[1]), lane_of(near[2])
        return [block, near[1], near[2], near[3], far[0], far[1], far[2], far[3]]

    mine, theirs = split(core, kv_weight)
    up = [[mine], [to_partner(theirs)]]
    down = [[x[0]] for x in up]

    def blocks(turns):
        found = {}
        for part in range(2):
            for turn in turns:
                if turn < len(up[part]):
                    found[part, turn] = up[part][turn]
                if 0 < turn < len(down[part]):
                    found[part, chips - turn] = down[part][turn]
        return found

    for turn in range(1, chips // 2):
        for part in range(2):
            up[part].append(along_ring(up[part][-1], 1))
            down[part].append(along_ring(down[part][-1], -1))
        if turn == 1:
            rows = pool(passage_states, memory_queries, memory_gain)
            *hops, rows = lax.optimization_barrier((*(x[-1] for x in up + down), rows))
            for chain, hop in zip(up + down, hops):
                chain[-1] = hop
            other_rows = to_partner(rows)
    up[0].append(along_ring(up[0][-1], 1))
    down[1].append(along_ring(down[1][-1], -1))
    early = project(chips, core, place, rows, other_rows, blocks((0, 1, 2)))
    memory_kv = project(chips, core, place, rows, other_rows, blocks((3, 4)), early)
    near = jnp.concatenate(line_by_line(memory_kv), axis=0)
    far = to_partner(near)

    lines = chips // 2
    of_chip = lax.div(retrieval, CHIP)
    back = lax.rem(lines + lax.div(chip, 2) - lax.div(of_chip, 2), lines)
    slot = back + lines * lax.rem(lax.rem(chip, 2) + lax.rem(of_chip, 2), 2)
    starts = (slot * CHIP + lax.rem(retrieval, CHIP)) * MEM
    rest = (starts, question_lengths, question_queries)
    context, begun = attend(core, *rest, near, question_kv, ahead=True)
    return attend(1 - core, *rest, far, question_kv, context, begun)


def solution(mesh):
    placed = (
        P(("groups", "pass"), None, None),
        P(),
        P(),
        P("pass", None),
        P(("groups", "pass"), None),
        P(("groups", "pass"), None, None),
        P(("groups", "pass"), None, None),
        P(("groups", "pass")),
    )
    return jax.shard_map(
        functools.partial(local, mesh.shape["pass"]),
        mesh=mesh,
        in_specs=placed,
        out_specs=P(("groups", "pass"), None, None),
        check_vma=False,
    )
```

```python
import functools
import math

import jax
import jax.numpy as jnp
from jax import lax
from jax.experimental import pallas as pl
from jax.experimental.pallas import tpu as pltpu
from jax.sharding import PartitionSpec as P

D = 4096
CH = 32
CHD = 128
MEM = 32
LEN = 128
QLEN = 64
TOPK = 16
H = 116
HD = 64
KVH = 4
GROUP = 29
KVW = 512

LANES = 2 * HD
PAIRS = GROUP
HALF = PAIRS * LANES
ROWS = TOPK * MEM
KEYS = 2 * (ROWS + QLEN)
NEG = -1e30
SUM_LOW, SUM_HIGH = 2.0 ** -40, 2.0 ** 60
POOL_WIDTH = 1024
FIRST_COST = 8 * 10**9
CHIP = 8
STEP = 5
BLOCK = 16
MIB = 1024 * 1024


def place_of(chip, ring):
    line, lane = lax.div(chip, 2), lax.rem(chip, 2)
    return line + lane * (ring - 1 - 2 * line)


def chip_at(place, ring):
    lane = lax.div(place, ring // 2)
    line = place + lane * (ring - 1 - 2 * place)
    return 2 * line + lane


def split_kernel(core_ref, weight_ref, mine_ref, theirs_ref):
    for out_ref, half in ((mine_ref, core_ref[0]), (theirs_ref, 1 - core_ref[0])):
        for n in range(2):
            at = pl.multiple_of(half * LANES + n * KVH * HD, LANES)
            out_ref[:, n * LANES:(n + 1) * LANES] = weight_ref[:, pl.ds(at, LANES)]


def split(core, weight):
    vmem = pl.BlockSpec(memory_space=pltpu.VMEM)
    return pl.pallas_call(
        split_kernel,
        in_specs=[pl.BlockSpec(memory_space=pltpu.SMEM), vmem],
        out_specs=[vmem, vmem],
        out_shape=[jax.ShapeDtypeStruct((weight.shape[0], 2 * LANES), weight.dtype)] * 2,
        compiler_params=pltpu.CompilerParams(vmem_limit_bytes=8 * MIB),
        cost_estimate=pl.CostEstimate(flops=FIRST_COST, bytes_accessed=4 * weight.size, transcendentals=0),
        name="split",
    )(core.reshape(1), weight)


def pool_kernel(states, queries, gain, out_ref, pooled):
    passages = states.shape[0]
    two = 2 * CHD
    zero = jnp.zeros((MEM, CHD), jnp.bfloat16)
    blank = jnp.zeros((2 * MEM, LEN), jnp.bfloat16)
    totals = [jnp.zeros((MEM, CHD), jnp.float32)] * passages
    for base in range(0, D, POOL_WIDTH):
        blocks = []
        for column in range(base, base + POOL_WIDTH, two):
            lhs = jnp.concatenate(
                [
                    jnp.concatenate([queries[:, column:column + CHD], zero], axis=1),
                    jnp.concatenate([zero, queries[:, column + CHD:column + two]], axis=1),
                ],
                axis=0,
            )
            for p in range(0, passages, 2):
                tokens = states[p:p + 2, :, column:column + two].reshape(2 * LEN, two)
                scores = lax.dot_general(
                    lhs, tokens, (((1,), (1,)), ((), ())), preferred_element_type=jnp.float32
                ) * (1.0 / math.sqrt(CHD))
                blocks.append((column, p, tokens, scores))
        for column, p, tokens, scores in blocks:
            rows = []
            for n in range(2):
                part = scores[:, n * LEN:(n + 1) * LEN]
                part = jnp.exp(part - jnp.max(part, axis=1, keepdims=True))
                part = (part / jnp.sum(part, axis=1, keepdims=True)).astype(jnp.bfloat16)
                rows.append(jnp.concatenate([blank, part] if n else [part, blank], axis=1))
            mixed = jnp.dot(jnp.concatenate(rows, axis=0), tokens, preferred_element_type=jnp.float32)
            for n in range(2):
                for head in range(2):
                    top = (2 * n + head) * MEM
                    block = mixed[top:top + MEM, head * CHD:(head + 1) * CHD]
                    place = slice(column + head * CHD, column + (head + 1) * CHD)
                    pooled[(p + n) * MEM:(p + n + 1) * MEM, place] = block
                    totals[p + n] = totals[p + n] + block * block
    mean_square = jnp.sum(jnp.concatenate(totals, axis=0), axis=1, keepdims=True) * (1.0 / D)
    scale = lax.rsqrt(mean_square + 1e-06)
    factor = gain[...].astype(jnp.float32).reshape(1, D)
    out_ref[...] = (pooled[...] * scale * factor).astype(jnp.bfloat16)


def pool(states, queries, gain):
    count = states.shape[0]
    vmem = pl.BlockSpec(memory_space=pltpu.VMEM)
    return pl.pallas_call(
        pool_kernel,
        in_specs=[vmem] * 3,
        out_specs=vmem,
        out_shape=jax.ShapeDtypeStruct((count * MEM, D), jnp.bfloat16),
        scratch_shapes=[pltpu.VMEM((count * MEM, D), jnp.float32)],
        compiler_params=pltpu.CompilerParams(vmem_limit_bytes=20 * MIB),
        cost_estimate=pl.CostEstimate(
            flops=4 * count * MEM * LEN * D, bytes_accessed=2 * count * LEN * D,
            transcendentals=count * CH * MEM * LEN,
        ),
        name="pool",
    )(states, queries, gain)


def attend_kernel(begun, ahead, half_ref, start_ref, length_ref, q_hbm, kv_ref, own_kv_ref, *rest):
    if ahead:
        other_at = pl.multiple_of((1 - half_ref[0]) * HALF, LANES)
        coming = pltpu.make_async_copy(q_hbm.at[0, :, pl.ds(other_at, HALF)], rest[-14], rest[-1])
        coming.start()
        out_hbm, rest = rest[-15], rest[:-1]
    else:
        out_hbm = rest[-13]
    (
        questions, answers, memory, key_side, value_side, weights, bias, marker, scores, all_weights,
        arrived, sent,
    ) = rest[-12:]
    count = q_hbm.shape[0]
    half_at = pl.multiple_of(half_ref[0] * HALF, LANES)
    own_at = pl.multiple_of(half_ref[0] * LANES, LANES)
    factor = math.log2(math.e) / math.sqrt(HD)

    def fetch(query):
        return pltpu.make_async_copy(
            q_hbm.at[query, :, pl.ds(half_at, HALF)], questions.at[query], arrived.at[query]
        )

    def send(query):
        return pltpu.make_async_copy(
            answers.at[query], out_hbm.at[query, :, pl.ds(half_at, HALF)], sent.at[query]
        )

    if begun:
        questions[0] = rest[0][...]
    else:
        fetch(0).start()
    lane = lax.broadcasted_iota(jnp.int32, (KEYS, LANES), 1)
    row = lax.broadcasted_iota(jnp.int32, (KEYS, LANES), 0)
    in_b = ((row >= ROWS) & (row < 2 * ROWS)) | (row >= 2 * ROWS + QLEN)
    ones = jnp.where((lane >= HD) == in_b, 1.0, 0.0).astype(jnp.bfloat16)
    key_side[...] = jnp.zeros_like(key_side)
    for g in range(2):
        value_side[g, :, LANES:] = ones

    half = PAIRS // 2
    chunks = []
    for g in range(2):
        tiles = list(range(half + 1)) if g == 0 else list(range(half, PAIRS))
        chunks += [(g, tiles[at:at + STEP]) for at in range(0, len(tiles), STEP)]

    def answer(query, carry):
        for slot in range(TOPK):
            start = pl.multiple_of(start_ref[query, slot], MEM)
            memory[slot * MEM:(slot + 1) * MEM, :] = kv_ref[pl.ds(start, MEM), :]
        length = length_ref[query]

        turned = jnp.transpose(memory[:, :LANES])
        own_k = own_kv_ref[query, :, pl.ds(own_at, LANES)]
        own_turned = jnp.transpose(jnp.concatenate([own_k, own_k], axis=0))
        column = lax.broadcasted_iota(jnp.int32, (HD, LANES), 1)
        for g in range(2):
            for member in range(2):
                rows = slice(member * HD, (member + 1) * HD)
                key_side[g, rows, member * ROWS:(member + 1) * ROWS] = turned[g * HD:(g + 1) * HD]
                own = own_turned[g * HD:(g + 1) * HD]
                mine = (column >= HD) if member else (column < HD)
                key_side[g, rows, 2 * ROWS:] = jnp.where(mine, own, jnp.zeros_like(own))

        token = lax.broadcasted_iota(jnp.int32, (QLEN, LANES), 0)
        low = lax.broadcasted_iota(jnp.int32, (QLEN, LANES), 1) < HD
        key = lax.rem(lax.broadcasted_iota(jnp.int32, (QLEN, LANES), 1), HD)
        bias[...] = jnp.where((key <= token) & (key < length), 0.0, NEG)
        alive = token < length
        sample = lax.div(key, HD // STEP)

        own_v_at = pl.multiple_of(own_at + KVH * HD, LANES)
        own_v = own_kv_ref[query, :, pl.ds(own_v_at, LANES)]
        for block, at in ((memory[:, LANES:], 0), (own_v, 2 * ROWS)):
            size = block.shape[0]
            swapped = jnp.concatenate([block[:, HD:], block[:, :HD]], axis=1)
            lower = lax.broadcasted_iota(jnp.int32, block.shape, 1) < HD
            zero = jnp.zeros_like(block)
            for g in range(2):
                one, two = (block, swapped) if g == 0 else (swapped, block)
                value_side[g, at:at + size, :LANES] = jnp.where(lower, one, zero)
                value_side[g, at + size:at + 2 * size, :LANES] = jnp.where(lower, zero, two)

        if begun:

            @pl.when(query > 0)
            def _():
                fetch(query).wait()
        else:
            fetch(query).wait()

        @pl.when(query + 1 < count)
        def _():
            fetch(query + 1).start()

        def stacked(tiles):
            return jnp.concatenate([questions[query, :, t * LANES:(t + 1) * LANES] for t in tiles], axis=0)

        def key_product(i):
            g, tiles = chunks[i]
            lhs = stacked(tiles)
            for c in range(0, KEYS, ROWS):
                part = slice(c, min(c + ROWS, KEYS))
                got = jnp.dot(lhs, key_side[g, :, part], preferred_element_type=jnp.float32) * factor
                if c == 2 * ROWS:
                    got = got + jnp.concatenate([bias[...]] * len(tiles), axis=0)
                weights[i % 2, :len(tiles) * QLEN, part] = jnp.exp2(got).astype(jnp.bfloat16)

        def finish(i, mixed):
            g, tiles = chunks[i]
            for n, t in enumerate(tiles):
                rows = slice(n * QLEN, (n + 1) * QLEN)
                sums = mixed[rows, LANES:]
                inverse = pl.reciprocal(sums, approx=True)
                inverse = inverse * (2.0 - sums * inverse)
                result = jnp.where(alive, mixed[rows, :LANES] * inverse, 0.0).astype(jnp.bfloat16)
                at = slice(t * LANES, (t + 1) * LANES)
                if t == half and g == 1:
                    result = jnp.where(low, answers[query, :, at], result)
                answers[query, :, at] = result

        def value_product(i, seen):
            g, tiles = chunks[i]
            size = len(tiles) * QLEN
            mixed = jnp.dot(weights[i % 2, :size, :], value_side[g], preferred_element_type=jnp.float32)
            sums = mixed[:QLEN, LANES:]
            for n in range(1, len(tiles)):
                sums = jnp.where(sample == n, mixed[n * QLEN:(n + 1) * QLEN, LANES:], sums)
            seen = jnp.where((sums > SUM_LOW) & (sums < SUM_HIGH), seen, 1.0)
            finish(i, mixed)
            return seen

        key_product(0)
        seen = jnp.zeros((QLEN, LANES), jnp.float32)
        for i in range(len(chunks)):
            if i + 1 < len(chunks):
                key_product(i + 1)
            seen = value_product(i, seen)
        marker[0] = jnp.max(seen)

        @pl.when(marker[0] > 0.0)
        def _():
            for i, (g, tiles) in enumerate(chunks):
                size = len(tiles) * QLEN
                scores[:size, :] = jnp.dot(stacked(tiles), key_side[g], preferred_element_type=jnp.float32)

                def soften(n, carry):
                    rows = pl.ds(pl.multiple_of(n * QLEN, QLEN), QLEN)
                    own_scores = scores[rows, 2 * ROWS:] + bias[...]
                    tops = []
                    for member in range(2):
                        columns = slice(member * ROWS, (member + 1) * ROWS)
                        top = jnp.where(low, own_scores, NEG) if member == 0 else jnp.where(low, NEG, own_scores)
                        top = jnp.maximum(
                            jnp.max(top, axis=1, keepdims=True),
                            jnp.max(scores[rows, columns], axis=1, keepdims=True),
                        )
                        all_weights[rows, columns] = jnp.exp2(
                            (scores[rows, columns] - top) * factor
                        ).astype(jnp.bfloat16)
                        tops.append(top)
                    all_weights[rows, 2 * ROWS:] = jnp.exp2(
                        (own_scores - jnp.where(low, tops[0], tops[1])) * factor
                    ).astype(jnp.bfloat16)
                    return carry

                lax.fori_loop(0, len(tiles), soften, 0)
                finish(
                    i, jnp.dot(all_weights[:size, :], value_side[g], preferred_element_type=jnp.float32)
                )

        send(query).start()
        return carry

    lax.fori_loop(0, count, answer, 0)
    for query in range(count):
        send(query).wait()
    if ahead:
        coming.wait()


def attend(half, starts, lengths, questions, memory_kv, own_kv, earlier=None, begun=None, ahead=False):
    count = questions.shape[0]
    hbm, vmem, smem = (pl.BlockSpec(memory_space=x) for x in (pltpu.HBM, pltpu.VMEM, pltpu.SMEM))
    operands = [half.reshape(1), starts, lengths, questions, memory_kv, own_kv]
    in_specs = [smem, smem, smem, hbm, vmem, vmem]
    aliases = {}
    if begun is not None:
        operands.append(begun)
        in_specs.append(vmem)
    if earlier is not None:
        aliases = {len(operands): 0}
        operands.append(earlier)
        in_specs.append(hbm)
    out_specs, extra = [hbm], []
    out_shape = [jax.ShapeDtypeStruct((count, QLEN, H * HD), jnp.bfloat16)]
    if ahead:
        out_specs.append(vmem)
        out_shape.append(jax.ShapeDtypeStruct((QLEN, HALF), jnp.bfloat16))
        extra = [pltpu.SemaphoreType.DMA]
    got = pl.pallas_call(
        functools.partial(attend_kernel, begun is not None, ahead),
        in_specs=in_specs,
        out_specs=out_specs,
        out_shape=out_shape,
        scratch_shapes=[
            pltpu.VMEM((count, QLEN, HALF), jnp.bfloat16),
            pltpu.VMEM((count, QLEN, HALF), jnp.bfloat16),
            pltpu.VMEM((ROWS, 2 * LANES), jnp.bfloat16),
            pltpu.VMEM((2, LANES, KEYS), jnp.bfloat16),
            pltpu.VMEM((2, KEYS, 2 * LANES), jnp.bfloat16),
            pltpu.VMEM((2, STEP * QLEN, KEYS), jnp.bfloat16),
            pltpu.VMEM((QLEN, LANES), jnp.float32),
            pltpu.SMEM((1,), jnp.float32),
            pltpu.VMEM((STEP * QLEN, KEYS), jnp.float32),
            pltpu.VMEM((STEP * QLEN, KEYS), jnp.bfloat16),
            pltpu.SemaphoreType.DMA((count,)),
            pltpu.SemaphoreType.DMA((count,)),
            *extra,
        ],
        input_output_aliases=aliases,
        compiler_params=pltpu.CompilerParams(vmem_limit_bytes=50 * MIB),
        cost_estimate=pl.CostEstimate(
            flops=2 * count * QLEN * H * HD * (ROWS + QLEN),
            bytes_accessed=2 * count * QLEN * H * HD,
            transcendentals=count * QLEN * H * (ROWS + QLEN) // 2,
        ),
        name="attend",
    )(*operands)
    return got if ahead else got[0]


def project_kernel(ring, pieces, more, core_ref, place_ref, own_ref, other_ref, *rest):
    weights, rest = rest[:len(pieces)], rest[len(pieces):]
    out_ref = rest[-1]
    count = own_ref.shape[0]
    depth = weights[0].shape[0]
    core = core_ref[0]
    total = jnp.zeros((2 * count, weights[0].shape[1]), jnp.float32) if more else rest[0][...]
    for (part, i), weight in zip(pieces, weights):
        chip = chip_at(lax.rem(ring + place_ref[0] - i, ring), ring)
        at = pl.multiple_of((2 * chip + (1 - core if part else core)) * depth, depth)
        rows = jnp.concatenate([own_ref[:, pl.ds(at, depth)], other_ref[:, pl.ds(at, depth)]], axis=0)
        total += jnp.dot(rows, weight[...], preferred_element_type=jnp.float32)
    if more:
        out_ref[...] = total
        return
    result = total.astype(jnp.bfloat16)
    out_ref[pl.ds(pl.multiple_of(core * count, count), count)] = result[:count]
    out_ref[pl.ds(pl.multiple_of((1 - core) * count, count), count)] = result[count:]


def project(ring, core, place, own_rows, other_rows, weights, sums=None):
    count = own_rows.shape[0]
    pieces, blocks = tuple(weights), list(weights.values())
    width = blocks[0].shape[1]
    vmem = pl.BlockSpec(memory_space=pltpu.VMEM)
    smem = pl.BlockSpec(memory_space=pltpu.SMEM)
    more = sums is None
    operands = [own_rows, other_rows, *blocks] + ([] if more else [sums])
    return pl.pallas_call(
        functools.partial(project_kernel, ring, pieces, more),
        in_specs=[smem, smem] + [vmem] * len(operands),
        out_specs=vmem,
        out_shape=jax.ShapeDtypeStruct((2 * count, width), jnp.float32 if more else jnp.bfloat16),
        compiler_params=pltpu.CompilerParams(vmem_limit_bytes=16 * MIB),
        cost_estimate=pl.CostEstimate(
            flops=count * D * width, bytes_accessed=32 * D * width, transcendentals=0
        ),
        name="project",
    )(core.reshape(1), place, *operands)


def local(
    extent,
    passage_states,
    memory_queries,
    memory_gain,
    kv_weight,
    retrieval,
    question_queries,
    question_kv,
    question_lengths,
):
    me = lax.axis_index("pass")
    core, chip = me & 1, lax.div(me, 2)
    chips = extent // 2
    depth = kv_weight.shape[0]

    if chips != 8 or depth % LANES:
        memory_rows = pool(passage_states, memory_queries, memory_gain)
        whole_weight = lax.all_gather(kv_weight, "pass", axis=0, tiled=True)
        memory_kv = jnp.dot(memory_rows, whole_weight, preferred_element_type=jnp.float32)
        everything = lax.all_gather(memory_kv.astype(jnp.bfloat16), "pass", axis=0, tiled=True)
        halves = everything.reshape(-1, 2, 2, LANES).transpose(2, 0, 1, 3).reshape(2, -1, 2 * LANES)
        rest = (retrieval * MEM, question_lengths, question_queries)
        context = attend(jnp.int32(0), *rest, halves[0], question_kv)
        return attend(jnp.int32(1), *rest, halves[1], question_kv, context)

    place = place_of(chip, chips).reshape(1)
    order = [2 * line for line in range(chips // 2)] + [2 * line + 1 for line in range(chips // 2)][::-1]

    def to_partner(x):
        return lax.ppermute(x, "pass", [(i, i ^ 1) for i in range(extent)])

    def along(x, target):
        pairs = [(c, target(c // 2, c % 2)) for c in range(chips)]
        return lax.ppermute(x, "pass", [(2 * s + c, 2 * d + c) for s, d in pairs for c in range(2)])

    def along_ring(x, step):
        return along(x, lambda line, lane: order[(order.index(2 * line + lane) + step) % chips])

    def line_by_line(block):
        lines = chips // 2

        def lane_of(x):
            return along(x, lambda line, lane: 2 * line + 1 - lane)

        near = {k: along(block, lambda line, lane: 2 * ((line + k) % lines) + lane) for k in (2, 1, 3)}
        far = {0: lane_of(block)}
        far[3] = along(block, lambda line, lane: 2 * ((line + 3) % lines) + 1 - lane)
        far[1], far[2] = lane_of(near[1]), lane_of(near[2])
        return [block, near[1], near[2], near[3], far[0], far[1], far[2], far[3]]

    mine, theirs = split(core, kv_weight)
    up = [[mine], [to_partner(theirs)]]
    down = [[x[0]] for x in up]

    def blocks(turns):
        found = {}
        for part in range(2):
            for turn in turns:
                if turn < len(up[part]):
                    found[part, turn] = up[part][turn]
                if 0 < turn < len(down[part]):
                    found[part, chips - turn] = down[part][turn]
        return found

    for turn in range(1, chips // 2):
        for part in range(2):
            up[part].append(along_ring(up[part][-1], 1))
            down[part].append(along_ring(down[part][-1], -1))
        if turn == 1:
            rows = pool(passage_states, memory_queries, memory_gain)
            *hops, rows = lax.optimization_barrier((*(x[-1] for x in up + down), rows))
            for chain, hop in zip(up + down, hops):
                chain[-1] = hop
            other_rows = to_partner(rows)
        elif turn == 2:
            early = project(chips, core, place, rows, other_rows, blocks((0, 1)))
            down[1][-1], early = lax.optimization_barrier((down[1][-1], early))
    up[0].append(along_ring(up[0][-1], 1))
    down[1].append(along_ring(down[1][-1], -1))
    memory_kv = project(chips, core, place, rows, other_rows, blocks((2, 3, 4)), early)
    near = jnp.concatenate(line_by_line(memory_kv), axis=0)
    far = to_partner(near)

    lines = chips // 2
    of_chip = lax.div(retrieval, CHIP)
    back = lax.rem(lines + lax.div(chip, 2) - lax.div(of_chip, 2), lines)
    slot = back + lines * lax.rem(lax.rem(chip, 2) + lax.rem(of_chip, 2), 2)
    starts = (slot * CHIP + lax.rem(retrieval, CHIP)) * MEM
    rest = (starts, question_lengths, question_queries)
    context, begun = attend(core, *rest, near, question_kv, ahead=True)
    return attend(1 - core, *rest, far, question_kv, context, begun)


def solution(mesh):
    placed = (
        P(("groups", "pass"), None, None),
        P(),
        P(),
        P("pass", None),
        P(("groups", "pass"), None),
        P(("groups", "pass"), None, None),
        P(("groups", "pass"), None, None),
        P(("groups", "pass")),
    )
    return jax.shard_map(
        functools.partial(local, mesh.shape["pass"]),
        mesh=mesh,
        in_specs=placed,
        out_specs=P(("groups", "pass"), None, None),
        check_vma=False,
    )
```

```python
import functools
import math

import jax
import jax.numpy as jnp
from jax import lax
from jax.experimental import pallas as pl
from jax.experimental.pallas import tpu as pltpu
from jax.sharding import PartitionSpec as P

D = 4096
CH = 32
CHD = 128
MEM = 32
LEN = 128
QLEN = 64
TOPK = 16
H = 116
HD = 64
KVH = 4
GROUP = 29
KVW = 512

LANES = 2 * HD
PAIRS = GROUP
HALF = PAIRS * LANES
ROWS = TOPK * MEM
KEYS = 2 * (ROWS + QLEN)
NEG = -1e30
SUM_LOW, SUM_HIGH = 2.0 ** -40, 2.0 ** 60
POOL_WIDTH = 1024
FIRST_COST = 8 * 10**9
CHIP = 8
STEP = 5
BLOCK = 16
MIB = 1024 * 1024


def place_of(chip, ring):
    line, lane = lax.div(chip, 2), lax.rem(chip, 2)
    return line + lane * (ring - 1 - 2 * line)


def chip_at(place, ring):
    lane = lax.div(place, ring // 2)
    line = place + lane * (ring - 1 - 2 * place)
    return 2 * line + lane


def split_kernel(core_ref, weight_ref, mine_ref, theirs_ref):
    for out_ref, half in ((mine_ref, core_ref[0]), (theirs_ref, 1 - core_ref[0])):
        for n in range(2):
            at = pl.multiple_of(half * LANES + n * KVH * HD, LANES)
            out_ref[:, n * LANES:(n + 1) * LANES] = weight_ref[:, pl.ds(at, LANES)]


def split(core, weight):
    vmem = pl.BlockSpec(memory_space=pltpu.VMEM)
    return pl.pallas_call(
        split_kernel,
        in_specs=[pl.BlockSpec(memory_space=pltpu.SMEM), vmem],
        out_specs=[vmem, vmem],
        out_shape=[jax.ShapeDtypeStruct((weight.shape[0], 2 * LANES), weight.dtype)] * 2,
        compiler_params=pltpu.CompilerParams(vmem_limit_bytes=8 * MIB),
        cost_estimate=pl.CostEstimate(flops=FIRST_COST, bytes_accessed=4 * weight.size, transcendentals=0),
        name="split",
    )(core.reshape(1), weight)


def pool_kernel(states, queries, gain, out_ref, pooled):
    passages = states.shape[0]
    two = 2 * CHD
    zero = jnp.zeros((MEM, CHD), jnp.bfloat16)
    blank = jnp.zeros((2 * MEM, LEN), jnp.bfloat16)
    totals = [jnp.zeros((MEM, CHD), jnp.float32)] * passages
    for base in range(0, D, POOL_WIDTH):
        blocks = []
        for column in range(base, base + POOL_WIDTH, two):
            lhs = jnp.concatenate(
                [
                    jnp.concatenate([queries[:, column:column + CHD], zero], axis=1),
                    jnp.concatenate([zero, queries[:, column + CHD:column + two]], axis=1),
                ],
                axis=0,
            )
            for p in range(0, passages, 2):
                tokens = states[p:p + 2, :, column:column + two].reshape(2 * LEN, two)
                scores = lax.dot_general(
                    lhs, tokens, (((1,), (1,)), ((), ())), preferred_element_type=jnp.float32
                ) * (1.0 / math.sqrt(CHD))
                blocks.append((column, p, tokens, scores))
        for column, p, tokens, scores in blocks:
            rows = []
            for n in range(2):
                part = scores[:, n * LEN:(n + 1) * LEN]
                part = jnp.exp(part - jnp.max(part, axis=1, keepdims=True))
                part = (part / jnp.sum(part, axis=1, keepdims=True)).astype(jnp.bfloat16)
                rows.append(jnp.concatenate([blank, part] if n else [part, blank], axis=1))
            mixed = jnp.dot(jnp.concatenate(rows, axis=0), tokens, preferred_element_type=jnp.float32)
            for n in range(2):
                for head in range(2):
                    top = (2 * n + head) * MEM
                    block = mixed[top:top + MEM, head * CHD:(head + 1) * CHD]
                    place = slice(column + head * CHD, column + (head + 1) * CHD)
                    pooled[(p + n) * MEM:(p + n + 1) * MEM, place] = block
                    totals[p + n] = totals[p + n] + block * block
    mean_square = jnp.sum(jnp.concatenate(totals, axis=0), axis=1, keepdims=True) * (1.0 / D)
    scale = lax.rsqrt(mean_square + 1e-06)
    factor = gain[...].astype(jnp.float32).reshape(1, D)
    out_ref[...] = (pooled[...] * scale * factor).astype(jnp.bfloat16)


def pool(states, queries, gain):
    count = states.shape[0]
    vmem = pl.BlockSpec(memory_space=pltpu.VMEM)
    return pl.pallas_call(
        pool_kernel,
        in_specs=[vmem] * 3,
        out_specs=vmem,
        out_shape=jax.ShapeDtypeStruct((count * MEM, D), jnp.bfloat16),
        scratch_shapes=[pltpu.VMEM((count * MEM, D), jnp.float32)],
        compiler_params=pltpu.CompilerParams(vmem_limit_bytes=20 * MIB),
        cost_estimate=pl.CostEstimate(
            flops=4 * count * MEM * LEN * D, bytes_accessed=2 * count * LEN * D,
            transcendentals=count * CH * MEM * LEN,
        ),
        name="pool",
    )(states, queries, gain)


def attend_kernel(begun, ahead, half_ref, start_ref, length_ref, q_hbm, kv_ref, own_kv_ref, *rest):
    if ahead:
        other_at = pl.multiple_of((1 - half_ref[0]) * HALF, LANES)
        coming = pltpu.make_async_copy(q_hbm.at[0, :, pl.ds(other_at, HALF)], rest[-14], rest[-1])
        coming.start()
        out_hbm, rest = rest[-15], rest[:-1]
    else:
        out_hbm = rest[-13]
    (
        questions, answers, memory, key_side, value_side, weights, bias, marker, scores, all_weights,
        arrived, sent,
    ) = rest[-12:]
    count = q_hbm.shape[0]
    half_at = pl.multiple_of(half_ref[0] * HALF, LANES)
    own_at = pl.multiple_of(half_ref[0] * LANES, LANES)
    factor = math.log2(math.e) / math.sqrt(HD)

    def fetch(query):
        return pltpu.make_async_copy(
            q_hbm.at[query, :, pl.ds(half_at, HALF)], questions.at[query], arrived.at[query]
        )

    def send(query):
        return pltpu.make_async_copy(
            answers.at[query], out_hbm.at[query, :, pl.ds(half_at, HALF)], sent.at[query]
        )

    if begun:
        questions[0] = rest[0][...]
    else:
        fetch(0).start()
    lane = lax.broadcasted_iota(jnp.int32, (KEYS, LANES), 1)
    row = lax.broadcasted_iota(jnp.int32, (KEYS, LANES), 0)
    in_b = ((row >= ROWS) & (row < 2 * ROWS)) | (row >= 2 * ROWS + QLEN)
    ones = jnp.where((lane >= HD) == in_b, 1.0, 0.0).astype(jnp.bfloat16)
    key_side[...] = jnp.zeros_like(key_side)
    for g in range(2):
        value_side[g, :, LANES:] = ones

    half = PAIRS // 2
    chunks = []
    for g in range(2):
        tiles = list(range(half + 1)) if g == 0 else list(range(half, PAIRS))
        chunks += [(g, tiles[at:at + STEP]) for at in range(0, len(tiles), STEP)]

    def answer(query, carry):
        for slot in range(TOPK):
            start = pl.multiple_of(start_ref[query, slot], MEM)
            memory[slot * MEM:(slot + 1) * MEM, :] = kv_ref[pl.ds(start, MEM), :]
        length = length_ref[query]

        turned = jnp.transpose(memory[:, :LANES])
        own_k = own_kv_ref[query, :, pl.ds(own_at, LANES)]
        own_turned = jnp.transpose(jnp.concatenate([own_k, own_k], axis=0))
        column = lax.broadcasted_iota(jnp.int32, (HD, LANES), 1)
        for g in range(2):
            for member in range(2):
                rows = slice(member * HD, (member + 1) * HD)
                key_side[g, rows, member * ROWS:(member + 1) * ROWS] = turned[g * HD:(g + 1) * HD]
                own = own_turned[g * HD:(g + 1) * HD]
                mine = (column >= HD) if member else (column < HD)
                key_side[g, rows, 2 * ROWS:] = jnp.where(mine, own, jnp.zeros_like(own))

        token = lax.broadcasted_iota(jnp.int32, (QLEN, LANES), 0)
        low = lax.broadcasted_iota(jnp.int32, (QLEN, LANES), 1) < HD
        key = lax.rem(lax.broadcasted_iota(jnp.int32, (QLEN, LANES), 1), HD)
        bias[...] = jnp.where((key <= token) & (key < length), 0.0, NEG)
        alive = token < length
        sample = lax.div(key, HD // STEP)

        own_v_at = pl.multiple_of(own_at + KVH * HD, LANES)
        own_v = own_kv_ref[query, :, pl.ds(own_v_at, LANES)]
        for block, at in ((memory[:, LANES:], 0), (own_v, 2 * ROWS)):
            size = block.shape[0]
            swapped = jnp.concatenate([block[:, HD:], block[:, :HD]], axis=1)
            lower = lax.broadcasted_iota(jnp.int32, block.shape, 1) < HD
            zero = jnp.zeros_like(block)
            for g in range(2):
                one, two = (block, swapped) if g == 0 else (swapped, block)
                value_side[g, at:at + size, :LANES] = jnp.where(lower, one, zero)
                value_side[g, at + size:at + 2 * size, :LANES] = jnp.where(lower, zero, two)

        if begun:

            @pl.when(query > 0)
            def _():
                fetch(query).wait()
        else:
            fetch(query).wait()

        @pl.when(query + 1 < count)
        def _():
            fetch(query + 1).start()

        def stacked(tiles):
            return jnp.concatenate([questions[query, :, t * LANES:(t + 1) * LANES] for t in tiles], axis=0)

        def key_product(i):
            g, tiles = chunks[i]
            lhs = stacked(tiles)
            for c in range(0, KEYS, ROWS):
                part = slice(c, min(c + ROWS, KEYS))
                got = jnp.dot(lhs, key_side[g, :, part], preferred_element_type=jnp.float32) * factor
                if c == 2 * ROWS:
                    got = got + jnp.concatenate([bias[...]] * len(tiles), axis=0)
                weights[i % 2, :len(tiles) * QLEN, part] = jnp.exp2(got).astype(jnp.bfloat16)

        def finish(i, mixed):
            g, tiles = chunks[i]
            for n, t in enumerate(tiles):
                rows = slice(n * QLEN, (n + 1) * QLEN)
                sums = mixed[rows, LANES:]
                inverse = pl.reciprocal(sums, approx=True)
                inverse = inverse * (2.0 - sums * inverse)
                result = jnp.where(alive, mixed[rows, :LANES] * inverse, 0.0).astype(jnp.bfloat16)
                at = slice(t * LANES, (t + 1) * LANES)
                if t == half and g == 1:
                    result = jnp.where(low, answers[query, :, at], result)
                answers[query, :, at] = result

        def value_product(i, seen):
            g, tiles = chunks[i]
            size = len(tiles) * QLEN
            mixed = jnp.dot(weights[i % 2, :size, :], value_side[g], preferred_element_type=jnp.float32)
            sums = mixed[:QLEN, LANES:]
            for n in range(1, len(tiles)):
                sums = jnp.where(sample == n, mixed[n * QLEN:(n + 1) * QLEN, LANES:], sums)
            seen = jnp.where((sums > SUM_LOW) & (sums < SUM_HIGH), seen, 1.0)
            finish(i, mixed)
            return seen

        key_product(0)
        seen = jnp.zeros((QLEN, LANES), jnp.float32)
        for i in range(len(chunks)):
            if i + 1 < len(chunks):
                key_product(i + 1)
            seen = value_product(i, seen)
        marker[0] = jnp.max(seen)

        @pl.when(marker[0] > 0.0)
        def _():
            for i, (g, tiles) in enumerate(chunks):
                size = len(tiles) * QLEN
                scores[:size, :] = jnp.dot(stacked(tiles), key_side[g], preferred_element_type=jnp.float32)

                def soften(n, carry):
                    rows = pl.ds(pl.multiple_of(n * QLEN, QLEN), QLEN)
                    own_scores = scores[rows, 2 * ROWS:] + bias[...]
                    tops = []
                    for member in range(2):
                        columns = slice(member * ROWS, (member + 1) * ROWS)
                        top = jnp.where(low, own_scores, NEG) if member == 0 else jnp.where(low, NEG, own_scores)
                        top = jnp.maximum(
                            jnp.max(top, axis=1, keepdims=True),
                            jnp.max(scores[rows, columns], axis=1, keepdims=True),
                        )
                        all_weights[rows, columns] = jnp.exp2(
                            (scores[rows, columns] - top) * factor
                        ).astype(jnp.bfloat16)
                        tops.append(top)
                    all_weights[rows, 2 * ROWS:] = jnp.exp2(
                        (own_scores - jnp.where(low, tops[0], tops[1])) * factor
                    ).astype(jnp.bfloat16)
                    return carry

                lax.fori_loop(0, len(tiles), soften, 0)
                finish(
                    i, jnp.dot(all_weights[:size, :], value_side[g], preferred_element_type=jnp.float32)
                )

        send(query).start()
        return carry

    lax.fori_loop(0, count, answer, 0)
    for query in range(count):
        send(query).wait()
    if ahead:
        coming.wait()


def attend(half, starts, lengths, questions, memory_kv, own_kv, earlier=None, begun=None, ahead=False):
    count = questions.shape[0]
    hbm, vmem, smem = (pl.BlockSpec(memory_space=x) for x in (pltpu.HBM, pltpu.VMEM, pltpu.SMEM))
    operands = [half.reshape(1), starts, lengths, questions, memory_kv, own_kv]
    in_specs = [smem, smem, smem, hbm, vmem, vmem]
    aliases = {}
    if begun is not None:
        operands.append(begun)
        in_specs.append(vmem)
    if earlier is not None:
        aliases = {len(operands): 0}
        operands.append(earlier)
        in_specs.append(hbm)
    out_specs, extra = [hbm], []
    out_shape = [jax.ShapeDtypeStruct((count, QLEN, H * HD), jnp.bfloat16)]
    if ahead:
        out_specs.append(vmem)
        out_shape.append(jax.ShapeDtypeStruct((QLEN, HALF), jnp.bfloat16))
        extra = [pltpu.SemaphoreType.DMA]
    got = pl.pallas_call(
        functools.partial(attend_kernel, begun is not None, ahead),
        in_specs=in_specs,
        out_specs=out_specs,
        out_shape=out_shape,
        scratch_shapes=[
            pltpu.VMEM((count, QLEN, HALF), jnp.bfloat16),
            pltpu.VMEM((count, QLEN, HALF), jnp.bfloat16),
            pltpu.VMEM((ROWS, 2 * LANES), jnp.bfloat16),
            pltpu.VMEM((2, LANES, KEYS), jnp.bfloat16),
            pltpu.VMEM((2, KEYS, 2 * LANES), jnp.bfloat16),
            pltpu.VMEM((2, STEP * QLEN, KEYS), jnp.bfloat16),
            pltpu.VMEM((QLEN, LANES), jnp.float32),
            pltpu.SMEM((1,), jnp.float32),
            pltpu.VMEM((STEP * QLEN, KEYS), jnp.float32),
            pltpu.VMEM((STEP * QLEN, KEYS), jnp.bfloat16),
            pltpu.SemaphoreType.DMA((count,)),
            pltpu.SemaphoreType.DMA((count,)),
            *extra,
        ],
        input_output_aliases=aliases,
        compiler_params=pltpu.CompilerParams(vmem_limit_bytes=50 * MIB),
        cost_estimate=pl.CostEstimate(
            flops=2 * count * QLEN * H * HD * (ROWS + QLEN),
            bytes_accessed=2 * count * QLEN * H * HD,
            transcendentals=count * QLEN * H * (ROWS + QLEN) // 2,
        ),
        name="attend",
    )(*operands)
    return got if ahead else got[0]


def project_kernel(ring, pieces, more, core_ref, place_ref, own_ref, other_ref, *rest):
    weights, rest = rest[:len(pieces)], rest[len(pieces):]
    out_ref = rest[-1]
    count = own_ref.shape[0]
    depth = weights[0].shape[0]
    core = core_ref[0]
    total = jnp.zeros((2 * count, weights[0].shape[1]), jnp.float32) if more else rest[0][...]
    for (part, i), weight in zip(pieces, weights):
        chip = chip_at(lax.rem(ring + place_ref[0] - i, ring), ring)
        at = pl.multiple_of((2 * chip + (1 - core if part else core)) * depth, depth)
        rows = jnp.concatenate([own_ref[:, pl.ds(at, depth)], other_ref[:, pl.ds(at, depth)]], axis=0)
        total += jnp.dot(rows, weight[...], preferred_element_type=jnp.float32)
    if more:
        out_ref[...] = total
        return
    result = total.astype(jnp.bfloat16)
    out_ref[pl.ds(pl.multiple_of(core * count, count), count)] = result[:count]
    out_ref[pl.ds(pl.multiple_of((1 - core) * count, count), count)] = result[count:]


def project(ring, core, place, own_rows, other_rows, weights, sums=None):
    count = own_rows.shape[0]
    pieces, blocks = tuple(weights), list(weights.values())
    width = blocks[0].shape[1]
    vmem = pl.BlockSpec(memory_space=pltpu.VMEM)
    smem = pl.BlockSpec(memory_space=pltpu.SMEM)
    more = sums is None
    operands = [own_rows, other_rows, *blocks] + ([] if more else [sums])
    return pl.pallas_call(
        functools.partial(project_kernel, ring, pieces, more),
        in_specs=[smem, smem] + [vmem] * len(operands),
        out_specs=vmem,
        out_shape=jax.ShapeDtypeStruct((2 * count, width), jnp.float32 if more else jnp.bfloat16),
        compiler_params=pltpu.CompilerParams(vmem_limit_bytes=16 * MIB),
        cost_estimate=pl.CostEstimate(
            flops=count * D * width, bytes_accessed=32 * D * width, transcendentals=0
        ),
        name="project",
    )(core.reshape(1), place, *operands)


def local(
    extent,
    passage_states,
    memory_queries,
    memory_gain,
    kv_weight,
    retrieval,
    question_queries,
    question_kv,
    question_lengths,
):
    me = lax.axis_index("pass")
    core, chip = me & 1, lax.div(me, 2)
    chips = extent // 2
    depth = kv_weight.shape[0]

    if chips != 8 or depth % LANES:
        memory_rows = pool(passage_states, memory_queries, memory_gain)
        whole_weight = lax.all_gather(kv_weight, "pass", axis=0, tiled=True)
        memory_kv = jnp.dot(memory_rows, whole_weight, preferred_element_type=jnp.float32)
        everything = lax.all_gather(memory_kv.astype(jnp.bfloat16), "pass", axis=0, tiled=True)
        halves = everything.reshape(-1, 2, 2, LANES).transpose(2, 0, 1, 3).reshape(2, -1, 2 * LANES)
        rest = (retrieval * MEM, question_lengths, question_queries)
        context = attend(jnp.int32(0), *rest, halves[0], question_kv)
        return attend(jnp.int32(1), *rest, halves[1], question_kv, context)

    place = place_of(chip, chips).reshape(1)
    order = [2 * line for line in range(chips // 2)] + [2 * line + 1 for line in range(chips // 2)][::-1]

    def to_partner(x):
        return lax.ppermute(x, "pass", [(i, i ^ 1) for i in range(extent)])

    def along(x, target):
        pairs = [(c, target(c // 2, c % 2)) for c in range(chips)]
        return lax.ppermute(x, "pass", [(2 * s + c, 2 * d + c) for s, d in pairs for c in range(2)])

    def along_ring(x, step):
        return along(x, lambda line, lane: order[(order.index(2 * line + lane) + step) % chips])

    def line_by_line(block, beside):
        lines = chips // 2

        def lane_of(x):
            return along(x, lambda line, lane: 2 * line + 1 - lane)

        near = {k: along(block, lambda line, lane: 2 * ((line + k) % lines) + lane) for k in (2, 1, 3)}
        far = {0: lane_of(block)}
        far[3] = along(block, lambda line, lane: 2 * ((line + 3) % lines) + 1 - lane)
        far[1], far[2] = lane_of(near[1]), lane_of(near[2])
        near[3], far[1], beside = lax.optimization_barrier((near[3], far[1], beside))
        return [block, near[1], near[2], near[3], far[0], far[1], far[2], far[3]], beside

    mine, theirs = split(core, kv_weight)
    up = [[mine], [to_partner(theirs)]]
    down = [[x[0]] for x in up]

    def blocks(turns):
        found = {}
        for part in range(2):
            for turn in turns:
                if turn < len(up[part]):
                    found[part, turn] = up[part][turn]
                if 0 < turn < len(down[part]):
                    found[part, chips - turn] = down[part][turn]
        return found

    for turn in range(1, chips // 2):
        for part in range(2):
            up[part].append(along_ring(up[part][-1], 1))
            down[part].append(along_ring(down[part][-1], -1))
        if turn == 1:
            rows = pool(passage_states, memory_queries, memory_gain)
            *hops, rows = lax.optimization_barrier((*(x[-1] for x in up + down), rows))
            for chain, hop in zip(up + down, hops):
                chain[-1] = hop
            other_rows = to_partner(rows)
        elif turn == 2:
            early = project(chips, core, place, rows, other_rows, blocks((0, 1)))
            down[1][-1], early = lax.optimization_barrier((down[1][-1], early))
    up[0].append(along_ring(up[0][-1], 1))
    down[1].append(along_ring(down[1][-1], -1))
    memory_kv = project(chips, core, place, rows, other_rows, blocks((2, 3, 4)), early)
    begun = lax.dynamic_slice(question_queries, (0, 0, core * HALF), (1, QLEN, HALF))[0]
    near_blocks, begun = line_by_line(memory_kv, begun)
    near = jnp.concatenate(near_blocks, axis=0)
    far = to_partner(near)

    lines = chips // 2
    of_chip = lax.div(retrieval, CHIP)
    back = lax.rem(lines + lax.div(chip, 2) - lax.div(of_chip, 2), lines)
    slot = back + lines * lax.rem(lax.rem(chip, 2) + lax.rem(of_chip, 2), 2)
    starts = (slot * CHIP + lax.rem(retrieval, CHIP)) * MEM
    rest = (starts, question_lengths, question_queries)
    context, begun = attend(core, *rest, near, question_kv, begun=begun, ahead=True)
    return attend(1 - core, *rest, far, question_kv, context, begun)


def solution(mesh):
    placed = (
        P(("groups", "pass"), None, None),
        P(),
        P(),
        P("pass", None),
        P(("groups", "pass"), None),
        P(("groups", "pass"), None, None),
        P(("groups", "pass"), None, None),
        P(("groups", "pass")),
    )
    return jax.shard_map(
        functools.partial(local, mesh.shape["pass"]),
        mesh=mesh,
        in_specs=placed,
        out_specs=P(("groups", "pass"), None, None),
        check_vma=False,
    )
```

```python
import functools
import math

import jax
import jax.numpy as jnp
from jax import lax
from jax.experimental import pallas as pl
from jax.experimental.pallas import tpu as pltpu
from jax.sharding import PartitionSpec as P

D = 4096
CH = 32
CHD = 128
MEM = 32
LEN = 128
QLEN = 64
TOPK = 16
H = 116
HD = 64
KVH = 4
GROUP = 29
KVW = 512

LANES = 2 * HD
PAIRS = GROUP
HALF = PAIRS * LANES
ROWS = TOPK * MEM
KEYS = 2 * (ROWS + QLEN)
NEG = -1e30
SUM_LOW, SUM_HIGH = 2.0 ** -40, 2.0 ** 60
POOL_WIDTH = 1024
FIRST_COST = 8 * 10**9
CHIP = 8
STEP = 5
BLOCK = 16
MIB = 1024 * 1024


def place_of(chip, ring):
    line, lane = lax.div(chip, 2), lax.rem(chip, 2)
    return line + lane * (ring - 1 - 2 * line)


def chip_at(place, ring):
    lane = lax.div(place, ring // 2)
    line = place + lane * (ring - 1 - 2 * place)
    return 2 * line + lane


def split_kernel(core_ref, weight_ref, mine_ref, theirs_ref):
    for out_ref, half in ((mine_ref, core_ref[0]), (theirs_ref, 1 - core_ref[0])):
        for n in range(2):
            at = pl.multiple_of(half * LANES + n * KVH * HD, LANES)
            out_ref[:, n * LANES:(n + 1) * LANES] = weight_ref[:, pl.ds(at, LANES)]


def split(core, weight):
    vmem = pl.BlockSpec(memory_space=pltpu.VMEM)
    return pl.pallas_call(
        split_kernel,
        in_specs=[pl.BlockSpec(memory_space=pltpu.SMEM), vmem],
        out_specs=[vmem, vmem],
        out_shape=[jax.ShapeDtypeStruct((weight.shape[0], 2 * LANES), weight.dtype)] * 2,
        compiler_params=pltpu.CompilerParams(vmem_limit_bytes=8 * MIB),
        cost_estimate=pl.CostEstimate(flops=FIRST_COST, bytes_accessed=4 * weight.size, transcendentals=0),
        name="split",
    )(core.reshape(1), weight)


def pool_kernel(states, queries, gain, out_ref, pooled):
    passages = states.shape[0]
    two = 2 * CHD
    zero = jnp.zeros((MEM, CHD), jnp.bfloat16)
    blank = jnp.zeros((2 * MEM, LEN), jnp.bfloat16)
    totals = [jnp.zeros((MEM, CHD), jnp.float32)] * passages
    for base in range(0, D, POOL_WIDTH):
        blocks = []
        for column in range(base, base + POOL_WIDTH, two):
            lhs = jnp.concatenate(
                [
                    jnp.concatenate([queries[:, column:column + CHD], zero], axis=1),
                    jnp.concatenate([zero, queries[:, column + CHD:column + two]], axis=1),
                ],
                axis=0,
            )
            for p in range(0, passages, 2):
                tokens = states[p:p + 2, :, column:column + two].reshape(2 * LEN, two)
                scores = lax.dot_general(
                    lhs, tokens, (((1,), (1,)), ((), ())), preferred_element_type=jnp.float32
                ) * (1.0 / math.sqrt(CHD))
                blocks.append((column, p, tokens, scores))
        for column, p, tokens, scores in blocks:
            rows = []
            for n in range(2):
                part = scores[:, n * LEN:(n + 1) * LEN]
                part = jnp.exp(part - jnp.max(part, axis=1, keepdims=True))
                part = (part / jnp.sum(part, axis=1, keepdims=True)).astype(jnp.bfloat16)
                rows.append(jnp.concatenate([blank, part] if n else [part, blank], axis=1))
            mixed = jnp.dot(jnp.concatenate(rows, axis=0), tokens, preferred_element_type=jnp.float32)
            for n in range(2):
                for head in range(2):
                    top = (2 * n + head) * MEM
                    block = mixed[top:top + MEM, head * CHD:(head + 1) * CHD]
                    place = slice(column + head * CHD, column + (head + 1) * CHD)
                    pooled[(p + n) * MEM:(p + n + 1) * MEM, place] = block
                    totals[p + n] = totals[p + n] + block * block
    mean_square = jnp.sum(jnp.concatenate(totals, axis=0), axis=1, keepdims=True) * (1.0 / D)
    scale = lax.rsqrt(mean_square + 1e-06)
    factor = gain[...].astype(jnp.float32).reshape(1, D)
    out_ref[...] = (pooled[...] * scale * factor).astype(jnp.bfloat16)


def pool(states, queries, gain):
    count = states.shape[0]
    vmem = pl.BlockSpec(memory_space=pltpu.VMEM)
    return pl.pallas_call(
        pool_kernel,
        in_specs=[vmem] * 3,
        out_specs=vmem,
        out_shape=jax.ShapeDtypeStruct((count * MEM, D), jnp.bfloat16),
        scratch_shapes=[pltpu.VMEM((count * MEM, D), jnp.float32)],
        compiler_params=pltpu.CompilerParams(vmem_limit_bytes=20 * MIB),
        cost_estimate=pl.CostEstimate(
            flops=4 * count * MEM * LEN * D, bytes_accessed=2 * count * LEN * D,
            transcendentals=count * CH * MEM * LEN,
        ),
        name="pool",
    )(states, queries, gain)


def attend_kernel(begun, ahead, half_ref, start_ref, length_ref, q_hbm, kv_ref, own_kv_ref, *rest):
    if ahead:
        other_at = pl.multiple_of((1 - half_ref[0]) * HALF, LANES)
        coming = pltpu.make_async_copy(q_hbm.at[0, :, pl.ds(other_at, HALF)], rest[-14], rest[-1])
        coming.start()
        out_hbm, rest = rest[-15], rest[:-1]
    else:
        out_hbm = rest[-13]
    (
        questions, answers, memory, key_side, value_side, weights, bias, marker, scores, all_weights,
        arrived, sent,
    ) = rest[-12:]
    count = q_hbm.shape[0]
    half_at = pl.multiple_of(half_ref[0] * HALF, LANES)
    own_at = pl.multiple_of(half_ref[0] * LANES, LANES)
    factor = math.log2(math.e) / math.sqrt(HD)

    def fetch(query):
        return pltpu.make_async_copy(
            q_hbm.at[query, :, pl.ds(half_at, HALF)], questions.at[query], arrived.at[query]
        )

    def send(query):
        return pltpu.make_async_copy(
            answers.at[query], out_hbm.at[query, :, pl.ds(half_at, HALF)], sent.at[query]
        )

    if begun:
        questions[0] = rest[0][...]
    else:
        fetch(0).start()
    lane = lax.broadcasted_iota(jnp.int32, (KEYS, LANES), 1)
    row = lax.broadcasted_iota(jnp.int32, (KEYS, LANES), 0)
    in_b = ((row >= ROWS) & (row < 2 * ROWS)) | (row >= 2 * ROWS + QLEN)
    ones = jnp.where((lane >= HD) == in_b, 1.0, 0.0).astype(jnp.bfloat16)
    key_side[...] = jnp.zeros_like(key_side)
    for g in range(2):
        value_side[g, :, LANES:] = ones

    half = PAIRS // 2
    chunks = []
    for g in range(2):
        tiles = list(range(half + 1)) if g == 0 else list(range(half, PAIRS))
        chunks += [(g, tiles[at:at + STEP]) for at in range(0, len(tiles), STEP)]

    def answer(query, carry):
        for slot in range(TOPK):
            start = pl.multiple_of(start_ref[query, slot], MEM)
            memory[slot * MEM:(slot + 1) * MEM, :] = kv_ref[pl.ds(start, MEM), :]
        length = length_ref[query]

        turned = jnp.transpose(memory[:, :LANES])
        own_k = own_kv_ref[query, :, pl.ds(own_at, LANES)]
        own_turned = jnp.transpose(jnp.concatenate([own_k, own_k], axis=0))
        column = lax.broadcasted_iota(jnp.int32, (HD, LANES), 1)
        for g in range(2):
            for member in range(2):
                rows = slice(member * HD, (member + 1) * HD)
                key_side[g, rows, member * ROWS:(member + 1) * ROWS] = turned[g * HD:(g + 1) * HD]
                own = own_turned[g * HD:(g + 1) * HD]
                mine = (column >= HD) if member else (column < HD)
                key_side[g, rows, 2 * ROWS:] = jnp.where(mine, own, jnp.zeros_like(own))

        token = lax.broadcasted_iota(jnp.int32, (QLEN, LANES), 0)
        low = lax.broadcasted_iota(jnp.int32, (QLEN, LANES), 1) < HD
        key = lax.rem(lax.broadcasted_iota(jnp.int32, (QLEN, LANES), 1), HD)
        bias[...] = jnp.where((key <= token) & (key < length), 0.0, NEG)
        alive = token < length
        sample = lax.div(key, HD // STEP)

        own_v_at = pl.multiple_of(own_at + KVH * HD, LANES)
        own_v = own_kv_ref[query, :, pl.ds(own_v_at, LANES)]
        for block, at in ((memory[:, LANES:], 0), (own_v, 2 * ROWS)):
            size = block.shape[0]
            swapped = jnp.concatenate([block[:, HD:], block[:, :HD]], axis=1)
            lower = lax.broadcasted_iota(jnp.int32, block.shape, 1) < HD
            zero = jnp.zeros_like(block)
            for g in range(2):
                one, two = (block, swapped) if g == 0 else (swapped, block)
                value_side[g, at:at + size, :LANES] = jnp.where(lower, one, zero)
                value_side[g, at + size:at + 2 * size, :LANES] = jnp.where(lower, zero, two)

        if begun:

            @pl.when(query > 0)
            def _():
                fetch(query).wait()
        else:
            fetch(query).wait()

        @pl.when(query + 1 < count)
        def _():
            fetch(query + 1).start()

        def stacked(tiles):
            return jnp.concatenate([questions[query, :, t * LANES:(t + 1) * LANES] for t in tiles], axis=0)

        def key_product(i):
            g, tiles = chunks[i]
            lhs = stacked(tiles)
            for c in range(0, KEYS, ROWS):
                part = slice(c, min(c + ROWS, KEYS))
                got = jnp.dot(lhs, key_side[g, :, part], preferred_element_type=jnp.float32) * factor
                if c == 2 * ROWS:
                    got = got + jnp.concatenate([bias[...]] * len(tiles), axis=0)
                weights[i % 2, :len(tiles) * QLEN, part] = jnp.exp2(got).astype(jnp.bfloat16)

        def finish(i, mixed):
            g, tiles = chunks[i]
            for n, t in enumerate(tiles):
                rows = slice(n * QLEN, (n + 1) * QLEN)
                sums = mixed[rows, LANES:]
                inverse = pl.reciprocal(sums, approx=True)
                inverse = inverse * (2.0 - sums * inverse)
                result = jnp.where(alive, mixed[rows, :LANES] * inverse, 0.0).astype(jnp.bfloat16)
                at = slice(t * LANES, (t + 1) * LANES)
                if t == half and g == 1:
                    result = jnp.where(low, answers[query, :, at], result)
                answers[query, :, at] = result

        def value_product(i, seen):
            g, tiles = chunks[i]
            size = len(tiles) * QLEN
            mixed = jnp.dot(weights[i % 2, :size, :], value_side[g], preferred_element_type=jnp.float32)
            sums = mixed[:QLEN, LANES:]
            for n in range(1, len(tiles)):
                sums = jnp.where(sample == n, mixed[n * QLEN:(n + 1) * QLEN, LANES:], sums)
            seen = jnp.where((sums > SUM_LOW) & (sums < SUM_HIGH), seen, 1.0)
            finish(i, mixed)
            return seen

        key_product(0)
        seen = jnp.zeros((QLEN, LANES), jnp.float32)
        for i in range(len(chunks)):
            if i + 1 < len(chunks):
                key_product(i + 1)
            seen = value_product(i, seen)
        marker[0] = jnp.max(seen)

        @pl.when(marker[0] > 0.0)
        def _():
            for i, (g, tiles) in enumerate(chunks):
                size = len(tiles) * QLEN
                scores[:size, :] = jnp.dot(stacked(tiles), key_side[g], preferred_element_type=jnp.float32)

                def soften(n, carry):
                    rows = pl.ds(pl.multiple_of(n * QLEN, QLEN), QLEN)
                    own_scores = scores[rows, 2 * ROWS:] + bias[...]
                    tops = []
                    for member in range(2):
                        columns = slice(member * ROWS, (member + 1) * ROWS)
                        top = jnp.where(low, own_scores, NEG) if member == 0 else jnp.where(low, NEG, own_scores)
                        top = jnp.maximum(
                            jnp.max(top, axis=1, keepdims=True),
                            jnp.max(scores[rows, columns], axis=1, keepdims=True),
                        )
                        all_weights[rows, columns] = jnp.exp2(
                            (scores[rows, columns] - top) * factor
                        ).astype(jnp.bfloat16)
                        tops.append(top)
                    all_weights[rows, 2 * ROWS:] = jnp.exp2(
                        (own_scores - jnp.where(low, tops[0], tops[1])) * factor
                    ).astype(jnp.bfloat16)
                    return carry

                lax.fori_loop(0, len(tiles), soften, 0)
                finish(
                    i, jnp.dot(all_weights[:size, :], value_side[g], preferred_element_type=jnp.float32)
                )

        send(query).start()
        return carry

    lax.fori_loop(0, count, answer, 0)
    for query in range(count):
        send(query).wait()
    if ahead:
        coming.wait()


def attend(half, starts, lengths, questions, memory_kv, own_kv, earlier=None, begun=None, ahead=False):
    count = questions.shape[0]
    hbm, vmem, smem = (pl.BlockSpec(memory_space=x) for x in (pltpu.HBM, pltpu.VMEM, pltpu.SMEM))
    operands = [half.reshape(1), starts, lengths, questions, memory_kv, own_kv]
    in_specs = [smem, smem, smem, hbm, vmem, vmem]
    aliases = {}
    if begun is not None:
        operands.append(begun)
        in_specs.append(vmem)
    if earlier is not None:
        aliases = {len(operands): 0}
        operands.append(earlier)
        in_specs.append(hbm)
    out_specs, extra = [hbm], []
    out_shape = [jax.ShapeDtypeStruct((count, QLEN, H * HD), jnp.bfloat16)]
    if ahead:
        out_specs.append(vmem)
        out_shape.append(jax.ShapeDtypeStruct((QLEN, HALF), jnp.bfloat16))
        extra = [pltpu.SemaphoreType.DMA]
    got = pl.pallas_call(
        functools.partial(attend_kernel, begun is not None, ahead),
        in_specs=in_specs,
        out_specs=out_specs,
        out_shape=out_shape,
        scratch_shapes=[
            pltpu.VMEM((count, QLEN, HALF), jnp.bfloat16),
            pltpu.VMEM((count, QLEN, HALF), jnp.bfloat16),
            pltpu.VMEM((ROWS, 2 * LANES), jnp.bfloat16),
            pltpu.VMEM((2, LANES, KEYS), jnp.bfloat16),
            pltpu.VMEM((2, KEYS, 2 * LANES), jnp.bfloat16),
            pltpu.VMEM((2, STEP * QLEN, KEYS), jnp.bfloat16),
            pltpu.VMEM((QLEN, LANES), jnp.float32),
            pltpu.SMEM((1,), jnp.float32),
            pltpu.VMEM((STEP * QLEN, KEYS), jnp.float32),
            pltpu.VMEM((STEP * QLEN, KEYS), jnp.bfloat16),
            pltpu.SemaphoreType.DMA((count,)),
            pltpu.SemaphoreType.DMA((count,)),
            *extra,
        ],
        input_output_aliases=aliases,
        compiler_params=pltpu.CompilerParams(vmem_limit_bytes=50 * MIB),
        cost_estimate=pl.CostEstimate(
            flops=2 * count * QLEN * H * HD * (ROWS + QLEN),
            bytes_accessed=2 * count * QLEN * H * HD,
            transcendentals=count * QLEN * H * (ROWS + QLEN) // 2,
        ),
        name="attend",
    )(*operands)
    return got if ahead else got[0]


def project_kernel(ring, pieces, more, core_ref, place_ref, own_ref, other_ref, *rest):
    weights, rest = rest[:len(pieces)], rest[len(pieces):]
    out_ref = rest[-1]
    count = own_ref.shape[0]
    depth = weights[0].shape[0]
    core = core_ref[0]
    total = jnp.zeros((2 * count, weights[0].shape[1]), jnp.float32) if more else rest[0][...]
    for (part, i), weight in zip(pieces, weights):
        chip = chip_at(lax.rem(ring + place_ref[0] - i, ring), ring)
        at = pl.multiple_of((2 * chip + (1 - core if part else core)) * depth, depth)
        rows = jnp.concatenate([own_ref[:, pl.ds(at, depth)], other_ref[:, pl.ds(at, depth)]], axis=0)
        total += jnp.dot(rows, weight[...], preferred_element_type=jnp.float32)
    if more:
        out_ref[...] = total
        return
    result = total.astype(jnp.bfloat16)
    out_ref[pl.ds(pl.multiple_of(core * count, count), count)] = result[:count]
    out_ref[pl.ds(pl.multiple_of((1 - core) * count, count), count)] = result[count:]


def project(ring, core, place, own_rows, other_rows, weights, sums=None):
    count = own_rows.shape[0]
    pieces, blocks = tuple(weights), list(weights.values())
    width = blocks[0].shape[1]
    vmem = pl.BlockSpec(memory_space=pltpu.VMEM)
    smem = pl.BlockSpec(memory_space=pltpu.SMEM)
    more = sums is None
    operands = [own_rows, other_rows, *blocks] + ([] if more else [sums])
    return pl.pallas_call(
        functools.partial(project_kernel, ring, pieces, more),
        in_specs=[smem, smem] + [vmem] * len(operands),
        out_specs=vmem,
        out_shape=jax.ShapeDtypeStruct((2 * count, width), jnp.float32 if more else jnp.bfloat16),
        compiler_params=pltpu.CompilerParams(vmem_limit_bytes=16 * MIB),
        cost_estimate=pl.CostEstimate(
            flops=count * D * width, bytes_accessed=32 * D * width, transcendentals=0
        ),
        name="project",
    )(core.reshape(1), place, *operands)


def local(
    extent,
    passage_states,
    memory_queries,
    memory_gain,
    kv_weight,
    retrieval,
    question_queries,
    question_kv,
    question_lengths,
):
    me = lax.axis_index("pass")
    core, chip = me & 1, lax.div(me, 2)
    chips = extent // 2
    depth = kv_weight.shape[0]

    if chips != 8 or depth % LANES:
        memory_rows = pool(passage_states, memory_queries, memory_gain)
        whole_weight = lax.all_gather(kv_weight, "pass", axis=0, tiled=True)
        memory_kv = jnp.dot(memory_rows, whole_weight, preferred_element_type=jnp.float32)
        everything = lax.all_gather(memory_kv.astype(jnp.bfloat16), "pass", axis=0, tiled=True)
        halves = everything.reshape(-1, 2, 2, LANES).transpose(2, 0, 1, 3).reshape(2, -1, 2 * LANES)
        rest = (retrieval * MEM, question_lengths, question_queries)
        context = attend(jnp.int32(0), *rest, halves[0], question_kv)
        return attend(jnp.int32(1), *rest, halves[1], question_kv, context)

    place = place_of(chip, chips).reshape(1)
    order = [2 * line for line in range(chips // 2)] + [2 * line + 1 for line in range(chips // 2)][::-1]

    def to_partner(x):
        return lax.ppermute(x, "pass", [(i, i ^ 1) for i in range(extent)])

    def along(x, target):
        pairs = [(c, target(c // 2, c % 2)) for c in range(chips)]
        return lax.ppermute(x, "pass", [(2 * s + c, 2 * d + c) for s, d in pairs for c in range(2)])

    def along_ring(x, step):
        return along(x, lambda line, lane: order[(order.index(2 * line + lane) + step) % chips])

    def line_by_line(block):
        lines = chips // 2

        def lane_of(x):
            return along(x, lambda line, lane: 2 * line + 1 - lane)

        near = {k: along(block, lambda line, lane: 2 * ((line + k) % lines) + lane) for k in (2, 1, 3)}
        far = {0: lane_of(block)}
        far[2] = along(block, lambda line, lane: 2 * ((line + 2) % lines) + 1 - lane)
        far[1], far[3] = lane_of(near[1]), lane_of(near[3])
        return [block, near[1], near[2], near[3], far[0], far[1], far[2], far[3]]

    mine, theirs = split(core, kv_weight)
    up = [[mine], [to_partner(theirs)]]
    down = [[x[0]] for x in up]

    def blocks(turns):
        found = {}
        for part in range(2):
            for turn in turns:
                if turn < len(up[part]):
                    found[part, turn] = up[part][turn]
                if 0 < turn < len(down[part]):
                    found[part, chips - turn] = down[part][turn]
        return found

    for turn in range(1, chips // 2):
        for part in range(2):
            up[part].append(along_ring(up[part][-1], 1))
            down[part].append(along_ring(down[part][-1], -1))
        if turn == 1:
            rows = pool(passage_states, memory_queries, memory_gain)
            *hops, rows = lax.optimization_barrier((*(x[-1] for x in up + down), rows))
            for chain, hop in zip(up + down, hops):
                chain[-1] = hop
            other_rows = to_partner(rows)
        elif turn == 2:
            early = project(chips, core, place, rows, other_rows, blocks((0, 1)))
            down[1][-1], early = lax.optimization_barrier((down[1][-1], early))
    up[0].append(along_ring(up[0][-1], 1))
    down[1].append(along_ring(down[1][-1], -1))
    memory_kv = project(chips, core, place, rows, other_rows, blocks((2, 3, 4)), early)
    near = jnp.concatenate(line_by_line(memory_kv), axis=0)
    far = to_partner(near)

    lines = chips // 2
    of_chip = lax.div(retrieval, CHIP)
    back = lax.rem(lines + lax.div(chip, 2) - lax.div(of_chip, 2), lines)
    slot = back + lines * lax.rem(lax.rem(chip, 2) + lax.rem(of_chip, 2), 2)
    starts = (slot * CHIP + lax.rem(retrieval, CHIP)) * MEM
    rest = (starts, question_lengths, question_queries)
    context, begun = attend(core, *rest, near, question_kv, ahead=True)
    return attend(1 - core, *rest, far, question_kv, context, begun)


def solution(mesh):
    placed = (
        P(("groups", "pass"), None, None),
        P(),
        P(),
        P("pass", None),
        P(("groups", "pass"), None),
        P(("groups", "pass"), None, None),
        P(("groups", "pass"), None, None),
        P(("groups", "pass")),
    )
    return jax.shard_map(
        functools.partial(local, mesh.shape["pass"]),
        mesh=mesh,
        in_specs=placed,
        out_specs=P(("groups", "pass"), None, None),
        check_vma=False,
    )
```

```python
import functools
import math

import jax
import jax.numpy as jnp
from jax import lax
from jax.experimental import pallas as pl
from jax.experimental.pallas import tpu as pltpu
from jax.sharding import PartitionSpec as P

D = 4096
CH = 32
CHD = 128
MEM = 32
LEN = 128
QLEN = 64
TOPK = 16
H = 116
HD = 64
KVH = 4
GROUP = 29
KVW = 512

LANES = 2 * HD
PAIRS = GROUP
HALF = PAIRS * LANES
ROWS = TOPK * MEM
KEYS = 2 * (ROWS + QLEN)
NEG = -1e30
SUM_LOW, SUM_HIGH = 2.0 ** -40, 2.0 ** 60
POOL_WIDTH = 1024
FIRST_COST = 8 * 10**9
CHIP = 8
STEP = 5
BLOCK = 16
MIB = 1024 * 1024


def place_of(chip, ring):
    line, lane = lax.div(chip, 2), lax.rem(chip, 2)
    return line + lane * (ring - 1 - 2 * line)


def chip_at(place, ring):
    lane = lax.div(place, ring // 2)
    line = place + lane * (ring - 1 - 2 * place)
    return 2 * line + lane


def split_kernel(core_ref, weight_ref, mine_ref, theirs_ref):
    for out_ref, half in ((mine_ref, core_ref[0]), (theirs_ref, 1 - core_ref[0])):
        for n in range(2):
            at = pl.multiple_of(half * LANES + n * KVH * HD, LANES)
            out_ref[:, n * LANES:(n + 1) * LANES] = weight_ref[:, pl.ds(at, LANES)]


def split(core, weight):
    vmem = pl.BlockSpec(memory_space=pltpu.VMEM)
    return pl.pallas_call(
        split_kernel,
        in_specs=[pl.BlockSpec(memory_space=pltpu.SMEM), vmem],
        out_specs=[vmem, vmem],
        out_shape=[jax.ShapeDtypeStruct((weight.shape[0], 2 * LANES), weight.dtype)] * 2,
        compiler_params=pltpu.CompilerParams(vmem_limit_bytes=8 * MIB),
        cost_estimate=pl.CostEstimate(flops=FIRST_COST, bytes_accessed=4 * weight.size, transcendentals=0),
        name="split",
    )(core.reshape(1), weight)


def pool_kernel(states, queries, gain, out_ref, pooled):
    passages = states.shape[0]
    two = 2 * CHD
    zero = jnp.zeros((MEM, CHD), jnp.bfloat16)
    blank = jnp.zeros((2 * MEM, LEN), jnp.bfloat16)
    totals = [jnp.zeros((MEM, CHD), jnp.float32)] * passages
    for base in range(0, D, POOL_WIDTH):
        blocks = []
        for column in range(base, base + POOL_WIDTH, two):
            lhs = jnp.concatenate(
                [
                    jnp.concatenate([queries[:, column:column + CHD], zero], axis=1),
                    jnp.concatenate([zero, queries[:, column + CHD:column + two]], axis=1),
                ],
                axis=0,
            )
            for p in range(0, passages, 2):
                tokens = states[p:p + 2, :, column:column + two].reshape(2 * LEN, two)
                scores = lax.dot_general(
                    lhs, tokens, (((1,), (1,)), ((), ())), preferred_element_type=jnp.float32
                ) * (1.0 / math.sqrt(CHD))
                blocks.append((column, p, tokens, scores))
        for column, p, tokens, scores in blocks:
            rows = []
            for n in range(2):
                part = scores[:, n * LEN:(n + 1) * LEN]
                part = jnp.exp(part - jnp.max(part, axis=1, keepdims=True))
                part = (part / jnp.sum(part, axis=1, keepdims=True)).astype(jnp.bfloat16)
                rows.append(jnp.concatenate([blank, part] if n else [part, blank], axis=1))
            mixed = jnp.dot(jnp.concatenate(rows, axis=0), tokens, preferred_element_type=jnp.float32)
            for n in range(2):
                for head in range(2):
                    top = (2 * n + head) * MEM
                    block = mixed[top:top + MEM, head * CHD:(head + 1) * CHD]
                    place = slice(column + head * CHD, column + (head + 1) * CHD)
                    pooled[(p + n) * MEM:(p + n + 1) * MEM, place] = block
                    totals[p + n] = totals[p + n] + block * block
    mean_square = jnp.sum(jnp.concatenate(totals, axis=0), axis=1, keepdims=True) * (1.0 / D)
    scale = lax.rsqrt(mean_square + 1e-06)
    factor = gain[...].astype(jnp.float32).reshape(1, D)
    out_ref[...] = (pooled[...] * scale * factor).astype(jnp.bfloat16)


def pool(states, queries, gain):
    count = states.shape[0]
    vmem = pl.BlockSpec(memory_space=pltpu.VMEM)
    return pl.pallas_call(
        pool_kernel,
        in_specs=[vmem] * 3,
        out_specs=vmem,
        out_shape=jax.ShapeDtypeStruct((count * MEM, D), jnp.bfloat16),
        scratch_shapes=[pltpu.VMEM((count * MEM, D), jnp.float32)],
        compiler_params=pltpu.CompilerParams(vmem_limit_bytes=20 * MIB),
        cost_estimate=pl.CostEstimate(
            flops=4 * count * MEM * LEN * D, bytes_accessed=2 * count * LEN * D,
            transcendentals=count * CH * MEM * LEN,
        ),
        name="pool",
    )(states, queries, gain)


def attend_kernel(begun, ahead, half_ref, start_ref, length_ref, q_hbm, kv_ref, own_kv_ref, *rest):
    if ahead:
        other_at = pl.multiple_of((1 - half_ref[0]) * HALF, LANES)
        coming = pltpu.make_async_copy(q_hbm.at[0, :, pl.ds(other_at, HALF)], rest[-14], rest[-1])
        coming.start()
        out_hbm, rest = rest[-15], rest[:-1]
    else:
        out_hbm = rest[-13]
    (
        questions, answers, memory, key_side, value_side, weights, bias, marker, scores, all_weights,
        arrived, sent,
    ) = rest[-12:]
    count = q_hbm.shape[0]
    half_at = pl.multiple_of(half_ref[0] * HALF, LANES)
    own_at = pl.multiple_of(half_ref[0] * LANES, LANES)
    factor = math.log2(math.e) / math.sqrt(HD)

    def fetch(query):
        return pltpu.make_async_copy(
            q_hbm.at[query, :, pl.ds(half_at, HALF)], questions.at[query], arrived.at[query]
        )

    def send(query):
        return pltpu.make_async_copy(
            answers.at[query], out_hbm.at[query, :, pl.ds(half_at, HALF)], sent.at[query]
        )

    if begun:
        questions[0] = rest[0][...]
    else:
        fetch(0).start()
    lane = lax.broadcasted_iota(jnp.int32, (KEYS, LANES), 1)
    row = lax.broadcasted_iota(jnp.int32, (KEYS, LANES), 0)
    in_b = ((row >= ROWS) & (row < 2 * ROWS)) | (row >= 2 * ROWS + QLEN)
    ones = jnp.where((lane >= HD) == in_b, 1.0, 0.0).astype(jnp.bfloat16)
    key_side[...] = jnp.zeros_like(key_side)
    for g in range(2):
        value_side[g, :, LANES:] = ones

    half = PAIRS // 2
    chunks = []
    for g in range(2):
        tiles = list(range(half + 1)) if g == 0 else list(range(half, PAIRS))
        chunks += [(g, tiles[at:at + STEP]) for at in range(0, len(tiles), STEP)]

    def answer(query, carry):
        for slot in range(TOPK):
            start = pl.multiple_of(start_ref[query, slot], MEM)
            memory[slot * MEM:(slot + 1) * MEM, :] = kv_ref[pl.ds(start, MEM), :]
        length = length_ref[query]

        turned = jnp.transpose(memory[:, :LANES])
        own_k = own_kv_ref[query, :, pl.ds(own_at, LANES)]
        own_turned = jnp.transpose(jnp.concatenate([own_k, own_k], axis=0))
        column = lax.broadcasted_iota(jnp.int32, (HD, LANES), 1)
        for g in range(2):
            for member in range(2):
                rows = slice(member * HD, (member + 1) * HD)
                key_side[g, rows, member * ROWS:(member + 1) * ROWS] = turned[g * HD:(g + 1) * HD]
                own = own_turned[g * HD:(g + 1) * HD]
                mine = (column >= HD) if member else (column < HD)
                key_side[g, rows, 2 * ROWS:] = jnp.where(mine, own, jnp.zeros_like(own))

        token = lax.broadcasted_iota(jnp.int32, (QLEN, LANES), 0)
        low = lax.broadcasted_iota(jnp.int32, (QLEN, LANES), 1) < HD
        key = lax.rem(lax.broadcasted_iota(jnp.int32, (QLEN, LANES), 1), HD)
        bias[...] = jnp.where((key <= token) & (key < length), 0.0, NEG)
        alive = token < length
        sample = lax.div(key, HD // STEP)

        own_v_at = pl.multiple_of(own_at + KVH * HD, LANES)
        own_v = own_kv_ref[query, :, pl.ds(own_v_at, LANES)]
        for block, at in ((memory[:, LANES:], 0), (own_v, 2 * ROWS)):
            size = block.shape[0]
            swapped = jnp.concatenate([block[:, HD:], block[:, :HD]], axis=1)
            lower = lax.broadcasted_iota(jnp.int32, block.shape, 1) < HD
            zero = jnp.zeros_like(block)
            for g in range(2):
                one, two = (block, swapped) if g == 0 else (swapped, block)
                value_side[g, at:at + size, :LANES] = jnp.where(lower, one, zero)
                value_side[g, at + size:at + 2 * size, :LANES] = jnp.where(lower, zero, two)

        if begun:

            @pl.when(query > 0)
            def _():
                fetch(query).wait()
        else:
            fetch(query).wait()

        @pl.when(query + 1 < count)
        def _():
            fetch(query + 1).start()

        def stacked(tiles):
            return jnp.concatenate([questions[query, :, t * LANES:(t + 1) * LANES] for t in tiles], axis=0)

        def key_product(i):
            g, tiles = chunks[i]
            lhs = stacked(tiles)
            for c in range(0, KEYS, ROWS):
                part = slice(c, min(c + ROWS, KEYS))
                got = jnp.dot(lhs, key_side[g, :, part], preferred_element_type=jnp.float32) * factor
                if c == 2 * ROWS:
                    got = got + jnp.concatenate([bias[...]] * len(tiles), axis=0)
                weights[i % 2, :len(tiles) * QLEN, part] = jnp.exp2(got).astype(jnp.bfloat16)

        def finish(i, mixed):
            g, tiles = chunks[i]
            for n, t in enumerate(tiles):
                rows = slice(n * QLEN, (n + 1) * QLEN)
                sums = mixed[rows, LANES:]
                inverse = pl.reciprocal(sums, approx=True)
                inverse = inverse * (2.0 - sums * inverse)
                result = jnp.where(alive, mixed[rows, :LANES] * inverse, 0.0).astype(jnp.bfloat16)
                at = slice(t * LANES, (t + 1) * LANES)
                if t == half and g == 1:
                    result = jnp.where(low, answers[query, :, at], result)
                answers[query, :, at] = result

        def value_product(i, seen):
            g, tiles = chunks[i]
            size = len(tiles) * QLEN
            mixed = jnp.dot(weights[i % 2, :size, :], value_side[g], preferred_element_type=jnp.float32)
            sums = mixed[:QLEN, LANES:]
            for n in range(1, len(tiles)):
                sums = jnp.where(sample == n, mixed[n * QLEN:(n + 1) * QLEN, LANES:], sums)
            seen = jnp.where((sums > SUM_LOW) & (sums < SUM_HIGH), seen, 1.0)
            finish(i, mixed)
            return seen

        key_product(0)
        seen = jnp.zeros((QLEN, LANES), jnp.float32)
        for i in range(len(chunks)):
            if i + 1 < len(chunks):
                key_product(i + 1)
            seen = value_product(i, seen)
        marker[0] = jnp.max(seen)

        @pl.when(marker[0] > 0.0)
        def _():
            for i, (g, tiles) in enumerate(chunks):
                size = len(tiles) * QLEN
                scores[:size, :] = jnp.dot(stacked(tiles), key_side[g], preferred_element_type=jnp.float32)

                def soften(n, carry):
                    rows = pl.ds(pl.multiple_of(n * QLEN, QLEN), QLEN)
                    own_scores = scores[rows, 2 * ROWS:] + bias[...]
                    tops = []
                    for member in range(2):
                        columns = slice(member * ROWS, (member + 1) * ROWS)
                        top = jnp.where(low, own_scores, NEG) if member == 0 else jnp.where(low, NEG, own_scores)
                        top = jnp.maximum(
                            jnp.max(top, axis=1, keepdims=True),
                            jnp.max(scores[rows, columns], axis=1, keepdims=True),
                        )
                        all_weights[rows, columns] = jnp.exp2(
                            (scores[rows, columns] - top) * factor
                        ).astype(jnp.bfloat16)
                        tops.append(top)
                    all_weights[rows, 2 * ROWS:] = jnp.exp2(
                        (own_scores - jnp.where(low, tops[0], tops[1])) * factor
                    ).astype(jnp.bfloat16)
                    return carry

                lax.fori_loop(0, len(tiles), soften, 0)
                finish(
                    i, jnp.dot(all_weights[:size, :], value_side[g], preferred_element_type=jnp.float32)
                )

        send(query).start()
        return carry

    lax.fori_loop(0, count, answer, 0)
    for query in range(count):
        send(query).wait()
    if ahead:
        coming.wait()


def attend(half, starts, lengths, questions, memory_kv, own_kv, earlier=None, begun=None, ahead=False):
    count = questions.shape[0]
    hbm, vmem, smem = (pl.BlockSpec(memory_space=x) for x in (pltpu.HBM, pltpu.VMEM, pltpu.SMEM))
    operands = [half.reshape(1), starts, lengths, questions, memory_kv, own_kv]
    in_specs = [smem, smem, smem, hbm, vmem, vmem]
    aliases = {}
    if begun is not None:
        operands.append(begun)
        in_specs.append(vmem)
    if earlier is not None:
        aliases = {len(operands): 0}
        operands.append(earlier)
        in_specs.append(hbm)
    out_specs, extra = [hbm], []
    out_shape = [jax.ShapeDtypeStruct((count, QLEN, H * HD), jnp.bfloat16)]
    if ahead:
        out_specs.append(vmem)
        out_shape.append(jax.ShapeDtypeStruct((QLEN, HALF), jnp.bfloat16))
        extra = [pltpu.SemaphoreType.DMA]
    got = pl.pallas_call(
        functools.partial(attend_kernel, begun is not None, ahead),
        in_specs=in_specs,
        out_specs=out_specs,
        out_shape=out_shape,
        scratch_shapes=[
            pltpu.VMEM((count, QLEN, HALF), jnp.bfloat16),
            pltpu.VMEM((count, QLEN, HALF), jnp.bfloat16),
            pltpu.VMEM((ROWS, 2 * LANES), jnp.bfloat16),
            pltpu.VMEM((2, LANES, KEYS), jnp.bfloat16),
            pltpu.VMEM((2, KEYS, 2 * LANES), jnp.bfloat16),
            pltpu.VMEM((2, STEP * QLEN, KEYS), jnp.bfloat16),
            pltpu.VMEM((QLEN, LANES), jnp.float32),
            pltpu.SMEM((1,), jnp.float32),
            pltpu.VMEM((STEP * QLEN, KEYS), jnp.float32),
            pltpu.VMEM((STEP * QLEN, KEYS), jnp.bfloat16),
            pltpu.SemaphoreType.DMA((count,)),
            pltpu.SemaphoreType.DMA((count,)),
            *extra,
        ],
        input_output_aliases=aliases,
        compiler_params=pltpu.CompilerParams(vmem_limit_bytes=50 * MIB),
        cost_estimate=pl.CostEstimate(
            flops=2 * count * QLEN * H * HD * (ROWS + QLEN),
            bytes_accessed=2 * count * QLEN * H * HD,
            transcendentals=count * QLEN * H * (ROWS + QLEN) // 2,
        ),
        name="attend",
    )(*operands)
    return got if ahead else got[0]


def project_kernel(ring, pieces, more, core_ref, place_ref, own_ref, other_ref, *rest):
    weights, rest = rest[:len(pieces)], rest[len(pieces):]
    out_ref = rest[-1]
    count = own_ref.shape[0]
    depth = weights[0].shape[0]
    core = core_ref[0]
    total = jnp.zeros((2 * count, weights[0].shape[1]), jnp.float32) if more else rest[0][...]
    for (part, i), weight in zip(pieces, weights):
        chip = chip_at(lax.rem(ring + place_ref[0] - i, ring), ring)
        at = pl.multiple_of((2 * chip + (1 - core if part else core)) * depth, depth)
        rows = jnp.concatenate([own_ref[:, pl.ds(at, depth)], other_ref[:, pl.ds(at, depth)]], axis=0)
        total += jnp.dot(rows, weight[...], preferred_element_type=jnp.float32)
    if more:
        out_ref[...] = total
        return
    result = total.astype(jnp.bfloat16)
    out_ref[pl.ds(pl.multiple_of(core * count, count), count)] = result[:count]
    out_ref[pl.ds(pl.multiple_of((1 - core) * count, count), count)] = result[count:]


def project(ring, core, place, own_rows, other_rows, weights, sums=None):
    count = own_rows.shape[0]
    pieces, blocks = tuple(weights), list(weights.values())
    width = blocks[0].shape[1]
    vmem = pl.BlockSpec(memory_space=pltpu.VMEM)
    smem = pl.BlockSpec(memory_space=pltpu.SMEM)
    more = sums is None
    operands = [own_rows, other_rows, *blocks] + ([] if more else [sums])
    return pl.pallas_call(
        functools.partial(project_kernel, ring, pieces, more),
        in_specs=[smem, smem] + [vmem] * len(operands),
        out_specs=vmem,
        out_shape=jax.ShapeDtypeStruct((2 * count, width), jnp.float32 if more else jnp.bfloat16),
        compiler_params=pltpu.CompilerParams(vmem_limit_bytes=16 * MIB),
        cost_estimate=pl.CostEstimate(
            flops=count * D * width, bytes_accessed=32 * D * width, transcendentals=0
        ),
        name="project",
    )(core.reshape(1), place, *operands)


def local(
    extent,
    passage_states,
    memory_queries,
    memory_gain,
    kv_weight,
    retrieval,
    question_queries,
    question_kv,
    question_lengths,
):
    me = lax.axis_index("pass")
    core, chip = me & 1, lax.div(me, 2)
    chips = extent // 2
    depth = kv_weight.shape[0]

    if chips != 8 or depth % LANES:
        memory_rows = pool(passage_states, memory_queries, memory_gain)
        whole_weight = lax.all_gather(kv_weight, "pass", axis=0, tiled=True)
        memory_kv = jnp.dot(memory_rows, whole_weight, preferred_element_type=jnp.float32)
        everything = lax.all_gather(memory_kv.astype(jnp.bfloat16), "pass", axis=0, tiled=True)
        halves = everything.reshape(-1, 2, 2, LANES).transpose(2, 0, 1, 3).reshape(2, -1, 2 * LANES)
        rest = (retrieval * MEM, question_lengths, question_queries)
        context = attend(jnp.int32(0), *rest, halves[0], question_kv)
        return attend(jnp.int32(1), *rest, halves[1], question_kv, context)

    place = place_of(chip, chips).reshape(1)
    order = [2 * line for line in range(chips // 2)] + [2 * line + 1 for line in range(chips // 2)][::-1]

    def to_partner(x):
        return lax.ppermute(x, "pass", [(i, i ^ 1) for i in range(extent)])

    def along(x, target):
        pairs = [(c, target(c // 2, c % 2)) for c in range(chips)]
        return lax.ppermute(x, "pass", [(2 * s + c, 2 * d + c) for s, d in pairs for c in range(2)])

    def along_ring(x, step):
        return along(x, lambda line, lane: order[(order.index(2 * line + lane) + step) % chips])

    def line_by_line(block):
        lines = chips // 2

        def lane_of(x):
            return along(x, lambda line, lane: 2 * line + 1 - lane)

        near = {k: along(block, lambda line, lane: 2 * ((line + k) % lines) + lane) for k in (2, 1, 3)}
        far = {0: lane_of(block)}
        far[3] = along(block, lambda line, lane: 2 * ((line + 3) % lines) + 1 - lane)
        far[1], far[2] = lane_of(near[1]), lane_of(near[2])
        return [block, near[1], near[2], near[3], far[0], far[1], far[2], far[3]]

    mine, theirs = split(core, kv_weight)
    up = [[mine], [to_partner(theirs)]]
    down = [[x[0]] for x in up]

    def blocks(turns):
        found = {}
        for part in range(2):
            for turn in turns:
                if turn < len(up[part]):
                    found[part, turn] = up[part][turn]
                if 0 < turn < len(down[part]):
                    found[part, chips - turn] = down[part][turn]
        return found

    for turn in range(1, chips // 2):
        for part in range(2):
            up[part].append(along_ring(up[part][-1], 1))
            down[part].append(along_ring(down[part][-1], -1))
        if turn == 1:
            rows = pool(passage_states, memory_queries, memory_gain)
            *hops, rows = lax.optimization_barrier((*(x[-1] for x in up + down), rows))
            for chain, hop in zip(up + down, hops):
                chain[-1] = hop
            other_rows = to_partner(rows)
        elif turn == 2:
            early = project(chips, core, place, rows, other_rows, blocks((0, 1)))
            down[1][-1], early = lax.optimization_barrier((down[1][-1], early))
    down[0].append(along_ring(down[0][-1], -1))
    up[1].append(along_ring(up[1][-1], 1))
    memory_kv = project(chips, core, place, rows, other_rows, blocks((2, 3, 4)), early)
    near = jnp.concatenate(line_by_line(memory_kv), axis=0)
    far = to_partner(near)

    lines = chips // 2
    of_chip = lax.div(retrieval, CHIP)
    back = lax.rem(lines + lax.div(chip, 2) - lax.div(of_chip, 2), lines)
    slot = back + lines * lax.rem(lax.rem(chip, 2) + lax.rem(of_chip, 2), 2)
    starts = (slot * CHIP + lax.rem(retrieval, CHIP)) * MEM
    rest = (starts, question_lengths, question_queries)
    context, begun = attend(core, *rest, near, question_kv, ahead=True)
    return attend(1 - core, *rest, far, question_kv, context, begun)


def solution(mesh):
    placed = (
        P(("groups", "pass"), None, None),
        P(),
        P(),
        P("pass", None),
        P(("groups", "pass"), None),
        P(("groups", "pass"), None, None),
        P(("groups", "pass"), None, None),
        P(("groups", "pass")),
    )
    return jax.shard_map(
        functools.partial(local, mesh.shape["pass"]),
        mesh=mesh,
        in_specs=placed,
        out_specs=P(("groups", "pass"), None, None),
        check_vma=False,
    )
```
